32 devices in a mesh: section: 2 (over core), seq: 16 (over z, y, x).
Axes of the slice: x: 2, y: 2, z: 4, core: 2. Of those that a mesh axis runs over, the one named last changes fastest.
Arguments:
- byte_values: int32 [3, 4096], P(None, 'seq'), may hold values from 0 to 255
- item_lengths: int32 [3, 4], replicated, may hold values from 0 to 4096, as said below
- embed_tables: bfloat16 [2, 256, 768], P('section'), may hold values from -6 to 6
- patch_weight: bfloat16 [6144, 768], P(('section', 'seq')), may hold values from -0.078125 to 0.078125
- norm_gains: float32 [2, 2, 768], P('section'), may hold values from 0.25 to 1.75
- norm_biases: float32 [2, 2, 768], P('section'), may hold values from -3 to 3
- heads_in: bfloat16 [2, 768, 2304], P('section'), may hold values from -0.21875 to 0.21875
- heads_out: bfloat16 [2, 768, 768], P('section'), may hold values from -0.875 to 0.875
- expand_weight: bfloat16 [2, 768, 3072], P('section'), may hold values from -0.21875 to 0.21875
- contract_weight: bfloat16 [2, 3072, 768], P('section'), may hold values from -0.109375 to 0.109375
- out_grad: bfloat16 [3, 4096, 768], P(None, 'seq'), may hold values from -6 to 6
Outputs:
- activations: bfloat16 [2, 3, 4096, 768], P('section', None, 'seq')
- table_grads: float32 [2, 256, 768], P('section', 'seq')
- patch_grads: float32 [6144, 768], P(('section', 'seq'))
- gain_grads: float32 [2, 2, 768], P('section', None, 'seq')
- bias_grads: float32 [2, 2, 768], P('section', None, 'seq')
- heads_in_grads: float32 [2, 768, 2304], P('section', 'seq')
- heads_out_grads: float32 [2, 768, 768], P('section', 'seq')
- expand_grads: float32 [2, 768, 3072], P('section', 'seq')
- contract_grads: float32 [2, 3072, 768], P('section', 'seq')
The draws below stay inside these ranges and needn't reach their ends.
Inputs may be any that keep to these rules, and one draw needn't show every extreme that they name: `item_lengths`: row m lists the byte lengths of the items of micro-batch m in order; a 0 is an empty slot; the items, each padded to whole patches, fit in 4096 bytes. In one micro-batch a single item fills all 4096 bytes and the other slots are empty; in the others every item has 1 to 1024 bytes.
All inputs are finite; a program needn't handle non-finite values.
Results may differ from the reference program's by a relative error of at most 0.02.
Values may be sent and summed in bfloat16 or wider, within the bound.
No kernel may reach another device: no remote copies, remote signals or barrier semaphores. Data moves between devices by JAX's collectives and lax.ppermute only.
A program may use at most 384 MiB of HBM per device.

```python
from functools import partial
import jax
import jax.numpy as jnp
from jax import lax

D = 768
HEADS = 12
HEAD_SIZE = 64
FF = 3072
VOCAB = 256
PATCH = 8
MB = 3
ITEMS = 4
NB = 4096
NP = 512


def draw_item_lengths(key, part):
    key = jax.random.fold_in(key, 7)
    full_key, rest_key = jax.random.split(key)
    full_batch = jax.random.randint(full_key, (), 0, MB)
    others = jax.random.randint(rest_key, (MB, ITEMS), 1, NB // ITEMS + 1)
    whole_row = jnp.where(jnp.arange(ITEMS) == 0, NB, 0)
    chosen = (jnp.arange(MB) == full_batch)[:, None]
    return jnp.where(chosen, whole_row[None, :], others).astype(jnp.int32)


def plant(result, own_key, low, top_value):
    longest = result.shape.index(max(result.shape))
    spots = []
    for shift in (0, 1):
        where = [jax.random.randint(jax.random.fold_in(own_key, axis), (), 0, length) for axis, length in enumerate(result.shape)]
        where[longest] = (where[longest] + shift) % result.shape[longest]
        spots.append(tuple(where))
    return result.at[spots[0]].set(low).at[spots[1]].set(top_value)


def steps_of(rng, shape, cuts, least, top_value):
    level = 1.0
    for dim, shards_of in cuts:
        heights = jax.random.uniform(jax.random.fold_in(jax.random.fold_in(rng, 6), dim), (shards_of,), jnp.float32, least / len(cuts), top_value / len(cuts))
        level = level * jnp.repeat(jnp.exp(heights), shape[dim] // shards_of).reshape((-1,) + (1,) * (len(shape) - 1 - dim))
    return level


def centred(own_key, dims, scale, reach, pieces=(), kind=jnp.bfloat16):
    entries = jax.random.normal(own_key, dims, jnp.float32) * scale
    if len(pieces) > 0:
        entries = steps_of(own_key, dims, pieces, -0.22, 0.18) * entries
    return jnp.clip(entries, min=-reach, max=reach).astype(kind)


def setup_inputs(seed: int = 0) -> dict:
    streams_of = jax.random.split(jax.random.key(seed), 12)
    byte_values = plant(jax.random.randint(streams_of[0], (MB, NB), 0, VOCAB), jax.random.fold_in(streams_of[0], 1), 0, VOCAB - 1).astype(jnp.int32)
    item_lengths = draw_item_lengths(jax.random.fold_in(streams_of[11], 71), 0)
    embed_tables = centred(streams_of[2], (2, VOCAB, D), 1.0, 6.0, ((0, 2),))
    patch_weight = centred(streams_of[3], (PATCH * D, D), (PATCH * D) ** -0.5, 0.078125, ((0, 32),))
    norm_gains = jnp.clip(1.0 + 0.15 * jax.random.normal(streams_of[4], (2, 2, D), jnp.float32), 0.25, 1.75)
    norm_biases = centred(streams_of[5], (2, 2, D), 0.5, 3.0, ((0, 2),), jnp.float32)
    heads_in = centred(streams_of[6], (2, D, 3 * D), D ** -0.5, 0.21875, ((0, 2),))
    heads_out = centred(streams_of[7], (2, D, D), (D // 16) ** -0.5, 0.875, ((0, 2),))
    expand_weight = centred(streams_of[8], (2, D, FF), D ** -0.5, 0.21875, ((0, 2),))
    contract_weight = centred(streams_of[9], (2, FF, D), FF ** -0.5, 0.109375, ((0, 2),))
    out_grad = centred(streams_of[10], (MB, NB, D), 1.0, 6.0, ((1, 16),))
    return {"byte_values": byte_values, "item_lengths": item_lengths, "embed_tables": embed_tables, "patch_weight": patch_weight, "norm_gains": norm_gains, "norm_biases": norm_biases, "heads_in": heads_in, "heads_out": heads_out, "expand_weight": expand_weight, "contract_weight": contract_weight, "out_grad": out_grad}


@jax.custom_vjp
def low(v):
    return lax.optimization_barrier(v.astype(jnp.bfloat16)).astype(jnp.float32)

@jax.custom_vjp
def low_back(v):
    return v

def low_keep(v):
    return (low(v), None)

def low_pass(kept, grad):
    return (grad,)

def back_keep(v):
    return (v, None)

def back_low(kept, grad):
    return (low(grad),)
low.defvjp(low_keep, low_pass)
low_back.defvjp(back_keep, back_low)
HIGHEST_PRECISION = lax.Precision.HIGHEST
EPSILON = 1e-05
MASKED = -1e+30

def matmul(former, latter):
    return jnp.dot(former, latter, precision=HIGHEST_PRECISION)

def layer_norm(values, norm_gain, norm_bias):
    average = lax.optimization_barrier(jnp.mean(values, axis=-1, keepdims=True))
    centered = values - average
    inverse_root = lax.rsqrt(lax.optimization_barrier(jnp.mean(centered * centered, axis=-1, keepdims=True)) + EPSILON)
    return centered * inverse_root * norm_gain + norm_bias

def locate(positions, lengths_row):
    padded = (lengths_row + PATCH - 1) // PATCH * PATCH
    item_ends = jnp.cumsum(padded).astype(jnp.int32)
    starts = item_ends - padded
    inside = (positions[:, None] >= starts[None, :]) & (positions[:, None] < item_ends[None, :])
    offsets = jnp.arange(ITEMS, dtype=jnp.int32)[None, :] - ITEMS
    owners = lax.optimization_barrier(jnp.sum(jnp.where(inside, offsets, 0), axis=1)) + ITEMS
    live_mask = jnp.any(inside & (positions[:, None] < (starts + lengths_row)[None, :]), axis=1)
    return (owners.astype(jnp.int32), live_mask)

def global_attend(queries, key_rows, value_rows, owners):
    row_count = queries.shape[0]
    places = jnp.arange(row_count, dtype=jnp.int32)
    allowed = (places[None, :] <= places[:, None]) & (owners[None, :] == owners[:, None])
    score_scale = HEAD_SIZE ** (-0.5)

    def one_head(operands):
        head_queries, head_keys, head_values = operands
        scores = low_back(matmul(head_queries, head_keys.T) * score_scale)
        probabilities = jax.nn.softmax(jnp.where(allowed, scores, MASKED), axis=-1)
        return matmul(low(probabilities), head_values)
    outputs = lax.map(jax.checkpoint(one_head), (jnp.swapaxes(queries, 0, 1), jnp.swapaxes(key_rows, 0, 1), jnp.swapaxes(value_rows, 0, 1)))
    return jnp.swapaxes(outputs, 0, 1).reshape(row_count, HEADS * HEAD_SIZE)

def local_attend(queries, key_rows, value_rows, live_mask):
    row_count = queries.shape[0]
    groups = row_count // PATCH
    shaped = (groups, PATCH, HEADS, HEAD_SIZE)
    scores = jnp.einsum('pqhd,pkhd->phqk', queries.reshape(shaped), key_rows.reshape(shaped), precision=HIGHEST_PRECISION) * HEAD_SIZE ** (-0.5)
    scores = low_back(scores)
    places = jnp.arange(PATCH, dtype=jnp.int32)
    causal = places[None, :] <= places[:, None]
    itself = places[None, :] == places[:, None]
    alive_keys = live_mask.reshape(groups, 1, 1, PATCH)
    allowed = causal[None, None] & (alive_keys | itself[None, None])
    probabilities = jax.nn.softmax(jnp.where(allowed, scores, MASKED), axis=-1)
    attended = jnp.einsum('phqk,pkhd->pqhd', low(probabilities), value_rows.reshape(shaped), precision=HIGHEST_PRECISION)
    return attended.reshape(row_count, HEADS * HEAD_SIZE)

def block(stream, layer_weights, attend):
    gain_rows, bias_rows, mix_in, mix_out, expand, contract = layer_weights
    row_count = stream.shape[0]
    normed = low(layer_norm(stream, gain_rows[0], bias_rows[0]))
    mixed_heads = low(low_back(matmul(normed, mix_in))).reshape(row_count, 3, HEADS, HEAD_SIZE)
    attended = low(low_back(attend(mixed_heads[:, 0], mixed_heads[:, 1], mixed_heads[:, 2])))
    middle = stream + low_back(matmul(attended, mix_out))
    normed_two = low(layer_norm(middle, gain_rows[1], bias_rows[1]))
    hidden = low(jax.nn.gelu(low_back(matmul(normed_two, expand))))
    return middle + low_back(matmul(hidden, contract))

def forward(tables, patch_weight, gain_rows, bias_rows, heads_in, heads_out, expand_weight, contract_weight, byte_values, item_lengths):
    vocabulary = jnp.arange(VOCAB, dtype=jnp.int32)
    positions = jnp.arange(NB, dtype=jnp.int32)
    global_layer = (gain_rows[0], bias_rows[0], heads_in[0], heads_out[0], expand_weight[0], contract_weight[0])
    local_layer = (gain_rows[1], bias_rows[1], heads_in[1], heads_out[1], expand_weight[1], contract_weight[1])
    finals = []
    firsts = []
    for micro_batch in range(MB):
        owners, live_mask = locate(positions, item_lengths[micro_batch])
        patch_owners = owners.reshape(NP, PATCH)[:, 0]
        onehot = (byte_values[micro_batch][:, None] == vocabulary[None, :]).astype(jnp.float32)
        embedded = low_back(matmul(onehot, tables[0]))
        stream = low_back(matmul(embedded.reshape(NP, PATCH * D), patch_weight))
        global_out = block(stream, global_layer, partial(global_attend, owners=patch_owners))
        sent_rows = low(low_back(global_out))
        earlier = jnp.concatenate([jnp.full((1,), -1, jnp.int32), patch_owners[:-1]])
        moved_rows = jnp.concatenate([jnp.zeros((1, D), jnp.float32), sent_rows[:-1]])
        shifted = jnp.where((earlier == patch_owners)[:, None], moved_rows, 0.0)
        local_in = low_back(matmul(onehot, tables[1])) + jnp.repeat(shifted, PATCH, axis=0)
        local_out = block(local_in, local_layer, partial(local_attend, live_mask=live_mask))
        live_rows = live_mask[:, None].astype(jnp.float32)
        finals.append(local_out * live_rows)
        firsts.append(jnp.repeat(sent_rows, PATCH, axis=0) * live_rows)
    return (jnp.stack(finals), jnp.stack(firsts))

def reference(byte_values, item_lengths, embed_tables, patch_weight, norm_gains, norm_biases, heads_in, heads_out, expand_weight, contract_weight, out_grad):
    floats = (embed_tables.astype(jnp.float32), patch_weight.astype(jnp.float32), norm_gains.astype(jnp.float32), norm_biases.astype(jnp.float32), heads_in.astype(jnp.float32), heads_out.astype(jnp.float32), expand_weight.astype(jnp.float32), contract_weight.astype(jnp.float32))

    def run(*params):
        return forward(*params, byte_values, item_lengths)
    finals, back_fn, firsts = jax.vjp(run, *floats, has_aux=True)
    gradients = back_fn(out_grad.astype(jnp.float32))
    activations = jnp.stack([firsts, finals]).astype(jnp.bfloat16)
    return (activations, gradients[0], gradients[1], gradients[2], gradients[3], gradients[4], gradients[5], gradients[6], gradients[7])
```

```python
from functools import partial

import jax
import jax.numpy as jnp
from jax import lax
from jax.experimental import pallas as pl
from jax.experimental.pallas import tpu as pltpu
from jax.sharding import PartitionSpec as P

HEADS = 12
HEAD_SIZE = 64
VOCAB = 256
PATCH = 8
ITEMS = 4
PAIRS = HEADS // 2
PAIR = 2 * HEAD_SIZE
SCALE = HEAD_SIZE ** (-0.5)
EPSILON = 1e-05
MASKED = -1e30
BLOCK = 128
VMEM = 48 * 1024 * 1024

bf16 = jnp.bfloat16
f32 = jnp.float32


def product(former, latter):
    return jnp.dot(former, latter, preferred_element_type=f32)


def transposed_product(former, latter):
    return lax.dot_general(former, latter, (((0,), (0,)), ((), ())), preferred_element_type=f32)


def product_transposed(former, latter):
    return lax.dot_general(former, latter, (((1,), (1,)), ((), ())), preferred_element_type=f32)


def normalise(values):
    average = jnp.mean(values, axis=-1, keepdims=True)
    centered = values - average
    inverse_root = lax.rsqrt(jnp.mean(centered * centered, axis=-1, keepdims=True) + EPSILON)
    return centered * inverse_root, inverse_root


def layer_norm(values, gain, bias):
    return normalise(values)[0] * gain + bias


def layer_norm_back(values, gain, grad):
    unit, inverse_root = normalise(values)
    scaled = grad * gain
    grad_values = inverse_root * (
        scaled
        - jnp.mean(scaled, axis=-1, keepdims=True)
        - unit * jnp.mean(scaled * unit, axis=-1, keepdims=True)
    )
    return grad_values, jnp.sum(grad * unit, axis=0), jnp.sum(grad, axis=0)


def locate(positions, lengths_row):
    padded = (lengths_row + PATCH - 1) // PATCH * PATCH
    item_ends = jnp.cumsum(padded)
    starts = item_ends - padded
    inside = (positions[:, None] >= starts[None, :]) & (positions[:, None] < item_ends[None, :])
    offsets = jnp.arange(ITEMS, dtype=jnp.int32)[None, :] - ITEMS
    owners = jnp.sum(jnp.where(inside, offsets, 0), axis=1) + ITEMS
    live_mask = jnp.any(inside & (positions[:, None] < (starts + lengths_row)[None, :]), axis=1)
    return (owners, live_mask)


def patch_mask(live_row):
    rows = lax.broadcasted_iota(jnp.int32, (BLOCK, BLOCK), 0)
    columns = lax.broadcasted_iota(jnp.int32, (BLOCK, BLOCK), 1)
    same = (rows // PATCH) == (columns // PATCH)
    return same & (columns <= rows) & ((live_row > 0) | (columns == rows))


def softmax_rows(scores):
    peak = jnp.max(scores, axis=-1, keepdims=True)
    exponents = jnp.exp(scores - peak)
    return exponents / jnp.sum(exponents, axis=-1, keepdims=True)


def local_forward_kernel(live_ref, mixed_ref, out_ref):
    width = HEADS * HEAD_SIZE
    allowed = patch_mask(live_ref[0])
    for pair in range(PAIRS):
        parts = []
        for head in (2 * pair, 2 * pair + 1):
            at = head * HEAD_SIZE
            queries = mixed_ref[:, at : at + HEAD_SIZE]
            keys = mixed_ref[:, width + at : width + at + HEAD_SIZE]
            values = mixed_ref[:, 2 * width + at : 2 * width + at + HEAD_SIZE]
            scores = jnp.where(allowed, product_transposed(queries, keys) * SCALE, MASKED)
            parts.append(product(softmax_rows(scores).astype(bf16), values))
        out_ref[:, pair * PAIR : (pair + 1) * PAIR] = jnp.concatenate(parts, axis=1).astype(bf16)


def local_backward_kernel(live_ref, mixed_ref, grad_ref, out_ref):
    width = HEADS * HEAD_SIZE
    allowed = patch_mask(live_ref[0])
    for pair in range(PAIRS):
        parts = ([], [], [])
        for head in (2 * pair, 2 * pair + 1):
            at = head * HEAD_SIZE
            queries = mixed_ref[:, at : at + HEAD_SIZE]
            keys = mixed_ref[:, width + at : width + at + HEAD_SIZE]
            values = mixed_ref[:, 2 * width + at : 2 * width + at + HEAD_SIZE]
            grads = grad_ref[:, at : at + HEAD_SIZE]
            scores = jnp.where(allowed, product_transposed(queries, keys) * SCALE, MASKED)
            probabilities = softmax_rows(scores)
            prob_grads = product_transposed(grads, values)
            delta = jnp.sum(probabilities * prob_grads, axis=-1, keepdims=True)
            score_grads = (probabilities * (prob_grads - delta)).astype(bf16)
            parts[0].append(product(score_grads, keys) * SCALE)
            parts[1].append(transposed_product(score_grads, queries) * SCALE)
            parts[2].append(transposed_product(probabilities.astype(bf16), grads))
        for which in range(3):
            at = which * width + pair * PAIR
            out_ref[:, at : at + PAIR] = jnp.concatenate(parts[which], axis=1).astype(bf16)


def local_attention(mixed, live_rows, grads=None):
    row_count, wide = mixed.shape
    width = wide // 3
    steps = row_count // BLOCK
    live_rows = live_rows.astype(jnp.int32).reshape(steps, 1, BLOCK)
    specs = [
        pl.BlockSpec((1, 1, BLOCK), lambda i: (i, 0, 0)),
        pl.BlockSpec((BLOCK, wide), lambda i: (i, 0)),
    ]
    if grads is None:
        return pl.pallas_call(
            local_forward_kernel,
            grid=(steps,),
            in_specs=specs,
            out_specs=pl.BlockSpec((BLOCK, width), lambda i: (i, 0)),
            out_shape=jax.ShapeDtypeStruct((row_count, width), bf16),
            compiler_params=pltpu.CompilerParams(vmem_limit_bytes=VMEM),
        )(live_rows, mixed)
    return pl.pallas_call(
        local_backward_kernel,
        grid=(steps,),
        in_specs=specs + [pl.BlockSpec((BLOCK, width), lambda i: (i, 0))],
        out_specs=pl.BlockSpec((BLOCK, wide), lambda i: (i, 0)),
        out_shape=jax.ShapeDtypeStruct((row_count, wide), bf16),
        compiler_params=pltpu.CompilerParams(vmem_limit_bytes=VMEM),
    )(live_rows, mixed, grads)


def causal_mask(start, owner_column, owner_row):
    shape = (BLOCK, owner_row.shape[1])
    rows = lax.broadcasted_iota(jnp.int32, shape, 0) + start
    columns = lax.broadcasted_iota(jnp.int32, shape, 1)
    return (columns <= rows) & (owner_column == owner_row)


def global_forward_kernel(column_ref, row_ref, qkv_ref, out_ref):
    start = pl.multiple_of(pl.program_id(0) * BLOCK, BLOCK)
    allowed = causal_mask(start, column_ref[...], row_ref[...])
    parts = []
    for head in range(2):
        at = head * HEAD_SIZE
        queries = qkv_ref[pl.ds(start, BLOCK), at : at + HEAD_SIZE]
        keys = qkv_ref[:, PAIR + at : PAIR + at + HEAD_SIZE]
        values = qkv_ref[:, 2 * PAIR + at : 2 * PAIR + at + HEAD_SIZE]
        scores = jnp.where(allowed, product_transposed(queries, keys) * SCALE, MASKED)
        parts.append(product(softmax_rows(scores).astype(bf16), values))
    out_ref[...] = jnp.concatenate(parts, axis=1).astype(bf16)


def global_backward_kernel(column_ref, row_ref, qkv_ref, grad_ref, out_ref, key_sum, value_sum):
    step = pl.program_id(0)
    start = pl.multiple_of(step * BLOCK, BLOCK)
    allowed = causal_mask(start, column_ref[...], row_ref[...])

    @pl.when(step == 0)
    def _():
        key_sum[...] = jnp.zeros_like(key_sum)
        value_sum[...] = jnp.zeros_like(value_sum)

    parts = ([], [], [])
    for head in range(2):
        at = head * HEAD_SIZE
        queries = qkv_ref[pl.ds(start, BLOCK), at : at + HEAD_SIZE]
        keys = qkv_ref[:, PAIR + at : PAIR + at + HEAD_SIZE]
        values = qkv_ref[:, 2 * PAIR + at : 2 * PAIR + at + HEAD_SIZE]
        grads = grad_ref[:, at : at + HEAD_SIZE]
        scores = jnp.where(allowed, product_transposed(queries, keys) * SCALE, MASKED)
        probabilities = softmax_rows(scores)
        prob_grads = product_transposed(grads, values)
        delta = jnp.sum(probabilities * prob_grads, axis=-1, keepdims=True)
        score_grads = (probabilities * (prob_grads - delta)).astype(bf16)
        parts[0].append(product(score_grads, keys) * SCALE)
        parts[1].append(transposed_product(score_grads, queries) * SCALE)
        parts[2].append(transposed_product(probabilities.astype(bf16), grads))
    out_ref[pl.ds(start, BLOCK), 0:PAIR] = jnp.concatenate(parts[0], axis=1).astype(bf16)
    key_sum[...] += jnp.concatenate(parts[1], axis=1)
    value_sum[...] += jnp.concatenate(parts[2], axis=1)

    @pl.when(step == pl.num_programs(0) - 1)
    def _():
        out_ref[:, PAIR : 2 * PAIR] = key_sum[...].astype(bf16)
        out_ref[:, 2 * PAIR : 3 * PAIR] = value_sum[...].astype(bf16)


def global_attention(qkv, owners, grads=None):
    count = qkv.shape[0]
    column, row = owners[:, None], owners[None, :]
    specs = [
        pl.BlockSpec((BLOCK, 1), lambda i: (i, 0)),
        pl.BlockSpec((1, count), lambda i: (0, 0)),
        pl.BlockSpec((count, 3 * PAIR), lambda i: (0, 0)),
    ]
    blocks = pl.BlockSpec((BLOCK, PAIR), lambda i: (i, 0))
    if grads is None:
        return pl.pallas_call(
            global_forward_kernel,
            grid=(count // BLOCK,),
            in_specs=specs,
            out_specs=blocks,
            out_shape=jax.ShapeDtypeStruct((count, PAIR), bf16),
            compiler_params=pltpu.CompilerParams(vmem_limit_bytes=VMEM),
        )(column, row, qkv)
    return pl.pallas_call(
        global_backward_kernel,
        grid=(count // BLOCK,),
        in_specs=specs + [blocks],
        out_specs=pl.BlockSpec((count, 3 * PAIR), lambda i: (0, 0)),
        out_shape=jax.ShapeDtypeStruct((count, 3 * PAIR), bf16),
        scratch_shapes=[pltpu.VMEM((count, PAIR), f32), pltpu.VMEM((count, PAIR), f32)],
        compiler_params=pltpu.CompilerParams(vmem_limit_bytes=VMEM),
    )(column, row, qkv, grads)


def section_send(x, origin, target, pairs):
    count = lax.axis_size("seq")
    joint = [(origin * count + i, target * count + j) for i, j in pairs]
    return lax.ppermute(x, ("section", "seq"), joint)


def scatter_sum(parts, section, order):
    count = lax.axis_size("seq")
    place = lax.axis_index("seq")
    bits = list(range(count.bit_length() - 1))[::-1]
    running = parts.reshape((2,) * len(bits) + parts.shape[1:])
    for step, bit in enumerate(order):
        axis = bits.index(bit)
        bits.pop(axis)
        mine = (place >> bit) & 1
        kept = lax.dynamic_index_in_dim(running, mine, axis, keepdims=False)
        leaving = lax.dynamic_index_in_dim(running, 1 - mine, axis, keepdims=False)
        pairs = [(i, i ^ (1 << bit)) for i in range(count)]
        arrived = section_send(leaving.astype(bf16), section, section, pairs)
        running = kept.astype(f32) + arrived.astype(f32)
        if step + 1 < len(order):
            running = running.astype(bf16)
    return running


def feed_forward(stream, attended, gains, biases, heads_out, expand, contract):
    middle = stream + product(attended, heads_out)
    normed_two = layer_norm(middle, gains[1], biases[1]).astype(bf16)
    upward = product(normed_two, expand)
    hidden = jax.nn.gelu(upward).astype(bf16)
    result = middle + product(hidden, contract)
    return result, (middle, normed_two, upward, hidden)


def feed_backward(grad_result, kept, attended, gains, heads_out, expand, contract):
    middle, normed_two, upward, hidden = kept
    branch = grad_result.astype(bf16)
    grad_contract = transposed_product(hidden, branch).astype(bf16)
    grad_hidden = product_transposed(branch, contract)
    grad_upward = jax.vjp(jax.nn.gelu, upward)[1](grad_hidden)[0].astype(bf16)
    grad_expand = transposed_product(normed_two, grad_upward).astype(bf16)
    grad_normed_two = product_transposed(grad_upward, expand)
    grad_middle, gain_two, bias_two = layer_norm_back(middle, gains[1], grad_normed_two)
    grad_middle = grad_middle + grad_result
    attend_branch = grad_middle.astype(bf16)
    grad_heads_out = transposed_product(attended, attend_branch).astype(bf16)
    grad_attended = product_transposed(attend_branch, heads_out).astype(bf16)
    return grad_middle, grad_attended, (gain_two, bias_two, grad_heads_out, grad_expand, grad_contract)


def heads_backward(grad_mixed, grad_middle, stream, normed, gains, heads_in):
    grad_heads_in = transposed_product(normed, grad_mixed).astype(bf16)
    grad_normed = product_transposed(grad_mixed, heads_in)
    grad_stream, gain_one, bias_one = layer_norm_back(stream, gains[0], grad_normed)
    return grad_stream + grad_middle, (gain_one, bias_one, grad_heads_in)


def on_device(
    byte_values,
    item_lengths,
    embed_tables,
    patch_weight,
    norm_gains,
    norm_biases,
    heads_in,
    heads_out,
    expand_weight,
    contract_weight,
    out_grad,
):
    place = lax.axis_index("seq")
    count = lax.axis_size("seq")
    section = lax.axis_index("section")
    is_global = section == 0
    batches, byte_rows = byte_values.shape
    patch_rows = byte_rows // PATCH
    width = heads_out.shape[2]
    rows = batches * patch_rows
    total_patches = patch_rows * count
    gains, biases = norm_gains[0], norm_biases[0]
    heads_in, heads_out = heads_in[0], heads_out[0]
    expand, contract = expand_weight[0], contract_weight[0]
    own_table = embed_tables[0]
    straight = [(i, i) for i in range(count)]
    vocabulary = jnp.arange(VOCAB, dtype=jnp.int32)

    def onehot_of(ids):
        return (ids[:, None] == vocabulary[None, :]).astype(bf16)

    quarters = PATCH // 2
    span = count // quarters
    group, member = place // span, place % span
    shard_rows = patch_weight.shape[0]
    byte_weight = jnp.zeros((span * shard_rows, width), bf16)
    byte_weight = lax.dynamic_update_slice(byte_weight, patch_weight, (member * shard_rows, 0))
    for k in range(1, span):
        piece = lax.ppermute(patch_weight, "seq", [(i, i ^ k) for i in range(count)])
        byte_weight = lax.dynamic_update_slice(byte_weight, piece, ((member ^ k) * shard_rows, 0))
    global_table = jnp.where(
        is_global, own_table, section_send(own_table, 0, 1, straight)
    )
    which_byte = section * quarters + group
    byte_ids = []
    for k in range(quarters):
        theirs = byte_values
        if k:
            theirs = lax.ppermute(byte_values, "seq", [(i, i ^ (k * span)) for i in range(count)])
        theirs = theirs.reshape(rows, PATCH)
        byte_ids.append(lax.dynamic_index_in_dim(theirs, which_byte, 1, keepdims=False))
    patch_onehot = onehot_of(jnp.concatenate(byte_ids))
    embedded = product(patch_onehot, global_table).astype(bf16)
    shares = product(embedded, byte_weight)
    shares = shares + section_send(shares.astype(bf16), 1, 0, straight).astype(f32)
    shares = shares.reshape(quarters, rows, width)
    stream = shares[0]
    for k in range(1, quarters):
        pairs = [(i, i ^ (k * span)) for i in range(count)]
        stream = stream + section_send(shares[k].astype(bf16), 0, 0, pairs).astype(f32)

    tasks = batches * PAIRS
    first_tasks = min(tasks, count)
    spare_tasks = tasks - first_tasks

    def to_tasks(blocks):
        columns = blocks.shape[2]
        slots = jnp.pad(blocks[:first_tasks], ((0, count - first_tasks), (0, 0), (0, 0)))
        if spare_tasks:
            spare = section_send(blocks[first_tasks:], 0, 1, straight)
            spare = jnp.pad(spare, ((0, count - spare_tasks), (0, 0), (0, 0)))
            slots = jnp.where(is_global, slots, spare)
        landed = lax.all_to_all(slots, "seq", 0, 0)
        return landed.reshape(total_patches, columns)

    def from_tasks(results):
        columns = results.shape[1]
        slots = lax.all_to_all(results.reshape(count, patch_rows, columns), "seq", 0, 0)
        blocks = slots[:first_tasks]
        if spare_tasks:
            spare = section_send(slots[:spare_tasks], 1, 0, straight)
            blocks = jnp.concatenate([blocks, spare])
        return blocks

    def by_pair(values, parts):
        split = values.reshape(batches, patch_rows, parts, PAIRS, PAIR)
        return jnp.transpose(split, (0, 3, 1, 2, 4)).reshape(tasks, patch_rows, parts * PAIR)

    def from_pairs(blocks, parts):
        split = blocks.reshape(batches, PAIRS, patch_rows, parts, PAIR)
        return jnp.transpose(split, (0, 2, 3, 1, 4)).reshape(rows, parts * width)

    task = jnp.minimum(jnp.where(is_global, place, first_tasks + place), tasks - 1)
    task_lengths = lax.dynamic_index_in_dim(item_lengths, task // PAIRS, 0, keepdims=False)
    task_owners = locate(jnp.arange(total_patches, dtype=jnp.int32) * PATCH, task_lengths)[0]

    normed = layer_norm(stream, gains[0], biases[0]).astype(bf16)
    mixed = product(normed, heads_in).astype(bf16)
    qkv = to_tasks(by_pair(mixed, 3))
    attended = from_pairs(from_tasks(global_attention(qkv, task_owners)), 1)
    global_out, global_kept = feed_forward(
        stream, attended, gains, biases, heads_out, expand, contract
    )
    sent = global_out.astype(bf16).reshape(batches, patch_rows, width)

    byte_places = place * byte_rows + jnp.arange(byte_rows, dtype=jnp.int32)
    patch_places = byte_places[::PATCH]
    live_rows = jnp.stack([locate(byte_places, item_lengths[m])[1] for m in range(batches)])
    same_item = jnp.stack(
        [
            locate(patch_places, item_lengths[m])[0]
            == locate(patch_places - PATCH, item_lengths[m])[0]
            for m in range(batches)
        ]
    )[:, :, None]
    onward = [(i, i + 1) for i in range(count - 1)]
    backward = [(i + 1, i) for i in range(count - 1)]
    near = section_send(sent, 0, 1, straight)
    edge = section_send(sent[:, -1:], 0, 1, onward)
    shifted = jnp.concatenate([edge, near[:, :-1]], axis=1)
    shifted = jnp.where(same_item, shifted, jnp.zeros((), bf16))

    byte_count = batches * byte_rows
    live_column = live_rows.reshape(byte_count, 1)
    local_onehot = onehot_of(byte_values.reshape(byte_count))
    spread = jnp.broadcast_to(
        shifted.astype(f32).reshape(rows, 1, width), (rows, PATCH, width)
    ).reshape(byte_count, width)
    local_stream = product(local_onehot, own_table) + spread
    local_normed = layer_norm(local_stream, gains[0], biases[0]).astype(bf16)
    local_mixed = product(local_normed, heads_in).astype(bf16)
    local_attended = local_attention(local_mixed, live_rows)
    local_out, local_kept = feed_forward(
        local_stream, local_attended, gains, biases, heads_out, expand, contract
    )
    own_sent = jnp.broadcast_to(
        sent.reshape(rows, 1, width), (rows, PATCH, width)
    ).reshape(byte_count, width)
    activations = jnp.where(
        live_column,
        jnp.where(is_global, own_sent, local_out.astype(bf16)),
        jnp.zeros((), bf16),
    ).reshape(batches, byte_rows, width)

    local_grad_out = jnp.where(
        live_column, out_grad.reshape(byte_count, width).astype(f32), 0.0
    )
    local_grad_middle, local_grad_attended, local_tops = feed_backward(
        local_grad_out, local_kept, local_attended, gains, heads_out, expand, contract
    )
    local_grad_mixed = local_attention(local_mixed, live_rows, local_grad_attended)
    local_grad_stream, local_bottoms = heads_backward(
        local_grad_mixed, local_grad_middle, local_stream, local_normed, gains, heads_in
    )
    local_table_grad = transposed_product(local_onehot, local_grad_stream.astype(bf16))
    grad_shifted = jnp.sum(local_grad_stream.reshape(batches, patch_rows, PATCH, width), axis=2)
    grad_shifted = jnp.where(same_item, grad_shifted.astype(bf16), jnp.zeros((), bf16))

    near_back = section_send(grad_shifted, 1, 0, straight)
    edge_back = section_send(grad_shifted[:, :1], 1, 0, backward)
    grad_sent = jnp.concatenate([near_back[:, 1:], edge_back], axis=1)
    grad_sent = grad_sent.reshape(rows, width).astype(f32)
    grad_middle, grad_attended, tops = feed_backward(
        grad_sent, global_kept, attended, gains, heads_out, expand, contract
    )
    task_grads = to_tasks(by_pair(grad_attended, 1))
    grad_mixed = from_pairs(
        from_tasks(global_attention(qkv, task_owners, task_grads)), 3
    )
    grad_stream, bottoms = heads_backward(grad_mixed, grad_middle, stream, normed, gains, heads_in)

    own_rows = grad_stream.astype(bf16)
    gathered = [own_rows]
    for k in range(1, quarters):
        pairs = [(i, i ^ (k * span)) for i in range(count)]
        gathered.append(section_send(own_rows, 0, 0, pairs))
    gathered = jnp.concatenate(gathered)
    gathered = jnp.where(is_global, gathered, section_send(gathered, 0, 1, straight))
    patch_share = transposed_product(embedded, gathered).astype(bf16)
    patch_share = patch_share.reshape(span, shard_rows, width)
    patch_grads = lax.dynamic_index_in_dim(patch_share, member, 0, keepdims=False).astype(f32)
    for k in range(1, span):
        leaving = lax.dynamic_index_in_dim(patch_share, member ^ k, 0, keepdims=False)
        patch_grads = patch_grads + lax.ppermute(
            leaving, "seq", [(i, i ^ k) for i in range(count)]
        ).astype(f32)
    grad_embedded = product_transposed(gathered, byte_weight).astype(bf16)
    table_share = transposed_product(patch_onehot, grad_embedded)
    table_share = table_share + section_send(
        table_share.astype(bf16), 1, 0, straight
    ).astype(f32)

    depth = count.bit_length() - 1
    up = list(range(depth))
    swapped = [1, 0] + up[2:]

    def reduced(from_section, grads):
        gain_two, bias_two, grad_heads_out, grad_expand, grad_contract = grads[0]
        gain_one, bias_one, grad_heads_in = grads[1]
        small = jnp.stack([gain_one, gain_two, bias_one, bias_two])
        small = jnp.transpose(small.reshape(4, count, width // count), (1, 0, 2))

        def split(x):
            return x.reshape(count, x.shape[0] // count, x.shape[1])

        contract_sum = scatter_sum(split(grad_contract), from_section, up)
        expand_sum = scatter_sum(split(grad_expand), from_section, swapped)
        out_sum = scatter_sum(split(grad_heads_out), from_section, up)
        in_sum = scatter_sum(split(grad_heads_in), from_section, swapped)
        table_sum = scatter_sum(split(grads[2].astype(bf16)), from_section, up)
        small_sum = scatter_sum(small.astype(bf16), from_section, up)
        return table_sum, small_sum, in_sum, out_sum, expand_sum, contract_sum

    local_sums = reduced(1, (local_tops, local_bottoms, local_table_grad))
    global_sums = reduced(0, (tops, bottoms, table_share))
    table_sum, small_sum, in_sum, out_sum, expand_sum, contract_sum = (
        jnp.where(is_global, upper, lower) for upper, lower in zip(global_sums, local_sums)
    )
    return (
        activations[None],
        table_sum[None],
        patch_grads,
        small_sum[None, 0:2],
        small_sum[None, 2:4],
        in_sum[None],
        out_sum[None],
        expand_sum[None],
        contract_sum[None],
    )


def solution(mesh):
    placed = (
        P(None, "seq"),
        P(),
        P("section", None, None),
        P(("section", "seq"), None),
        P("section", None, None),
        P("section", None, None),
        P("section", None, None),
        P("section", None, None),
        P("section", None, None),
        P("section", None, None),
        P(None, "seq", None),
    )
    return jax.shard_map(
        on_device,
        mesh=mesh,
        in_specs=placed,
        out_specs=(
            P("section", None, "seq", None),
            P("section", "seq", None),
            P(("section", "seq"), None),
            P("section", None, "seq"),
            P("section", None, "seq"),
            P("section", "seq", None),
            P("section", "seq", None),
            P("section", "seq", None),
            P("section", "seq", None),
        ),
        check_vma=False,
    )
```

```python
from functools import partial

import jax
import jax.numpy as jnp
from jax import lax
from jax.experimental import pallas as pl
from jax.experimental.pallas import tpu as pltpu
from jax.sharding import PartitionSpec as P

HEADS = 12
HEAD_SIZE = 64
VOCAB = 256
PATCH = 8
ITEMS = 4
PAIRS = HEADS // 2
PAIR = 2 * HEAD_SIZE
SCALE = HEAD_SIZE ** (-0.5)
EPSILON = 1e-05
MASKED = -1e30
BLOCK = 128
TILE = 384
GROUPS = 16
VMEM = 60 * 1024 * 1024

bf16 = jnp.bfloat16
f32 = jnp.float32


def product(former, latter):
    return jnp.dot(former, latter, preferred_element_type=f32)


def transposed_product(former, latter):
    return lax.dot_general(former, latter, (((0,), (0,)), ((), ())), preferred_element_type=f32)


def product_transposed(former, latter):
    return lax.dot_general(former, latter, (((1,), (1,)), ((), ())), preferred_element_type=f32)


def normalise(values):
    average = jnp.mean(values, axis=-1, keepdims=True)
    centered = values - average
    inverse_root = lax.rsqrt(jnp.mean(centered * centered, axis=-1, keepdims=True) + EPSILON)
    return centered * inverse_root, inverse_root


def layer_norm(values, gain, bias):
    return normalise(values)[0] * gain + bias


def layer_norm_back(values, gain, grad):
    unit, inverse_root = normalise(values)
    scaled = grad * gain
    grad_values = inverse_root * (
        scaled
        - jnp.mean(scaled, axis=-1, keepdims=True)
        - unit * jnp.mean(scaled * unit, axis=-1, keepdims=True)
    )
    return (
        grad_values,
        jnp.sum(grad * unit, axis=0, keepdims=True),
        jnp.sum(grad, axis=0, keepdims=True),
    )


def locate(positions, lengths_row):
    padded = (lengths_row + PATCH - 1) // PATCH * PATCH
    item_ends = jnp.cumsum(padded)
    starts = item_ends - padded
    inside = (positions[:, None] >= starts[None, :]) & (positions[:, None] < item_ends[None, :])
    offsets = jnp.arange(ITEMS, dtype=jnp.int32)[None, :] - ITEMS
    owners = jnp.sum(jnp.where(inside, offsets, 0), axis=1) + ITEMS
    live_mask = jnp.any(inside & (positions[:, None] < (starts + lengths_row)[None, :]), axis=1)
    return (owners, live_mask)


def slot_of(q, count, swap):
    if count != GROUPS:
        return q
    bits = [(q >> b) & 1 for b in range(GROUPS.bit_length() - 1)]
    if swap:
        bits[0], bits[1] = bits[1], bits[0]
    slot = 0
    for bit in bits:
        slot = 2 * slot + bit
    return slot


def store_rows(buffer, value, count, swap, start, columns=slice(None)):
    rows = value.shape[0] // GROUPS
    for q in range(GROUPS):
        buffer[slot_of(q, count, swap), pl.ds(start, rows), columns] = value[
            q * rows : (q + 1) * rows
        ].astype(bf16)


def patch_bias(live_row):
    rows = lax.broadcasted_iota(jnp.int32, (BLOCK, BLOCK), 0)
    columns = lax.broadcasted_iota(jnp.int32, (BLOCK, BLOCK), 1)
    same = (rows // PATCH) == (columns // PATCH)
    allowed = same & (columns <= rows) & ((live_row > 0) | (columns == rows))
    bias = jnp.where(allowed, 0.0, MASKED)
    return jnp.concatenate([bias, bias], axis=0)


def softmax_rows(scores):
    peak = jnp.max(scores, axis=-1, keepdims=True)
    exponents = jnp.exp(scores - peak)
    return exponents * (1.0 / jnp.sum(exponents, axis=-1, keepdims=True))


def lane_masks():
    lanes = lax.broadcasted_iota(jnp.int32, (1, PAIR), 1)
    low = jnp.where(lanes < HEAD_SIZE, 1.0, 0.0)
    return lanes < HEAD_SIZE, low.astype(bf16), (1.0 - low).astype(bf16)


def stacked(values, low, high, scale=1.0):
    return jnp.concatenate([values * (low * scale), values * (high * scale)], axis=0)


def unstacked(values, is_low):
    half = values.shape[0] // 2
    return jnp.where(is_low, values[:half], values[half:])


def pair_forward(queries, keys, values, bias, masks):
    is_low, low, high = masks
    scores = product_transposed(stacked(queries, low, high, SCALE), keys) + bias
    return unstacked(product(softmax_rows(scores).astype(bf16), values), is_low)


def pair_backward(queries, keys, values, grads, bias, masks):
    is_low, low, high = masks
    both = stacked(queries, low, high, SCALE)
    both_grads = stacked(grads, low, high)
    probabilities = softmax_rows(product_transposed(both, keys) + bias)
    prob_grads = product_transposed(both_grads, values)
    delta = jnp.sum(probabilities * prob_grads, axis=-1, keepdims=True)
    score_grads = (probabilities * (prob_grads - delta)).astype(bf16)
    return (
        unstacked(product(score_grads, keys), is_low) * SCALE,
        transposed_product(score_grads, both),
        transposed_product(probabilities.astype(bf16), both_grads),
    )


def gelu_and_slope(x):
    root = 0.7978845608028654
    cubic = 0.044715
    square = x * x
    bent = jnp.tanh(x * (root + (root * cubic) * square))
    half = 0.5 * (1.0 + bent)
    slope = half + (0.5 * x) * (1.0 - bent * bent) * (root + (3.0 * root * cubic) * square)
    return x * half, slope


def fetch(section, own, arrived, target, sem):
    @pl.when(section == 0)
    def _():
        pltpu.make_async_copy(arrived, target, sem).start()

    @pl.when(section != 0)
    def _():
        pltpu.make_async_copy(own, target, sem).start()


def leave(section, first, second, keep, send, sems):
    @pl.when(section == 0)
    def _():
        pltpu.make_async_copy(first, keep, sems.at[0]).start()
        pltpu.make_async_copy(second, send, sems.at[1]).start()

    @pl.when(section != 0)
    def _():
        pltpu.make_async_copy(second, keep, sems.at[0]).start()
        pltpu.make_async_copy(first, send, sems.at[1]).start()

    pltpu.make_async_copy(first, keep, sems.at[0]).wait()
    pltpu.make_async_copy(second, send, sems.at[1]).wait()


def local_first_kernel(
    count,
    section_ref,
    ids_ref,
    table_ref,
    shifted_ref,
    gains_ref,
    biases_ref,
    live_row_ref,
    live_column_ref,
    out_grad_ref,
    own_in,
    own_out,
    own_expand,
    own_contract,
    new_in,
    new_out,
    new_expand,
    new_contract,
    act_ref,
    stream_ref,
    normed_ref,
    mixed_ref,
    attended_ref,
    grad_middle_ref,
    small_ref,
    keep_ref,
    send_ref,
    w_in,
    w_out,
    w_expand,
    w_contract,
    middle_ref,
    normed_two_ref,
    branch_ref,
    hidden_ref,
    slope_ref,
    upward_ref,
    contract_sum,
    expand_sum,
    sems,
    out_sems,
):
    section = section_ref[0]
    fetch(section, own_in, new_in, w_in, sems.at[0])
    fetch(section, own_out, new_out, w_out, sems.at[1])
    fetch(section, own_expand, new_expand, w_expand, sems.at[2])
    fetch(section, own_contract, new_contract, w_contract, sems.at[3])
    rows, width = act_ref.shape
    steps = rows // BLOCK
    hidden_width = hidden_ref.shape[1]
    patches = shifted_ref.shape[0]

    def row_block(i):
        return pl.ds(pl.multiple_of(i * BLOCK, BLOCK), BLOCK)

    def column_block(i, size):
        return pl.ds(pl.multiple_of(i * size, 128), size)

    @pl.loop(0, steps)
    def _(i):
        at = row_block(i)
        vocabulary = lax.broadcasted_iota(jnp.int32, (BLOCK, VOCAB), 1)
        onehot = jnp.where(ids_ref[at, :] == vocabulary, 1.0, 0.0).astype(bf16)
        places = lax.broadcasted_iota(jnp.int32, (BLOCK, patches), 0) // PATCH
        columns = lax.broadcasted_iota(jnp.int32, (BLOCK, patches), 1)
        spread = jnp.where(places + i * (BLOCK // PATCH) == columns, 1.0, 0.0).astype(bf16)
        stream = product(onehot, table_ref[...]) + product(spread, shifted_ref[...])
        stream_ref[at, :] = stream
        normed_ref[at, :] = layer_norm(stream, gains_ref[0:1], biases_ref[0:1]).astype(bf16)
        branch_ref[at, :] = jnp.where(
            live_column_ref[at, :] > 0, out_grad_ref[at, :].astype(f32), 0.0
        ).astype(bf16)

    pltpu.make_async_copy(own_in, w_in, sems.at[0]).wait()

    @pl.loop(0, 3 * width // TILE)
    def _(i):
        at = column_block(i, TILE)
        mixed_ref[:, at] = product(normed_ref[...], w_in[:, at]).astype(bf16)

    masks = lane_masks()

    @pl.loop(0, steps)
    def _(i):
        at = row_block(i)
        bias = patch_bias(live_row_ref[i])
        for pair in range(PAIRS):
            first = slice(pair * PAIR, (pair + 1) * PAIR)
            second = slice(width + pair * PAIR, width + (pair + 1) * PAIR)
            third = slice(2 * width + pair * PAIR, 2 * width + (pair + 1) * PAIR)
            attended_ref[at, first] = pair_forward(
                mixed_ref[at, first], mixed_ref[at, second], mixed_ref[at, third], bias, masks
            ).astype(bf16)

    pltpu.make_async_copy(own_out, w_out, sems.at[1]).wait()

    @pl.loop(0, steps)
    def _(i):
        at = row_block(i)
        middle = stream_ref[at, :] + product(attended_ref[at, :], w_out[...])
        middle_ref[at, :] = middle
        normed_two_ref[at, :] = layer_norm(middle, gains_ref[1:2], biases_ref[1:2]).astype(bf16)

    pltpu.make_async_copy(own_expand, w_expand, sems.at[2]).wait()

    @pl.loop(0, hidden_width // TILE)
    def _(i):
        at = column_block(i, TILE)
        hidden, slope = gelu_and_slope(product(normed_two_ref[...], w_expand[:, at]))
        hidden_ref[:, at] = hidden.astype(bf16)
        slope_ref[:, at] = slope.astype(bf16)

    pltpu.make_async_copy(own_contract, w_contract, sems.at[3]).wait()

    @pl.loop(0, width // 256)
    def _(i):
        at = column_block(i, 256)
        result = middle_ref[:, at] + product(hidden_ref[...], w_contract[:, at])
        act_ref[:, at] = jnp.where(live_column_ref[...] > 0, result, 0.0).astype(bf16)

    tile_rows = TILE // (hidden_width // GROUPS)
    halves = width // TILE

    @pl.loop(0, hidden_width // width)
    def _(chunk):
        for half in range(halves):
            i = chunk * halves + half
            at = column_block(i, TILE)
            grad_hidden = product_transposed(branch_ref[...], w_contract[at, :])
            grad_upward = (grad_hidden * slope_ref[:, at].astype(f32)).astype(bf16)
            upward_ref[:, at] = grad_upward
            part = transposed_product(normed_two_ref[...], grad_upward)
            store_rows(
                expand_sum,
                part,
                count,
                True,
                pl.multiple_of(chunk * (width // GROUPS), 16),
                slice(half * TILE, (half + 1) * TILE),
            )

    for i in range(hidden_width // TILE):
        part = transposed_product(hidden_ref[:, i * TILE : (i + 1) * TILE], branch_ref[...])
        size = TILE // tile_rows
        for k in range(tile_rows):
            slot = slot_of(i * tile_rows + k, count, False)
            contract_sum[slot] = part[k * size : (k + 1) * size].astype(bf16)

    @pl.loop(0, width // 256)
    def _(i):
        at = column_block(i, 256)
        grad_middle_ref[:, at] = product_transposed(upward_ref[...], w_expand[at, :])

    def norm_back(i, sums):
        at = row_block(i)
        grad = grad_middle_ref[at, :]
        back, gain, bias = layer_norm_back(middle_ref[at, :], gains_ref[1:2], grad)
        grad_middle_ref[at, :] = back + branch_ref[at, :].astype(f32)
        return sums[0] + gain, sums[1] + bias

    zero = jnp.zeros((1, width), f32)
    gain, bias = lax.fori_loop(0, steps, norm_back, (zero, zero))
    small_ref[...] = jnp.concatenate([gain, bias], axis=0)
    leave(section, contract_sum, expand_sum, keep_ref, send_ref, out_sems)


def local_second_kernel(
    count,
    section_ref,
    ids_ref,
    same_ref,
    gains_ref,
    live_row_ref,
    stream_ref,
    normed_ref,
    mixed_ref,
    attended_ref,
    grad_middle_ref,
    small_ref,
    own_in,
    own_out,
    new_in,
    new_out,
    shifted_ref,
    keep_ref,
    send_ref,
    w_in,
    w_out,
    branch_ref,
    grad_attended_ref,
    grad_mixed_ref,
    grad_stream_ref,
    first_sum,
    second_sum,
    sems,
    out_sems,
):
    section = section_ref[0]
    fetch(section, own_out, new_out, w_out, sems.at[1])
    fetch(section, own_in, new_in, w_in, sems.at[0])
    rows, width = normed_ref.shape
    steps = rows // BLOCK
    shard = width // GROUPS

    def row_block(i):
        return pl.ds(pl.multiple_of(i * BLOCK, BLOCK), BLOCK)

    def column_block(i, size):
        return pl.ds(pl.multiple_of(i * size, 128), size)

    branch_ref[...] = grad_middle_ref[...].astype(bf16)
    store_rows(first_sum, transposed_product(attended_ref[...], branch_ref[...]), count, False, shard)
    pltpu.make_async_copy(own_out, w_out, sems.at[1]).wait()
    grad_attended_ref[...] = product_transposed(branch_ref[...], w_out[...]).astype(bf16)
    masks = lane_masks()

    @pl.loop(0, steps)
    def _(i):
        at = row_block(i)
        bias = patch_bias(live_row_ref[i])
        for pair in range(PAIRS):
            first = slice(pair * PAIR, (pair + 1) * PAIR)
            second = slice(width + pair * PAIR, width + (pair + 1) * PAIR)
            third = slice(2 * width + pair * PAIR, 2 * width + (pair + 1) * PAIR)
            parts = pair_backward(
                mixed_ref[at, first],
                mixed_ref[at, second],
                mixed_ref[at, third],
                grad_attended_ref[at, first],
                bias,
                masks,
            )
            for where, part in zip((first, second, third), parts):
                grad_mixed_ref[at, where] = part.astype(bf16)

    pltpu.make_async_copy(own_in, w_in, sems.at[0]).wait()

    @pl.loop(0, width // 256)
    def _(i):
        at = column_block(i, 256)
        grad_stream_ref[:, at] = product_transposed(grad_mixed_ref[...], w_in[at, :])

    def norm_back(i, sums):
        at = row_block(i)
        back, gain, bias = layer_norm_back(
            stream_ref[at, :], gains_ref[0:1], grad_stream_ref[at, :]
        )
        grad_stream_ref[at, :] = back + grad_middle_ref[at, :]
        return sums[0] + gain, sums[1] + bias

    zero = jnp.zeros((1, width), f32)
    gain, bias = lax.fori_loop(0, steps, norm_back, (zero, zero))
    summed = jnp.sum(grad_stream_ref[...].reshape(rows // PATCH, PATCH, width), axis=1)
    shifted_ref[...] = jnp.where(same_ref[...] > 0, summed, 0.0).astype(bf16)

    for chunk in range(3):
        part = transposed_product(
            normed_ref[...], grad_mixed_ref[:, chunk * width : (chunk + 1) * width]
        )
        if chunk == 0:
            store_rows(first_sum, part, count, False, 0)
        else:
            store_rows(second_sum, part, count, True, (chunk - 1) * shard)
    vocabulary = lax.broadcasted_iota(jnp.int32, (rows, VOCAB), 1)
    onehot = jnp.where(ids_ref[...] == vocabulary, 1.0, 0.0).astype(bf16)
    part = transposed_product(onehot, grad_stream_ref[...].astype(bf16))
    store_rows(first_sum, part, count, False, 2 * shard)
    store_small(first_sum, second_sum, gain, small_ref[0:1], bias, small_ref[1:2], shard)
    leave(section, first_sum, second_sum, keep_ref, send_ref, out_sems)


def store_small(first_sum, second_sum, gain_one, gain_two, bias_one, bias_two, shard):
    room = VOCAB // GROUPS
    width = gain_one.shape[1]
    small = jnp.concatenate(
        [gain_one, gain_two, bias_one, bias_two, jnp.zeros((room - 4, width), f32)], axis=0
    ).astype(bf16)
    for q in range(GROUPS):
        first_sum[q, 2 * shard + room : 2 * shard + 2 * room, :] = small
        second_sum[q, 2 * shard : 2 * shard + 2 * room, :] = jnp.zeros((2 * room, width), bf16)


ANY = pl.BlockSpec(memory_space=pl.ANY)
WHOLE = pl.BlockSpec(memory_space=pltpu.VMEM)
SCALARS = pl.BlockSpec(memory_space=pltpu.SMEM)


def local_first(count, section, ids, table, shifted, gains, biases, live, out_grad, own, new):
    rows, width = out_grad.shape
    hidden_width = own[3].shape[0]
    steps = rows // BLOCK
    shard = hidden_width // GROUPS
    flops = 2 * rows * width * (4 * width + 2 * hidden_width) + 8 * rows * width * hidden_width
    live = live.astype(jnp.int32)
    sums = jax.ShapeDtypeStruct((GROUPS, shard, width), bf16)

    def vmem(*shape, kind=bf16):
        return pltpu.VMEM(shape, kind)

    return pl.pallas_call(
        partial(local_first_kernel, count),
        in_specs=[SCALARS] + [WHOLE] * 8 + [ANY] * 8,
        out_specs=[WHOLE] * 7 + [ANY] * 2,
        out_shape=[
            jax.ShapeDtypeStruct((rows, width), bf16),
            jax.ShapeDtypeStruct((rows, width), f32),
            jax.ShapeDtypeStruct((rows, width), bf16),
            jax.ShapeDtypeStruct((rows, 3 * width), bf16),
            jax.ShapeDtypeStruct((rows, width), bf16),
            jax.ShapeDtypeStruct((rows, width), f32),
            jax.ShapeDtypeStruct((2, width), f32),
            sums,
            sums,
        ],
        scratch_shapes=[
            vmem(*own[0].shape),
            vmem(*own[1].shape),
            vmem(*own[2].shape),
            vmem(*own[3].shape),
            vmem(rows, width, kind=f32),
            vmem(rows, width),
            vmem(rows, width),
            vmem(rows, hidden_width),
            vmem(rows, hidden_width),
            vmem(rows, hidden_width),
            vmem(*sums.shape),
            vmem(*sums.shape),
            pltpu.SemaphoreType.DMA((4,)),
            pltpu.SemaphoreType.DMA((2,)),
        ],
        compiler_params=pltpu.CompilerParams(vmem_limit_bytes=VMEM),
        cost_estimate=pl.CostEstimate(
            flops=flops, bytes_accessed=40_000_000, transcendentals=rows * hidden_width
        ),
    )(
        section,
        ids.reshape(rows, 1),
        table,
        shifted,
        gains,
        biases,
        live.reshape(steps, 1, BLOCK),
        live.reshape(rows, 1),
        out_grad,
        *own,
        *new,
    )


def local_second(count, section, ids, same, gains, live, saved, small, own, new):
    stream, normed, mixed, attended, grad_middle = saved
    rows, width = normed.shape
    steps = rows // BLOCK
    sums = jax.ShapeDtypeStruct((GROUPS, 2 * (width + VOCAB) // GROUPS, width), bf16)
    flops = 2 * rows * width * 10 * width

    def vmem(*shape, kind=bf16):
        return pltpu.VMEM(shape, kind)

    return pl.pallas_call(
        partial(local_second_kernel, count),
        in_specs=[SCALARS] + [WHOLE] * 10 + [ANY] * 4,
        out_specs=[WHOLE] + [ANY] * 2,
        out_shape=[jax.ShapeDtypeStruct((rows // PATCH, width), bf16), sums, sums],
        scratch_shapes=[
            vmem(*own[0].shape),
            vmem(*own[1].shape),
            vmem(rows, width),
            vmem(rows, width),
            vmem(rows, 3 * width),
            vmem(rows, width, kind=f32),
            vmem(*sums.shape),
            vmem(*sums.shape),
            pltpu.SemaphoreType.DMA((2,)),
            pltpu.SemaphoreType.DMA((2,)),
        ],
        compiler_params=pltpu.CompilerParams(vmem_limit_bytes=VMEM),
        cost_estimate=pl.CostEstimate(
            flops=flops, bytes_accessed=20_000_000, transcendentals=rows * HEADS * BLOCK
        ),
    )(
        section,
        ids.reshape(rows, 1),
        same,
        gains,
        live.astype(jnp.int32).reshape(steps, 1, BLOCK),
        stream,
        normed,
        mixed,
        attended,
        grad_middle,
        small,
        own[0],
        own[1],
        new[0],
        new[1],
    )


def global_feed_kernel(count, hidden_ref, branch_ref, normed_two_ref, upward_ref, first, second):
    hidden_width, width = hidden_ref.shape[1], branch_ref.shape[1]
    halves = width // TILE
    tile_rows = TILE // (hidden_width // GROUPS)
    for i in range(hidden_width // TILE):
        part = transposed_product(hidden_ref[:, i * TILE : (i + 1) * TILE], branch_ref[...])
        size = TILE // tile_rows
        for k in range(tile_rows):
            slot = slot_of(i * tile_rows + k, count, False)
            first[slot] = part[k * size : (k + 1) * size].astype(bf16)

    @pl.loop(0, hidden_width // width)
    def _(chunk):
        for half in range(halves):
            i = chunk * halves + half
            at = pl.ds(pl.multiple_of(i * TILE, 128), TILE)
            part = transposed_product(normed_two_ref[...], upward_ref[:, at])
            store_rows(
                second,
                part,
                count,
                True,
                pl.multiple_of(chunk * (width // GROUPS), 16),
                slice(half * TILE, (half + 1) * TILE),
            )


def global_feed(count, hidden, branch, normed_two, upward):
    hidden_width, width = hidden.shape[1], branch.shape[1]
    sums = jax.ShapeDtypeStruct((GROUPS, hidden_width // GROUPS, width), bf16)
    return pl.pallas_call(
        partial(global_feed_kernel, count),
        out_shape=[sums, sums],
        compiler_params=pltpu.CompilerParams(vmem_limit_bytes=VMEM),
        cost_estimate=pl.CostEstimate(
            flops=4 * hidden.shape[0] * hidden_width * width,
            bytes_accessed=10_000_000,
            transcendentals=0,
        ),
    )(hidden, branch, normed_two, upward)


def global_heads_kernel(
    count, normed_ref, grad_mixed_ref, attended_ref, branch_ref, small_ref, first, second
):
    width = normed_ref.shape[1]
    shard = width // GROUPS
    room = VOCAB // GROUPS
    store_rows(first, transposed_product(attended_ref[...], branch_ref[...]), count, False, shard)
    for chunk in range(3):
        part = transposed_product(
            normed_ref[...], grad_mixed_ref[:, chunk * width : (chunk + 1) * width]
        )
        if chunk == 0:
            store_rows(first, part, count, False, 0)
        else:
            store_rows(second, part, count, True, (chunk - 1) * shard)
    for q in range(GROUPS):
        first[q, 2 * shard : 2 * shard + room, :] = jnp.zeros((room, width), bf16)
    small = [small_ref[k : k + 1] for k in range(4)]
    store_small(first, second, *small, shard)


def global_heads(count, normed, grad_mixed, attended, branch, small):
    rows, width = normed.shape
    sums = jax.ShapeDtypeStruct((GROUPS, 2 * (width + VOCAB) // GROUPS, width), bf16)
    return pl.pallas_call(
        partial(global_heads_kernel, count),
        out_shape=[sums, sums],
        compiler_params=pltpu.CompilerParams(vmem_limit_bytes=VMEM),
        cost_estimate=pl.CostEstimate(
            flops=8 * rows * width * width, bytes_accessed=7_000_000, transcendentals=0
        ),
    )(normed, grad_mixed, attended, branch, small)


def causal_bias(start, owner_column, owner_row):
    shape = (BLOCK, owner_row.shape[1])
    rows = lax.broadcasted_iota(jnp.int32, shape, 0) + start
    columns = lax.broadcasted_iota(jnp.int32, shape, 1)
    bias = jnp.where((columns <= rows) & (owner_column == owner_row), 0.0, MASKED)
    return jnp.concatenate([bias, bias], axis=0)


def global_forward_kernel(column_ref, row_ref, qkv_ref, out_ref):
    start = pl.multiple_of(pl.program_id(0) * BLOCK, BLOCK)
    bias = causal_bias(start, column_ref[...], row_ref[...])
    out_ref[...] = pair_forward(
        qkv_ref[pl.ds(start, BLOCK), 0:PAIR],
        qkv_ref[:, PAIR : 2 * PAIR],
        qkv_ref[:, 2 * PAIR : 3 * PAIR],
        bias,
        lane_masks(),
    ).astype(bf16)


def global_backward_kernel(column_ref, row_ref, qkv_ref, grad_ref, out_ref, key_sum, value_sum):
    step = pl.program_id(0)
    start = pl.multiple_of(step * BLOCK, BLOCK)
    bias = causal_bias(start, column_ref[...], row_ref[...])

    @pl.when(step == 0)
    def _():
        key_sum[...] = jnp.zeros_like(key_sum)
        value_sum[...] = jnp.zeros_like(value_sum)

    grad_queries, grad_keys, grad_values = pair_backward(
        qkv_ref[pl.ds(start, BLOCK), 0:PAIR],
        qkv_ref[:, PAIR : 2 * PAIR],
        qkv_ref[:, 2 * PAIR : 3 * PAIR],
        grad_ref[...],
        bias,
        lane_masks(),
    )
    out_ref[pl.ds(start, BLOCK), 0:PAIR] = grad_queries.astype(bf16)
    key_sum[...] += grad_keys
    value_sum[...] += grad_values

    @pl.when(step == pl.num_programs(0) - 1)
    def _():
        out_ref[:, PAIR : 2 * PAIR] = key_sum[...].astype(bf16)
        out_ref[:, 2 * PAIR : 3 * PAIR] = value_sum[...].astype(bf16)


def global_attention(qkv, owners, grads=None):
    count = qkv.shape[0]
    column, row = owners[:, None], owners[None, :]
    specs = [
        pl.BlockSpec((BLOCK, 1), lambda i: (i, 0)),
        pl.BlockSpec((1, count), lambda i: (0, 0)),
        pl.BlockSpec((count, 3 * PAIR), lambda i: (0, 0)),
    ]
    blocks = pl.BlockSpec((BLOCK, PAIR), lambda i: (i, 0))
    if grads is None:
        return pl.pallas_call(
            global_forward_kernel,
            grid=(count // BLOCK,),
            in_specs=specs,
            out_specs=blocks,
            out_shape=jax.ShapeDtypeStruct((count, PAIR), bf16),
            compiler_params=pltpu.CompilerParams(vmem_limit_bytes=VMEM),
        )(column, row, qkv)
    return pl.pallas_call(
        global_backward_kernel,
        grid=(count // BLOCK,),
        in_specs=specs + [blocks],
        out_specs=pl.BlockSpec((count, 3 * PAIR), lambda i: (0, 0)),
        out_shape=jax.ShapeDtypeStruct((count, 3 * PAIR), bf16),
        scratch_shapes=[pltpu.VMEM((count, PAIR), f32), pltpu.VMEM((count, PAIR), f32)],
        compiler_params=pltpu.CompilerParams(vmem_limit_bytes=VMEM),
    )(column, row, qkv, grads)


def section_send(x, origin, target, pairs):
    count = lax.axis_size("seq")
    joint = [(origin * count + i, target * count + j) for i, j in pairs]
    return lax.ppermute(x, ("section", "seq"), joint)


def section_swap(x):
    return lax.ppermute(x, "section", [(0, 1), (1, 0)])


def by_slot(buffer, count, swap, pieces):
    if count == GROUPS:
        return buffer
    depth = count.bit_length() - 1
    split = count // GROUPS
    parts, start = [], 0
    for size, shared in pieces:
        part = buffer[:, start : start + size]
        start += size
        kept = shared or size // split
        if shared:
            part = jnp.broadcast_to(part[:, None, :shared], (GROUPS, split, shared, part.shape[2]))
        parts.append(part.reshape(count, kept, part.shape[-1]))
    whole = jnp.concatenate(parts, axis=1)
    order = list(range(depth))
    if swap:
        order[0], order[1] = order[1], order[0]
    bits = whole.reshape((2,) * depth + whole.shape[1:])
    bits = jnp.transpose(bits, [depth - 1 - b for b in order] + [depth, depth + 1])
    return bits.reshape(whole.shape)


def halving_sum(parts):
    count = lax.axis_size("seq")
    place = lax.axis_index("seq")
    section = lax.axis_index("section")
    depth = count.bit_length() - 1
    shape = parts[0].shape[1:]
    held = [(part, 0) for part in parts]
    half = count
    for step in range(depth):
        bits = [step, step]
        if step < 2:
            bits[1] = 1 - step
        mine = jnp.where(section == 0, (place >> bits[0]) & 1, (place >> bits[1]) & 1)
        half //= 2

        def piece(entry, which):
            array, start = entry
            return lax.dynamic_slice(array, (start + which * half, 0, 0), (half,) + shape)

        leaving = sum(piece(entry, 1 - mine).astype(f32) for entry in held).astype(bf16)
        joint = []
        for origin in range(2):
            joint += [
                (origin * count + i, origin * count + (i ^ (1 << bits[origin])))
                for i in range(count)
            ]
        arrived = lax.ppermute(leaving, ("section", "seq"), joint)
        held = [(array, start + mine * half) for array, start in held] + [(arrived, 0)]
    total = sum(
        lax.dynamic_slice(array, (start, 0, 0), (1,) + shape).astype(f32) for array, start in held
    )
    return total[0]


def feed_forward(stream, attended, gains, biases, heads_out, expand, contract):
    middle = stream + product(attended, heads_out)
    normed_two = layer_norm(middle, gains[1], biases[1]).astype(bf16)
    hidden, slope = gelu_and_slope(product(normed_two, expand))
    hidden = hidden.astype(bf16)
    result = middle + product(hidden, contract)
    return result, (middle, normed_two, slope, hidden)


def feed_backward(grad_result, kept, gains, heads_out, expand, contract):
    middle, normed_two, slope, hidden = kept
    branch = grad_result.astype(bf16)
    grad_upward = (slope * product_transposed(branch, contract)).astype(bf16)
    grad_normed_two = product_transposed(grad_upward, expand)
    grad_middle, gain_two, bias_two = layer_norm_back(middle, gains[1:2], grad_normed_two)
    grad_middle = grad_middle + grad_result
    attend_branch = grad_middle.astype(bf16)
    grad_attended = product_transposed(attend_branch, heads_out).astype(bf16)
    return grad_middle, attend_branch, grad_attended, branch, grad_upward, (gain_two, bias_two)


def on_device(
    byte_values,
    item_lengths,
    embed_tables,
    patch_weight,
    norm_gains,
    norm_biases,
    heads_in,
    heads_out,
    expand_weight,
    contract_weight,
    out_grad,
):
    place = lax.axis_index("seq")
    count = lax.axis_size("seq")
    section = lax.axis_index("section")
    is_global = section == 0
    batches, byte_rows = byte_values.shape
    patch_rows = byte_rows // PATCH
    width = heads_out.shape[2]
    rows = batches * patch_rows
    total_patches = patch_rows * count
    gains, biases = norm_gains[0], norm_biases[0]
    heads_in, heads_out = heads_in[0], heads_out[0]
    expand, contract = expand_weight[0], contract_weight[0]
    own_table = embed_tables[0]
    straight = [(i, i) for i in range(count)]
    vocabulary = jnp.arange(VOCAB, dtype=jnp.int32)

    def onehot_of(ids):
        return (ids[:, None] == vocabulary[None, :]).astype(bf16)

    quarters = PATCH // 2
    span = count // quarters
    group, member = place // span, place % span
    shard_rows = patch_weight.shape[0]
    byte_weight = jnp.zeros((span * shard_rows, width), bf16)
    byte_weight = lax.dynamic_update_slice(byte_weight, patch_weight, (member * shard_rows, 0))
    for k in range(1, span):
        piece = lax.ppermute(patch_weight, "seq", [(i, i ^ k) for i in range(count)])
        byte_weight = lax.dynamic_update_slice(byte_weight, piece, ((member ^ k) * shard_rows, 0))
    other_table = section_swap(own_table)
    global_table = jnp.where(is_global, own_table, other_table)
    local_table = jnp.where(is_global, other_table, own_table)
    which_byte = section * quarters + group
    byte_ids = []
    for k in range(quarters):
        theirs = byte_values
        if k:
            theirs = lax.ppermute(byte_values, "seq", [(i, i ^ (k * span)) for i in range(count)])
        theirs = theirs.reshape(rows, PATCH)
        byte_ids.append(lax.dynamic_index_in_dim(theirs, which_byte, 1, keepdims=False))
    patch_onehot = onehot_of(jnp.concatenate(byte_ids))
    embedded = product(patch_onehot, global_table).astype(bf16)
    shares = product(embedded, byte_weight)
    shares = shares + section_send(shares.astype(bf16), 1, 0, straight).astype(f32)
    shares = shares.reshape(quarters, rows, width)
    stream = shares[0]
    for k in range(1, quarters):
        pairs = [(i, i ^ (k * span)) for i in range(count)]
        stream = stream + section_send(shares[k].astype(bf16), 0, 0, pairs).astype(f32)

    arrived = [section_send(w, 1, 0, straight) for w in (heads_in, heads_out, expand, contract)]
    other_norms = section_swap(jnp.concatenate([gains, biases]))
    local_gains = jnp.where(is_global, other_norms[:2], gains)
    local_biases = jnp.where(is_global, other_norms[2:], biases)

    tasks = batches * PAIRS
    first_tasks = min(tasks, count)
    spare_tasks = tasks - first_tasks

    def to_tasks(blocks):
        columns = blocks.shape[2]
        slots = jnp.pad(blocks[:first_tasks], ((0, count - first_tasks), (0, 0), (0, 0)))
        if spare_tasks:
            spare = section_send(blocks[first_tasks:], 0, 1, straight)
            spare = jnp.pad(spare, ((0, count - spare_tasks), (0, 0), (0, 0)))
            slots = jnp.where(is_global, slots, spare)
        landed = lax.all_to_all(slots, "seq", 0, 0)
        return landed.reshape(total_patches, columns)

    def from_tasks(results):
        columns = results.shape[1]
        slots = lax.all_to_all(results.reshape(count, patch_rows, columns), "seq", 0, 0)
        blocks = slots[:first_tasks]
        if spare_tasks:
            spare = section_send(slots[:spare_tasks], 1, 0, straight)
            blocks = jnp.concatenate([blocks, spare])
        return blocks

    def by_pair(values, parts):
        split = values.reshape(batches, patch_rows, parts, PAIRS, PAIR)
        return jnp.transpose(split, (0, 3, 1, 2, 4)).reshape(tasks, patch_rows, parts * PAIR)

    def from_pairs(blocks, parts):
        split = blocks.reshape(batches, PAIRS, patch_rows, parts, PAIR)
        return jnp.transpose(split, (0, 2, 3, 1, 4)).reshape(rows, parts * width)

    task = jnp.minimum(jnp.where(is_global, place, first_tasks + place), tasks - 1)
    task_lengths = lax.dynamic_index_in_dim(item_lengths, task // PAIRS, 0, keepdims=False)
    task_owners = locate(jnp.arange(total_patches, dtype=jnp.int32) * PATCH, task_lengths)[0]

    normed = layer_norm(stream, gains[0], biases[0]).astype(bf16)
    mixed = product(normed, heads_in).astype(bf16)
    qkv = to_tasks(by_pair(mixed, 3))
    attended = from_pairs(from_tasks(global_attention(qkv, task_owners)), 1)
    global_out, global_kept = feed_forward(
        stream, attended, gains, biases, heads_out, expand, contract
    )
    sent = global_out.astype(bf16).reshape(batches, patch_rows, width)

    half = patch_rows // 2
    half_bytes = half * PATCH
    chunks = half_bytes // BLOCK
    onward = [(i, i + 1) for i in range(count - 1)]
    backward = [(i + 1, i) for i in range(count - 1)]
    near = section_send(sent[:, half - 1 : patch_rows - 1], 0, 1, straight)
    edge = section_send(sent[:, patch_rows - 1 :], 0, 0, onward)
    shifted = jnp.where(is_global, jnp.concatenate([edge, sent[:, : half - 1]], axis=1), near)

    byte_places = place * byte_rows + jnp.arange(byte_rows, dtype=jnp.int32)
    live_bytes = jnp.stack([locate(byte_places, item_lengths[m])[1] for m in range(batches)])
    patch_places = place * byte_rows + section * half_bytes + PATCH * jnp.arange(half, dtype=jnp.int32)
    same_item = jnp.stack(
        [
            locate(patch_places, item_lengths[m])[0]
            == locate(patch_places - PATCH, item_lengths[m])[0]
            for m in range(batches)
        ]
    )[:, :, None]
    shifted = jnp.where(same_item, shifted, jnp.zeros((), bf16))
    half_start = section * half_bytes
    own_ids = lax.dynamic_slice_in_dim(byte_values, half_start, half_bytes, 1)
    own_live = lax.dynamic_slice_in_dim(live_bytes, half_start, half_bytes, 1)
    own_grad = lax.dynamic_slice_in_dim(out_grad, half_start, half_bytes, 1)
    weights = (heads_in, heads_out, expand, contract)
    flag = section.reshape(1).astype(jnp.int32)
    block_patches = BLOCK // PATCH

    local_outs, feed_sums, heads_sums, grads_shifted = [], [], [], []
    for c in range(chunks):
        here = slice(c * BLOCK, (c + 1) * BLOCK)
        there = slice(c * block_patches, (c + 1) * block_patches)
        ids = own_ids[:, here].reshape(batches * BLOCK)
        live = own_live[:, here].reshape(batches * BLOCK)
        same = same_item[:, there].astype(jnp.int32).reshape(batches * block_patches, 1)
        act, *saved, small, keep, send = local_first(
            count,
            flag,
            ids,
            local_table,
            shifted[:, there].reshape(batches * block_patches, width),
            local_gains,
            local_biases,
            live,
            own_grad[:, here].reshape(batches * BLOCK, width),
            weights,
            arrived,
        )
        local_outs.append(act.reshape(batches, BLOCK, width))
        feed_sums.append((keep, send))
        grad_shifted, keep, send = local_second(
            count, flag, ids, same, local_gains, live, saved, small, weights, arrived
        )
        heads_sums.append((keep, send))
        grads_shifted.append(grad_shifted.reshape(batches, block_patches, width))
    local_out = jnp.concatenate(local_outs, axis=1)
    grad_shifted = jnp.concatenate(grads_shifted, axis=1)

    other_out = section_send(local_out, 0, 1, straight)
    own_sent = jnp.broadcast_to(
        sent[:, :, None, :], (batches, patch_rows, PATCH, width)
    ).reshape(batches, byte_rows, width)
    own_sent = jnp.where(live_bytes[:, :, None], own_sent, jnp.zeros((), bf16))
    activations = jnp.where(
        is_global, own_sent, jnp.concatenate([other_out, local_out], axis=1)
    )

    near_back = section_send(grad_shifted, 1, 0, straight)
    edge_back = section_send(grad_shifted[:, :1], 0, 0, backward)
    grad_sent = jnp.concatenate([grad_shifted[:, 1:], near_back, edge_back], axis=1)
    grad_sent = grad_sent.reshape(rows, width).astype(f32)
    grad_middle, attend_branch, grad_attended, branch, grad_upward, twos = feed_backward(
        grad_sent, global_kept, gains, heads_out, expand, contract
    )
    task_grads = to_tasks(by_pair(grad_attended, 1))
    grad_mixed = from_pairs(from_tasks(global_attention(qkv, task_owners, task_grads)), 3)
    grad_normed = product_transposed(grad_mixed, heads_in)
    back, gain_one, bias_one = layer_norm_back(stream, gains[0:1], grad_normed)
    grad_stream = back + grad_middle

    own_rows = grad_stream.astype(bf16)
    gathered = [own_rows]
    for k in range(1, quarters):
        pairs = [(i, i ^ (k * span)) for i in range(count)]
        gathered.append(section_send(own_rows, 0, 0, pairs))
    gathered = jnp.concatenate(gathered)
    gathered = jnp.where(is_global, gathered, section_send(gathered, 0, 1, straight))
    patch_share = transposed_product(embedded, gathered).astype(bf16)
    patch_share = patch_share.reshape(span, shard_rows, width)
    patch_grads = lax.dynamic_index_in_dim(patch_share, member, 0, keepdims=False).astype(f32)
    for k in range(1, span):
        leaving = lax.dynamic_index_in_dim(patch_share, member ^ k, 0, keepdims=False)
        patch_grads = patch_grads + lax.ppermute(
            leaving, "seq", [(i, i ^ k) for i in range(count)]
        ).astype(f32)
    grad_embedded = product_transposed(gathered, byte_weight).astype(bf16)
    table_share = transposed_product(patch_onehot, grad_embedded).astype(bf16)
    table_share = table_share + section_send(table_share, 1, 0, straight)
    table_parts = lax.all_to_all(table_share.reshape(count, VOCAB // count, width), "seq", 0, 0)
    global_table_grad = jnp.sum(table_parts.astype(f32), axis=0)

    shard = width // count
    room = VOCAB // count
    group_shard, group_room = width // GROUPS, VOCAB // GROUPS
    small_rows = max(4, room)
    feed_pieces = {
        False: [(contract.shape[0] // GROUPS, 0)],
        True: [(group_shard, 0)] * (expand.shape[1] // width),
    }
    heads_pieces = {
        False: [(group_shard, 0), (group_shard, 0), (group_room, 0), (group_room, small_rows)],
        True: [(group_shard, 0), (group_shard, 0), (2 * group_room, room + small_rows)],
    }

    def ordered(buffer, pieces):
        if count == GROUPS:
            return buffer
        return jnp.where(
            is_global,
            by_slot(buffer, count, False, pieces[False]),
            by_slot(buffer, count, True, pieces[True]),
        )

    def local_sum(entries, pieces):
        parts = []
        for keep, send in entries:
            parts += [ordered(keep, pieces), ordered(section_swap(send), pieces)]
        return halving_sum(parts)

    def global_sum(first, second, pieces):
        crossed = section_send(second, 0, 1, straight)
        return halving_sum([ordered(jnp.where(is_global, first, crossed), pieces)])

    local_feed = local_sum(feed_sums, feed_pieces)
    local_heads = local_sum(heads_sums, heads_pieces)
    global_feed_sum = global_sum(
        *global_feed(count, global_kept[3], branch, global_kept[1], grad_upward), feed_pieces
    )
    small = jnp.concatenate([gain_one, twos[0], bias_one, twos[1]])
    global_heads_sum = global_sum(
        *global_heads(count, normed, grad_mixed, attended, attend_branch, small), heads_pieces
    )
    own_local = jnp.concatenate([local_feed, local_heads])
    own_global = jnp.concatenate([global_feed_sum, global_heads_sum])
    crossed = section_swap(jnp.where(is_global, own_local, own_global).astype(bf16)).astype(f32)
    first = jnp.where(is_global, own_global, crossed)
    second = jnp.where(is_global, crossed, own_local)

    feed_rows = contract.shape[0] // count
    contract_grad = first[:feed_rows]
    expand_grad = jnp.concatenate(
        [second[k * shard : (k + 1) * shard] for k in range(feed_rows // shard)], axis=1
    )
    first, second = first[feed_rows:], second[feed_rows:]
    in_grad = jnp.concatenate([first[:shard], second[:shard], second[shard : 2 * shard]], axis=1)
    out_grads = first[shard : 2 * shard]
    table_grad = jnp.where(is_global, global_table_grad, first[2 * shard : 2 * shard + room])
    small = lax.dynamic_slice_in_dim(first[2 * shard + room :][:4], place * shard, shard, 1)
    return (
        activations[None],
        table_grad[None],
        patch_grads,
        small[None, 0:2],
        small[None, 2:4],
        in_grad[None],
        out_grads[None],
        expand_grad[None],
        contract_grad[None],
    )


def solution(mesh):
    placed = (
        P(None, "seq"),
        P(),
        P("section", None, None),
        P(("section", "seq"), None),
        P("section", None, None),
        P("section", None, None),
        P("section", None, None),
        P("section", None, None),
        P("section", None, None),
        P("section", None, None),
        P(None, "seq", None),
    )
    return jax.shard_map(
        on_device,
        mesh=mesh,
        in_specs=placed,
        out_specs=(
            P("section", None, "seq", None),
            P("section", "seq", None),
            P(("section", "seq"), None),
            P("section", None, "seq"),
            P("section", None, "seq"),
            P("section", "seq", None),
            P("section", "seq", None),
            P("section", "seq", None),
            P("section", "seq", None),
        ),
        check_vma=False,
    )
```

```python
from functools import partial

import jax
import jax.numpy as jnp
from jax import lax
from jax.experimental import pallas as pl
from jax.experimental.pallas import tpu as pltpu
from jax.sharding import PartitionSpec as P

HEADS = 12
HEAD_SIZE = 64
VOCAB = 256
PATCH = 8
ITEMS = 4
PAIRS = HEADS // 2
PAIR = 2 * HEAD_SIZE
SCALE = HEAD_SIZE ** (-0.5)
EPSILON = 1e-05
MASKED = -1e30
BLOCK = 128
TILE = 384
GROUPS = 16
SPAN = 4
VMEM = 60 * 1024 * 1024

bf16 = jnp.bfloat16
f32 = jnp.float32


def cost(micros):
    return pl.CostEstimate(flops=int(micros * 2.2e9), bytes_accessed=1, transcendentals=0)


def product(former, latter):
    return jnp.dot(former, latter, preferred_element_type=f32)


def transposed_product(former, latter):
    return lax.dot_general(former, latter, (((0,), (0,)), ((), ())), preferred_element_type=f32)


def product_transposed(former, latter):
    return lax.dot_general(former, latter, (((1,), (1,)), ((), ())), preferred_element_type=f32)


def normalise(values):
    average = jnp.mean(values, axis=-1, keepdims=True)
    centered = values - average
    inverse_root = lax.rsqrt(jnp.mean(centered * centered, axis=-1, keepdims=True) + EPSILON)
    return centered * inverse_root, inverse_root


def layer_norm(values, gain, bias):
    return normalise(values)[0] * gain + bias


def layer_norm_back(values, gain, grad):
    unit, inverse_root = normalise(values)
    scaled = grad * gain
    grad_values = inverse_root * (
        scaled
        - jnp.mean(scaled, axis=-1, keepdims=True)
        - unit * jnp.mean(scaled * unit, axis=-1, keepdims=True)
    )
    return (
        grad_values,
        jnp.sum(grad * unit, axis=0, keepdims=True),
        jnp.sum(grad, axis=0, keepdims=True),
    )


def locate(positions, lengths_row):
    padded = (lengths_row + PATCH - 1) // PATCH * PATCH
    item_ends = jnp.cumsum(padded)
    starts = item_ends - padded
    inside = (positions[:, None] >= starts[None, :]) & (positions[:, None] < item_ends[None, :])
    offsets = jnp.arange(ITEMS, dtype=jnp.int32)[None, :] - ITEMS
    owners = jnp.sum(jnp.where(inside, offsets, 0), axis=1) + ITEMS
    live_mask = jnp.any(inside & (positions[:, None] < (starts + lengths_row)[None, :]), axis=1)
    return (owners, live_mask)


def slot_of(q, count, swap):
    if count != GROUPS:
        return q
    bits = [(q >> b) & 1 for b in range(GROUPS.bit_length() - 1)]
    if swap:
        bits[0], bits[1] = bits[1], bits[0]
    slot = 0
    for bit in bits:
        slot = 2 * slot + bit
    return slot


def store_rows(buffer, value, count, swap, start, columns=slice(None)):
    rows = value.shape[0] // GROUPS
    for q in range(GROUPS):
        buffer[slot_of(q, count, swap), pl.ds(start, rows), columns] = value[
            q * rows : (q + 1) * rows
        ].astype(bf16)


def patch_bias(live_row):
    rows = lax.broadcasted_iota(jnp.int32, (BLOCK, BLOCK), 0)
    columns = lax.broadcasted_iota(jnp.int32, (BLOCK, BLOCK), 1)
    same = (rows // PATCH) == (columns // PATCH)
    allowed = same & (columns <= rows) & ((live_row > 0) | (columns == rows))
    bias = jnp.where(allowed, 0.0, MASKED)
    return jnp.concatenate([bias, bias], axis=0)


def softmax_rows(scores):
    peak = jnp.max(scores, axis=-1, keepdims=True)
    exponents = jnp.exp(scores - peak)
    return exponents * (1.0 / jnp.sum(exponents, axis=-1, keepdims=True))


def lane_masks():
    lanes = lax.broadcasted_iota(jnp.int32, (1, PAIR), 1)
    low = jnp.where(lanes < HEAD_SIZE, 1.0, 0.0)
    return lanes < HEAD_SIZE, low.astype(bf16), (1.0 - low).astype(bf16)


def stacked(values, low, high, scale=1.0):
    return jnp.concatenate([values * (low * scale), values * (high * scale)], axis=0)


def unstacked(values, is_low):
    half = values.shape[0] // 2
    return jnp.where(is_low, values[:half], values[half:])


def pair_forward(queries, keys, values, bias, masks):
    is_low, low, high = masks
    scores = product_transposed(stacked(queries, low, high, SCALE), keys) + bias
    return unstacked(product(softmax_rows(scores).astype(bf16), values), is_low)


def pair_backward(queries, keys, values, grads, bias, masks):
    is_low, low, high = masks
    both = stacked(queries, low, high, SCALE)
    both_grads = stacked(grads, low, high)
    probabilities = softmax_rows(product_transposed(both, keys) + bias)
    prob_grads = product_transposed(both_grads, values)
    delta = jnp.sum(probabilities * prob_grads, axis=-1, keepdims=True)
    score_grads = (probabilities * (prob_grads - delta)).astype(bf16)
    return (
        unstacked(product(score_grads, keys), is_low) * SCALE,
        transposed_product(score_grads, both),
        transposed_product(probabilities.astype(bf16), both_grads),
    )


def gelu_and_slope(x):
    root = 0.7978845608028654
    cubic = 0.044715
    square = x * x
    bent = jnp.tanh(x * (root + (root * cubic) * square))
    half = 0.5 * (1.0 + bent)
    slope = half + (0.5 * x) * (1.0 - bent * bent) * (root + (3.0 * root * cubic) * square)
    return x * half, slope


def fetch(section, own, arrived, target, sem):
    @pl.when(section == 0)
    def _():
        pltpu.make_async_copy(arrived, target, sem).start()

    @pl.when(section != 0)
    def _():
        pltpu.make_async_copy(own, target, sem).start()


def leave(section, first, second, keep, send, sems):
    @pl.when(section == 0)
    def _():
        pltpu.make_async_copy(first, keep, sems.at[0]).start()
        pltpu.make_async_copy(second, send, sems.at[1]).start()

    @pl.when(section != 0)
    def _():
        pltpu.make_async_copy(second, keep, sems.at[0]).start()
        pltpu.make_async_copy(first, send, sems.at[1]).start()

    pltpu.make_async_copy(first, keep, sems.at[0]).wait()
    pltpu.make_async_copy(second, send, sems.at[1]).wait()


def local_first_kernel(
    count,
    section_ref,
    ids_ref,
    table_ref,
    shifted_ref,
    gains_ref,
    biases_ref,
    live_row_ref,
    live_column_ref,
    out_grad_ref,
    own_in,
    own_out,
    own_expand,
    own_contract,
    new_in,
    new_out,
    new_expand,
    new_contract,
    act_ref,
    stream_ref,
    normed_ref,
    mixed_ref,
    attended_ref,
    grad_middle_ref,
    small_ref,
    keep_ref,
    send_ref,
    w_in,
    w_out,
    w_expand,
    w_contract,
    middle_ref,
    normed_two_ref,
    branch_ref,
    hidden_ref,
    slope_ref,
    upward_ref,
    contract_sum,
    expand_sum,
    sems,
    out_sems,
):
    section = section_ref[0]
    fetch(section, own_in, new_in, w_in, sems.at[0])
    fetch(section, own_out, new_out, w_out, sems.at[1])
    fetch(section, own_expand, new_expand, w_expand, sems.at[2])
    fetch(section, own_contract, new_contract, w_contract, sems.at[3])
    rows, width = act_ref.shape
    steps = rows // BLOCK
    hidden_width = hidden_ref.shape[1]
    patches = shifted_ref.shape[0]

    def row_block(i):
        return pl.ds(pl.multiple_of(i * BLOCK, BLOCK), BLOCK)

    def column_block(i, size):
        return pl.ds(pl.multiple_of(i * size, 128), size)

    @pl.loop(0, steps)
    def _(i):
        at = row_block(i)
        vocabulary = lax.broadcasted_iota(jnp.int32, (BLOCK, VOCAB), 1)
        onehot = jnp.where(ids_ref[at, :] == vocabulary, 1.0, 0.0).astype(bf16)
        places = lax.broadcasted_iota(jnp.int32, (BLOCK, patches), 0) // PATCH
        columns = lax.broadcasted_iota(jnp.int32, (BLOCK, patches), 1)
        spread = jnp.where(places + i * (BLOCK // PATCH) == columns, 1.0, 0.0).astype(bf16)
        stream = product(onehot, table_ref[...]) + product(spread, shifted_ref[...])
        stream_ref[at, :] = stream
        normed_ref[at, :] = layer_norm(stream, gains_ref[0:1], biases_ref[0:1]).astype(bf16)
        branch_ref[at, :] = jnp.where(
            live_column_ref[at, :] > 0, out_grad_ref[at, :].astype(f32), 0.0
        ).astype(bf16)

    pltpu.make_async_copy(own_in, w_in, sems.at[0]).wait()

    @pl.loop(0, 3 * width // TILE)
    def _(i):
        at = column_block(i, TILE)
        mixed_ref[:, at] = product(normed_ref[...], w_in[:, at]).astype(bf16)

    masks = lane_masks()

    @pl.loop(0, steps)
    def _(i):
        at = row_block(i)
        bias = patch_bias(live_row_ref[i])
        for pair in range(PAIRS):
            first = slice(pair * PAIR, (pair + 1) * PAIR)
            second = slice(width + pair * PAIR, width + (pair + 1) * PAIR)
            third = slice(2 * width + pair * PAIR, 2 * width + (pair + 1) * PAIR)
            attended_ref[at, first] = pair_forward(
                mixed_ref[at, first], mixed_ref[at, second], mixed_ref[at, third], bias, masks
            ).astype(bf16)

    pltpu.make_async_copy(own_out, w_out, sems.at[1]).wait()

    @pl.loop(0, steps)
    def _(i):
        at = row_block(i)
        middle = stream_ref[at, :] + product(attended_ref[at, :], w_out[...])
        middle_ref[at, :] = middle
        normed_two_ref[at, :] = layer_norm(middle, gains_ref[1:2], biases_ref[1:2]).astype(bf16)

    pltpu.make_async_copy(own_expand, w_expand, sems.at[2]).wait()

    @pl.loop(0, hidden_width // TILE)
    def _(i):
        at = column_block(i, TILE)
        hidden, slope = gelu_and_slope(product(normed_two_ref[...], w_expand[:, at]))
        hidden_ref[:, at] = hidden.astype(bf16)
        slope_ref[:, at] = slope.astype(bf16)

    pltpu.make_async_copy(own_contract, w_contract, sems.at[3]).wait()

    @pl.loop(0, width // 256)
    def _(i):
        at = column_block(i, 256)
        result = middle_ref[:, at] + product(hidden_ref[...], w_contract[:, at])
        act_ref[:, at] = jnp.where(live_column_ref[...] > 0, result, 0.0).astype(bf16)

    tile_rows = TILE // (hidden_width // GROUPS)
    halves = width // TILE

    @pl.loop(0, hidden_width // width)
    def _(chunk):
        for half in range(halves):
            i = chunk * halves + half
            at = column_block(i, TILE)
            grad_hidden = product_transposed(branch_ref[...], w_contract[at, :])
            grad_upward = (grad_hidden * slope_ref[:, at].astype(f32)).astype(bf16)
            upward_ref[:, at] = grad_upward
            part = transposed_product(normed_two_ref[...], grad_upward)
            store_rows(
                expand_sum,
                part,
                count,
                True,
                pl.multiple_of(chunk * (width // GROUPS), 16),
                slice(half * TILE, (half + 1) * TILE),
            )

    for i in range(hidden_width // TILE):
        part = transposed_product(hidden_ref[:, i * TILE : (i + 1) * TILE], branch_ref[...])
        size = TILE // tile_rows
        for k in range(tile_rows):
            slot = slot_of(i * tile_rows + k, count, False)
            contract_sum[slot] = part[k * size : (k + 1) * size].astype(bf16)

    @pl.loop(0, width // 256)
    def _(i):
        at = column_block(i, 256)
        grad_middle_ref[:, at] = product_transposed(upward_ref[...], w_expand[at, :])

    def norm_back(i, sums):
        at = row_block(i)
        grad = grad_middle_ref[at, :]
        back, gain, bias = layer_norm_back(middle_ref[at, :], gains_ref[1:2], grad)
        grad_middle_ref[at, :] = back + branch_ref[at, :].astype(f32)
        return sums[0] + gain, sums[1] + bias

    zero = jnp.zeros((1, width), f32)
    gain, bias = lax.fori_loop(0, steps, norm_back, (zero, zero))
    small_ref[...] = jnp.concatenate([gain, bias], axis=0)
    leave(section, contract_sum, expand_sum, keep_ref, send_ref, out_sems)


def local_second_kernel(
    count,
    section_ref,
    ids_ref,
    same_ref,
    gains_ref,
    live_row_ref,
    stream_ref,
    normed_ref,
    mixed_ref,
    attended_ref,
    grad_middle_ref,
    small_ref,
    own_in,
    own_out,
    new_in,
    new_out,
    shifted_ref,
    keep_ref,
    send_ref,
    w_in,
    w_out,
    branch_ref,
    grad_attended_ref,
    grad_mixed_ref,
    grad_stream_ref,
    first_sum,
    second_sum,
    sems,
    out_sems,
):
    section = section_ref[0]
    fetch(section, own_out, new_out, w_out, sems.at[1])
    fetch(section, own_in, new_in, w_in, sems.at[0])
    rows, width = normed_ref.shape
    steps = rows // BLOCK
    shard = width // GROUPS

    def row_block(i):
        return pl.ds(pl.multiple_of(i * BLOCK, BLOCK), BLOCK)

    def column_block(i, size):
        return pl.ds(pl.multiple_of(i * size, 128), size)

    branch_ref[...] = grad_middle_ref[...].astype(bf16)
    store_rows(first_sum, transposed_product(attended_ref[...], branch_ref[...]), count, False, shard)
    pltpu.make_async_copy(own_out, w_out, sems.at[1]).wait()
    grad_attended_ref[...] = product_transposed(branch_ref[...], w_out[...]).astype(bf16)
    masks = lane_masks()

    @pl.loop(0, steps)
    def _(i):
        at = row_block(i)
        bias = patch_bias(live_row_ref[i])
        for pair in range(PAIRS):
            first = slice(pair * PAIR, (pair + 1) * PAIR)
            second = slice(width + pair * PAIR, width + (pair + 1) * PAIR)
            third = slice(2 * width + pair * PAIR, 2 * width + (pair + 1) * PAIR)
            parts = pair_backward(
                mixed_ref[at, first],
                mixed_ref[at, second],
                mixed_ref[at, third],
                grad_attended_ref[at, first],
                bias,
                masks,
            )
            for where, part in zip((first, second, third), parts):
                grad_mixed_ref[at, where] = part.astype(bf16)

    pltpu.make_async_copy(own_in, w_in, sems.at[0]).wait()

    @pl.loop(0, width // 256)
    def _(i):
        at = column_block(i, 256)
        grad_stream_ref[:, at] = product_transposed(grad_mixed_ref[...], w_in[at, :])

    def norm_back(i, sums):
        at = row_block(i)
        back, gain, bias = layer_norm_back(
            stream_ref[at, :], gains_ref[0:1], grad_stream_ref[at, :]
        )
        grad_stream_ref[at, :] = back + grad_middle_ref[at, :]
        return sums[0] + gain, sums[1] + bias

    zero = jnp.zeros((1, width), f32)
    gain, bias = lax.fori_loop(0, steps, norm_back, (zero, zero))
    summed = jnp.sum(grad_stream_ref[...].reshape(rows // PATCH, PATCH, width), axis=1)
    shifted_ref[...] = jnp.where(same_ref[...] > 0, summed, 0.0).astype(bf16)

    for chunk in range(3):
        part = transposed_product(
            normed_ref[...], grad_mixed_ref[:, chunk * width : (chunk + 1) * width]
        )
        if chunk == 0:
            store_rows(first_sum, part, count, False, 0)
        else:
            store_rows(second_sum, part, count, True, (chunk - 1) * shard)
    vocabulary = lax.broadcasted_iota(jnp.int32, (rows, VOCAB), 1)
    onehot = jnp.where(ids_ref[...] == vocabulary, 1.0, 0.0).astype(bf16)
    part = transposed_product(onehot, grad_stream_ref[...].astype(bf16))
    store_rows(first_sum, part, count, False, 2 * shard)
    store_small(first_sum, second_sum, gain, small_ref[0:1], bias, small_ref[1:2], shard)
    leave(section, first_sum, second_sum, keep_ref, send_ref, out_sems)


def store_small(first_sum, second_sum, gain_one, gain_two, bias_one, bias_two, shard):
    room = VOCAB // GROUPS
    width = gain_one.shape[1]
    small = jnp.concatenate(
        [gain_one, gain_two, bias_one, bias_two, jnp.zeros((room - 4, width), f32)], axis=0
    ).astype(bf16)
    for q in range(GROUPS):
        first_sum[q, 2 * shard + room : 2 * shard + 2 * room, :] = small
        second_sum[q, 2 * shard : 2 * shard + 2 * room, :] = jnp.zeros((2 * room, width), bf16)


ANY = pl.BlockSpec(memory_space=pl.ANY)
WHOLE = pl.BlockSpec(memory_space=pltpu.VMEM)
SCALARS = pl.BlockSpec(memory_space=pltpu.SMEM)


def local_first(count, section, ids, table, shifted, gains, biases, live, out_grad, own, new):
    rows, width = out_grad.shape
    hidden_width = own[3].shape[0]
    steps = rows // BLOCK
    shard = hidden_width // GROUPS
    live = live.astype(jnp.int32)
    sums = jax.ShapeDtypeStruct((GROUPS, shard, width), bf16)

    def vmem(*shape, kind=bf16):
        return pltpu.VMEM(shape, kind)

    return pl.pallas_call(
        partial(local_first_kernel, count),
        in_specs=[SCALARS] + [WHOLE] * 8 + [ANY] * 8,
        out_specs=[WHOLE] * 7 + [ANY] * 2,
        out_shape=[
            jax.ShapeDtypeStruct((rows, width), bf16),
            jax.ShapeDtypeStruct((rows, width), f32),
            jax.ShapeDtypeStruct((rows, width), bf16),
            jax.ShapeDtypeStruct((rows, 3 * width), bf16),
            jax.ShapeDtypeStruct((rows, width), bf16),
            jax.ShapeDtypeStruct((rows, width), f32),
            jax.ShapeDtypeStruct((2, width), f32),
            sums,
            sums,
        ],
        scratch_shapes=[
            vmem(*own[0].shape),
            vmem(*own[1].shape),
            vmem(*own[2].shape),
            vmem(*own[3].shape),
            vmem(rows, width, kind=f32),
            vmem(rows, width),
            vmem(rows, width),
            vmem(rows, hidden_width),
            vmem(rows, hidden_width),
            vmem(rows, hidden_width),
            vmem(*sums.shape),
            vmem(*sums.shape),
            pltpu.SemaphoreType.DMA((4,)),
            pltpu.SemaphoreType.DMA((2,)),
        ],
        compiler_params=pltpu.CompilerParams(vmem_limit_bytes=VMEM),
        cost_estimate=cost(38),
    )(
        section,
        ids.reshape(rows, 1),
        table,
        shifted,
        gains,
        biases,
        live.reshape(steps, 1, BLOCK),
        live.reshape(rows, 1),
        out_grad,
        *own,
        *new,
    )


def local_second(count, section, ids, same, gains, live, saved, small, own, new):
    stream, normed, mixed, attended, grad_middle = saved
    rows, width = normed.shape
    steps = rows // BLOCK
    sums = jax.ShapeDtypeStruct((GROUPS, 2 * (width + VOCAB) // GROUPS, width), bf16)

    def vmem(*shape, kind=bf16):
        return pltpu.VMEM(shape, kind)

    return pl.pallas_call(
        partial(local_second_kernel, count),
        in_specs=[SCALARS] + [WHOLE] * 10 + [ANY] * 4,
        out_specs=[WHOLE] + [ANY] * 2,
        out_shape=[jax.ShapeDtypeStruct((rows // PATCH, width), bf16), sums, sums],
        scratch_shapes=[
            vmem(*own[0].shape),
            vmem(*own[1].shape),
            vmem(rows, width),
            vmem(rows, width),
            vmem(rows, 3 * width),
            vmem(rows, width, kind=f32),
            vmem(*sums.shape),
            vmem(*sums.shape),
            pltpu.SemaphoreType.DMA((2,)),
            pltpu.SemaphoreType.DMA((2,)),
        ],
        compiler_params=pltpu.CompilerParams(vmem_limit_bytes=VMEM),
        cost_estimate=cost(23),
    )(
        section,
        ids.reshape(rows, 1),
        same,
        gains,
        live.astype(jnp.int32).reshape(steps, 1, BLOCK),
        stream,
        normed,
        mixed,
        attended,
        grad_middle,
        small,
        own[0],
        own[1],
        new[0],
        new[1],
    )


def global_feed_kernel(
    count, hidden_ref, branch_ref, normed_two_ref, upward_ref, first, second
):
    hidden_width, width = hidden_ref.shape[1], branch_ref.shape[1]
    halves = width // TILE
    tile_rows = TILE // (hidden_width // GROUPS)
    for i in range(hidden_width // TILE):
        part = transposed_product(hidden_ref[:, i * TILE : (i + 1) * TILE], branch_ref[...])
        size = TILE // tile_rows
        for k in range(tile_rows):
            slot = slot_of(i * tile_rows + k, count, False)
            first[slot] = part[k * size : (k + 1) * size].astype(bf16)

    @pl.loop(0, hidden_width // width)
    def _(chunk):
        for half in range(halves):
            i = chunk * halves + half
            at = pl.ds(pl.multiple_of(i * TILE, 128), TILE)
            part = transposed_product(normed_two_ref[...], upward_ref[:, at])
            store_rows(
                second,
                part,
                count,
                True,
                pl.multiple_of(chunk * (width // GROUPS), 16),
                slice(half * TILE, (half + 1) * TILE),
            )


def global_feed(count, hidden, branch, normed_two, upward, deps=()):
    hidden_width, width = hidden.shape[1], branch.shape[1]
    sums = jax.ShapeDtypeStruct((GROUPS, hidden_width // GROUPS, width), bf16)
    return call(
        partial(global_feed_kernel, count),
        (hidden, branch, normed_two, upward),
        [WHOLE] * 4,
        [sums, sums],
        [WHOLE] * 2,
        deps=deps,
        micros=8,
    )


def global_heads_kernel(
    count, normed_ref, grad_mixed_ref, attended_ref, branch_ref, small_ref, first, second
):
    width = normed_ref.shape[1]
    shard = width // GROUPS
    room = VOCAB // GROUPS
    store_rows(first, transposed_product(attended_ref[...], branch_ref[...]), count, False, shard)
    for chunk in range(3):
        part = transposed_product(
            normed_ref[...], grad_mixed_ref[:, chunk * width : (chunk + 1) * width]
        )
        if chunk == 0:
            store_rows(first, part, count, False, 0)
        else:
            store_rows(second, part, count, True, (chunk - 1) * shard)
    for q in range(GROUPS):
        first[q, 2 * shard : 2 * shard + room, :] = jnp.zeros((room, width), bf16)
    small = [small_ref[k : k + 1] for k in range(4)]
    store_small(first, second, *small, shard)


def global_heads(count, normed, grad_mixed, attended, branch, small):
    rows, width = normed.shape
    sums = jax.ShapeDtypeStruct((GROUPS, 2 * (width + VOCAB) // GROUPS, width), bf16)
    return pl.pallas_call(
        partial(global_heads_kernel, count),
        out_shape=[sums, sums],
        compiler_params=pltpu.CompilerParams(vmem_limit_bytes=VMEM),
        cost_estimate=cost(6),
    )(normed, grad_mixed, attended, branch, small)


def causal_bias(start, owner_column, owner_row):
    shape = (BLOCK, owner_row.shape[1])
    rows = lax.broadcasted_iota(jnp.int32, shape, 0) + start
    columns = lax.broadcasted_iota(jnp.int32, shape, 1)
    bias = jnp.where((columns <= rows) & (owner_column == owner_row), 0.0, MASKED)
    return jnp.concatenate([bias, bias], axis=0)


def global_forward_kernel(column_ref, row_ref, qkv_ref, out_ref):
    start = pl.multiple_of(pl.program_id(0) * BLOCK, BLOCK)
    bias = causal_bias(start, column_ref[...], row_ref[...])
    out_ref[...] = pair_forward(
        qkv_ref[pl.ds(start, BLOCK), 0:PAIR],
        qkv_ref[:, PAIR : 2 * PAIR],
        qkv_ref[:, 2 * PAIR : 3 * PAIR],
        bias,
        lane_masks(),
    ).astype(bf16)


def global_backward_kernel(column_ref, row_ref, qkv_ref, grad_ref, out_ref, key_sum, value_sum):
    step = pl.program_id(0)
    start = pl.multiple_of(step * BLOCK, BLOCK)
    bias = causal_bias(start, column_ref[...], row_ref[...])

    @pl.when(step == 0)
    def _():
        key_sum[...] = jnp.zeros_like(key_sum)
        value_sum[...] = jnp.zeros_like(value_sum)

    grad_queries, grad_keys, grad_values = pair_backward(
        qkv_ref[pl.ds(start, BLOCK), 0:PAIR],
        qkv_ref[:, PAIR : 2 * PAIR],
        qkv_ref[:, 2 * PAIR : 3 * PAIR],
        grad_ref[...],
        bias,
        lane_masks(),
    )
    out_ref[pl.ds(start, BLOCK), 0:PAIR] = grad_queries.astype(bf16)
    key_sum[...] += grad_keys
    value_sum[...] += grad_values

    @pl.when(step == pl.num_programs(0) - 1)
    def _():
        out_ref[:, PAIR : 2 * PAIR] = key_sum[...].astype(bf16)
        out_ref[:, 2 * PAIR : 3 * PAIR] = value_sum[...].astype(bf16)


def global_attention(qkv, owners, grads=None, deps=()):
    count = qkv.shape[0]
    column, row = owners[:, None], owners[None, :]
    specs = [
        pl.BlockSpec((BLOCK, 1), lambda i: (i, 0)),
        pl.BlockSpec((1, count), lambda i: (0, 0)),
        pl.BlockSpec((count, 3 * PAIR), lambda i: (0, 0)),
    ]
    blocks = pl.BlockSpec((BLOCK, PAIR), lambda i: (i, 0))
    if grads is None:
        return pl.pallas_call(
            global_forward_kernel,
            grid=(count // BLOCK,),
            in_specs=specs,
            out_specs=blocks,
            out_shape=jax.ShapeDtypeStruct((count, PAIR), bf16),
            compiler_params=pltpu.CompilerParams(vmem_limit_bytes=VMEM),
            cost_estimate=cost(15),
        )(column, row, qkv)

    def body(*refs):
        global_backward_kernel(*refs[:4], *refs[4 + len(deps) :])

    return pl.pallas_call(
        body,
        grid=(count // BLOCK,),
        in_specs=specs + [blocks] + [ANY] * len(deps),
        out_specs=pl.BlockSpec((count, 3 * PAIR), lambda i: (0, 0)),
        out_shape=jax.ShapeDtypeStruct((count, 3 * PAIR), bf16),
        scratch_shapes=[pltpu.VMEM((count, PAIR), f32), pltpu.VMEM((count, PAIR), f32)],
        compiler_params=pltpu.CompilerParams(vmem_limit_bytes=VMEM),
        cost_estimate=cost(30),
    )(column, row, qkv, grads, *deps)


def call(kernel, args, specs, out_shape, out_specs, scratch=(), deps=(), micros=1):
    count = len(args)

    def body(*refs):
        kernel(*refs[:count], *refs[count + len(deps) :])

    return pl.pallas_call(
        body,
        in_specs=list(specs) + [ANY] * len(deps),
        out_specs=out_specs,
        out_shape=out_shape,
        scratch_shapes=list(scratch),
        compiler_params=pltpu.CompilerParams(vmem_limit_bytes=VMEM),
        cost_estimate=cost(micros),
    )(*args, *deps)


def shaped(*shape, kind=bf16):
    return jax.ShapeDtypeStruct(shape, kind)


def patch_forward(member, ids, table, pieces, deps=()):
    rows = ids.shape[0]
    shard, width = pieces[0].shape
    span = len(pieces)

    def kernel(member_ref, ids_ref, table_ref, *rest):
        piece_refs, (embedded_ref, weight_ref, share_ref, low_ref) = rest[:span], rest[span:]
        member_now = member_ref[0]
        for k in range(span):
            start = pl.multiple_of((member_now ^ k) * shard, shard)
            weight_ref[pl.ds(start, shard), :] = piece_refs[k][...]
        vocabulary = lax.broadcasted_iota(jnp.int32, (rows, VOCAB), 1)
        onehot = jnp.where(ids_ref[...] == vocabulary, 1.0, 0.0).astype(bf16)
        embedded_ref[...] = product(onehot, table_ref[...]).astype(bf16)
        share = product(embedded_ref[...], weight_ref[...])
        share_ref[...] = share
        low_ref[...] = share.astype(bf16)

    return call(
        kernel,
        (member, ids.reshape(rows, 1), table, *pieces),
        [SCALARS] + [WHOLE] * (2 + span),
        [
            shaped(rows, width),
            shaped(span * shard, width),
            shaped(rows, width, kind=f32),
            shaped(rows, width),
        ],
        [WHOLE] * 4,
        deps=deps,
        micros=4,
    )


def split_heads(values, target, start, batches, part, width_of_task):
    patch_rows = values.shape[0] // batches
    for m in range(batches):
        for pair in range(PAIRS):
            target[m * PAIRS + pair, :, part * PAIR : (part + 1) * PAIR] = values[
                m * patch_rows : (m + 1) * patch_rows, pair * PAIR : (pair + 1) * PAIR
            ]


def merge_heads(blocks, target, batches, parts):
    patch_rows = target.shape[0] // batches
    width = PAIRS * PAIR
    for t in range(batches * PAIRS):
        m, pair = t // PAIRS, t % PAIRS
        first = blocks[0].shape[0]
        block = blocks[0].at[t] if t < first else blocks[1].at[t - first]
        for part in range(parts):
            at = part * width + pair * PAIR
            target[m * patch_rows : (m + 1) * patch_rows, at : at + PAIR] = block[
                :, part * PAIR : (part + 1) * PAIR
            ]


def strided(values, target, span, offset):
    size = values.shape[1] // (4 * span)
    for k in range(span):
        parts = [
            values[:, (group * span + k) * size : (group * span + k + 1) * size]
            for group in range(4)
        ]
        target[k, :, offset : offset + 4 * size] = jnp.concatenate(parts, axis=1)


def global_start(batches, own, others, gains, biases, heads_in):
    rows, width = own.shape
    patch_rows = rows // batches

    def kernel(own_ref, gains_ref, biases_ref, weight_hbm, *rest):
        other_refs, (stream_ref, normed_ref, task_ref, share_ref, weight, sem) = (
            rest[: len(others)],
            rest[len(others) :],
        )
        load = pltpu.make_async_copy(weight_hbm, weight, sem)
        load.start()
        stream = own_ref[...]
        for ref in other_refs:
            stream = stream + ref[...].astype(f32)
        stream_ref[...] = stream
        normed = layer_norm(stream, gains_ref[0:1], biases_ref[0:1]).astype(bf16)
        normed_ref[...] = normed
        strided(normed, share_ref, SPAN, 0)
        load.wait()
        for part in range(3):
            mixed = product(normed, weight[:, part * width : (part + 1) * width]).astype(bf16)
            split_heads(mixed, task_ref, 0, batches, part, width)

    return call(
        kernel,
        (own, gains, biases, heads_in, *others),
        [WHOLE] * 3 + [ANY] + [WHOLE] * len(others),
        [
            shaped(rows, width, kind=f32),
            shaped(rows, width),
            shaped(batches * PAIRS, patch_rows, 3 * PAIR),
            shaped(SPAN, rows, width // SPAN),
        ],
        [WHOLE] * 4,
        [pltpu.VMEM(heads_in.shape, bf16), pltpu.SemaphoreType.DMA],
        micros=5,
    )


def global_feed_forward(batches, blocks, stream, gains, biases, heads_out, expand, contract):
    rows, width = stream.shape
    hidden_width = expand.shape[1]
    n = len(blocks)

    def kernel(stream_ref, gains_ref, biases_ref, out_hbm, expand_hbm, contract_hbm, *rest):
        block_refs, rest = rest[:n], rest[n:]
        (attended_ref, middle_ref, normed_two_ref, slope_ref, hidden_ref, sent_ref) = rest[:6]
        share_ref, w_out, w_expand, w_contract, sems = rest[6:]
        loads = [
            pltpu.make_async_copy(out_hbm, w_out, sems.at[0]),
            pltpu.make_async_copy(expand_hbm, w_expand, sems.at[1]),
            pltpu.make_async_copy(contract_hbm, w_contract, sems.at[2]),
        ]
        for load in loads:
            load.start()
        merge_heads(block_refs, attended_ref, batches, 1)
        loads[0].wait()
        middle = stream_ref[...] + product(attended_ref[...], w_out[...])
        middle_ref[...] = middle
        normed_two_ref[...] = layer_norm(middle, gains_ref[1:2], biases_ref[1:2]).astype(bf16)
        loads[1].wait()

        @pl.loop(0, hidden_width // width)
        def _(i):
            at = pl.ds(pl.multiple_of(i * width, 128), width)
            hidden, slope = gelu_and_slope(product(normed_two_ref[...], w_expand[:, at]))
            hidden_ref[:, at] = hidden.astype(bf16)
            slope_ref[:, at] = slope.astype(bf16)

        loads[2].wait()
        result = middle_ref[...] + product(hidden_ref[...], w_contract[...])
        sent_ref[...] = result.astype(bf16)
        strided(hidden_ref[...], share_ref, SPAN, 0)
        strided(normed_two_ref[...], share_ref, SPAN, hidden_width // SPAN)
        strided(attended_ref[...], share_ref, SPAN, (hidden_width + width) // SPAN)

    return call(
        kernel,
        (stream, gains, biases, heads_out, expand, contract, *blocks),
        [WHOLE] * 3 + [ANY] * 3 + [WHOLE] * n,
        [
            shaped(rows, width),
            shaped(rows, width, kind=f32),
            shaped(rows, width),
            shaped(rows, hidden_width),
            shaped(rows, hidden_width),
            shaped(rows, width),
            shaped(SPAN, rows, (hidden_width + 2 * width) // SPAN),
        ],
        [WHOLE] * 7,
        [
            pltpu.VMEM(heads_out.shape, bf16),
            pltpu.VMEM(expand.shape, bf16),
            pltpu.VMEM(contract.shape, bf16),
            pltpu.SemaphoreType.DMA((3,)),
        ],
        micros=8,
    )


def global_feed_backward(
    batches, grad, middle, slope, gains, heads_out, expand, contract, member, share, deps=()
):
    rows, width = grad.shape
    hidden_width = expand.shape[1]
    patch_rows = rows // batches
    own = share.shape[2]
    whole = own + 2 * width + hidden_width

    def kernel(
        member_ref, grad_ref, middle_ref, slope_ref, gains_ref, share_ref,
        out_hbm, expand_hbm, contract_hbm,
        upward_ref, grad_middle_ref, branch_ref, task_ref, small_ref, *rest,
    ):
        sent_refs, (w_out, w_expand, w_contract, sems) = rest[:SPAN], rest[SPAN:]
        loads = [
            pltpu.make_async_copy(contract_hbm, w_contract, sems.at[2]),
            pltpu.make_async_copy(expand_hbm, w_expand, sems.at[1]),
            pltpu.make_async_copy(out_hbm, w_out, sems.at[0]),
        ]
        for load in loads:
            load.start()
        loads[0].wait()

        @pl.loop(0, hidden_width // width)
        def _(i):
            at = pl.ds(pl.multiple_of(i * width, 128), width)
            grad_hidden = product_transposed(grad_ref[...], w_contract[at, :])
            upward_ref[:, at] = (grad_hidden * slope_ref[:, at].astype(f32)).astype(bf16)

        loads[1].wait()
        grad_normed = product_transposed(upward_ref[...], w_expand[...])
        back, gain, bias = layer_norm_back(middle_ref[...], gains_ref[1:2], grad_normed)
        grad_middle = back + grad_ref[...].astype(f32)
        grad_middle_ref[...] = grad_middle
        branch = grad_middle.astype(bf16)
        branch_ref[...] = branch
        small_ref[...] = jnp.concatenate([gain, bias], axis=0)
        loads[2].wait()
        attended = product_transposed(branch, w_out[...]).astype(bf16)
        split_heads(attended, task_ref, 0, batches, 0, width)
        for k in range(SPAN):
            sent_refs[k][:, 0:own] = share_ref[member_ref[0] ^ k]
            sent_refs[k][:, own : own + width] = grad_ref[...]
            sent_refs[k][:, own + width : own + 2 * width] = branch
            sent_refs[k][:, own + 2 * width :] = upward_ref[...]

    return call(
        kernel,
        (member, grad, middle, slope, gains, share, heads_out, expand, contract),
        [SCALARS] + [WHOLE] * 5 + [ANY] * 3,
        [
            shaped(rows, hidden_width),
            shaped(rows, width, kind=f32),
            shaped(rows, width),
            shaped(batches * PAIRS, patch_rows, PAIR),
            shaped(2, width, kind=f32),
        ]
        + [shaped(rows, whole)] * SPAN,
        [WHOLE] * (5 + SPAN),
        [
            pltpu.VMEM(heads_out.shape, bf16),
            pltpu.VMEM(expand.shape, bf16),
            pltpu.VMEM(contract.shape, bf16),
            pltpu.SemaphoreType.DMA((3,)),
        ],
        deps=deps,
        micros=10,
    )


def global_end(
    batches, blocks, stream, grad_middle, small, gains, heads_in, member, share, deps=()
):
    rows, width = stream.shape
    n = len(blocks)
    room = 16

    def kernel(
        member_ref, stream_ref, grad_middle_ref, small_ref, gains_ref, share_ref, weight_hbm, *rest
    ):
        block_refs, rest = rest[:n], rest[n:]
        mixed_ref, low_ref, all_small_ref = rest[:3]
        sent_refs, (weight, sem) = rest[3 : 3 + SPAN], rest[3 + SPAN :]
        load = pltpu.make_async_copy(weight_hbm, weight, sem)
        load.start()
        merge_heads(block_refs, mixed_ref, batches, 3)
        load.wait()
        grad_normed = product_transposed(mixed_ref[...], weight[...])
        back, gain, bias = layer_norm_back(stream_ref[...], gains_ref[0:1], grad_normed)
        low_ref[...] = (back + grad_middle_ref[...]).astype(bf16)
        smalls = jnp.concatenate([gain, small_ref[0:1], bias, small_ref[1:2]], axis=0)
        all_small_ref[...] = smalls
        tail = jnp.concatenate([smalls, jnp.zeros((room - 4, width), f32)], axis=0).astype(bf16)
        for k in range(SPAN):
            sent_refs[k][0:rows, 0 : 3 * width] = mixed_ref[...]
            sent_refs[k][0:rows, 3 * width :] = share_ref[member_ref[0] ^ k]
            sent_refs[k][rows:, 0:width] = tail
            sent_refs[k][rows:, width:] = jnp.zeros((room, 2 * width + share_ref.shape[2]), bf16)

    return call(
        kernel,
        (member, stream, grad_middle, small, gains, share, heads_in, *blocks),
        [SCALARS] + [WHOLE] * 5 + [ANY] + [WHOLE] * n,
        [shaped(rows, 3 * width), shaped(rows, width), shaped(4, width, kind=f32)]
        + [shaped(rows + room, 3 * width + share.shape[2])] * SPAN,
        [WHOLE] * (3 + SPAN),
        [pltpu.VMEM(heads_in.shape, bf16), pltpu.SemaphoreType.DMA],
        deps=deps,
        micros=6,
    )


def patch_backward(section, ids, embedded, weight, own, crossed, deps=()):
    rows, width = embedded.shape
    block = own[0].shape[0]
    n = len(own)

    def kernel(section_ref, ids_ref, embedded_ref, weight_ref, crossed_ref, *rest):
        own_refs, (patch_ref, table_ref, gathered) = rest[:n], rest[n:]

        @pl.when(section_ref[0] == 0)
        def _():
            for k in range(n):
                gathered[k * block : (k + 1) * block, :] = own_refs[k][...]

        @pl.when(section_ref[0] != 0)
        def _():
            gathered[...] = crossed_ref[...]

        patch_ref[...] = transposed_product(embedded_ref[...], gathered[...]).astype(bf16)
        grad_embedded = product_transposed(gathered[...], weight_ref[...]).astype(bf16)
        vocabulary = lax.broadcasted_iota(jnp.int32, (rows, VOCAB), 1)
        onehot = jnp.where(ids_ref[...] == vocabulary, 1.0, 0.0).astype(bf16)
        table_ref[...] = transposed_product(onehot, grad_embedded).astype(bf16)

    return call(
        kernel,
        (section, ids.reshape(rows, 1), embedded, weight, crossed, *own),
        [SCALARS] + [WHOLE] * (4 + n),
        [shaped(weight.shape[0], width), shaped(VOCAB, width)],
        [WHOLE] * 2,
        [pltpu.VMEM((rows, width), bf16)],
        deps=deps,
        micros=6,
    )


def leave_by_group(group, buffer, targets, sems):
    for j in range(len(targets)):
        for k in range(len(targets)):

            @pl.when((group ^ j) == k)
            def _(j=j, k=k):
                pltpu.make_async_copy(buffer.at[j], targets[k], sems.at[k]).start()

    for k in range(len(targets)):
        pltpu.make_async_copy(buffer.at[0], targets[k], sems.at[k]).wait()


def feed_gradients(group, sent, own, width, deps=()):
    rows = sent[0].shape[0]
    hidden_width = sent[0].shape[1] - own - 2 * width
    deep, thin = hidden_width // GROUPS, width // GROUPS
    chunks = hidden_width // width
    block = deep + (chunks + 1) * thin

    def kernel(group_ref, *refs):
        sent_refs, targets = refs[: len(sent)], refs[len(sent) : len(sent) + 4]
        buffer, sems = refs[len(sent) + 4 :]

        def columns(start, size):
            return jnp.concatenate([ref[:, start : start + size] for ref in sent_refs], axis=0)

        part = transposed_product(columns(0, 4 * deep), columns(own, width))
        for j in range(4):
            buffer[j, 0:deep, :] = part[j * deep : (j + 1) * deep].astype(bf16)
        left = columns(4 * deep, 4 * thin)
        for c in range(chunks):
            part = transposed_product(left, columns(own + (2 + c) * width, width))
            for j in range(4):
                at = deep + c * thin
                buffer[j, at : at + thin, :] = part[j * thin : (j + 1) * thin].astype(bf16)
        part = transposed_product(columns(4 * (deep + thin), 4 * thin), columns(own + width, width))
        for j in range(4):
            buffer[j, block - thin : block, :] = part[j * thin : (j + 1) * thin].astype(bf16)
        leave_by_group(group_ref[0], buffer, targets, sems)

    return call(
        kernel,
        (group, *sent),
        [SCALARS] + [WHOLE] * len(sent),
        [shaped(block, width)] * 4,
        [ANY] * 4,
        [pltpu.VMEM((4, block, width), bf16), pltpu.SemaphoreType.DMA((4,))],
        deps=deps,
        micros=6,
    )


def heads_gradients(group, sent, rows, width, deps=()):
    thin = width // GROUPS
    room = sent[0].shape[0] - rows
    block = 3 * thin + room

    def kernel(group_ref, *refs):
        sent_refs, targets = refs[: len(sent)], refs[len(sent) : len(sent) + 4]
        buffer, sems = refs[len(sent) + 4 :]

        def columns(start, size):
            return jnp.concatenate([ref[0:rows, start : start + size] for ref in sent_refs], axis=0)

        left = columns(3 * width, 4 * thin)
        for c in range(3):
            part = transposed_product(left, columns(c * width, width))
            for j in range(4):
                buffer[j, c * thin : (c + 1) * thin, :] = part[j * thin : (j + 1) * thin].astype(bf16)
        small = sum(ref[rows:, 0:width].astype(f32) for ref in sent_refs).astype(bf16)
        for j in range(4):
            buffer[j, 3 * thin :, :] = small
        leave_by_group(group_ref[0], buffer, targets, sems)

    return call(
        kernel,
        (group, *sent),
        [SCALARS] + [WHOLE] * len(sent),
        [shaped(block, width)] * 4,
        [ANY] * 4,
        [pltpu.VMEM((4, block, width), bf16), pltpu.SemaphoreType.DMA((4,))],
        deps=deps,
        micros=4,
    )


def section_send(x, origin, target, pairs):
    count = lax.axis_size("seq")
    joint = [(origin * count + i, target * count + j) for i, j in pairs]
    return lax.ppermute(x, ("section", "seq"), joint)


def section_swap(x):
    return lax.ppermute(x, "section", [(0, 1), (1, 0)])


def by_slot(buffer, count, swap, pieces):
    if count == GROUPS:
        return buffer
    depth = count.bit_length() - 1
    split = count // GROUPS
    parts, start = [], 0
    for size, shared in pieces:
        part = buffer[:, start : start + size]
        start += size
        kept = shared or size // split
        if shared:
            part = jnp.broadcast_to(part[:, None, :shared], (GROUPS, split, shared, part.shape[2]))
        parts.append(part.reshape(count, kept, part.shape[-1]))
    whole = jnp.concatenate(parts, axis=1)
    order = list(range(depth))
    if swap:
        order[0], order[1] = order[1], order[0]
    bits = whole.reshape((2,) * depth + whole.shape[1:])
    bits = jnp.transpose(bits, [depth - 1 - b for b in order] + [depth, depth + 1])
    return bits.reshape(whole.shape)


def added(held, length, kind=bf16, deps=()):
    count = len(held)
    shape = held[0][0].shape[1:]
    if not deps:
        total = 0.0
        for array, start, taken in held:
            term = lax.dynamic_slice(array, (start, 0, 0), (length,) + shape).astype(f32)
            total = total + (term if taken is None else jnp.where(taken > 0, term, 0.0))
        return total.astype(kind)
    size = max(1, length // 4)
    scalars = [start for _, start, _ in held] + [1 if t is None else t for _, _, t in held]
    scalars = jnp.stack([jnp.asarray(x, jnp.int32) for x in scalars])

    def kernel(scalar_ref, *refs):
        total = jnp.zeros((size,) + shape, f32)
        for j in range(count):
            term = refs[j][...].astype(f32)
            if held[j][2] is not None:
                term = jnp.where(scalar_ref[count + j] > 0, term, 0.0)
            total = total + term
        refs[-1][...] = total.astype(kind)

    def spec(j):
        return pl.BlockSpec((size,) + shape, lambda i, ref: (ref[j] // size + i, 0, 0))

    return pl.pallas_call(
        kernel,
        grid_spec=pltpu.PrefetchScalarGridSpec(
            num_scalar_prefetch=1,
            grid=(length // size,),
            in_specs=[spec(j) for j in range(count)] + [ANY] * len(deps),
            out_specs=pl.BlockSpec((size,) + shape, lambda i, ref: (i, 0, 0)),
        ),
        out_shape=jax.ShapeDtypeStruct((length,) + shape, kind),
        compiler_params=pltpu.CompilerParams(vmem_limit_bytes=VMEM),
        cost_estimate=cost(4),
    )(scalars, *[array for array, _, _ in held], *deps)


class Halving:
    def __init__(self, parts):
        self.count = lax.axis_size("seq")
        self.depth = self.count.bit_length() - 1
        self.held = [(part, 0, taken) for part, taken in parts]
        self.step = 0
        self.leaving = None

    def send(self, *deps):
        place, section = lax.axis_index("seq"), lax.axis_index("section")
        bits = [self.step, self.step]
        if self.step < 2:
            bits[1] = 1 - self.step
        mine = jnp.where(section == 0, (place >> bits[0]) & 1, (place >> bits[1]) & 1)
        half = self.count >> (self.step + 1)
        self.leaving = added(
            [(array, start + (1 - mine) * half, taken) for array, start, taken in self.held],
            half,
            deps=deps,
        )
        joint = [
            (origin * self.count + i, origin * self.count + (i ^ (1 << bits[origin])))
            for origin in range(2)
            for i in range(self.count)
        ]
        arrived = lax.ppermute(self.leaving, ("section", "seq"), joint)
        self.held = [(array, start + mine * half, taken) for array, start, taken in self.held]
        self.held.append((arrived, 0, None))
        self.step += 1

    def total(self):
        while self.step < self.depth:
            self.send()
        return added(self.held, 1, f32)[0]


def on_device(
    byte_values,
    item_lengths,
    embed_tables,
    patch_weight,
    norm_gains,
    norm_biases,
    heads_in,
    heads_out,
    expand_weight,
    contract_weight,
    out_grad,
):
    place = lax.axis_index("seq")
    count = lax.axis_size("seq")
    section = lax.axis_index("section")
    is_global = section == 0
    batches, byte_rows = byte_values.shape
    patch_rows = byte_rows // PATCH
    width = heads_out.shape[2]
    rows = batches * patch_rows
    total_patches = patch_rows * count
    gains, biases = norm_gains[0], norm_biases[0]
    heads_in, heads_out = heads_in[0], heads_out[0]
    expand, contract = expand_weight[0], contract_weight[0]
    own_table = embed_tables[0]
    straight = [(i, i) for i in range(count)]

    quarters = PATCH // 2
    span = count // quarters
    group, member = place // span, place % span
    shard_rows = patch_weight.shape[0]
    pieces = [patch_weight]
    for k in range(1, span):
        pieces.append(lax.ppermute(patch_weight, "seq", [(i, i ^ k) for i in range(count)]))
    other_table = section_swap(own_table)
    global_table = jnp.where(is_global, own_table, other_table)
    local_table = jnp.where(is_global, other_table, own_table)
    which_byte = section * quarters + group
    byte_ids = []
    for k in range(quarters):
        theirs = byte_values
        if k:
            theirs = lax.ppermute(byte_values, "seq", [(i, i ^ (k * span)) for i in range(count)])
        theirs = theirs.reshape(rows, PATCH)
        byte_ids.append(lax.dynamic_index_in_dim(theirs, which_byte, 1, keepdims=False))
    byte_ids = jnp.concatenate(byte_ids)
    embedded, byte_weight, shares, low_shares = patch_forward(
        member.reshape(1).astype(jnp.int32), byte_ids, global_table, pieces
    )
    shares = shares + section_send(low_shares, 1, 0, straight).astype(f32)
    shares = shares.reshape(quarters, rows, width)
    parts = []
    for k in range(1, quarters):
        pairs = [(i, i ^ (k * span)) for i in range(count)]
        parts.append(section_send(shares[k].astype(bf16), 0, 0, pairs))

    arrived = [section_send(w, 1, 0, straight) for w in (heads_in, heads_out, expand, contract)]
    other_norms = section_swap(jnp.concatenate([gains, biases]))
    local_gains = jnp.where(is_global, other_norms[:2], gains)
    local_biases = jnp.where(is_global, other_norms[2:], biases)

    tasks = batches * PAIRS
    first_tasks = min(tasks, count)
    spare_tasks = tasks - first_tasks

    def to_tasks(blocks):
        columns = blocks.shape[2]
        slots = jnp.pad(blocks[:first_tasks], ((0, count - first_tasks), (0, 0), (0, 0)))
        if spare_tasks:
            spare = section_send(blocks[first_tasks:], 0, 1, straight)
            spare = jnp.pad(spare, ((0, count - spare_tasks), (0, 0), (0, 0)))
            slots = jnp.where(is_global, slots, spare)
        landed = lax.all_to_all(slots, "seq", 0, 0)
        return landed.reshape(total_patches, columns)

    def from_tasks(results):
        columns = results.shape[1]
        slots = lax.all_to_all(results.reshape(count, patch_rows, columns), "seq", 0, 0)
        if spare_tasks:
            return [slots, section_send(slots[:spare_tasks], 1, 0, straight)]
        return [slots]

    task = jnp.minimum(jnp.where(is_global, place, first_tasks + place), tasks - 1)
    task_lengths = lax.dynamic_index_in_dim(item_lengths, task // PAIRS, 0, keepdims=False)
    task_owners = locate(jnp.arange(total_patches, dtype=jnp.int32) * PATCH, task_lengths)[0]

    stream, normed, tasks_out, normed_share = global_start(
        batches, shares[0], parts, gains, biases, heads_in
    )
    qkv = to_tasks(tasks_out)
    attended, middle, normed_two, slope, hidden, sent, feed_share = global_feed_forward(
        batches,
        from_tasks(global_attention(qkv, task_owners)),
        stream,
        gains,
        biases,
        heads_out,
        expand,
        contract,
    )
    sent = sent.reshape(batches, patch_rows, width)

    half = patch_rows // 2
    half_bytes = half * PATCH
    chunks = half_bytes // BLOCK
    onward = [(i, i + 1) for i in range(count - 1)]
    backward = [(i + 1, i) for i in range(count - 1)]
    near = section_send(sent[:, half - 1 : patch_rows - 1], 0, 1, straight)
    edge = section_send(sent[:, patch_rows - 1 :], 0, 0, onward)
    shifted = jnp.where(is_global, jnp.concatenate([edge, sent[:, : half - 1]], axis=1), near)

    byte_places = place * byte_rows + jnp.arange(byte_rows, dtype=jnp.int32)
    live_bytes = jnp.stack([locate(byte_places, item_lengths[m])[1] for m in range(batches)])
    patch_places = place * byte_rows + section * half_bytes + PATCH * jnp.arange(half, dtype=jnp.int32)
    same_item = jnp.stack(
        [
            locate(patch_places, item_lengths[m])[0]
            == locate(patch_places - PATCH, item_lengths[m])[0]
            for m in range(batches)
        ]
    )[:, :, None]
    shifted = jnp.where(same_item, shifted, jnp.zeros((), bf16))
    half_start = section * half_bytes
    own_ids = lax.dynamic_slice_in_dim(byte_values, half_start, half_bytes, 1)
    own_live = lax.dynamic_slice_in_dim(live_bytes, half_start, half_bytes, 1)
    own_grad = lax.dynamic_slice_in_dim(out_grad, half_start, half_bytes, 1)
    weights = (heads_in, heads_out, expand, contract)
    flag = section.reshape(1).astype(jnp.int32)
    block_patches = BLOCK // PATCH

    local_outs, feed_sums, heads_sums, grads_shifted = [], [], [], []
    for c in range(chunks):
        here = slice(c * BLOCK, (c + 1) * BLOCK)
        there = slice(c * block_patches, (c + 1) * block_patches)
        ids = own_ids[:, here].reshape(batches * BLOCK)
        live = own_live[:, here].reshape(batches * BLOCK)
        same = same_item[:, there].astype(jnp.int32).reshape(batches * block_patches, 1)
        act, *saved, small, keep, send = local_first(
            count,
            flag,
            ids,
            local_table,
            shifted[:, there].reshape(batches * block_patches, width),
            local_gains,
            local_biases,
            live,
            own_grad[:, here].reshape(batches * BLOCK, width),
            weights,
            arrived,
        )
        local_outs.append(act.reshape(batches, BLOCK, width))
        feed_sums.append((keep, send))
        grad_shifted, keep, send = local_second(
            count, flag, ids, same, local_gains, live, saved, small, weights, arrived
        )
        heads_sums.append((keep, send))
        grads_shifted.append(grad_shifted.reshape(batches, block_patches, width))
    local_out = jnp.concatenate(local_outs, axis=1)
    grad_shifted = jnp.concatenate(grads_shifted, axis=1)

    other_out = section_send(local_out, 0, 1, straight)
    own_sent = jnp.broadcast_to(
        sent[:, :, None, :], (batches, patch_rows, PATCH, width)
    ).reshape(batches, byte_rows, width)
    own_sent = jnp.where(live_bytes[:, :, None], own_sent, jnp.zeros((), bf16))
    activations = jnp.where(
        is_global, own_sent, jnp.concatenate([other_out, local_out], axis=1)
    )

    shard = width // count
    room = VOCAB // count
    group_shard, group_room = width // GROUPS, VOCAB // GROUPS
    small_rows = max(4, room)
    feed_pieces = {
        False: [(contract.shape[0] // GROUPS, 0)],
        True: [(group_shard, 0)] * (expand.shape[1] // width),
    }
    heads_pieces = {
        False: [(group_shard, 0), (group_shard, 0), (group_room, 0), (group_room, small_rows)],
        True: [(group_shard, 0), (group_shard, 0), (2 * group_room, room + small_rows)],
    }

    def ordered(buffer, pieces):
        if count == GROUPS:
            return buffer
        return jnp.where(
            is_global,
            by_slot(buffer, count, False, pieces[False]),
            by_slot(buffer, count, True, pieces[True]),
        )

    def local_parts(entries, pieces):
        parts = []
        for keep, send in entries:
            parts += [(ordered(keep, pieces), None), (ordered(section_swap(send), pieces), None)]
        return parts

    def global_parts(first, second, pieces):
        crossed = section_send(second, 0, 1, straight)
        if count != GROUPS:
            return [(ordered(jnp.where(is_global, first, crossed), pieces), None)]
        return [(first, is_global.astype(jnp.int32)), (crossed, section)]

    near_back = section_send(grad_shifted, 1, 0, straight)
    edge_back = section_send(grad_shifted[:, :1], 0, 0, backward)
    grad_sent = jnp.concatenate([grad_shifted[:, 1:], near_back, edge_back], axis=1)
    grad_sent = grad_sent.reshape(rows, width)

    in_plane = span == SPAN and count == GROUPS
    member_flag = (member % SPAN).reshape(1).astype(jnp.int32)
    group_flag = group.reshape(1).astype(jnp.int32)

    def plane_send(blocks):
        return [blocks[0]] + [
            section_send(blocks[k], 0, 0, [(i, i ^ k) for i in range(count)])
            for k in range(1, SPAN)
        ]

    def group_sum(blocks):
        return sum(
            [blocks[0].astype(f32)]
            + [
                section_send(
                    blocks[k], 0, 0, [(i, i ^ (k * span)) for i in range(count)]
                ).astype(f32)
                for k in range(1, quarters)
            ]
        )

    local_feed = Halving(local_parts(feed_sums, feed_pieces))
    local_heads = Halving(local_parts(heads_sums, heads_pieces))
    local_feed.send(grad_sent)
    local_heads.send(grad_sent)
    grad_upward, grad_middle, attend_branch, task_grads, small, *feed_sent = global_feed_backward(
        batches,
        grad_sent,
        middle,
        slope,
        gains,
        heads_out,
        expand,
        contract,
        member_flag,
        feed_share,
        [local_feed.leaving, local_heads.leaving],
    )
    if in_plane:
        feed_sent = plane_send(feed_sent)
    task_grads = to_tasks(task_grads)
    local_feed.send()
    grad_mixed = from_tasks(
        global_attention(qkv, task_owners, task_grads, [local_feed.leaving])
    )
    local_heads.send()
    local_feed.send()
    grad_mixed, own_rows, small, *heads_sent = global_end(
        batches,
        grad_mixed,
        stream,
        grad_middle,
        small,
        gains,
        heads_in,
        member_flag,
        normed_share,
        [local_feed.leaving, local_heads.leaving],
    )
    if in_plane:
        feed_blocks = feed_gradients(group_flag, feed_sent, feed_share.shape[2], width)
        heads_blocks = heads_gradients(group_flag, plane_send(heads_sent), rows, width)

    gathered = [own_rows]
    for k in range(1, quarters):
        pairs = [(i, i ^ (k * span)) for i in range(count)]
        gathered.append(section_send(own_rows, 0, 0, pairs))
    crossed = section_send(jnp.concatenate(gathered), 0, 1, straight)
    local_feed.send()
    local_heads.send()
    patch_share, table_share = patch_backward(
        flag,
        byte_ids,
        embedded,
        byte_weight,
        gathered,
        crossed,
        [local_feed.leaving, local_heads.leaving],
    )
    patch_share = patch_share.reshape(span, shard_rows, width)
    patch_grads = lax.dynamic_index_in_dim(patch_share, member, 0, keepdims=False).astype(f32)
    for k in range(1, span):
        leaving = lax.dynamic_index_in_dim(patch_share, member ^ k, 0, keepdims=False)
        patch_grads = patch_grads + lax.ppermute(
            leaving, "seq", [(i, i ^ k) for i in range(count)]
        ).astype(f32)
    table_share = table_share + section_send(table_share, 1, 0, straight)
    table_parts = lax.all_to_all(table_share.reshape(count, VOCAB // count, width), "seq", 0, 0)
    global_table_grad = jnp.sum(table_parts.astype(f32), axis=0)

    def ordered_rows(first, second):
        feed_rows = contract.shape[0] // count
        expand_sum = [second[k * shard : (k + 1) * shard] for k in range(feed_rows // shard)]
        ins = [first[feed_rows :][:shard], second[feed_rows :][:shard]]
        ins.append(second[feed_rows + shard :][:shard])
        rest = first[feed_rows + shard :]
        return (
            first[:feed_rows],
            jnp.concatenate(expand_sum, axis=1),
            jnp.concatenate(ins, axis=1),
            rest[:shard],
            rest[shard : shard + room],
            rest[shard + room : shard + room + 4],
        )

    own_local = jnp.concatenate([local_feed.total(), local_heads.total()])
    if in_plane:
        feed_block, heads_block = group_sum(feed_blocks), group_sum(heads_blocks)
        deep = contract.shape[0] // count
        chunks_of = [feed_block[deep + k * shard : deep + (k + 1) * shard] for k in range(5)]
        ins = [heads_block[k * shard : (k + 1) * shard] for k in range(3)]
        global_sums = (
            feed_block[:deep],
            jnp.concatenate(chunks_of[:4], axis=1),
            jnp.concatenate(ins, axis=1),
            chunks_of[4],
            global_table_grad,
            heads_block[3 * shard :][:4],
        )
        crossed = section_send(own_local.astype(bf16), 0, 1, straight).astype(f32)
        local_sums = ordered_rows(crossed, own_local)
    else:
        feed_sum = Halving(
            global_parts(
                *global_feed(count, hidden, grad_sent, normed_two, grad_upward), feed_pieces
            )
        )
        heads_sum = Halving(
            global_parts(
                *global_heads(count, normed, grad_mixed, attended, attend_branch, small),
                heads_pieces,
            )
        )
        own_global = jnp.concatenate([feed_sum.total(), heads_sum.total()])
        crossed = section_swap(jnp.where(is_global, own_local, own_global).astype(bf16)).astype(f32)
        global_sums = ordered_rows(own_global, crossed)
        global_sums = global_sums[:4] + (global_table_grad, global_sums[5])
        local_sums = ordered_rows(crossed, own_local)
    contract_grad, expand_grad, in_grad, out_grads, table_grad, small = (
        jnp.where(is_global, upper, lower) for upper, lower in zip(global_sums, local_sums)
    )
    small = lax.dynamic_slice_in_dim(small, place * shard, shard, 1)
    return (
        activations[None],
        table_grad[None],
        patch_grads,
        small[None, 0:2],
        small[None, 2:4],
        in_grad[None],
        out_grads[None],
        expand_grad[None],
        contract_grad[None],
    )


def solution(mesh):
    placed = (
        P(None, "seq"),
        P(),
        P("section", None, None),
        P(("section", "seq"), None),
        P("section", None, None),
        P("section", None, None),
        P("section", None, None),
        P("section", None, None),
        P("section", None, None),
        P("section", None, None),
        P(None, "seq", None),
    )
    return jax.shard_map(
        on_device,
        mesh=mesh,
        in_specs=placed,
        out_specs=(
            P("section", None, "seq", None),
            P("section", "seq", None),
            P(("section", "seq"), None),
            P("section", None, "seq"),
            P("section", None, "seq"),
            P("section", "seq", None),
            P("section", "seq", None),
            P("section", "seq", None),
            P("section", "seq", None),
        ),
        check_vma=False,
    )
```

```python
from functools import partial

import jax
import jax.numpy as jnp
from jax import lax
from jax.experimental import pallas as pl
from jax.experimental.pallas import tpu as pltpu
from jax.sharding import PartitionSpec as P

HEADS = 12
HEAD_SIZE = 64
VOCAB = 256
PATCH = 8
ITEMS = 4
PAIRS = HEADS // 2
PAIR = 2 * HEAD_SIZE
SCALE = HEAD_SIZE ** (-0.5)
EPSILON = 1e-05
MASKED = -1e30
BLOCK = 128
TILE = 384
GROUPS = 16
SPAN = 4
VMEM = 60 * 1024 * 1024

bf16 = jnp.bfloat16
f32 = jnp.float32


def cost(micros):
    return pl.CostEstimate(flops=int(micros * 1.1e9), bytes_accessed=1, transcendentals=0)


def product(former, latter):
    return jnp.dot(former, latter, preferred_element_type=f32)


def transposed_product(former, latter):
    return lax.dot_general(former, latter, (((0,), (0,)), ((), ())), preferred_element_type=f32)


def product_transposed(former, latter):
    return lax.dot_general(former, latter, (((1,), (1,)), ((), ())), preferred_element_type=f32)


def normalise(values):
    average = jnp.mean(values, axis=-1, keepdims=True)
    centered = values - average
    inverse_root = lax.rsqrt(jnp.mean(centered * centered, axis=-1, keepdims=True) + EPSILON)
    return centered * inverse_root, inverse_root


def layer_norm(values, gain, bias):
    return normalise(values)[0] * gain + bias


def layer_norm_back(values, gain, grad):
    unit, inverse_root = normalise(values)
    scaled = grad * gain
    grad_values = inverse_root * (
        scaled
        - jnp.mean(scaled, axis=-1, keepdims=True)
        - unit * jnp.mean(scaled * unit, axis=-1, keepdims=True)
    )
    return (
        grad_values,
        jnp.sum(grad * unit, axis=0, keepdims=True),
        jnp.sum(grad, axis=0, keepdims=True),
    )


def locate(positions, lengths_row):
    padded = (lengths_row + PATCH - 1) // PATCH * PATCH
    item_ends = jnp.cumsum(padded)
    starts = item_ends - padded
    inside = (positions[:, None] >= starts[None, :]) & (positions[:, None] < item_ends[None, :])
    offsets = jnp.arange(ITEMS, dtype=jnp.int32)[None, :] - ITEMS
    owners = jnp.sum(jnp.where(inside, offsets, 0), axis=1) + ITEMS
    live_mask = jnp.any(inside & (positions[:, None] < (starts + lengths_row)[None, :]), axis=1)
    return (owners, live_mask)


def slot_of(q, count):
    if count != GROUPS:
        return q
    return (q % SPAN) * (GROUPS // SPAN) + q // SPAN


def store_rows(buffer, value, count, start, columns=slice(None)):
    rows = value.shape[0] // GROUPS
    for q in range(GROUPS):
        buffer[slot_of(q, count), pl.ds(start, rows), columns] = value[
            q * rows : (q + 1) * rows
        ].astype(bf16)


def patch_bias(live_row):
    rows = lax.broadcasted_iota(jnp.int32, (BLOCK, BLOCK), 0)
    columns = lax.broadcasted_iota(jnp.int32, (BLOCK, BLOCK), 1)
    same = (rows // PATCH) == (columns // PATCH)
    allowed = same & (columns <= rows) & ((live_row > 0) | (columns == rows))
    bias = jnp.where(allowed, 0.0, MASKED)
    return jnp.concatenate([bias, bias], axis=0)


def softmax_rows(scores):
    peak = jnp.max(scores, axis=-1, keepdims=True)
    exponents = jnp.exp(scores - peak)
    return exponents * (1.0 / jnp.sum(exponents, axis=-1, keepdims=True))


def lane_masks():
    lanes = lax.broadcasted_iota(jnp.int32, (1, PAIR), 1)
    low = jnp.where(lanes < HEAD_SIZE, 1.0, 0.0)
    return lanes < HEAD_SIZE, low.astype(bf16), (1.0 - low).astype(bf16)


def stacked(values, low, high, scale=1.0):
    return jnp.concatenate([values * (low * scale), values * (high * scale)], axis=0)


def unstacked(values, is_low):
    half = values.shape[0] // 2
    return jnp.where(is_low, values[:half], values[half:])


def pair_probabilities(queries, keys, bias, masks):
    _, low, high = masks
    return softmax_rows(product_transposed(stacked(queries, low, high, SCALE), keys) + bias)


def pair_forward(queries, keys, values, bias, masks):
    probabilities = pair_probabilities(queries, keys, bias, masks)
    return unstacked(product(probabilities.astype(bf16), values), masks[0])


def pair_backward(queries, keys, values, grads, probabilities, masks):
    is_low, low, high = masks
    both = stacked(queries, low, high, SCALE)
    both_grads = stacked(grads, low, high)
    prob_grads = product_transposed(both_grads, values)
    delta = jnp.sum(probabilities * prob_grads, axis=-1, keepdims=True)
    score_grads = (probabilities * (prob_grads - delta)).astype(bf16)
    return (
        unstacked(product(score_grads, keys), is_low) * SCALE,
        transposed_product(score_grads, both),
        transposed_product(probabilities.astype(bf16), both_grads),
    )


def gelu_and_slope(x):
    root = 0.7978845608028654
    cubic = 0.044715
    square = x * x
    bent = jnp.tanh(x * (root + (root * cubic) * square))
    half = 0.5 * (1.0 + bent)
    slope = half + (0.5 * x) * (1.0 - bent * bent) * (root + (3.0 * root * cubic) * square)
    return x * half, slope


def fetch(section, own, arrived, target, sem):
    @pl.when(section == 0)
    def _():
        pltpu.make_async_copy(arrived, target, sem).start()

    @pl.when(section != 0)
    def _():
        pltpu.make_async_copy(own, target, sem).start()


def section_columns(hidden_width, width):
    tables = []
    for names in (
        ("hidden", "branch", "attended", "attend_branch", "normed", "queries", "stream"),
        ("upward", "normed_two", "normed", "keys", "values"),
    ):
        table, start = {}, 0
        for name in names:
            size = hidden_width if start == 0 else width
            table[name] = slice(start, start + size)
            start += size
        tables.append((table, start))
    return tables


SMALL_ROWS = 16


def item_spans(numbers_ref, first, batch):
    spans, start = [], 0
    for k in range(ITEMS):
        length = numbers_ref[first + batch * ITEMS + k]
        stop = start + (length + PATCH - 1) // PATCH * PATCH
        spans.append((start, start + length, stop))
        start = stop
    return spans


def is_live(positions, spans):
    live = jnp.zeros(positions.shape, jnp.bool_)
    for start, live_end, _ in spans:
        live = live | ((positions >= start) & (positions < live_end))
    return live


def owner_of(positions, spans):
    owner = jnp.full(positions.shape, ITEMS, jnp.int32)
    for k, (start, _, stop) in enumerate(spans):
        owner = jnp.where((positions >= start) & (positions < stop), k, owner)
    return owner


def local_kernel(
    patch_rows,
    numbers_ref,
    ids_ref,
    table_ref,
    sent_ref,
    edge_ref,
    near_ref,
    gains_ref,
    biases_ref,
    out_grad_hbm,
    own_in,
    own_out,
    own_expand,
    own_contract,
    new_in,
    new_out,
    new_expand,
    new_contract,
    act_ref,
    grad_shifted_ref,
    grad_edge_ref,
    keep_ref,
    send_ref,
    w_in,
    w_out,
    w_expand,
    w_contract,
    first,
    second,
    out_grad_ref,
    source_ref,
    stream_ref,
    mixed_ref,
    middle_ref,
    slope_ref,
    grad_middle_ref,
    grad_attended_ref,
    grad_stream_ref,
    probability_ref,
    sems,
    out_sems,
):
    section, offset, chunk = numbers_ref[0], numbers_ref[1], numbers_ref[2]
    rows, width = act_ref.shape
    batches = rows // BLOCK
    hidden_width = w_expand.shape[1]
    half = patch_rows // 2
    block_patches = BLOCK // PATCH
    lane = pl.multiple_of(section * (half * PATCH) + chunk * BLOCK, BLOCK)
    base = offset + lane
    grads_in = [
        pltpu.make_async_copy(
            out_grad_hbm.at[m, pl.ds(lane, BLOCK)],
            out_grad_ref.at[m * BLOCK : (m + 1) * BLOCK],
            sems.at[4 + m],
        )
        for m in range(batches)
    ]
    fetch(section, own_in, new_in, w_in, sems.at[0])
    for copy in grads_in:
        copy.start()
    fetch(section, own_out, new_out, w_out, sems.at[1])
    fetch(section, own_expand, new_expand, w_expand, sems.at[2])
    fetch(section, own_contract, new_contract, w_contract, sems.at[3])
    (to_first, first_width), (to_second, second_width) = section_columns(hidden_width, width)
    body = slice(0, rows)
    out_count = [0]

    def leave(from_first, columns, at_rows=body):
        source = first if from_first else second
        sem = out_sems.at[out_count[0]]
        out_count[0] += 1
        part = source.at[at_rows, columns]

        @pl.when(section == (0 if from_first else 1))
        def _():
            pltpu.make_async_copy(part, keep_ref.at[at_rows, columns], sem).start()

        @pl.when(section != (0 if from_first else 1))
        def _():
            pltpu.make_async_copy(part, send_ref.at[at_rows, columns], sem).start()

        return pltpu.make_async_copy(part, keep_ref.at[at_rows, columns], sem)

    blocks = [slice(m * BLOCK, (m + 1) * BLOCK) for m in range(batches)]
    spans = [item_spans(numbers_ref, 3, m) for m in range(batches)]
    column = lax.broadcasted_iota(jnp.int32, (BLOCK, 1), 0)
    row = lax.broadcasted_iota(jnp.int32, (1, BLOCK), 1)
    live_columns = [is_live(base + column, span) for span in spans]
    biases_of = [
        patch_bias(jnp.where(is_live(base + row, span), 1, 0)) for span in spans
    ]
    sent_rows, edge_rows = sent_ref.shape[0], edge_ref.shape[0]
    source_ref[0:sent_rows, :] = sent_ref[...]
    source_ref[sent_rows : sent_rows + edge_rows, :] = edge_ref[...]
    source_ref[sent_rows + edge_rows :, :] = near_ref[...]

    for copy in grads_in:
        copy.wait()
    for m, at in enumerate(blocks):
        vocabulary = lax.broadcasted_iota(jnp.int32, (VOCAB, BLOCK), 0)
        ids = ids_ref[m : m + 1, pl.ds(lane, BLOCK)]
        onehot = jnp.where(ids == vocabulary, 1.0, 0.0).astype(bf16)
        patch = column // PATCH
        place = chunk * block_patches + patch
        start = base + patch * PATCH
        same = owner_of(start, spans[m]) == owner_of(start - PATCH, spans[m])
        inside = jnp.where(place == 0, sent_rows + m, m * patch_rows + place - 1)
        chosen = jnp.where(section == 0, inside, sent_rows + edge_rows + m * half + place)
        chosen = jnp.where(same, chosen, -1)
        columns = lax.broadcasted_iota(jnp.int32, (BLOCK, source_ref.shape[0]), 1)
        spread = jnp.where(columns == chosen, 1.0, 0.0).astype(bf16)
        stream = transposed_product(onehot, table_ref[...]) + product(spread, source_ref[...])
        stream_ref[at, :] = stream
        normed = layer_norm(stream, gains_ref[0:1], biases_ref[0:1]).astype(bf16)
        first[at, to_first["normed"]] = normed
        second[at, to_second["normed"]] = normed
        first[at, to_first["branch"]] = jnp.where(
            live_columns[m], out_grad_ref[at, :].astype(f32), 0.0
        ).astype(bf16)

    pltpu.make_async_copy(own_in, w_in, sems.at[0]).wait()
    for i in range(3 * width // TILE):
        at = slice(i * TILE, (i + 1) * TILE)
        mixed_ref[:, at] = product(first[body, to_first["normed"]], w_in[:, at]).astype(bf16)

    masks = lane_masks()

    def pair_columns(pair, start=0):
        return slice(start + pair * PAIR, start + (pair + 1) * PAIR)

    for m, at in enumerate(blocks):
        for pair in range(PAIRS):
            probabilities = pair_probabilities(
                mixed_ref[at, pair_columns(pair)],
                mixed_ref[at, pair_columns(pair, width)],
                biases_of[m],
                masks,
            )
            probability_ref[m * PAIRS + pair] = probabilities
            attended = product(
                probabilities.astype(bf16), mixed_ref[at, pair_columns(pair, 2 * width)]
            )
            first[at, pair_columns(pair, to_first["attended"].start)] = unstacked(
                attended, masks[0]
            ).astype(bf16)

    pltpu.make_async_copy(own_out, w_out, sems.at[1]).wait()
    for at in blocks:
        middle = stream_ref[at, :] + product(first[at, to_first["attended"]], w_out[...])
        middle_ref[at, :] = middle
        normed_two = layer_norm(middle, gains_ref[1:2], biases_ref[1:2]).astype(bf16)
        second[at, to_second["normed_two"]] = normed_two

    pltpu.make_async_copy(own_expand, w_expand, sems.at[2]).wait()
    for i in range(hidden_width // TILE):
        at = slice(i * TILE, (i + 1) * TILE)
        hidden, slope = gelu_and_slope(
            product(second[body, to_second["normed_two"]], w_expand[:, at])
        )
        first[body, at] = hidden.astype(bf16)
        slope_ref[:, at] = slope.astype(bf16)

    copies = [leave(True, slice(0, to_first["attended"].stop))]
    pltpu.make_async_copy(own_contract, w_contract, sems.at[3]).wait()
    live_column = jnp.concatenate([jnp.where(x, 1, 0) for x in live_columns], axis=0)
    for i in range(width // 256):
        at = slice(i * 256, (i + 1) * 256)
        result = middle_ref[:, at] + product(first[body, to_first["hidden"]], w_contract[:, at])
        act_ref[:, at] = jnp.where(live_column > 0, result, 0.0).astype(bf16)

    for i in range(hidden_width // TILE):
        at = slice(i * TILE, (i + 1) * TILE)
        grad_hidden = product_transposed(first[body, to_first["branch"]], w_contract[at, :])
        second[body, at] = (grad_hidden * slope_ref[:, at].astype(f32)).astype(bf16)

    copies.append(leave(False, slice(0, to_second["normed"].stop)))
    for i in range(width // 256):
        at = slice(i * 256, (i + 1) * 256)
        grad_middle_ref[:, at] = product_transposed(
            second[body, to_second["upward"]], w_expand[at, :]
        )

    gain_two = bias_two = gain_one = bias_one = jnp.zeros((1, width), f32)
    for at in blocks:
        back, gain, bias = layer_norm_back(
            middle_ref[at, :], gains_ref[1:2], grad_middle_ref[at, :]
        )
        grad_middle = back + first[at, to_first["branch"]].astype(f32)
        grad_middle_ref[at, :] = grad_middle
        branch = grad_middle.astype(bf16)
        first[at, to_first["attend_branch"]] = branch
        grad_attended_ref[at, :] = product_transposed(branch, w_out[...]).astype(bf16)
        gain_two, bias_two = gain_two + gain, bias_two + bias

    copies.append(leave(True, slice(to_first["attend_branch"].start, to_first["normed"].stop)))
    for m, at in enumerate(blocks):
        for pair in range(PAIRS):
            parts = pair_backward(
                mixed_ref[at, pair_columns(pair)],
                mixed_ref[at, pair_columns(pair, width)],
                mixed_ref[at, pair_columns(pair, 2 * width)],
                grad_attended_ref[at, pair_columns(pair)],
                probability_ref[m * PAIRS + pair],
                masks,
            )
            first[at, pair_columns(pair, to_first["queries"].start)] = parts[0].astype(bf16)
            second[at, pair_columns(pair, to_second["keys"].start)] = parts[1].astype(bf16)
            second[at, pair_columns(pair, to_second["values"].start)] = parts[2].astype(bf16)

    keys_values = slice(to_second["keys"].start, to_second["values"].stop)
    copies.append(leave(False, keys_values))
    for i in range(width // 256):
        at = slice(i * 256, (i + 1) * 256)
        grad_stream_ref[:, at] = product_transposed(
            first[body, to_first["queries"]], w_in[at, 0:width]
        ) + product_transposed(second[body, keys_values], w_in[at, width:])

    for m, at in enumerate(blocks):
        back, gain, bias = layer_norm_back(
            stream_ref[at, :], gains_ref[0:1], grad_stream_ref[at, :]
        )
        grad_stream = back + grad_middle_ref[at, :]
        first[at, to_first["stream"]] = grad_stream.astype(bf16)
        gain_one, bias_one = gain_one + gain, bias_one + bias
        summed = jnp.sum(grad_stream.reshape(block_patches, PATCH, width), axis=1)
        start = base + PATCH * lax.broadcasted_iota(jnp.int32, (block_patches, 1), 0)
        same = owner_of(start, spans[m]) == owner_of(start - PATCH, spans[m])
        summed = jnp.where(same, summed, 0.0).astype(bf16)
        grad_shifted_ref[m * block_patches : (m + 1) * block_patches, :] = summed
        grad_edge_ref[m : m + 1, :] = summed[0:1]

    grad_edge_ref[batches:, :] = jnp.zeros((SMALL_ROWS - batches, width), bf16)
    small = jnp.concatenate(
        [gain_one, gain_two, bias_one, bias_two, jnp.zeros((SMALL_ROWS - 4, width), f32)], axis=0
    )
    second[rows:, 0:width] = small.astype(bf16)
    copies.append(leave(False, slice(0, width), slice(rows, rows + SMALL_ROWS)))
    copies.append(leave(True, slice(to_first["queries"].start, first_width)))
    for copy in copies:
        copy.wait()


ANY = pl.BlockSpec(memory_space=pl.ANY)
WHOLE = pl.BlockSpec(memory_space=pltpu.VMEM)
SCALARS = pl.BlockSpec(memory_space=pltpu.SMEM)


def vmem(*shape, kind=bf16):
    return pltpu.VMEM(shape, kind)


def local_block(numbers, ids, table, sent, edge, near, gains, biases, out_grad, patch_rows, own, new):
    batches, width = out_grad.shape[0], out_grad.shape[2]
    rows = batches * BLOCK
    hidden_width = own[3].shape[0]
    (_, first_width), (_, second_width) = section_columns(hidden_width, width)
    part = jax.ShapeDtypeStruct((rows + SMALL_ROWS, first_width), bf16)
    return pl.pallas_call(
        partial(local_kernel, patch_rows),
        in_specs=[SCALARS] + [WHOLE] * 7 + [ANY] * 9,
        out_specs=[WHOLE] * 3 + [ANY] * 2,
        out_shape=[
            jax.ShapeDtypeStruct((rows, width), bf16),
            jax.ShapeDtypeStruct((rows // PATCH, width), bf16),
            jax.ShapeDtypeStruct((SMALL_ROWS, width), bf16),
            part,
            part,
        ],
        scratch_shapes=[
            vmem(*own[0].shape),
            vmem(*own[1].shape),
            vmem(*own[2].shape),
            vmem(*own[3].shape),
            vmem(*part.shape),
            vmem(part.shape[0], second_width),
            vmem(rows, width),
            vmem(sent.shape[0] + edge.shape[0] + near.shape[0], width),
            vmem(rows, width, kind=f32),
            vmem(rows, 3 * width),
            vmem(rows, width, kind=f32),
            vmem(rows, hidden_width),
            vmem(rows, width, kind=f32),
            vmem(rows, width),
            vmem(rows, width, kind=f32),
            vmem(batches * PAIRS, 2 * BLOCK, BLOCK, kind=f32),
            pltpu.SemaphoreType.DMA((4 + batches,)),
            pltpu.SemaphoreType.DMA((6,)),
        ],
        compiler_params=pltpu.CompilerParams(vmem_limit_bytes=VMEM),
        cost_estimate=cost(35),
    )(numbers, ids, table, sent, edge, near, gains, biases, out_grad, *own, *new)


def local_gradients(count, numbers, ids, keep, arrived, hidden_width, width, half, deps=()):
    rows = keep.shape[0] - SMALL_ROWS
    (to_first, first_width), (to_second, _) = section_columns(hidden_width, width)
    deep, shard, room = hidden_width // GROUPS, width // GROUPS, VOCAB // GROUPS
    block = deep + 2 * shard + room
    cuts = (slice(0, hidden_width + width), slice(hidden_width + width, first_width))

    def kernel(numbers_ref, ids_ref, keep_ref, new_ref, *rest):
        out_ref, held, smalls, sums, sems, out_sems = rest[len(deps) :]
        copies = []
        for k, cut in enumerate(cuts):
            for j, ref in enumerate((keep_ref, new_ref)):
                copies.append(
                    pltpu.make_async_copy(
                        ref.at[0:rows, cut], held.at[j * rows : (j + 1) * rows, cut], sems.at[2 * k + j]
                    )
                )
        for j, ref in enumerate((keep_ref, new_ref)):
            copies.append(
                pltpu.make_async_copy(
                    ref.at[rows : rows + SMALL_ROWS, 0:width], smalls.at[j], sems.at[4 + j]
                )
            )
        for copy in copies:
            copy.start()
        section_now, chunk = numbers_ref[0], numbers_ref[2]
        tile_shards = TILE // deep

        copies[0].wait()
        copies[1].wait()

        @pl.when(section_now == 0)
        def _():
            for i in range(hidden_width // TILE):
                part = transposed_product(
                    held[:, i * TILE : (i + 1) * TILE], held[:, to_first["branch"]]
                )
                for k in range(tile_shards):
                    slot = slot_of(i * tile_shards + k, count)
                    sums[slot, 0:deep, :] = part[k * deep : (k + 1) * deep].astype(bf16)

        @pl.when(section_now != 0)
        def _():
            for i in range(hidden_width // TILE):
                part = transposed_product(
                    held[:, to_second["normed_two"]], held[:, i * TILE : (i + 1) * TILE]
                )
                chunk, at = i * TILE // width, i * TILE % width
                store_rows(sums, part, count, chunk * shard, slice(at, at + TILE))

        feed = pl.ds(0, deep)
        pltpu.make_async_copy(sums.at[:, feed], out_ref.at[:, feed], out_sems.at[0]).start()
        for copy in copies[2:]:
            copy.wait()

        @pl.when(section_now == 0)
        def _():
            part = transposed_product(
                held[:, to_first["attended"]], held[:, to_first["attend_branch"]]
            )
            store_rows(sums, part, count, deep)
            part = transposed_product(held[:, to_first["normed"]], held[:, to_first["queries"]])
            store_rows(sums, part, count, deep + shard)
            vocabulary = lax.broadcasted_iota(jnp.int32, (VOCAB, BLOCK), 0)
            onehots = []
            for where in (section_now, 1 - section_now):
                lane = pl.multiple_of(where * half + chunk * BLOCK, BLOCK)
                for m in range(rows // BLOCK):
                    ids_row = ids_ref[m : m + 1, pl.ds(lane, BLOCK)]
                    onehots.append(jnp.where(ids_row == vocabulary, 1.0, 0.0).astype(bf16))
            part = product(jnp.concatenate(onehots, axis=1), held[:, to_first["stream"]])
            store_rows(sums, part, count, deep + 2 * shard)

        @pl.when(section_now != 0)
        def _():
            for k, name in enumerate(("keys", "values")):
                part = transposed_product(held[:, to_second["normed"]], held[:, to_second[name]])
                store_rows(sums, part, count, deep + k * shard)
            small = (smalls[0].astype(f32) + smalls[1].astype(f32)).astype(bf16)
            for q in range(GROUPS):
                sums[q, deep + 2 * shard :, :] = small

        heads = pl.ds(deep, block - deep)
        pltpu.make_async_copy(sums.at[:, heads], out_ref.at[:, heads], out_sems.at[1]).start()
        pltpu.make_async_copy(sums.at[:, feed], out_ref.at[:, feed], out_sems.at[0]).wait()
        pltpu.make_async_copy(sums.at[:, heads], out_ref.at[:, heads], out_sems.at[1]).wait()

    return pl.pallas_call(
        kernel,
        in_specs=[SCALARS, WHOLE, ANY, ANY] + [ANY] * len(deps),
        out_specs=ANY,
        out_shape=jax.ShapeDtypeStruct((GROUPS, block, width), bf16),
        scratch_shapes=[
            vmem(2 * rows, first_width),
            vmem(2, SMALL_ROWS, width),
            vmem(GROUPS, block, width),
            pltpu.SemaphoreType.DMA((6,)),
            pltpu.SemaphoreType.DMA((2,)),
        ],
        compiler_params=pltpu.CompilerParams(vmem_limit_bytes=VMEM),
        cost_estimate=cost(12),
    )(numbers, ids, keep, arrived, *deps)


def global_sums_kernel(
    count, hidden_ref, branch_ref, normed_two_ref, upward_ref, normed_ref, grad_mixed_ref,
    attended_ref, attend_branch_ref, small_ref, first, second,
):
    hidden_width, width = hidden_ref.shape[1], branch_ref.shape[1]
    deep, shard, room = hidden_width // GROUPS, width // GROUPS, VOCAB // GROUPS
    tile_shards = TILE // deep
    for i in range(hidden_width // TILE):
        columns = slice(i * TILE, (i + 1) * TILE)
        part = transposed_product(hidden_ref[:, columns], branch_ref[...])
        for k in range(tile_shards):
            slot = slot_of(i * tile_shards + k, count)
            first[slot, 0:deep, :] = part[k * deep : (k + 1) * deep].astype(bf16)
        part = transposed_product(normed_two_ref[...], upward_ref[:, columns])
        chunk, at = i * TILE // width, i * TILE % width
        store_rows(second, part, count, chunk * shard, slice(at, at + TILE))
    part = transposed_product(attended_ref[...], attend_branch_ref[...])
    store_rows(first, part, count, deep)
    targets = ((first, deep + shard), (second, deep), (second, deep + shard))
    for chunk, (target, start) in enumerate(targets):
        columns = slice(chunk * width, (chunk + 1) * width)
        part = transposed_product(normed_ref[...], grad_mixed_ref[:, columns])
        store_rows(target, part, count, start)
    small = jnp.concatenate([small_ref[...], jnp.zeros((room - 4, width), f32)], axis=0)
    for q in range(GROUPS):
        first[q, deep + 2 * shard :, :] = jnp.zeros((room, width), bf16)
        second[q, deep + 2 * shard :, :] = small.astype(bf16)


def global_sums_of(count, *arrays):
    hidden, branch = arrays[:2]
    hidden_width, width = hidden.shape[1], branch.shape[1]
    block = hidden_width // GROUPS + (2 * width + VOCAB) // GROUPS
    sums = jax.ShapeDtypeStruct((GROUPS, block, width), bf16)
    return pl.pallas_call(
        partial(global_sums_kernel, count),
        out_shape=[sums, sums],
        compiler_params=pltpu.CompilerParams(vmem_limit_bytes=VMEM),
        cost_estimate=cost(14),
    )(*arrays)


def causal_bias(start, owner_column, owner_row):
    shape = (BLOCK, owner_row.shape[1])
    rows = lax.broadcasted_iota(jnp.int32, shape, 0) + start
    columns = lax.broadcasted_iota(jnp.int32, shape, 1)
    bias = jnp.where((columns <= rows) & (owner_column == owner_row), 0.0, MASKED)
    return jnp.concatenate([bias, bias], axis=0)


def global_forward_kernel(column_ref, row_ref, qkv_ref, out_ref):
    start = pl.multiple_of(pl.program_id(0) * BLOCK, BLOCK)
    bias = causal_bias(start, column_ref[...], row_ref[...])
    out_ref[...] = pair_forward(
        qkv_ref[pl.ds(start, BLOCK), 0:PAIR],
        qkv_ref[:, PAIR : 2 * PAIR],
        qkv_ref[:, 2 * PAIR : 3 * PAIR],
        bias,
        lane_masks(),
    ).astype(bf16)


def global_backward_kernel(column_ref, row_ref, qkv_ref, grad_ref, out_ref, key_sum, value_sum):
    step = pl.program_id(0)
    start = pl.multiple_of(step * BLOCK, BLOCK)
    bias = causal_bias(start, column_ref[...], row_ref[...])

    @pl.when(step == 0)
    def _():
        key_sum[...] = jnp.zeros_like(key_sum)
        value_sum[...] = jnp.zeros_like(value_sum)

    queries, keys = qkv_ref[pl.ds(start, BLOCK), 0:PAIR], qkv_ref[:, PAIR : 2 * PAIR]
    masks = lane_masks()
    grad_queries, grad_keys, grad_values = pair_backward(
        queries,
        keys,
        qkv_ref[:, 2 * PAIR : 3 * PAIR],
        grad_ref[...],
        pair_probabilities(queries, keys, bias, masks),
        masks,
    )
    out_ref[pl.ds(start, BLOCK), 0:PAIR] = grad_queries.astype(bf16)
    key_sum[...] += grad_keys
    value_sum[...] += grad_values

    @pl.when(step == pl.num_programs(0) - 1)
    def _():
        out_ref[:, PAIR : 2 * PAIR] = key_sum[...].astype(bf16)
        out_ref[:, 2 * PAIR : 3 * PAIR] = value_sum[...].astype(bf16)


def global_attention(qkv, owners, grads=None, deps=()):
    count = qkv.shape[0]
    column, row = owners[:, None], owners[None, :]
    specs = [
        pl.BlockSpec((BLOCK, 1), lambda i: (i, 0)),
        pl.BlockSpec((1, count), lambda i: (0, 0)),
        pl.BlockSpec((count, 3 * PAIR), lambda i: (0, 0)),
    ]
    blocks = pl.BlockSpec((BLOCK, PAIR), lambda i: (i, 0))
    if grads is None:
        return pl.pallas_call(
            global_forward_kernel,
            grid=(count // BLOCK,),
            in_specs=specs,
            out_specs=blocks,
            out_shape=jax.ShapeDtypeStruct((count, PAIR), bf16),
            compiler_params=pltpu.CompilerParams(vmem_limit_bytes=VMEM),
            cost_estimate=cost(15),
        )(column, row, qkv)

    def body(*refs):
        global_backward_kernel(*refs[:4], *refs[4 + len(deps) :])

    return pl.pallas_call(
        body,
        grid=(count // BLOCK,),
        in_specs=specs + [blocks] + [ANY] * len(deps),
        out_specs=pl.BlockSpec((count, 3 * PAIR), lambda i: (0, 0)),
        out_shape=jax.ShapeDtypeStruct((count, 3 * PAIR), bf16),
        scratch_shapes=[pltpu.VMEM((count, PAIR), f32), pltpu.VMEM((count, PAIR), f32)],
        compiler_params=pltpu.CompilerParams(vmem_limit_bytes=VMEM),
        cost_estimate=cost(30),
    )(column, row, qkv, grads, *deps)


def call(kernel, args, specs, out_shape, out_specs, scratch=(), deps=(), micros=1):
    count = len(args)

    def body(*refs):
        kernel(*refs[:count], *refs[count + len(deps) :])

    return pl.pallas_call(
        body,
        in_specs=list(specs) + [ANY] * len(deps),
        out_specs=out_specs,
        out_shape=out_shape,
        scratch_shapes=list(scratch),
        compiler_params=pltpu.CompilerParams(vmem_limit_bytes=VMEM),
        cost_estimate=cost(micros),
    )(*args, *deps)


def shaped(*shape, kind=bf16):
    return jax.ShapeDtypeStruct(shape, kind)


def patch_forward(member, ids, table, pieces, deps=()):
    rows = ids.shape[0]
    shard, width = pieces[0].shape
    span = len(pieces)

    def kernel(member_ref, ids_ref, table_ref, *rest):
        piece_refs, (embedded_ref, weight_ref, share_ref, low_ref) = rest[:span], rest[span:]
        member_now = member_ref[0]
        for k in range(span):
            start = pl.multiple_of((member_now ^ k) * shard, shard)
            weight_ref[pl.ds(start, shard), :] = piece_refs[k][...]
        vocabulary = lax.broadcasted_iota(jnp.int32, (rows, VOCAB), 1)
        onehot = jnp.where(ids_ref[...] == vocabulary, 1.0, 0.0).astype(bf16)
        embedded_ref[...] = product(onehot, table_ref[...]).astype(bf16)
        share = product(embedded_ref[...], weight_ref[...])
        share_ref[...] = share
        low_ref[...] = share.astype(bf16)

    return call(
        kernel,
        (member, ids.reshape(rows, 1), table, *pieces),
        [SCALARS] + [WHOLE] * (2 + span),
        [
            shaped(rows, width),
            shaped(span * shard, width),
            shaped(rows, width, kind=f32),
            shaped(rows, width),
        ],
        [WHOLE] * 4,
        deps=deps,
        micros=4,
    )


def split_heads(values, target, start, batches, part, width_of_task):
    patch_rows = values.shape[0] // batches
    for m in range(batches):
        for pair in range(PAIRS):
            target[m * PAIRS + pair, :, part * PAIR : (part + 1) * PAIR] = values[
                m * patch_rows : (m + 1) * patch_rows, pair * PAIR : (pair + 1) * PAIR
            ]


def merge_heads(blocks, target, batches, parts):
    patch_rows = target.shape[0] // batches
    width = PAIRS * PAIR
    for t in range(batches * PAIRS):
        m, pair = t // PAIRS, t % PAIRS
        first = blocks[0].shape[0]
        block = blocks[0].at[t] if t < first else blocks[1].at[t - first]
        for part in range(parts):
            at = part * width + pair * PAIR
            target[m * patch_rows : (m + 1) * patch_rows, at : at + PAIR] = block[
                :, part * PAIR : (part + 1) * PAIR
            ]


def strided(values, target, span, offset):
    size = values.shape[1] // (4 * span)
    for k in range(span):
        parts = [
            values[:, (group * span + k) * size : (group * span + k + 1) * size]
            for group in range(4)
        ]
        target[k, :, offset : offset + 4 * size] = jnp.concatenate(parts, axis=1)


def global_start(batches, own, others, gains, biases, heads_in):
    rows, width = own.shape
    patch_rows = rows // batches

    def kernel(own_ref, gains_ref, biases_ref, weight_hbm, *rest):
        other_refs, (stream_ref, normed_ref, task_ref, share_ref, weight, sem) = (
            rest[: len(others)],
            rest[len(others) :],
        )
        load = pltpu.make_async_copy(weight_hbm, weight, sem)
        load.start()
        stream = own_ref[...]
        for ref in other_refs:
            stream = stream + ref[...].astype(f32)
        stream_ref[...] = stream
        normed = layer_norm(stream, gains_ref[0:1], biases_ref[0:1]).astype(bf16)
        normed_ref[...] = normed
        strided(normed, share_ref, SPAN, 0)
        load.wait()
        for part in range(3):
            mixed = product(normed, weight[:, part * width : (part + 1) * width]).astype(bf16)
            split_heads(mixed, task_ref, 0, batches, part, width)

    return call(
        kernel,
        (own, gains, biases, heads_in, *others),
        [WHOLE] * 3 + [ANY] + [WHOLE] * len(others),
        [
            shaped(rows, width, kind=f32),
            shaped(rows, width),
            shaped(batches * PAIRS, patch_rows, 3 * PAIR),
            shaped(SPAN, rows, width // SPAN),
        ],
        [WHOLE] * 4,
        [pltpu.VMEM(heads_in.shape, bf16), pltpu.SemaphoreType.DMA],
        micros=5,
    )


def global_feed_forward(batches, blocks, stream, gains, biases, heads_out, expand, contract):
    rows, width = stream.shape
    hidden_width = expand.shape[1]
    n = len(blocks)
    patch_rows = rows // batches
    half = patch_rows // 2

    def kernel(stream_ref, gains_ref, biases_ref, out_hbm, expand_hbm, contract_hbm, *rest):
        block_refs, rest = rest[:n], rest[n:]
        (attended_ref, middle_ref, normed_two_ref, slope_ref, hidden_ref, sent_ref) = rest[:6]
        share_ref, edge_ref, near_ref, w_out, w_expand, w_contract, sems = rest[6:]
        loads = [
            pltpu.make_async_copy(out_hbm, w_out, sems.at[0]),
            pltpu.make_async_copy(expand_hbm, w_expand, sems.at[1]),
            pltpu.make_async_copy(contract_hbm, w_contract, sems.at[2]),
        ]
        for load in loads:
            load.start()
        merge_heads(block_refs, attended_ref, batches, 1)
        loads[0].wait()
        middle = stream_ref[...] + product(attended_ref[...], w_out[...])
        middle_ref[...] = middle
        normed_two_ref[...] = layer_norm(middle, gains_ref[1:2], biases_ref[1:2]).astype(bf16)
        loads[1].wait()

        @pl.loop(0, hidden_width // width)
        def _(i):
            at = pl.ds(pl.multiple_of(i * width, 128), width)
            hidden, slope = gelu_and_slope(product(normed_two_ref[...], w_expand[:, at]))
            hidden_ref[:, at] = hidden.astype(bf16)
            slope_ref[:, at] = slope.astype(bf16)

        loads[2].wait()
        result = middle_ref[...] + product(hidden_ref[...], w_contract[...])
        sent = result.astype(bf16)
        sent_ref[...] = sent
        edge_ref[...] = jnp.zeros(edge_ref.shape, bf16)
        for m in range(batches):
            stop = (m + 1) * patch_rows
            edge_ref[m : m + 1, :] = sent[stop - 1 : stop]
            near_ref[m * half : (m + 1) * half, :] = sent[stop - half - 1 : stop - 1]
        strided(hidden_ref[...], share_ref, SPAN, 0)
        strided(normed_two_ref[...], share_ref, SPAN, hidden_width // SPAN)
        strided(attended_ref[...], share_ref, SPAN, (hidden_width + width) // SPAN)

    return call(
        kernel,
        (stream, gains, biases, heads_out, expand, contract, *blocks),
        [WHOLE] * 3 + [ANY] * 3 + [WHOLE] * n,
        [
            shaped(rows, width),
            shaped(rows, width, kind=f32),
            shaped(rows, width),
            shaped(rows, hidden_width),
            shaped(rows, hidden_width),
            shaped(rows, width),
            shaped(SPAN, rows, (hidden_width + 2 * width) // SPAN),
            shaped(SMALL_ROWS, width),
            shaped(batches * half, width),
        ],
        [WHOLE] * 9,
        [
            pltpu.VMEM(heads_out.shape, bf16),
            pltpu.VMEM(expand.shape, bf16),
            pltpu.VMEM(contract.shape, bf16),
            pltpu.SemaphoreType.DMA((3,)),
        ],
        micros=8,
    )


def global_feed_backward(
    batches, own, near, edge, middle, slope, gains, heads_out, expand, contract, deps=()
):
    rows, width = middle.shape
    hidden_width = expand.shape[1]
    patch_rows = rows // batches
    half = patch_rows // 2

    def kernel(
        own_ref, near_ref, edge_ref, middle_ref, slope_ref, gains_ref, out_hbm, expand_hbm,
        contract_hbm, upward_ref, grad_middle_ref, branch_ref, task_ref, small_ref, grad_ref,
        w_out, w_expand, w_contract, sems,
    ):
        loads = [
            pltpu.make_async_copy(contract_hbm, w_contract, sems.at[2]),
            pltpu.make_async_copy(expand_hbm, w_expand, sems.at[1]),
            pltpu.make_async_copy(out_hbm, w_out, sems.at[0]),
        ]
        for load in loads:
            load.start()
        source = jnp.concatenate([own_ref[...], near_ref[...], edge_ref[...]], axis=0)
        index = lax.broadcasted_iota(jnp.int32, (rows, 1), 0)
        batch, place = index // patch_rows, index % patch_rows
        chosen = jnp.where(
            place < half - 1,
            batch * half + place + 1,
            jnp.where(
                place < patch_rows - 1,
                batches * half + batch * half + place - (half - 1),
                2 * batches * half + batch,
            ),
        )
        columns = lax.broadcasted_iota(jnp.int32, (rows, source.shape[0]), 1)
        picked = jnp.where(columns == chosen, 1.0, 0.0).astype(bf16)
        grad_ref[...] = product(picked, source).astype(bf16)
        loads[0].wait()

        @pl.loop(0, hidden_width // width)
        def _(i):
            at = pl.ds(pl.multiple_of(i * width, 128), width)
            grad_hidden = product_transposed(grad_ref[...], w_contract[at, :])
            upward_ref[:, at] = (grad_hidden * slope_ref[:, at].astype(f32)).astype(bf16)

        loads[1].wait()
        grad_normed = product_transposed(upward_ref[...], w_expand[...])
        back, gain, bias = layer_norm_back(middle_ref[...], gains_ref[1:2], grad_normed)
        grad_middle = back + grad_ref[...].astype(f32)
        grad_middle_ref[...] = grad_middle
        branch = grad_middle.astype(bf16)
        branch_ref[...] = branch
        small_ref[...] = jnp.concatenate([gain, bias], axis=0)
        loads[2].wait()
        attended = product_transposed(branch, w_out[...]).astype(bf16)
        split_heads(attended, task_ref, 0, batches, 0, width)

    return call(
        kernel,
        (own, near, edge, middle, slope, gains, heads_out, expand, contract),
        [WHOLE] * 6 + [ANY] * 3,
        [
            shaped(rows, hidden_width),
            shaped(rows, width, kind=f32),
            shaped(rows, width),
            shaped(batches * PAIRS, patch_rows, PAIR),
            shaped(2, width, kind=f32),
            shaped(rows, width),
        ],
        [WHOLE] * 6,
        [
            pltpu.VMEM(heads_out.shape, bf16),
            pltpu.VMEM(expand.shape, bf16),
            pltpu.VMEM(contract.shape, bf16),
            pltpu.SemaphoreType.DMA((3,)),
        ],
        deps=deps,
        micros=10,
    )


def global_end(batches, blocks, stream, grad_middle, small, gains, heads_in, deps=()):
    rows, width = stream.shape
    n = len(blocks)

    def kernel(stream_ref, grad_middle_ref, small_ref, gains_ref, weight_hbm, *rest):
        block_refs, (mixed_ref, low_ref, all_small_ref, weight, sem) = rest[:n], rest[n:]
        load = pltpu.make_async_copy(weight_hbm, weight, sem)
        load.start()
        merge_heads(block_refs, mixed_ref, batches, 3)
        load.wait()
        grad_normed = product_transposed(mixed_ref[...], weight[...])
        back, gain, bias = layer_norm_back(stream_ref[...], gains_ref[0:1], grad_normed)
        low_ref[0:rows, :] = (back + grad_middle_ref[...]).astype(bf16)
        smalls = jnp.concatenate([gain, small_ref[0:1], bias, small_ref[1:2]], axis=0)
        all_small_ref[...] = smalls
        rest = jnp.zeros((SMALL_ROWS - 4, width), f32)
        low_ref[rows:, :] = jnp.concatenate([smalls, rest], axis=0).astype(bf16)

    return call(
        kernel,
        (stream, grad_middle, small, gains, heads_in, *blocks),
        [WHOLE] * 4 + [ANY] + [WHOLE] * n,
        [
            shaped(rows, 3 * width),
            shaped(rows + SMALL_ROWS, width),
            shaped(4, width, kind=f32),
        ],
        [WHOLE] * 3,
        [pltpu.VMEM(heads_in.shape, bf16), pltpu.SemaphoreType.DMA],
        deps=deps,
        micros=6,
    )


def patch_backward(section, ids, embedded, weight, own, crossed, span, deps=()):
    rows, width = embedded.shape
    block = own[0].shape[0]
    n = len(own)
    used = rows // n
    shard = weight.shape[0] // span

    def kernel(section_ref, ids_ref, embedded_ref, weight_ref, crossed_ref, *rest):
        own_refs, (patch_ref, table_ref, gathered, small) = rest[:n], rest[n:]

        @pl.when(section_ref[0] == 0)
        def _():
            for k in range(n):
                gathered[k * used : (k + 1) * used, :] = own_refs[k][0:used, :]
            total = sum(ref[used:, :].astype(f32) for ref in own_refs)
            small[...] = total.astype(bf16)

        @pl.when(section_ref[0] != 0)
        def _():
            for k in range(n):
                gathered[k * used : (k + 1) * used, :] = crossed_ref[k * block : k * block + used, :]
            small[...] = jnp.zeros_like(small)

        part = transposed_product(embedded_ref[...], gathered[...]).astype(bf16)
        for k in range(span):
            patch_ref[k, 0:shard, :] = part[k * shard : (k + 1) * shard]
            patch_ref[k, shard:, :] = small[...]
        grad_embedded = product_transposed(gathered[...], weight_ref[...]).astype(bf16)
        vocabulary = lax.broadcasted_iota(jnp.int32, (rows, VOCAB), 1)
        onehot = jnp.where(ids_ref[...] == vocabulary, 1.0, 0.0).astype(bf16)
        table_ref[...] = transposed_product(onehot, grad_embedded).astype(bf16)

    return call(
        kernel,
        (section, ids.reshape(rows, 1), embedded, weight, crossed, *own),
        [SCALARS] + [WHOLE] * (4 + n),
        [shaped(span, shard + SMALL_ROWS, width), shaped(VOCAB, width)],
        [WHOLE] * 2,
        [pltpu.VMEM((rows, width), bf16), pltpu.VMEM((SMALL_ROWS, width), bf16)],
        deps=deps,
        micros=6,
    )


def leave_by_group(group, buffer, targets, sems):
    for j in range(len(targets)):
        for k in range(len(targets)):

            @pl.when((group ^ j) == k)
            def _(j=j, k=k):
                pltpu.make_async_copy(buffer.at[j], targets[k], sems.at[k]).start()

    for k in range(len(targets)):
        pltpu.make_async_copy(buffer.at[0], targets[k], sems.at[k]).wait()


def plane_parts(hidden_width, width):
    starts, start = {}, 0
    for name, size in (
        ("hidden", hidden_width // SPAN),
        ("normed_two", width // SPAN),
        ("attended", width // SPAN),
        ("branch", width),
        ("attend_branch", width),
        ("upward", hidden_width),
        ("mixed", 3 * width),
        ("normed", width // SPAN),
    ):
        starts[name] = slice(start, start + size)
        start += size
    return starts, start


def pack(member, feed_share, normed_share, branch, attend_branch, upward, mixed, deps=()):
    rows, width = branch.shape
    hidden_width = upward.shape[1]
    parts, whole = plane_parts(hidden_width, width)
    own = slice(0, feed_share.shape[2])

    def kernel(member_ref, feed_ref, normed_ref, branch_ref, attend_ref, upward_ref, mixed_ref, *sent_refs):
        for k in range(SPAN):
            sent_refs[k][0:rows, own] = feed_ref[member_ref[0] ^ k]
            sent_refs[k][0:rows, parts["branch"]] = branch_ref[...]
            sent_refs[k][0:rows, parts["attend_branch"]] = attend_ref[...]
            sent_refs[k][0:rows, parts["upward"]] = upward_ref[...]
            sent_refs[k][0:rows, parts["mixed"]] = mixed_ref[...]
            sent_refs[k][0:rows, parts["normed"]] = normed_ref[member_ref[0] ^ k]

    return call(
        kernel,
        (member, feed_share, normed_share, branch, attend_branch, upward, mixed),
        [SCALARS] + [WHOLE] * 6,
        [shaped(rows, whole)] * SPAN,
        [WHOLE] * SPAN,
        deps=deps,
        micros=4,
    )


def plane_gradients(group, sent, rows, hidden_width, width, deps=()):
    parts, _ = plane_parts(hidden_width, width)
    deep, thin = hidden_width // GROUPS, width // GROUPS
    chunks = hidden_width // width
    block = deep + (chunks + 4) * thin

    def kernel(group_ref, *refs):
        sent_refs, (keep_ref, leave_ref, buffer, sems) = refs[: len(sent)], refs[len(sent) :]

        def columns(name, chunk=None):
            at = parts[name]
            if chunk is not None:
                at = slice(at.start + chunk * width, at.start + (chunk + 1) * width)
            return jnp.concatenate([ref[0:rows, at] for ref in sent_refs], axis=0)

        def store(part, start, size):
            for j in range(4):
                buffer[j, start : start + size, :] = part[j * size : (j + 1) * size].astype(bf16)

        store(transposed_product(columns("hidden"), columns("branch")), 0, deep)
        left, at = columns("normed_two"), deep
        for c in range(chunks):
            store(transposed_product(left, columns("upward", c)), at, thin)
            at += thin
        store(transposed_product(columns("attended"), columns("attend_branch")), at, thin)
        left = columns("normed")
        for c in range(3):
            at += thin
            store(transposed_product(left, columns("mixed", c)), at, thin)
        for j in range(4):
            mine = ((group_ref[0] ^ j) & 1) == 0

            @pl.when(mine)
            def _(j=j):
                pltpu.make_async_copy(buffer.at[j], keep_ref.at[j >> 1], sems.at[j]).start()

            @pl.when(jnp.logical_not(mine))
            def _(j=j):
                pltpu.make_async_copy(buffer.at[j], leave_ref.at[j >> 1], sems.at[j]).start()

        for j in range(4):
            pltpu.make_async_copy(buffer.at[j], keep_ref.at[j >> 1], sems.at[j]).wait()

    return call(
        kernel,
        (group, *sent),
        [SCALARS] + [WHOLE] * len(sent),
        [shaped(2, block, width)] * 2,
        [ANY] * 2,
        [pltpu.VMEM((4, block, width), bf16), pltpu.SemaphoreType.DMA((4,))],
        deps=deps,
        micros=8,
    )


def half_sum(which, kept, near, deps=()):
    shape = kept.shape[1:]

    def kernel(which_ref, kept_ref, near_ref, out_ref):
        total = kept_ref[0].astype(f32) + near_ref[0].astype(f32)
        out_ref[...] = total.astype(bf16)

    count = len(deps)

    def body(*refs):
        kernel(*refs[:3], refs[-1])

    steps = 1 if shape[0] % 32 else 2
    size = shape[0] // steps
    spec = pl.BlockSpec((1, size, shape[1]), lambda i, ref: (ref[0], i, 0))
    return pl.pallas_call(
        body,
        grid_spec=pltpu.PrefetchScalarGridSpec(
            num_scalar_prefetch=1,
            grid=(steps,),
            in_specs=[spec, spec] + [ANY] * count,
            out_specs=pl.BlockSpec((size, shape[1]), lambda i, ref: (i, 0)),
        ),
        out_shape=shaped(*shape),
        compiler_params=pltpu.CompilerParams(vmem_limit_bytes=VMEM),
        cost_estimate=cost(2),
    )(which, kept, near, *deps)


def finish(section, upper, deep, shard, room, block, own, crossed, table_parts, patch_parts):
    width = own.shape[1]
    chunks = deep // shard
    p = len(patch_parts)

    def kernel(section_ref, upper_ref, kept_ref, near_ref, far_ref, own_ref, crossed_ref, table_ref, *refs):
        patch_refs = refs[:p]
        contract, expand, ins, out, table, small, patch = refs[p:]
        heads_start = deep + (chunks + 1) * shard
        mine = upper_ref[0]

        def total(start, size):
            at = slice(start, start + size)
            return kept_ref[mine, at].astype(f32) + near_ref[mine, at].astype(f32) + far_ref[at].astype(f32)

        def taken(ref, start, size):
            return ref[start : start + size, :]

        total_patch = sum(ref[...].astype(f32) for ref in patch_refs)
        patch[...] = total_patch[: patch.shape[0]]

        @pl.when(section_ref[0] == 0)
        def _():
            contract[...] = total(0, deep)
            for c in range(chunks):
                expand[:, c * width : (c + 1) * width] = total(deep + c * shard, shard)
            out[...] = total(deep + chunks * shard, shard)
            for c in range(3):
                ins[:, c * width : (c + 1) * width] = total(heads_start + c * shard, shard)
            small[...] = total_patch[patch.shape[0] :]
            sums = jnp.zeros((room, width), f32)
            for k in range(table_ref.shape[0]):
                sums = sums + table_ref[k].astype(f32)
            table[...] = sums

        @pl.when(section_ref[0] != 0)
        def _():
            contract[...] = taken(crossed_ref, 0, deep)
            for c in range(chunks):
                expand[:, c * width : (c + 1) * width] = taken(own_ref, c * shard, shard)
            out[...] = taken(crossed_ref, deep, shard)
            ins[:, 0:width] = taken(crossed_ref, deep + shard, shard)
            for c in range(2):
                ins[:, (c + 1) * width : (c + 2) * width] = taken(own_ref, deep + c * shard, shard)
            small[...] = taken(own_ref, deep + 2 * shard, small.shape[0])
            table[...] = taken(crossed_ref, deep + 2 * shard, room)

    return call(
        kernel,
        (section, upper, *block, own, crossed, table_parts, *patch_parts),
        [SCALARS] * 2 + [WHOLE] * (6 + p),
        [
            shaped(deep, width, kind=f32),
            shaped(shard, chunks * width, kind=f32),
            shaped(shard, 3 * width, kind=f32),
            shaped(shard, width, kind=f32),
            shaped(room, width, kind=f32),
            shaped(SMALL_ROWS, width, kind=f32),
            shaped(patch_parts[0].shape[0] - SMALL_ROWS, width, kind=f32),
        ],
        [WHOLE] * 7,
        micros=4,
    )


SEQ = ("group", "member")


def section_send(x, origin, target, pairs):
    count = lax.axis_size(SEQ)
    joint = [(origin * count + i, target * count + j) for i, j in pairs]
    return lax.ppermute(x, ("section",) + SEQ, joint)


def section_swap(x):
    return lax.ppermute(x, "section", [(0, 1), (1, 0)])


def by_slot(buffer, count, pieces):
    split = count // GROUPS
    parts, start = [], 0
    for size, shared in pieces:
        part = buffer[:, start : start + size]
        start += size
        kept = shared or size // split
        if shared:
            part = jnp.broadcast_to(part[:, None, :shared], (GROUPS, split, shared, part.shape[2]))
        parts.append(part.reshape(count, kept, part.shape[-1]))
    whole = jnp.concatenate(parts, axis=1)
    turned = whole.reshape((4, count // 4) + whole.shape[1:])
    return jnp.swapaxes(turned, 0, 1).reshape(whole.shape)


def place_sum(shares):
    shares = lax.psum_scatter(shares, "member", scatter_dimension=0, tiled=True)
    return lax.psum_scatter(shares, "group", scatter_dimension=0, tiled=True)[0]


def on_device(
    byte_values,
    item_lengths,
    embed_tables,
    patch_weight,
    norm_gains,
    norm_biases,
    heads_in,
    heads_out,
    expand_weight,
    contract_weight,
    out_grad,
):
    place = lax.axis_index(SEQ)
    count = lax.axis_size(SEQ)
    section = lax.axis_index("section")
    is_global = section == 0
    batches, byte_rows = byte_values.shape
    patch_rows = byte_rows // PATCH
    width = heads_out.shape[2]
    rows = batches * patch_rows
    total_patches = patch_rows * count
    gains, biases = norm_gains[0], norm_biases[0]
    heads_in, heads_out = heads_in[0], heads_out[0]
    expand, contract = expand_weight[0], contract_weight[0]
    own_table = embed_tables[0]
    straight = [(i, i) for i in range(count)]

    quarters = PATCH // 2
    span = count // quarters
    group, member = place // span, place % span
    shard_rows = patch_weight.shape[0]
    pieces = [patch_weight]
    for k in range(1, span):
        pieces.append(lax.ppermute(patch_weight, SEQ, [(i, i ^ k) for i in range(count)]))
    other_table = section_swap(own_table)
    global_table = jnp.where(is_global, own_table, other_table)
    local_table = jnp.where(is_global, other_table, own_table)
    which_byte = section * quarters + group
    byte_ids = []
    for k in range(quarters):
        theirs = byte_values
        if k:
            theirs = lax.ppermute(byte_values, SEQ, [(i, i ^ (k * span)) for i in range(count)])
        theirs = theirs.reshape(rows, PATCH)
        byte_ids.append(lax.dynamic_index_in_dim(theirs, which_byte, 1, keepdims=False))
    byte_ids = jnp.concatenate(byte_ids)
    embedded, byte_weight, shares, low_shares = patch_forward(
        member.reshape(1).astype(jnp.int32), byte_ids, global_table, pieces
    )
    shares = shares + section_send(low_shares, 1, 0, straight).astype(f32)
    shares = shares.reshape(quarters, rows, width)
    parts = []
    for k in range(1, quarters):
        pairs = [(i, i ^ (k * span)) for i in range(count)]
        parts.append(section_send(shares[k].astype(bf16), 0, 0, pairs))

    arrived = [section_send(w, 1, 0, straight) for w in (heads_in, heads_out, expand, contract)]
    other_norms = section_swap(jnp.concatenate([gains, biases]))
    local_gains = jnp.where(is_global, other_norms[:2], gains)
    local_biases = jnp.where(is_global, other_norms[2:], biases)

    tasks = batches * PAIRS
    first_tasks = min(tasks, count)
    spare_tasks = tasks - first_tasks

    def to_tasks(blocks):
        columns = blocks.shape[2]
        slots = jnp.pad(blocks[:first_tasks], ((0, count - first_tasks), (0, 0), (0, 0)))
        if spare_tasks:
            spare = section_send(blocks[first_tasks:], 0, 1, straight)
            spare = jnp.pad(spare, ((0, count - spare_tasks), (0, 0), (0, 0)))
            slots = jnp.where(is_global, slots, spare)
        landed = lax.all_to_all(slots, SEQ, 0, 0)
        return landed.reshape(total_patches, columns)

    def from_tasks(results):
        columns = results.shape[1]
        slots = lax.all_to_all(results.reshape(count, patch_rows, columns), SEQ, 0, 0)
        if spare_tasks:
            return [slots, section_send(slots[:spare_tasks], 1, 0, straight)]
        return [slots]

    task = jnp.minimum(jnp.where(is_global, place, first_tasks + place), tasks - 1)
    task_lengths = lax.dynamic_index_in_dim(item_lengths, task // PAIRS, 0, keepdims=False)
    task_owners = locate(jnp.arange(total_patches, dtype=jnp.int32) * PATCH, task_lengths)[0]

    stream, normed, tasks_out, normed_share = global_start(
        batches, shares[0], parts, gains, biases, heads_in
    )
    qkv = to_tasks(tasks_out)
    attended, middle, normed_two, slope, hidden, sent, feed_share, edge, near = global_feed_forward(
        batches,
        from_tasks(global_attention(qkv, task_owners)),
        stream,
        gains,
        biases,
        heads_out,
        expand,
        contract,
    )
    half = patch_rows // 2
    half_bytes = half * PATCH
    chunks = half_bytes // BLOCK
    onward = [(i, i + 1) for i in range(count - 1)]
    backward = [(i + 1, i) for i in range(count - 1)]
    near = section_send(near, 0, 1, straight)
    edge = section_send(edge, 0, 0, onward)
    weights = (heads_in, heads_out, expand, contract)
    flag = section.reshape(1).astype(jnp.int32)
    block_patches = BLOCK // PATCH
    local_outs, activations_of, grads_shifted, grads_edge = [], [], [], []
    for c in range(chunks):
        numbers = jnp.concatenate(
            [
                jnp.stack([section, place * byte_rows, jnp.int32(c)]).astype(jnp.int32),
                item_lengths.reshape(-1),
            ]
        )
        act, grad_shifted, grad_edge, keep, send = local_block(
            numbers,
            byte_values,
            local_table,
            sent,
            edge,
            near,
            local_gains,
            local_biases,
            out_grad,
            patch_rows,
            weights,
            arrived,
        )
        local_outs.append(act.reshape(batches, BLOCK, width))
        grads_shifted.append(grad_shifted.reshape(batches, block_patches, width))
        grads_edge.append(grad_edge)
        activations_of.append((numbers, keep, section_swap(send)))
    local_out = jnp.concatenate(local_outs, axis=1)
    grad_shifted = jnp.concatenate(grads_shifted, axis=1).reshape(batches * half, width)

    other_out = section_send(local_out, 0, 1, straight)
    byte_places = place * byte_rows + jnp.arange(byte_rows, dtype=jnp.int32)
    live_bytes = jnp.stack([locate(byte_places, item_lengths[m])[1] for m in range(batches)])
    own_sent = jnp.broadcast_to(
        sent.reshape(batches, patch_rows, 1, width), (batches, patch_rows, PATCH, width)
    ).reshape(batches, byte_rows, width)
    own_sent = jnp.where(live_bytes[:, :, None], own_sent, jnp.zeros((), bf16))
    activations = jnp.where(
        is_global, own_sent, jnp.concatenate([other_out, local_out], axis=1)
    )

    shard = width // count
    room = VOCAB // count
    group_shard, group_room = width // GROUPS, VOCAB // GROUPS
    small_rows = max(4, room)
    pieces = {
        False: [(contract.shape[0] // GROUPS, 0), (group_shard, 0), (group_shard, 0), (group_room, 0)],
        True: [(group_shard, 0)] * (expand.shape[1] // width + 2) + [(group_room, small_rows)],
    }

    def ordered(buffer):
        if count == GROUPS:
            return buffer
        upper, lower = by_slot(buffer, count, pieces[False]), by_slot(buffer, count, pieces[True])
        rows_of = max(upper.shape[1], lower.shape[1])
        upper, lower = (
            jnp.pad(x, ((0, 0), (0, rows_of - x.shape[1]), (0, 0))) for x in (upper, lower)
        )
        return jnp.where(is_global, upper, lower)

    near_back = section_send(grad_shifted, 1, 0, straight)
    edge_back = section_send(grads_edge[0], 0, 0, backward)
    in_plane = span == SPAN and count == GROUPS
    member_flag = (member % SPAN).reshape(1).astype(jnp.int32)
    group_flag = group.reshape(1).astype(jnp.int32)

    def plane_send(blocks):
        return [blocks[0]] + [
            section_send(blocks[k], 0, 0, [(i, i ^ k) for i in range(count)])
            for k in range(1, SPAN)
        ]

    upper = (group >> 1) & 1
    upper_flag = upper.reshape(1).astype(jnp.int32)

    def group_pairs(step):
        return [(i, i ^ (step * span)) for i in range(count)]

    def both_send(x, pairs):
        joint = [(s * count + i, s * count + j) for s in range(2) for i, j in pairs]
        return lax.ppermute(x, ("section",) + SEQ, joint)

    grad_upward, grad_middle, attend_branch, task_grads, small, grad_sent = global_feed_backward(
        batches,
        grad_shifted,
        near_back,
        edge_back,
        middle,
        slope,
        gains,
        heads_out,
        expand,
        contract,
    )
    half_locals = [
        ordered(
            local_gradients(
                count,
                numbers,
                byte_values,
                keep,
                crossed,
                contract.shape[0],
                width,
                half_bytes,
                [grad_sent],
            )
        )
        for numbers, keep, crossed in activations_of
    ]
    if chunks > 1:
        half_locals = [sum(x.astype(f32) for x in half_locals).astype(bf16)]
    half_locals = half_locals[0]
    task_grads = to_tasks(task_grads)
    task_mixed = global_attention(qkv, task_owners, task_grads)
    grad_mixed, own_rows, small = global_end(
        batches,
        from_tasks(task_mixed),
        stream,
        grad_middle,
        small,
        gains,
        heads_in,
    )

    gathered = [own_rows]
    for k in range(1, quarters):
        pairs = [(i, i ^ (k * span)) for i in range(count)]
        gathered.append(section_send(own_rows, 0, 0, pairs))
    crossed = section_send(jnp.concatenate(gathered), 0, 1, straight)
    patch_share, table_share = patch_backward(
        flag,
        byte_ids,
        embedded,
        byte_weight,
        gathered,
        crossed,
        span,
    )
    if in_plane:
        in_planes = lax.psum_scatter(half_locals, "member", scatter_dimension=0, tiled=True)
        in_planes = in_planes.reshape((2, 2) + in_planes.shape[1:])
        parity = group & 1
        local_near = both_send(
            lax.dynamic_index_in_dim(in_planes, 1 - parity, 1, keepdims=False), group_pairs(1)
        )
        local_kept = lax.dynamic_index_in_dim(in_planes, parity, 1, keepdims=False)
    else:
        own_local = place_sum(half_locals)
    patch_parts = [lax.dynamic_index_in_dim(patch_share, member, 0, keepdims=False)]
    for k in range(1, span):
        leaving = lax.dynamic_index_in_dim(patch_share, member ^ k, 0, keepdims=False)
        patch_parts.append(lax.ppermute(leaving, SEQ, [(i, i ^ k) for i in range(count)]))
    table_share = table_share + section_send(table_share, 1, 0, straight)
    table_parts = lax.all_to_all(table_share.reshape(count, VOCAB // count, width), SEQ, 0, 0)

    def ordered_rows(first, second):
        feed_rows = contract.shape[0] // count
        expand_sum = [second[k * shard : (k + 1) * shard] for k in range(feed_rows // shard)]
        rest, others = first[feed_rows:], second[feed_rows:]
        ins = [rest[shard : 2 * shard], others[:shard], others[shard : 2 * shard]]
        return (
            first[:feed_rows],
            jnp.concatenate(expand_sum, axis=1),
            jnp.concatenate(ins, axis=1),
            rest[:shard],
            rest[2 * shard : 2 * shard + room],
            others[2 * shard : 2 * shard + 4],
        )

    if in_plane:
        sent_parts = pack(
            member_flag, feed_share, normed_share, grad_sent, attend_branch, grad_upward, grad_mixed,
        )
        kept, leaving = plane_gradients(
            group_flag, plane_send(sent_parts), rows, contract.shape[0], width, [patch_share]
        )
        local_far = both_send(
            half_sum(1 - upper_flag, local_kept, local_near), group_pairs(2)
        )
        near = section_send(leaving, 0, 0, group_pairs(1))
        far = section_send(
            half_sum(1 - upper_flag, kept, near, patch_parts[1:]), 0, 0, group_pairs(2)
        )
        own_local = sum(
            lax.dynamic_index_in_dim(x, upper, 0, keepdims=False).astype(f32)
            for x in (local_kept, local_near)
        ) + local_far.astype(f32)
        crossed = section_send(own_local, 0, 1, straight)
        contract_grad, expand_grad, in_grad, out_grads, table_grad, small, patch_grads = finish(
            flag,
            upper_flag,
            contract.shape[0] // count,
            shard,
            room,
            (kept, near, far),
            own_local,
            crossed,
            table_parts,
            patch_parts,
        )
        small = small[:4]
    else:
        upper, lower = global_sums_of(
            count, hidden, grad_sent, normed_two, grad_upward, normed, grad_mixed, attended,
            attend_branch, small,
        )
        own_global = ordered(jnp.where(is_global, upper, section_send(lower, 0, 1, straight)))
        own_global = place_sum(own_global)
        crossed = section_swap(jnp.where(is_global, own_local, own_global)).astype(f32)
        global_sums = ordered_rows(own_global.astype(f32), crossed)
        global_table = jnp.sum(table_parts.astype(f32), axis=0)
        global_sums = global_sums[:4] + (global_table, global_sums[5])
        local_sums = ordered_rows(crossed, own_local.astype(f32))
        contract_grad, expand_grad, in_grad, out_grads, table_grad, small = (
            jnp.where(is_global, upper, lower) for upper, lower in zip(global_sums, local_sums)
        )
        patch_grads = sum(x.astype(f32) for x in patch_parts)[:shard_rows]
    small = lax.dynamic_slice_in_dim(small, place * shard, shard, 1)
    return (
        activations[None],
        table_grad[None],
        patch_grads,
        small[None, 0:2],
        small[None, 2:4],
        in_grad[None],
        out_grads[None],
        expand_grad[None],
        contract_grad[None],
    )


def solution(mesh):
    devices = mesh.devices
    groups = PATCH // 2
    split = jax.sharding.Mesh(
        devices.reshape(devices.shape[0], groups, devices.shape[1] // groups), ("section",) + SEQ
    )
    both = ("section",) + SEQ
    placed = (
        P(None, SEQ),
        P(),
        P("section", None, None),
        P(both, None),
        P("section", None, None),
        P("section", None, None),
        P("section", None, None),
        P("section", None, None),
        P("section", None, None),
        P("section", None, None),
        P(None, SEQ, None),
    )
    return jax.shard_map(
        on_device,
        mesh=split,
        in_specs=placed,
        out_specs=(
            P("section", None, SEQ, None),
            P("section", SEQ, None),
            P(both, None),
            P("section", None, SEQ),
            P("section", None, SEQ),
            P("section", SEQ, None),
            P("section", SEQ, None),
            P("section", SEQ, None),
            P("section", SEQ, None),
        ),
        check_vma=False,
    )
```

```python
from functools import partial

import jax
import jax.numpy as jnp
from jax import lax
from jax.experimental import pallas as pl
from jax.experimental.pallas import tpu as pltpu
from jax.sharding import PartitionSpec as P

HEADS = 12
HEAD_SIZE = 64
VOCAB = 256
PATCH = 8
ITEMS = 4
PAIRS = HEADS // 2
PAIR = 2 * HEAD_SIZE
SCALE = HEAD_SIZE ** (-0.5)
EPSILON = 1e-05
MASKED = -1e30
BLOCK = 128
TILE = 384
GROUPS = 16
SPAN = 4
VMEM = 60 * 1024 * 1024

bf16 = jnp.bfloat16
f32 = jnp.float32


def cost(micros):
    return pl.CostEstimate(flops=int(micros * 1.1e9), bytes_accessed=1, transcendentals=0)


def product(former, latter):
    return jnp.dot(former, latter, preferred_element_type=f32)


def transposed_product(former, latter):
    return lax.dot_general(former, latter, (((0,), (0,)), ((), ())), preferred_element_type=f32)


def product_transposed(former, latter):
    return lax.dot_general(former, latter, (((1,), (1,)), ((), ())), preferred_element_type=f32)


def normalise(values):
    average = jnp.mean(values, axis=-1, keepdims=True)
    centered = values - average
    inverse_root = lax.rsqrt(jnp.mean(centered * centered, axis=-1, keepdims=True) + EPSILON)
    return centered * inverse_root, inverse_root


def layer_norm(values, gain, bias):
    return normalise(values)[0] * gain + bias


def layer_norm_back(values, gain, grad):
    unit, inverse_root = normalise(values)
    scaled = grad * gain
    grad_values = inverse_root * (
        scaled
        - jnp.mean(scaled, axis=-1, keepdims=True)
        - unit * jnp.mean(scaled * unit, axis=-1, keepdims=True)
    )
    return (
        grad_values,
        jnp.sum(grad * unit, axis=0, keepdims=True),
        jnp.sum(grad, axis=0, keepdims=True),
    )


def locate(positions, lengths_row):
    padded = (lengths_row + PATCH - 1) // PATCH * PATCH
    item_ends = jnp.cumsum(padded)
    starts = item_ends - padded
    inside = (positions[:, None] >= starts[None, :]) & (positions[:, None] < item_ends[None, :])
    offsets = jnp.arange(ITEMS, dtype=jnp.int32)[None, :] - ITEMS
    owners = jnp.sum(jnp.where(inside, offsets, 0), axis=1) + ITEMS
    live_mask = jnp.any(inside & (positions[:, None] < (starts + lengths_row)[None, :]), axis=1)
    return (owners, live_mask)


def slot_of(q, count):
    if count != GROUPS:
        return q
    return (q % SPAN) * (GROUPS // SPAN) + q // SPAN


def store_rows(buffer, value, count, start, columns=slice(None)):
    rows = value.shape[0] // GROUPS
    for q in range(GROUPS):
        buffer[slot_of(q, count), pl.ds(start, rows), columns] = value[
            q * rows : (q + 1) * rows
        ].astype(bf16)


def patch_bias(live_row):
    rows = lax.broadcasted_iota(jnp.int32, (BLOCK, BLOCK), 0)
    columns = lax.broadcasted_iota(jnp.int32, (BLOCK, BLOCK), 1)
    same = (rows // PATCH) == (columns // PATCH)
    allowed = same & (columns <= rows) & ((live_row > 0) | (columns == rows))
    bias = jnp.where(allowed, 0.0, MASKED)
    return jnp.concatenate([bias, bias], axis=0)


def softmax_rows(scores):
    peak = jnp.max(scores, axis=-1, keepdims=True)
    exponents = jnp.exp(scores - peak)
    return exponents * (1.0 / jnp.sum(exponents, axis=-1, keepdims=True))


def lane_masks():
    lanes = lax.broadcasted_iota(jnp.int32, (1, PAIR), 1)
    low = jnp.where(lanes < HEAD_SIZE, 1.0, 0.0)
    return lanes < HEAD_SIZE, low.astype(bf16), (1.0 - low).astype(bf16)


def stacked(values, low, high, scale=1.0):
    return jnp.concatenate([values * (low * scale), values * (high * scale)], axis=0)


def unstacked(values, is_low):
    half = values.shape[0] // 2
    return jnp.where(is_low, values[:half], values[half:])


def pair_probabilities(queries, keys, bias, masks):
    _, low, high = masks
    return softmax_rows(product_transposed(stacked(queries, low, high, SCALE), keys) + bias)


def pair_forward(queries, keys, values, bias, masks):
    probabilities = pair_probabilities(queries, keys, bias, masks)
    return unstacked(product(probabilities.astype(bf16), values), masks[0])


def pair_backward(queries, keys, values, grads, probabilities, masks):
    is_low, low, high = masks
    both = stacked(queries, low, high, SCALE)
    both_grads = stacked(grads, low, high)
    prob_grads = product_transposed(both_grads, values)
    delta = jnp.sum(probabilities * prob_grads, axis=-1, keepdims=True)
    score_grads = (probabilities * (prob_grads - delta)).astype(bf16)
    return (
        unstacked(product(score_grads, keys), is_low) * SCALE,
        transposed_product(score_grads, both),
        transposed_product(probabilities.astype(bf16), both_grads),
    )


def gelu_and_slope(x):
    root = 0.7978845608028654
    cubic = 0.044715
    square = x * x
    bent = jnp.tanh(x * (root + (root * cubic) * square))
    half = 0.5 * (1.0 + bent)
    slope = half + (0.5 * x) * (1.0 - bent * bent) * (root + (3.0 * root * cubic) * square)
    return x * half, slope


def fetch(section, own, arrived, target, sem):
    @pl.when(section == 0)
    def _():
        pltpu.make_async_copy(arrived, target, sem).start()

    @pl.when(section != 0)
    def _():
        pltpu.make_async_copy(own, target, sem).start()


def section_columns(hidden_width, width):
    tables = []
    for names in (
        ("hidden", "branch", "attended", "attend_branch", "normed", "queries", "stream"),
        ("upward", "normed_two", "normed", "keys", "values"),
    ):
        table, start = {}, 0
        for name in names:
            size = hidden_width if start == 0 else width
            table[name] = slice(start, start + size)
            start += size
        tables.append((table, start))
    return tables


SMALL_ROWS = 16


def item_spans(numbers_ref, first, batch):
    spans, start = [], 0
    for k in range(ITEMS):
        length = numbers_ref[first + batch * ITEMS + k]
        stop = start + (length + PATCH - 1) // PATCH * PATCH
        spans.append((start, start + length, stop))
        start = stop
    return spans


def is_live(positions, spans):
    live = jnp.zeros(positions.shape, jnp.bool_)
    for start, live_end, _ in spans:
        live = live | ((positions >= start) & (positions < live_end))
    return live


def owner_of(positions, spans):
    owner = jnp.full(positions.shape, ITEMS, jnp.int32)
    for k, (start, _, stop) in enumerate(spans):
        owner = jnp.where((positions >= start) & (positions < stop), k, owner)
    return owner


def local_kernel(
    patch_rows,
    numbers_ref,
    ids_ref,
    table_ref,
    sent_ref,
    edge_ref,
    near_ref,
    gains_ref,
    biases_ref,
    out_grad_hbm,
    own_in,
    own_out,
    own_expand,
    own_contract,
    new_in,
    new_out,
    new_expand,
    new_contract,
    act_ref,
    grad_shifted_ref,
    grad_edge_ref,
    keep_ref,
    send_ref,
    w_in,
    w_out,
    w_expand,
    w_contract,
    first,
    second,
    out_grad_ref,
    source_ref,
    stream_ref,
    mixed_ref,
    middle_ref,
    slope_ref,
    grad_middle_ref,
    grad_attended_ref,
    grad_stream_ref,
    probability_ref,
    sems,
    out_sems,
):
    section, offset, chunk = numbers_ref[0], numbers_ref[1], numbers_ref[2]
    rows, width = act_ref.shape
    batches = rows // BLOCK
    hidden_width = w_expand.shape[1]
    half = patch_rows // 2
    block_patches = BLOCK // PATCH
    lane = pl.multiple_of(section * (half * PATCH) + chunk * BLOCK, BLOCK)
    base = offset + lane
    grads_in = [
        pltpu.make_async_copy(
            out_grad_hbm.at[m, pl.ds(lane, BLOCK)],
            out_grad_ref.at[m * BLOCK : (m + 1) * BLOCK],
            sems.at[4 + m],
        )
        for m in range(batches)
    ]
    fetch(section, own_in, new_in, w_in, sems.at[0])
    for copy in grads_in:
        copy.start()
    fetch(section, own_out, new_out, w_out, sems.at[1])
    fetch(section, own_expand, new_expand, w_expand, sems.at[2])
    fetch(section, own_contract, new_contract, w_contract, sems.at[3])
    (to_first, first_width), (to_second, second_width) = section_columns(hidden_width, width)
    body = slice(0, rows)
    out_count = [0]

    def leave(from_first, columns, at_rows=body):
        source = first if from_first else second
        sem = out_sems.at[out_count[0]]
        out_count[0] += 1
        part = source.at[at_rows, columns]

        @pl.when(section == (0 if from_first else 1))
        def _():
            pltpu.make_async_copy(part, keep_ref.at[at_rows, columns], sem).start()

        @pl.when(section != (0 if from_first else 1))
        def _():
            pltpu.make_async_copy(part, send_ref.at[at_rows, columns], sem).start()

        return pltpu.make_async_copy(part, keep_ref.at[at_rows, columns], sem)

    blocks = [slice(m * BLOCK, (m + 1) * BLOCK) for m in range(batches)]
    spans = [item_spans(numbers_ref, 3, m) for m in range(batches)]
    column = lax.broadcasted_iota(jnp.int32, (BLOCK, 1), 0)
    row = lax.broadcasted_iota(jnp.int32, (1, BLOCK), 1)
    live_columns = [is_live(base + column, span) for span in spans]
    biases_of = [
        patch_bias(jnp.where(is_live(base + row, span), 1, 0)) for span in spans
    ]
    sent_rows, edge_rows = sent_ref.shape[0], edge_ref.shape[0]
    source_ref[0:sent_rows, :] = sent_ref[...]
    source_ref[sent_rows : sent_rows + edge_rows, :] = edge_ref[...]
    source_ref[sent_rows + edge_rows :, :] = near_ref[...]

    for copy in grads_in:
        copy.wait()
    for m, at in enumerate(blocks):
        vocabulary = lax.broadcasted_iota(jnp.int32, (VOCAB, BLOCK), 0)
        ids = ids_ref[m : m + 1, pl.ds(lane, BLOCK)]
        onehot = jnp.where(ids == vocabulary, 1.0, 0.0).astype(bf16)
        patch = column // PATCH
        place = chunk * block_patches + patch
        start = base + patch * PATCH
        same = owner_of(start, spans[m]) == owner_of(start - PATCH, spans[m])
        inside = jnp.where(place == 0, sent_rows + m, m * patch_rows + place - 1)
        chosen = jnp.where(section == 0, inside, sent_rows + edge_rows + m * half + place)
        chosen = jnp.where(same, chosen, -1)
        columns = lax.broadcasted_iota(jnp.int32, (BLOCK, source_ref.shape[0]), 1)
        spread = jnp.where(columns == chosen, 1.0, 0.0).astype(bf16)
        stream = transposed_product(onehot, table_ref[...]) + product(spread, source_ref[...])
        stream_ref[at, :] = stream
        normed = layer_norm(stream, gains_ref[0:1], biases_ref[0:1]).astype(bf16)
        first[at, to_first["normed"]] = normed
        second[at, to_second["normed"]] = normed
        first[at, to_first["branch"]] = jnp.where(
            live_columns[m], out_grad_ref[at, :].astype(f32), 0.0
        ).astype(bf16)

    pltpu.make_async_copy(own_in, w_in, sems.at[0]).wait()
    for i in range(3 * width // TILE):
        at = slice(i * TILE, (i + 1) * TILE)
        mixed_ref[:, at] = product(first[body, to_first["normed"]], w_in[:, at]).astype(bf16)

    masks = lane_masks()

    def pair_columns(pair, start=0):
        return slice(start + pair * PAIR, start + (pair + 1) * PAIR)

    for m, at in enumerate(blocks):
        for pair in range(PAIRS):
            probabilities = pair_probabilities(
                mixed_ref[at, pair_columns(pair)],
                mixed_ref[at, pair_columns(pair, width)],
                biases_of[m],
                masks,
            )
            probability_ref[m * PAIRS + pair] = probabilities
            attended = product(
                probabilities.astype(bf16), mixed_ref[at, pair_columns(pair, 2 * width)]
            )
            first[at, pair_columns(pair, to_first["attended"].start)] = unstacked(
                attended, masks[0]
            ).astype(bf16)

    pltpu.make_async_copy(own_out, w_out, sems.at[1]).wait()
    for at in blocks:
        middle = stream_ref[at, :] + product(first[at, to_first["attended"]], w_out[...])
        middle_ref[at, :] = middle
        normed_two = layer_norm(middle, gains_ref[1:2], biases_ref[1:2]).astype(bf16)
        second[at, to_second["normed_two"]] = normed_two

    pltpu.make_async_copy(own_expand, w_expand, sems.at[2]).wait()
    for i in range(hidden_width // TILE):
        at = slice(i * TILE, (i + 1) * TILE)
        hidden, slope = gelu_and_slope(
            product(second[body, to_second["normed_two"]], w_expand[:, at])
        )
        first[body, at] = hidden.astype(bf16)
        slope_ref[:, at] = slope.astype(bf16)

    copies = [leave(True, slice(0, to_first["attended"].stop))]
    pltpu.make_async_copy(own_contract, w_contract, sems.at[3]).wait()
    live_column = jnp.concatenate([jnp.where(x, 1, 0) for x in live_columns], axis=0)
    for i in range(width // 256):
        at = slice(i * 256, (i + 1) * 256)
        result = middle_ref[:, at] + product(first[body, to_first["hidden"]], w_contract[:, at])
        act_ref[:, at] = jnp.where(live_column > 0, result, 0.0).astype(bf16)

    for i in range(hidden_width // TILE):
        at = slice(i * TILE, (i + 1) * TILE)
        grad_hidden = product_transposed(first[body, to_first["branch"]], w_contract[at, :])
        second[body, at] = (grad_hidden * slope_ref[:, at].astype(f32)).astype(bf16)

    copies.append(leave(False, slice(0, to_second["normed"].stop)))
    for i in range(width // 256):
        at = slice(i * 256, (i + 1) * 256)
        grad_middle_ref[:, at] = product_transposed(
            second[body, to_second["upward"]], w_expand[at, :]
        )

    gain_two = bias_two = gain_one = bias_one = jnp.zeros((1, width), f32)
    for at in blocks:
        back, gain, bias = layer_norm_back(
            middle_ref[at, :], gains_ref[1:2], grad_middle_ref[at, :]
        )
        grad_middle = back + first[at, to_first["branch"]].astype(f32)
        grad_middle_ref[at, :] = grad_middle
        branch = grad_middle.astype(bf16)
        first[at, to_first["attend_branch"]] = branch
        grad_attended_ref[at, :] = product_transposed(branch, w_out[...]).astype(bf16)
        gain_two, bias_two = gain_two + gain, bias_two + bias

    copies.append(leave(True, slice(to_first["attend_branch"].start, to_first["normed"].stop)))
    for m, at in enumerate(blocks):
        for pair in range(PAIRS):
            parts = pair_backward(
                mixed_ref[at, pair_columns(pair)],
                mixed_ref[at, pair_columns(pair, width)],
                mixed_ref[at, pair_columns(pair, 2 * width)],
                grad_attended_ref[at, pair_columns(pair)],
                probability_ref[m * PAIRS + pair],
                masks,
            )
            first[at, pair_columns(pair, to_first["queries"].start)] = parts[0].astype(bf16)
            second[at, pair_columns(pair, to_second["keys"].start)] = parts[1].astype(bf16)
            second[at, pair_columns(pair, to_second["values"].start)] = parts[2].astype(bf16)

    keys_values = slice(to_second["keys"].start, to_second["values"].stop)
    copies.append(leave(False, keys_values))
    for i in range(width // 256):
        at = slice(i * 256, (i + 1) * 256)
        grad_stream_ref[:, at] = product_transposed(
            first[body, to_first["queries"]], w_in[at, 0:width]
        ) + product_transposed(second[body, keys_values], w_in[at, width:])

    for m, at in enumerate(blocks):
        back, gain, bias = layer_norm_back(
            stream_ref[at, :], gains_ref[0:1], grad_stream_ref[at, :]
        )
        grad_stream = back + grad_middle_ref[at, :]
        first[at, to_first["stream"]] = grad_stream.astype(bf16)
        gain_one, bias_one = gain_one + gain, bias_one + bias
        summed = jnp.sum(grad_stream.reshape(block_patches, PATCH, width), axis=1)
        start = base + PATCH * lax.broadcasted_iota(jnp.int32, (block_patches, 1), 0)
        same = owner_of(start, spans[m]) == owner_of(start - PATCH, spans[m])
        summed = jnp.where(same, summed, 0.0).astype(bf16)
        grad_shifted_ref[m * block_patches : (m + 1) * block_patches, :] = summed
        grad_edge_ref[m : m + 1, :] = summed[0:1]

    grad_edge_ref[batches:, :] = jnp.zeros((SMALL_ROWS - batches, width), bf16)
    small = jnp.concatenate(
        [gain_one, gain_two, bias_one, bias_two, jnp.zeros((SMALL_ROWS - 4, width), f32)], axis=0
    )
    second[rows:, 0:width] = small.astype(bf16)
    copies.append(leave(False, slice(0, width), slice(rows, rows + SMALL_ROWS)))
    copies.append(leave(True, slice(to_first["queries"].start, first_width)))
    for copy in copies:
        copy.wait()


ANY = pl.BlockSpec(memory_space=pl.ANY)
WHOLE = pl.BlockSpec(memory_space=pltpu.VMEM)
SCALARS = pl.BlockSpec(memory_space=pltpu.SMEM)


def vmem(*shape, kind=bf16):
    return pltpu.VMEM(shape, kind)


def local_block(numbers, ids, table, sent, edge, near, gains, biases, out_grad, patch_rows, own, new):
    batches, width = out_grad.shape[0], out_grad.shape[2]
    rows = batches * BLOCK
    hidden_width = own[3].shape[0]
    (_, first_width), (_, second_width) = section_columns(hidden_width, width)
    part = jax.ShapeDtypeStruct((rows + SMALL_ROWS, first_width), bf16)
    return pl.pallas_call(
        partial(local_kernel, patch_rows),
        in_specs=[SCALARS] + [WHOLE] * 7 + [ANY] * 9,
        out_specs=[WHOLE] * 3 + [ANY] * 2,
        out_shape=[
            jax.ShapeDtypeStruct((rows, width), bf16),
            jax.ShapeDtypeStruct((rows // PATCH, width), bf16),
            jax.ShapeDtypeStruct((SMALL_ROWS, width), bf16),
            part,
            part,
        ],
        scratch_shapes=[
            vmem(*own[0].shape),
            vmem(*own[1].shape),
            vmem(*own[2].shape),
            vmem(*own[3].shape),
            vmem(*part.shape),
            vmem(part.shape[0], second_width),
            vmem(rows, width),
            vmem(sent.shape[0] + edge.shape[0] + near.shape[0], width),
            vmem(rows, width, kind=f32),
            vmem(rows, 3 * width),
            vmem(rows, width, kind=f32),
            vmem(rows, hidden_width),
            vmem(rows, width, kind=f32),
            vmem(rows, width),
            vmem(rows, width, kind=f32),
            vmem(batches * PAIRS, 2 * BLOCK, BLOCK, kind=f32),
            pltpu.SemaphoreType.DMA((4 + batches,)),
            pltpu.SemaphoreType.DMA((6,)),
        ],
        compiler_params=pltpu.CompilerParams(vmem_limit_bytes=VMEM),
        cost_estimate=cost(35),
    )(numbers, ids, table, sent, edge, near, gains, biases, out_grad, *own, *new)


def local_gradients(count, numbers, ids, keep, arrived, hidden_width, width, half, deps=()):
    rows = keep.shape[0] - SMALL_ROWS
    (to_first, first_width), (to_second, _) = section_columns(hidden_width, width)
    deep, shard, room = hidden_width // GROUPS, width // GROUPS, VOCAB // GROUPS
    block = deep + 2 * shard + room
    cuts = (slice(0, hidden_width + width), slice(hidden_width + width, first_width))

    def kernel(numbers_ref, ids_ref, keep_ref, new_ref, *rest):
        out_ref, held, smalls, sums, sems, out_sems = rest[len(deps) :]
        copies = []
        for k, cut in enumerate(cuts):
            for j, ref in enumerate((keep_ref, new_ref)):
                copies.append(
                    pltpu.make_async_copy(
                        ref.at[0:rows, cut], held.at[j * rows : (j + 1) * rows, cut], sems.at[2 * k + j]
                    )
                )
        for j, ref in enumerate((keep_ref, new_ref)):
            copies.append(
                pltpu.make_async_copy(
                    ref.at[rows : rows + SMALL_ROWS, 0:width], smalls.at[j], sems.at[4 + j]
                )
            )
        for copy in copies:
            copy.start()
        section_now, chunk = numbers_ref[0], numbers_ref[2]
        tile_shards = TILE // deep

        copies[0].wait()
        copies[1].wait()

        @pl.when(section_now == 0)
        def _():
            for i in range(hidden_width // TILE):
                part = transposed_product(
                    held[:, i * TILE : (i + 1) * TILE], held[:, to_first["branch"]]
                )
                for k in range(tile_shards):
                    slot = slot_of(i * tile_shards + k, count)
                    sums[slot, 0:deep, :] = part[k * deep : (k + 1) * deep].astype(bf16)

        @pl.when(section_now != 0)
        def _():
            for i in range(hidden_width // TILE):
                part = transposed_product(
                    held[:, to_second["normed_two"]], held[:, i * TILE : (i + 1) * TILE]
                )
                chunk, at = i * TILE // width, i * TILE % width
                store_rows(sums, part, count, chunk * shard, slice(at, at + TILE))

        feed = pl.ds(0, deep)
        pltpu.make_async_copy(sums.at[:, feed], out_ref.at[:, feed], out_sems.at[0]).start()
        for copy in copies[2:]:
            copy.wait()

        @pl.when(section_now == 0)
        def _():
            part = transposed_product(
                held[:, to_first["attended"]], held[:, to_first["attend_branch"]]
            )
            store_rows(sums, part, count, deep)
            part = transposed_product(held[:, to_first["normed"]], held[:, to_first["queries"]])
            store_rows(sums, part, count, deep + shard)
            vocabulary = lax.broadcasted_iota(jnp.int32, (VOCAB, BLOCK), 0)
            onehots = []
            for where in (section_now, 1 - section_now):
                lane = pl.multiple_of(where * half + chunk * BLOCK, BLOCK)
                for m in range(rows // BLOCK):
                    ids_row = ids_ref[m : m + 1, pl.ds(lane, BLOCK)]
                    onehots.append(jnp.where(ids_row == vocabulary, 1.0, 0.0).astype(bf16))
            part = product(jnp.concatenate(onehots, axis=1), held[:, to_first["stream"]])
            store_rows(sums, part, count, deep + 2 * shard)

        @pl.when(section_now != 0)
        def _():
            for k, name in enumerate(("keys", "values")):
                part = transposed_product(held[:, to_second["normed"]], held[:, to_second[name]])
                store_rows(sums, part, count, deep + k * shard)
            small = (smalls[0].astype(f32) + smalls[1].astype(f32)).astype(bf16)
            for q in range(GROUPS):
                sums[q, deep + 2 * shard :, :] = small

        heads = pl.ds(deep, block - deep)
        pltpu.make_async_copy(sums.at[:, heads], out_ref.at[:, heads], out_sems.at[1]).start()
        pltpu.make_async_copy(sums.at[:, feed], out_ref.at[:, feed], out_sems.at[0]).wait()
        pltpu.make_async_copy(sums.at[:, heads], out_ref.at[:, heads], out_sems.at[1]).wait()

    return pl.pallas_call(
        kernel,
        in_specs=[SCALARS, WHOLE, ANY, ANY] + [ANY] * len(deps),
        out_specs=ANY,
        out_shape=jax.ShapeDtypeStruct((GROUPS, block, width), bf16),
        scratch_shapes=[
            vmem(2 * rows, first_width),
            vmem(2, SMALL_ROWS, width),
            vmem(GROUPS, block, width),
            pltpu.SemaphoreType.DMA((6,)),
            pltpu.SemaphoreType.DMA((2,)),
        ],
        compiler_params=pltpu.CompilerParams(vmem_limit_bytes=VMEM),
        cost_estimate=cost(12),
    )(numbers, ids, keep, arrived, *deps)


def global_sums_kernel(
    count, hidden_ref, branch_ref, normed_two_ref, upward_ref, normed_ref, grad_mixed_ref,
    attended_ref, attend_branch_ref, small_ref, first, second,
):
    hidden_width, width = hidden_ref.shape[1], branch_ref.shape[1]
    deep, shard, room = hidden_width // GROUPS, width // GROUPS, VOCAB // GROUPS
    tile_shards = TILE // deep
    for i in range(hidden_width // TILE):
        columns = slice(i * TILE, (i + 1) * TILE)
        part = transposed_product(hidden_ref[:, columns], branch_ref[...])
        for k in range(tile_shards):
            slot = slot_of(i * tile_shards + k, count)
            first[slot, 0:deep, :] = part[k * deep : (k + 1) * deep].astype(bf16)
        part = transposed_product(normed_two_ref[...], upward_ref[:, columns])
        chunk, at = i * TILE // width, i * TILE % width
        store_rows(second, part, count, chunk * shard, slice(at, at + TILE))
    part = transposed_product(attended_ref[...], attend_branch_ref[...])
    store_rows(first, part, count, deep)
    targets = ((first, deep + shard), (second, deep), (second, deep + shard))
    for chunk, (target, start) in enumerate(targets):
        columns = slice(chunk * width, (chunk + 1) * width)
        part = transposed_product(normed_ref[...], grad_mixed_ref[:, columns])
        store_rows(target, part, count, start)
    small = jnp.concatenate([small_ref[...], jnp.zeros((room - 4, width), f32)], axis=0)
    for q in range(GROUPS):
        first[q, deep + 2 * shard :, :] = jnp.zeros((room, width), bf16)
        second[q, deep + 2 * shard :, :] = small.astype(bf16)


def global_sums_of(count, *arrays):
    hidden, branch = arrays[:2]
    hidden_width, width = hidden.shape[1], branch.shape[1]
    block = hidden_width // GROUPS + (2 * width + VOCAB) // GROUPS
    sums = jax.ShapeDtypeStruct((GROUPS, block, width), bf16)
    return pl.pallas_call(
        partial(global_sums_kernel, count),
        out_shape=[sums, sums],
        compiler_params=pltpu.CompilerParams(vmem_limit_bytes=VMEM),
        cost_estimate=cost(14),
    )(*arrays)


def causal_bias(start, owner_column, owner_row):
    shape = (BLOCK, owner_row.shape[1])
    rows = lax.broadcasted_iota(jnp.int32, shape, 0) + start
    columns = lax.broadcasted_iota(jnp.int32, shape, 1)
    bias = jnp.where((columns <= rows) & (owner_column == owner_row), 0.0, MASKED)
    return jnp.concatenate([bias, bias], axis=0)


def global_forward_kernel(column_ref, row_ref, qkv_ref, out_ref):
    start = pl.multiple_of(pl.program_id(0) * BLOCK, BLOCK)
    bias = causal_bias(start, column_ref[...], row_ref[...])
    out_ref[...] = pair_forward(
        qkv_ref[pl.ds(start, BLOCK), 0:PAIR],
        qkv_ref[:, PAIR : 2 * PAIR],
        qkv_ref[:, 2 * PAIR : 3 * PAIR],
        bias,
        lane_masks(),
    ).astype(bf16)


def global_backward_kernel(column_ref, row_ref, qkv_ref, grad_ref, out_ref, key_sum, value_sum):
    step = pl.program_id(0)
    start = pl.multiple_of(step * BLOCK, BLOCK)
    bias = causal_bias(start, column_ref[...], row_ref[...])

    @pl.when(step == 0)
    def _():
        key_sum[...] = jnp.zeros_like(key_sum)
        value_sum[...] = jnp.zeros_like(value_sum)

    queries, keys = qkv_ref[pl.ds(start, BLOCK), 0:PAIR], qkv_ref[:, PAIR : 2 * PAIR]
    masks = lane_masks()
    grad_queries, grad_keys, grad_values = pair_backward(
        queries,
        keys,
        qkv_ref[:, 2 * PAIR : 3 * PAIR],
        grad_ref[...],
        pair_probabilities(queries, keys, bias, masks),
        masks,
    )
    out_ref[pl.ds(start, BLOCK), 0:PAIR] = grad_queries.astype(bf16)
    key_sum[...] += grad_keys
    value_sum[...] += grad_values

    @pl.when(step == pl.num_programs(0) - 1)
    def _():
        out_ref[:, PAIR : 2 * PAIR] = key_sum[...].astype(bf16)
        out_ref[:, 2 * PAIR : 3 * PAIR] = value_sum[...].astype(bf16)


def global_attention(qkv, owners, grads=None, deps=()):
    count = qkv.shape[0]
    column, row = owners[:, None], owners[None, :]
    specs = [
        pl.BlockSpec((BLOCK, 1), lambda i: (i, 0)),
        pl.BlockSpec((1, count), lambda i: (0, 0)),
        pl.BlockSpec((count, 3 * PAIR), lambda i: (0, 0)),
    ]
    blocks = pl.BlockSpec((BLOCK, PAIR), lambda i: (i, 0))
    if grads is None:
        return pl.pallas_call(
            global_forward_kernel,
            grid=(count // BLOCK,),
            in_specs=specs,
            out_specs=blocks,
            out_shape=jax.ShapeDtypeStruct((count, PAIR), bf16),
            compiler_params=pltpu.CompilerParams(vmem_limit_bytes=VMEM),
            cost_estimate=cost(15),
        )(column, row, qkv)

    def body(*refs):
        global_backward_kernel(*refs[:4], *refs[4 + len(deps) :])

    return pl.pallas_call(
        body,
        grid=(count // BLOCK,),
        in_specs=specs + [blocks] + [ANY] * len(deps),
        out_specs=pl.BlockSpec((count, 3 * PAIR), lambda i: (0, 0)),
        out_shape=jax.ShapeDtypeStruct((count, 3 * PAIR), bf16),
        scratch_shapes=[pltpu.VMEM((count, PAIR), f32), pltpu.VMEM((count, PAIR), f32)],
        compiler_params=pltpu.CompilerParams(vmem_limit_bytes=VMEM),
        cost_estimate=cost(30),
    )(column, row, qkv, grads, *deps)


def call(kernel, args, specs, out_shape, out_specs, scratch=(), deps=(), micros=1):
    count = len(args)

    def body(*refs):
        kernel(*refs[:count], *refs[count + len(deps) :])

    return pl.pallas_call(
        body,
        in_specs=list(specs) + [ANY] * len(deps),
        out_specs=out_specs,
        out_shape=out_shape,
        scratch_shapes=list(scratch),
        compiler_params=pltpu.CompilerParams(vmem_limit_bytes=VMEM),
        cost_estimate=cost(micros),
    )(*args, *deps)


def shaped(*shape, kind=bf16):
    return jax.ShapeDtypeStruct(shape, kind)


def patch_forward(member, ids, table, pieces, deps=()):
    rows = ids.shape[0]
    shard, width = pieces[0].shape
    span = len(pieces)

    def kernel(member_ref, ids_ref, table_ref, *rest):
        piece_refs, (embedded_ref, weight_ref, share_ref, low_ref) = rest[:span], rest[span:]
        member_now = member_ref[0]
        for k in range(span):
            start = pl.multiple_of((member_now ^ k) * shard, shard)
            weight_ref[pl.ds(start, shard), :] = piece_refs[k][...]
        vocabulary = lax.broadcasted_iota(jnp.int32, (rows, VOCAB), 1)
        onehot = jnp.where(ids_ref[...] == vocabulary, 1.0, 0.0).astype(bf16)
        embedded_ref[...] = product(onehot, table_ref[...]).astype(bf16)
        share = product(embedded_ref[...], weight_ref[...])
        share_ref[...] = share
        low_ref[...] = share.astype(bf16)

    return call(
        kernel,
        (member, ids.reshape(rows, 1), table, *pieces),
        [SCALARS] + [WHOLE] * (2 + span),
        [
            shaped(rows, width),
            shaped(span * shard, width),
            shaped(rows, width, kind=f32),
            shaped(rows, width),
        ],
        [WHOLE] * 4,
        deps=deps,
        micros=4,
    )


def split_heads(values, target, start, batches, part, width_of_task):
    patch_rows = values.shape[0] // batches
    for m in range(batches):
        for pair in range(PAIRS):
            target[m * PAIRS + pair, :, part * PAIR : (part + 1) * PAIR] = values[
                m * patch_rows : (m + 1) * patch_rows, pair * PAIR : (pair + 1) * PAIR
            ]


def merge_heads(blocks, target, batches, parts):
    patch_rows = target.shape[0] // batches
    width = PAIRS * PAIR
    for t in range(batches * PAIRS):
        m, pair = t // PAIRS, t % PAIRS
        first = blocks[0].shape[0]
        block = blocks[0].at[t] if t < first else blocks[1].at[t - first]
        for part in range(parts):
            at = part * width + pair * PAIR
            target[m * patch_rows : (m + 1) * patch_rows, at : at + PAIR] = block[
                :, part * PAIR : (part + 1) * PAIR
            ]


def strided(values, target, span, offset):
    size = values.shape[1] // (4 * span)
    for k in range(span):
        parts = [
            values[:, (group * span + k) * size : (group * span + k + 1) * size]
            for group in range(4)
        ]
        target[k, :, offset : offset + 4 * size] = jnp.concatenate(parts, axis=1)


def global_start(batches, own, others, gains, biases, heads_in):
    rows, width = own.shape
    patch_rows = rows // batches

    def kernel(own_ref, gains_ref, biases_ref, weight_hbm, *rest):
        other_refs, (stream_ref, normed_ref, task_ref, share_ref, weight, sem) = (
            rest[: len(others)],
            rest[len(others) :],
        )
        load = pltpu.make_async_copy(weight_hbm, weight, sem)
        load.start()
        stream = own_ref[...]
        for ref in other_refs:
            stream = stream + ref[...].astype(f32)
        stream_ref[...] = stream
        normed = layer_norm(stream, gains_ref[0:1], biases_ref[0:1]).astype(bf16)
        normed_ref[...] = normed
        strided(normed, share_ref, SPAN, 0)
        load.wait()
        for part in range(3):
            mixed = product(normed, weight[:, part * width : (part + 1) * width]).astype(bf16)
            split_heads(mixed, task_ref, 0, batches, part, width)

    return call(
        kernel,
        (own, gains, biases, heads_in, *others),
        [WHOLE] * 3 + [ANY] + [WHOLE] * len(others),
        [
            shaped(rows, width, kind=f32),
            shaped(rows, width),
            shaped(batches * PAIRS, patch_rows, 3 * PAIR),
            shaped(SPAN, rows, width // SPAN),
        ],
        [WHOLE] * 4,
        [pltpu.VMEM(heads_in.shape, bf16), pltpu.SemaphoreType.DMA],
        micros=5,
    )


def global_feed_forward(batches, blocks, stream, gains, biases, heads_out, expand, contract):
    rows, width = stream.shape
    hidden_width = expand.shape[1]
    n = len(blocks)
    patch_rows = rows // batches
    half = patch_rows // 2

    def kernel(stream_ref, gains_ref, biases_ref, out_hbm, expand_hbm, contract_hbm, *rest):
        block_refs, rest = rest[:n], rest[n:]
        (attended_ref, middle_ref, normed_two_ref, slope_ref, hidden_ref, sent_ref) = rest[:6]
        share_ref, other_share_ref, edge_ref, near_ref, w_out, w_expand, w_contract, sems = rest[6:]
        loads = [
            pltpu.make_async_copy(out_hbm, w_out, sems.at[0]),
            pltpu.make_async_copy(expand_hbm, w_expand, sems.at[1]),
            pltpu.make_async_copy(contract_hbm, w_contract, sems.at[2]),
        ]
        for load in loads:
            load.start()
        merge_heads(block_refs, attended_ref, batches, 1)
        loads[0].wait()
        middle = stream_ref[...] + product(attended_ref[...], w_out[...])
        middle_ref[...] = middle
        normed_two_ref[...] = layer_norm(middle, gains_ref[1:2], biases_ref[1:2]).astype(bf16)
        loads[1].wait()

        @pl.loop(0, hidden_width // width)
        def _(i):
            at = pl.ds(pl.multiple_of(i * width, 128), width)
            hidden, slope = gelu_and_slope(product(normed_two_ref[...], w_expand[:, at]))
            hidden_ref[:, at] = hidden.astype(bf16)
            slope_ref[:, at] = slope.astype(bf16)

        loads[2].wait()
        result = middle_ref[...] + product(hidden_ref[...], w_contract[...])
        sent = result.astype(bf16)
        sent_ref[...] = sent
        edge_ref[...] = jnp.zeros(edge_ref.shape, bf16)
        for m in range(batches):
            stop = (m + 1) * patch_rows
            edge_ref[m : m + 1, :] = sent[stop - 1 : stop]
            near_ref[m * half : (m + 1) * half, :] = sent[stop - half - 1 : stop - 1]
        strided(hidden_ref[...], share_ref, SPAN, 0)
        strided(normed_two_ref[...], other_share_ref, SPAN, 0)
        strided(attended_ref[...], other_share_ref, SPAN, width // SPAN)

    return call(
        kernel,
        (stream, gains, biases, heads_out, expand, contract, *blocks),
        [WHOLE] * 3 + [ANY] * 3 + [WHOLE] * n,
        [
            shaped(rows, width),
            shaped(rows, width, kind=f32),
            shaped(rows, width),
            shaped(rows, hidden_width),
            shaped(rows, hidden_width),
            shaped(rows, width),
            shaped(SPAN, rows, hidden_width // SPAN),
            shaped(SPAN, rows, 2 * width // SPAN),
            shaped(SMALL_ROWS, width),
            shaped(batches * half, width),
        ],
        [WHOLE] * 10,
        [
            pltpu.VMEM(heads_out.shape, bf16),
            pltpu.VMEM(expand.shape, bf16),
            pltpu.VMEM(contract.shape, bf16),
            pltpu.SemaphoreType.DMA((3,)),
        ],
        micros=8,
    )


def global_feed_backward(
    batches, own, near, edge, middle, slope, gains, heads_out, expand, contract, deps=()
):
    rows, width = middle.shape
    hidden_width = expand.shape[1]
    patch_rows = rows // batches
    half = patch_rows // 2

    def kernel(
        own_ref, near_ref, edge_ref, middle_ref, slope_ref, gains_ref, out_hbm, expand_hbm,
        contract_hbm, upward_ref, grad_middle_ref, branch_ref, task_ref, small_ref, grad_ref,
        w_out, w_expand, w_contract, sems,
    ):
        loads = [
            pltpu.make_async_copy(contract_hbm, w_contract, sems.at[2]),
            pltpu.make_async_copy(expand_hbm, w_expand, sems.at[1]),
            pltpu.make_async_copy(out_hbm, w_out, sems.at[0]),
        ]
        for load in loads:
            load.start()
        source = jnp.concatenate([own_ref[...], near_ref[...], edge_ref[...]], axis=0)
        index = lax.broadcasted_iota(jnp.int32, (rows, 1), 0)
        batch, place = index // patch_rows, index % patch_rows
        chosen = jnp.where(
            place < half - 1,
            batch * half + place + 1,
            jnp.where(
                place < patch_rows - 1,
                batches * half + batch * half + place - (half - 1),
                2 * batches * half + batch,
            ),
        )
        columns = lax.broadcasted_iota(jnp.int32, (rows, source.shape[0]), 1)
        picked = jnp.where(columns == chosen, 1.0, 0.0).astype(bf16)
        grad_ref[...] = product(picked, source).astype(bf16)
        loads[0].wait()

        @pl.loop(0, hidden_width // width)
        def _(i):
            at = pl.ds(pl.multiple_of(i * width, 128), width)
            grad_hidden = product_transposed(grad_ref[...], w_contract[at, :])
            upward_ref[:, at] = (grad_hidden * slope_ref[:, at].astype(f32)).astype(bf16)

        loads[1].wait()
        grad_normed = product_transposed(upward_ref[...], w_expand[...])
        back, gain, bias = layer_norm_back(middle_ref[...], gains_ref[1:2], grad_normed)
        grad_middle = back + grad_ref[...].astype(f32)
        grad_middle_ref[...] = grad_middle
        branch = grad_middle.astype(bf16)
        branch_ref[...] = branch
        small_ref[...] = jnp.concatenate([gain, bias], axis=0)
        loads[2].wait()
        attended = product_transposed(branch, w_out[...]).astype(bf16)
        split_heads(attended, task_ref, 0, batches, 0, width)

    return call(
        kernel,
        (own, near, edge, middle, slope, gains, heads_out, expand, contract),
        [WHOLE] * 6 + [ANY] * 3,
        [
            shaped(rows, hidden_width),
            shaped(rows, width, kind=f32),
            shaped(rows, width),
            shaped(batches * PAIRS, patch_rows, PAIR),
            shaped(2, width, kind=f32),
            shaped(rows, width),
        ],
        [WHOLE] * 6,
        [
            pltpu.VMEM(heads_out.shape, bf16),
            pltpu.VMEM(expand.shape, bf16),
            pltpu.VMEM(contract.shape, bf16),
            pltpu.SemaphoreType.DMA((3,)),
        ],
        deps=deps,
        micros=10,
    )


def global_end(batches, blocks, stream, grad_middle, small, gains, heads_in, deps=()):
    rows, width = stream.shape
    n = len(blocks)

    def kernel(stream_ref, grad_middle_ref, small_ref, gains_ref, weight_hbm, *rest):
        block_refs, (mixed_ref, low_ref, all_small_ref, weight, sem) = rest[:n], rest[n:]
        load = pltpu.make_async_copy(weight_hbm, weight, sem)
        load.start()
        merge_heads(block_refs, mixed_ref, batches, 3)
        load.wait()
        grad_normed = product_transposed(mixed_ref[...], weight[...])
        back, gain, bias = layer_norm_back(stream_ref[...], gains_ref[0:1], grad_normed)
        low_ref[0:rows, :] = (back + grad_middle_ref[...]).astype(bf16)
        smalls = jnp.concatenate([gain, small_ref[0:1], bias, small_ref[1:2]], axis=0)
        all_small_ref[...] = smalls
        rest = jnp.zeros((SMALL_ROWS - 4, width), f32)
        low_ref[rows:, :] = jnp.concatenate([smalls, rest], axis=0).astype(bf16)

    return call(
        kernel,
        (stream, grad_middle, small, gains, heads_in, *blocks),
        [WHOLE] * 4 + [ANY] + [WHOLE] * n,
        [
            shaped(rows, 3 * width),
            shaped(rows + SMALL_ROWS, width),
            shaped(4, width, kind=f32),
        ],
        [WHOLE] * 3,
        [pltpu.VMEM(heads_in.shape, bf16), pltpu.SemaphoreType.DMA],
        deps=deps,
        micros=6,
    )


def patch_backward(section, ids, embedded, weight, own, crossed, span, deps=()):
    rows, width = embedded.shape
    block = own[0].shape[0]
    n = len(own)
    used = rows // n
    shard = weight.shape[0] // span

    def kernel(section_ref, ids_ref, embedded_ref, weight_ref, crossed_ref, *rest):
        own_refs, (patch_ref, table_ref, gathered, small) = rest[:n], rest[n:]

        @pl.when(section_ref[0] == 0)
        def _():
            for k in range(n):
                gathered[k * used : (k + 1) * used, :] = own_refs[k][0:used, :]
            total = sum(ref[used:, :].astype(f32) for ref in own_refs)
            small[...] = total.astype(bf16)

        @pl.when(section_ref[0] != 0)
        def _():
            for k in range(n):
                gathered[k * used : (k + 1) * used, :] = crossed_ref[k * block : k * block + used, :]
            small[...] = jnp.zeros_like(small)

        part = transposed_product(embedded_ref[...], gathered[...]).astype(bf16)
        for k in range(span):
            patch_ref[k, 0:shard, :] = part[k * shard : (k + 1) * shard]
            patch_ref[k, shard:, :] = small[...]
        grad_embedded = product_transposed(gathered[...], weight_ref[...]).astype(bf16)
        vocabulary = lax.broadcasted_iota(jnp.int32, (rows, VOCAB), 1)
        onehot = jnp.where(ids_ref[...] == vocabulary, 1.0, 0.0).astype(bf16)
        table_ref[...] = transposed_product(onehot, grad_embedded).astype(bf16)

    return call(
        kernel,
        (section, ids.reshape(rows, 1), embedded, weight, crossed, *own),
        [SCALARS] + [WHOLE] * (4 + n),
        [shaped(span, shard + SMALL_ROWS, width), shaped(VOCAB, width)],
        [WHOLE] * 2,
        [pltpu.VMEM((rows, width), bf16), pltpu.VMEM((SMALL_ROWS, width), bf16)],
        deps=deps,
        micros=6,
    )


def leave_by_group(group, buffer, targets, sems):
    for j in range(len(targets)):
        for k in range(len(targets)):

            @pl.when((group ^ j) == k)
            def _(j=j, k=k):
                pltpu.make_async_copy(buffer.at[j], targets[k], sems.at[k]).start()

    for k in range(len(targets)):
        pltpu.make_async_copy(buffer.at[0], targets[k], sems.at[k]).wait()


def pack_columns(hidden_width, width):
    deep, thin = hidden_width // SPAN, width // SPAN
    first = [
        (slice(0, deep), slice(deep, deep + width)),
        (slice(deep + width, deep + width + thin), slice(deep + width + thin, deep + 4 * width + thin)),
    ]
    right = 2 * thin
    second = [
        (slice(0, thin), slice(right, right + hidden_width)),
        (slice(thin, right), slice(right + hidden_width, right + hidden_width + width)),
    ]
    return first, second, max(first[-1][1].stop, second[-1][1].stop)


def pack_second(member, share, attend_branch, upward, whole, deps=()):
    rows, width = attend_branch.shape
    own, hidden_width = share.shape[2], upward.shape[1]

    def kernel(member_ref, share_ref, attend_ref, upward_ref, out_ref):
        for k in range(SPAN):
            out_ref[k, :, 0:own] = share_ref[member_ref[0] ^ k]
            out_ref[k, :, own : own + hidden_width] = upward_ref[...]
            out_ref[k, :, own + hidden_width : own + hidden_width + width] = attend_ref[...]

    return call(
        kernel,
        (member, share, attend_branch, upward),
        [SCALARS] + [WHOLE] * 3,
        shaped(SPAN, rows, whole),
        WHOLE,
        deps=deps,
        micros=3,
    )


def pack(section, member, share, normed_share, branch, mixed, second, passed, deps=()):
    rows, width = branch.shape
    deep, thin, whole = share.shape[2], normed_share.shape[2], second.shape[2]

    def kernel(
        section_ref, member_ref, share_ref, normed_ref, branch_ref, mixed_ref, passed_ref,
        second_ref, *rest,
    ):
        sent_refs, same_ref, sems = rest[:SPAN], rest[SPAN], rest[SPAN + 1]
        same_ref[...] = passed_ref[...]

        @pl.when(section_ref[0] == 0)
        def _():
            for k in range(SPAN):
                sent_refs[k][:, 0:deep] = share_ref[member_ref[0] ^ k]
                sent_refs[k][:, deep : deep + width] = branch_ref[...]
                sent_refs[k][:, deep + width : deep + width + thin] = normed_ref[member_ref[0] ^ k]
                sent_refs[k][:, deep + width + thin : deep + 4 * width + thin] = mixed_ref[...]

        @pl.when(section_ref[0] != 0)
        def _():
            copies = [
                pltpu.make_async_copy(second_ref.at[k], sent_refs[k], sems.at[k])
                for k in range(SPAN)
            ]
            for copy in copies:
                copy.start()
            for copy in copies:
                copy.wait()

    return call(
        kernel,
        (section, member, share, normed_share, branch, mixed, passed, second),
        [SCALARS] * 2 + [WHOLE] * 5 + [ANY],
        [shaped(rows, whole)] * SPAN + [shaped(*passed.shape)],
        [WHOLE] * (SPAN + 1),
        [pltpu.SemaphoreType.DMA((SPAN,))],
        deps=deps,
        micros=4,
    )


def plane_gradients(section, group, sent, hidden_width, width, deps=()):
    halves = pack_columns(hidden_width, width)[:2]
    rows_of = [
        sum(
            (left.stop - left.start) // 4 * ((right.stop - right.start) // width)
            for left, right in pairs
        )
        for pairs in halves
    ]
    block = max(rows_of)

    def kernel(section_ref, group_ref, *refs):
        sent_refs, (keep_ref, leave_ref, buffer, sems) = refs[: len(sent)], refs[len(sent) :]

        def columns(at):
            return jnp.concatenate([ref[:, at] for ref in sent_refs], axis=0)

        def fill(pairs):
            start = 0
            for left, right in pairs:
                former, size = columns(left), (left.stop - left.start) // 4
                for first in range(right.start, right.stop, width):
                    part = transposed_product(former, columns(slice(first, first + width)))
                    for j in range(4):
                        buffer[j, start : start + size, :] = part[
                            j * size : (j + 1) * size
                        ].astype(bf16)
                    start += size
            if start < block:
                for j in range(4):
                    buffer[j, start:block, :] = jnp.zeros((block - start, width), bf16)

        @pl.when(section_ref[0] == 0)
        def _():
            fill(halves[0])

        @pl.when(section_ref[0] != 0)
        def _():
            fill(halves[1])

        for j in range(4):
            mine = ((group_ref[0] ^ j) & 1) == 0

            @pl.when(mine)
            def _(j=j):
                pltpu.make_async_copy(buffer.at[j], keep_ref.at[j >> 1], sems.at[j]).start()

            @pl.when(jnp.logical_not(mine))
            def _(j=j):
                pltpu.make_async_copy(buffer.at[j], leave_ref.at[j >> 1], sems.at[j]).start()

        for j in range(4):
            pltpu.make_async_copy(buffer.at[j], keep_ref.at[j >> 1], sems.at[j]).wait()

    return call(
        kernel,
        (section, group, *sent),
        [SCALARS] * 2 + [WHOLE] * len(sent),
        [shaped(2, block, width)] * 2,
        [ANY] * 2,
        [pltpu.VMEM((4, block, width), bf16), pltpu.SemaphoreType.DMA((4,))],
        deps=deps,
        micros=6,
    )


def by_parity(parity, sums, deps=()):
    count, rows, width = sums.shape

    def kernel(parity_ref, sums_ref, kept_ref, leaving_ref):
        for k in range(count // 2):
            kept_ref[k] = sums_ref[2 * k + parity_ref[0]]
            leaving_ref[k] = sums_ref[2 * k + 1 - parity_ref[0]]

    return call(
        kernel,
        (parity, sums),
        [SCALARS, WHOLE],
        [shaped(count // 2, rows, width)] * 2,
        [WHOLE] * 2,
        deps=deps,
        micros=3,
    )


def half_sum(which, kept, near, deps=()):
    shape = kept.shape[1:]

    def kernel(which_ref, kept_ref, near_ref, out_ref):
        total = kept_ref[0].astype(f32) + near_ref[0].astype(f32)
        out_ref[...] = total.astype(bf16)

    count = len(deps)

    def body(*refs):
        kernel(*refs[:3], refs[-1])

    steps = 1 if shape[0] % 32 else 2
    size = shape[0] // steps
    spec = pl.BlockSpec((1, size, shape[1]), lambda i, ref: (ref[0], i, 0))
    return pl.pallas_call(
        body,
        grid_spec=pltpu.PrefetchScalarGridSpec(
            num_scalar_prefetch=1,
            grid=(steps,),
            in_specs=[spec, spec] + [ANY] * count,
            out_specs=pl.BlockSpec((size, shape[1]), lambda i, ref: (i, 0)),
        ),
        out_shape=shaped(*shape),
        compiler_params=pltpu.CompilerParams(vmem_limit_bytes=VMEM),
        cost_estimate=cost(2),
    )(which, kept, near, *deps)


def finish(section, deep, shard, room, own_global, own_local, crossed, fars, table_parts, patch_parts):
    width = own_local.shape[1]
    chunks = deep // shard
    p = len(patch_parts)

    def kernel(section_ref, global_ref, local_ref, crossed_ref, table_ref, *refs):
        (global_one, global_two, local_one, local_two), refs = refs[:4], refs[4:]
        patch_refs = refs[:p]
        contract, expand, ins, out, table, small, patch = refs[p:]

        def total(some, start, size):
            return sum(ref[start : start + size, :].astype(f32) for ref in some)

        total_patch = sum(ref[...].astype(f32) for ref in patch_refs)
        patch[...] = total_patch[: patch.shape[0]]

        @pl.when(section_ref[0] == 0)
        def _():
            one, two = (global_ref, global_one), (crossed_ref, global_two)
            contract[...] = total(one, 0, deep)
            for c in range(3):
                ins[:, c * width : (c + 1) * width] = total(one, deep + c * shard, shard)
            for c in range(chunks):
                expand[:, c * width : (c + 1) * width] = total(two, c * shard, shard)
            out[...] = total(two, chunks * shard, shard)
            small[...] = total_patch[patch.shape[0] :]
            sums = jnp.zeros((room, width), f32)
            for k in range(table_ref.shape[0]):
                sums = sums + table_ref[k].astype(f32)
            table[...] = sums

        @pl.when(section_ref[0] != 0)
        def _():
            one, two = (crossed_ref, local_one), (local_ref, local_two)
            contract[...] = total(one, 0, deep)
            out[...] = total(one, deep, shard)
            ins[:, 0:width] = total(one, deep + shard, shard)
            table[...] = total(one, deep + 2 * shard, room)
            for c in range(chunks):
                expand[:, c * width : (c + 1) * width] = total(two, c * shard, shard)
            for c in range(2):
                ins[:, (c + 1) * width : (c + 2) * width] = total(two, deep + c * shard, shard)
            small[...] = total(two, deep + 2 * shard, small.shape[0])

    return call(
        kernel,
        (section, own_global, own_local, crossed, table_parts, *fars, *patch_parts),
        [SCALARS] + [WHOLE] * (8 + p),
        [
            shaped(deep, width, kind=f32),
            shaped(shard, chunks * width, kind=f32),
            shaped(shard, 3 * width, kind=f32),
            shaped(shard, width, kind=f32),
            shaped(room, width, kind=f32),
            shaped(SMALL_ROWS, width, kind=f32),
            shaped(patch_parts[0].shape[0] - SMALL_ROWS, width, kind=f32),
        ],
        [WHOLE] * 7,
        micros=4,
    )


SEQ = ("group", "member")


def section_send(x, origin, target, pairs):
    count = lax.axis_size(SEQ)
    joint = [(origin * count + i, target * count + j) for i, j in pairs]
    return lax.ppermute(x, ("section",) + SEQ, joint)


def section_swap(x):
    return lax.ppermute(x, "section", [(0, 1), (1, 0)])


def by_slot(buffer, count, pieces):
    split = count // GROUPS
    parts, start = [], 0
    for size, shared in pieces:
        part = buffer[:, start : start + size]
        start += size
        kept = shared or size // split
        if shared:
            part = jnp.broadcast_to(part[:, None, :shared], (GROUPS, split, shared, part.shape[2]))
        parts.append(part.reshape(count, kept, part.shape[-1]))
    whole = jnp.concatenate(parts, axis=1)
    turned = whole.reshape((4, count // 4) + whole.shape[1:])
    return jnp.swapaxes(turned, 0, 1).reshape(whole.shape)


def place_sum(shares):
    shares = lax.psum_scatter(shares, "member", scatter_dimension=0, tiled=True)
    return lax.psum_scatter(shares, "group", scatter_dimension=0, tiled=True)[0]


def on_device(
    byte_values,
    item_lengths,
    embed_tables,
    patch_weight,
    norm_gains,
    norm_biases,
    heads_in,
    heads_out,
    expand_weight,
    contract_weight,
    out_grad,
):
    place = lax.axis_index(SEQ)
    count = lax.axis_size(SEQ)
    section = lax.axis_index("section")
    is_global = section == 0
    batches, byte_rows = byte_values.shape
    patch_rows = byte_rows // PATCH
    width = heads_out.shape[2]
    rows = batches * patch_rows
    total_patches = patch_rows * count
    gains, biases = norm_gains[0], norm_biases[0]
    heads_in, heads_out = heads_in[0], heads_out[0]
    expand, contract = expand_weight[0], contract_weight[0]
    own_table = embed_tables[0]
    straight = [(i, i) for i in range(count)]

    quarters = PATCH // 2
    span = count // quarters
    group, member = place // span, place % span
    shard_rows = patch_weight.shape[0]
    pieces = [patch_weight]
    for k in range(1, span):
        pieces.append(lax.ppermute(patch_weight, SEQ, [(i, i ^ k) for i in range(count)]))
    other_table = section_swap(own_table)
    global_table = jnp.where(is_global, own_table, other_table)
    local_table = jnp.where(is_global, other_table, own_table)
    which_byte = section * quarters + group
    byte_ids = []
    for k in range(quarters):
        theirs = byte_values
        if k:
            theirs = lax.ppermute(byte_values, SEQ, [(i, i ^ (k * span)) for i in range(count)])
        theirs = theirs.reshape(rows, PATCH)
        byte_ids.append(lax.dynamic_index_in_dim(theirs, which_byte, 1, keepdims=False))
    byte_ids = jnp.concatenate(byte_ids)
    embedded, byte_weight, shares, low_shares = patch_forward(
        member.reshape(1).astype(jnp.int32), byte_ids, global_table, pieces
    )
    shares = shares + section_send(low_shares, 1, 0, straight).astype(f32)
    shares = shares.reshape(quarters, rows, width)
    parts = []
    for k in range(1, quarters):
        pairs = [(i, i ^ (k * span)) for i in range(count)]
        parts.append(section_send(shares[k].astype(bf16), 0, 0, pairs))

    arrived = [section_send(w, 1, 0, straight) for w in (heads_in, heads_out, expand, contract)]
    other_norms = section_swap(jnp.concatenate([gains, biases]))
    local_gains = jnp.where(is_global, other_norms[:2], gains)
    local_biases = jnp.where(is_global, other_norms[2:], biases)

    tasks = batches * PAIRS
    first_tasks = min(tasks, count)
    spare_tasks = tasks - first_tasks

    def to_tasks(blocks):
        columns = blocks.shape[2]
        slots = jnp.pad(blocks[:first_tasks], ((0, count - first_tasks), (0, 0), (0, 0)))
        if spare_tasks:
            spare = section_send(blocks[first_tasks:], 0, 1, straight)
            spare = jnp.pad(spare, ((0, count - spare_tasks), (0, 0), (0, 0)))
            slots = jnp.where(is_global, slots, spare)
        landed = lax.all_to_all(slots, SEQ, 0, 0)
        return landed.reshape(total_patches, columns)

    def from_tasks(results):
        columns = results.shape[1]
        slots = lax.all_to_all(results.reshape(count, patch_rows, columns), SEQ, 0, 0)
        if spare_tasks:
            return [slots, section_send(slots[:spare_tasks], 1, 0, straight)]
        return [slots]

    task = jnp.minimum(jnp.where(is_global, place, first_tasks + place), tasks - 1)
    task_lengths = lax.dynamic_index_in_dim(item_lengths, task // PAIRS, 0, keepdims=False)
    task_owners = locate(jnp.arange(total_patches, dtype=jnp.int32) * PATCH, task_lengths)[0]

    stream, normed, tasks_out, normed_share = global_start(
        batches, shares[0], parts, gains, biases, heads_in
    )
    qkv = to_tasks(tasks_out)
    attended, middle, normed_two, slope, hidden, sent, feed_share, other_share, edge, near = global_feed_forward(
        batches,
        from_tasks(global_attention(qkv, task_owners)),
        stream,
        gains,
        biases,
        heads_out,
        expand,
        contract,
    )
    half = patch_rows // 2
    half_bytes = half * PATCH
    chunks = half_bytes // BLOCK
    onward = [(i, i + 1) for i in range(count - 1)]
    backward = [(i + 1, i) for i in range(count - 1)]
    near = section_send(near, 0, 1, straight)
    edge = section_send(edge, 0, 0, onward)
    weights = (heads_in, heads_out, expand, contract)
    flag = section.reshape(1).astype(jnp.int32)
    block_patches = BLOCK // PATCH
    local_outs, activations_of, grads_shifted, grads_edge = [], [], [], []
    for c in range(chunks):
        numbers = jnp.concatenate(
            [
                jnp.stack([section, place * byte_rows, jnp.int32(c)]).astype(jnp.int32),
                item_lengths.reshape(-1),
            ]
        )
        act, grad_shifted, grad_edge, keep, send = local_block(
            numbers,
            byte_values,
            local_table,
            sent,
            edge,
            near,
            local_gains,
            local_biases,
            out_grad,
            patch_rows,
            weights,
            arrived,
        )
        local_outs.append(act.reshape(batches, BLOCK, width))
        grads_shifted.append(grad_shifted.reshape(batches, block_patches, width))
        grads_edge.append(grad_edge)
        activations_of.append((numbers, keep, section_swap(send)))
    local_out = jnp.concatenate(local_outs, axis=1)
    grad_shifted = jnp.concatenate(grads_shifted, axis=1).reshape(batches * half, width)

    other_out = section_send(local_out, 0, 1, straight)
    byte_places = place * byte_rows + jnp.arange(byte_rows, dtype=jnp.int32)
    live_bytes = jnp.stack([locate(byte_places, item_lengths[m])[1] for m in range(batches)])
    own_sent = jnp.broadcast_to(
        sent.reshape(batches, patch_rows, 1, width), (batches, patch_rows, PATCH, width)
    ).reshape(batches, byte_rows, width)
    own_sent = jnp.where(live_bytes[:, :, None], own_sent, jnp.zeros((), bf16))
    activations = jnp.where(
        is_global, own_sent, jnp.concatenate([other_out, local_out], axis=1)
    )

    shard = width // count
    room = VOCAB // count
    group_shard, group_room = width // GROUPS, VOCAB // GROUPS
    small_rows = max(4, room)
    pieces = {
        False: [(contract.shape[0] // GROUPS, 0), (group_shard, 0), (group_shard, 0), (group_room, 0)],
        True: [(group_shard, 0)] * (expand.shape[1] // width + 2) + [(group_room, small_rows)],
    }

    def ordered(buffer):
        if count == GROUPS:
            return buffer
        upper, lower = by_slot(buffer, count, pieces[False]), by_slot(buffer, count, pieces[True])
        rows_of = max(upper.shape[1], lower.shape[1])
        upper, lower = (
            jnp.pad(x, ((0, 0), (0, rows_of - x.shape[1]), (0, 0))) for x in (upper, lower)
        )
        return jnp.where(is_global, upper, lower)

    near_back = section_send(grad_shifted, 1, 0, straight)
    edge_back = section_send(grads_edge[0], 0, 0, backward)
    in_plane = span == SPAN and count == GROUPS
    member_flag = (member % SPAN).reshape(1).astype(jnp.int32)
    group_flag = group.reshape(1).astype(jnp.int32)

    def plane_send(blocks):
        return [blocks[0]] + [
            both_send(blocks[k], [(i, i ^ k) for i in range(count)]) for k in range(1, SPAN)
        ]

    upper = (group >> 1) & 1
    upper_flag = upper.reshape(1).astype(jnp.int32)

    def group_pairs(step):
        return [(i, i ^ (step * span)) for i in range(count)]

    def both_send(x, pairs):
        joint = [(s * count + i, s * count + j) for s in range(2) for i, j in pairs]
        return lax.ppermute(x, ("section",) + SEQ, joint)

    half_locals = [
        ordered(
            local_gradients(
                count,
                numbers,
                byte_values,
                keep,
                crossed,
                contract.shape[0],
                width,
                half_bytes,
                [near_back, edge_back],
            )
        )
        for numbers, keep, crossed in activations_of
    ]
    if chunks > 1:
        half_locals = [sum(x.astype(f32) for x in half_locals).astype(bf16)]
    half_locals = half_locals[0]
    grad_upward, grad_middle, attend_branch, task_grads, small, grad_sent = global_feed_backward(
        batches,
        grad_shifted,
        near_back,
        edge_back,
        middle,
        slope,
        gains,
        heads_out,
        expand,
        contract,
        [half_locals],
    )
    if in_plane:
        whole = pack_columns(contract.shape[0], width)[2]
        second_parts = section_send(
            pack_second(member_flag, other_share, attend_branch, grad_upward, whole), 0, 1, straight
        )
    task_grads = to_tasks(task_grads)
    task_mixed = global_attention(qkv, task_owners, task_grads)
    grad_mixed, own_rows, small = global_end(
        batches,
        from_tasks(task_mixed),
        stream,
        grad_middle,
        small,
        gains,
        heads_in,
    )

    if in_plane:
        *sent_parts, own_rows = pack(
            flag, member_flag, feed_share, normed_share, grad_sent, grad_mixed, second_parts, own_rows
        )
        arrived_parts = plane_send(sent_parts)

    gathered = [own_rows]
    for k in range(1, quarters):
        pairs = [(i, i ^ (k * span)) for i in range(count)]
        gathered.append(section_send(own_rows, 0, 0, pairs))
    crossed = section_send(jnp.concatenate(gathered), 0, 1, straight)
    patch_share, table_share = patch_backward(
        flag,
        byte_ids,
        embedded,
        byte_weight,
        gathered,
        crossed,
        span,
        arrived_parts[1:] if in_plane else (),
    )
    if in_plane:
        in_planes = lax.psum_scatter(half_locals, "member", scatter_dimension=0, tiled=True)
        parity_flag = (group & 1).reshape(1).astype(jnp.int32)
        local_kept, local_leaving = by_parity(parity_flag, in_planes, [crossed])
        local_near = both_send(local_leaving, group_pairs(1))
    else:
        own_local = place_sum(half_locals)
    patch_parts = [lax.dynamic_index_in_dim(patch_share, member, 0, keepdims=False)]
    for k in range(1, span):
        leaving = lax.dynamic_index_in_dim(patch_share, member ^ k, 0, keepdims=False)
        patch_parts.append(lax.ppermute(leaving, SEQ, [(i, i ^ k) for i in range(count)]))
    table_share = table_share + section_send(table_share, 1, 0, straight)
    table_parts = lax.all_to_all(table_share.reshape(count, VOCAB // count, width), SEQ, 0, 0)

    def ordered_rows(first, second):
        feed_rows = contract.shape[0] // count
        expand_sum = [second[k * shard : (k + 1) * shard] for k in range(feed_rows // shard)]
        rest, others = first[feed_rows:], second[feed_rows:]
        ins = [rest[shard : 2 * shard], others[:shard], others[shard : 2 * shard]]
        return (
            first[:feed_rows],
            jnp.concatenate(expand_sum, axis=1),
            jnp.concatenate(ins, axis=1),
            rest[:shard],
            rest[2 * shard : 2 * shard + room],
            others[2 * shard : 2 * shard + 4],
        )

    if in_plane:
        local_far = half_sum(1 - upper_flag, local_kept, local_near)
        local_mine = half_sum(upper_flag, local_kept, local_near)
        across = group_pairs(2)
        local_fars = [
            section_send(local_far, 0, 1, across),
            section_send(local_far, 1, 1, across),
        ]
        kept, leaving = plane_gradients(
            flag,
            group_flag,
            arrived_parts,
            contract.shape[0],
            width,
            [patch_share, *local_fars],
        )
        near = both_send(leaving, group_pairs(1))
        far = half_sum(1 - upper_flag, kept, near, patch_parts[1:])
        mine = half_sum(upper_flag, kept, near, [far])
        extra = mine.shape[0] - local_mine.shape[0]
        crossed = section_swap(
            jnp.where(is_global, jnp.pad(local_mine, ((0, extra), (0, 0))), mine)
        )
        fars = [
            section_send(far, 0, 0, across),
            section_send(far, 1, 0, across),
            *local_fars,
        ]
        contract_grad, expand_grad, in_grad, out_grads, table_grad, small, patch_grads = finish(
            flag,
            contract.shape[0] // count,
            shard,
            room,
            mine,
            local_mine,
            crossed,
            fars,
            table_parts,
            patch_parts,
        )
        small = small[:4]
    else:
        upper, lower = global_sums_of(
            count, hidden, grad_sent, normed_two, grad_upward, normed, grad_mixed, attended,
            attend_branch, small,
        )
        own_global = ordered(jnp.where(is_global, upper, section_send(lower, 0, 1, straight)))
        own_global = place_sum(own_global)
        crossed = section_swap(jnp.where(is_global, own_local, own_global)).astype(f32)
        global_sums = ordered_rows(own_global.astype(f32), crossed)
        global_table = jnp.sum(table_parts.astype(f32), axis=0)
        global_sums = global_sums[:4] + (global_table, global_sums[5])
        local_sums = ordered_rows(crossed, own_local.astype(f32))
        contract_grad, expand_grad, in_grad, out_grads, table_grad, small = (
            jnp.where(is_global, upper, lower) for upper, lower in zip(global_sums, local_sums)
        )
        patch_grads = sum(x.astype(f32) for x in patch_parts)[:shard_rows]
    small = lax.dynamic_slice_in_dim(small, place * shard, shard, 1)
    return (
        activations[None],
        table_grad[None],
        patch_grads,
        small[None, 0:2],
        small[None, 2:4],
        in_grad[None],
        out_grads[None],
        expand_grad[None],
        contract_grad[None],
    )


def solution(mesh):
    devices = mesh.devices
    groups = PATCH // 2
    split = jax.sharding.Mesh(
        devices.reshape(devices.shape[0], groups, devices.shape[1] // groups), ("section",) + SEQ
    )
    both = ("section",) + SEQ
    placed = (
        P(None, SEQ),
        P(),
        P("section", None, None),
        P(both, None),
        P("section", None, None),
        P("section", None, None),
        P("section", None, None),
        P("section", None, None),
        P("section", None, None),
        P("section", None, None),
        P(None, SEQ, None),
    )
    return jax.shard_map(
        on_device,
        mesh=split,
        in_specs=placed,
        out_specs=(
            P("section", None, SEQ, None),
            P("section", SEQ, None),
            P(both, None),
            P("section", None, SEQ),
            P("section", None, SEQ),
            P("section", SEQ, None),
            P("section", SEQ, None),
            P("section", SEQ, None),
            P("section", SEQ, None),
        ),
        check_vma=False,
    )
```

```python
from functools import partial

import jax
import jax.numpy as jnp
from jax import lax
from jax.experimental import pallas as pl
from jax.experimental.pallas import tpu as pltpu
from jax.sharding import PartitionSpec as P

HEADS = 12
HEAD_SIZE = 64
VOCAB = 256
PATCH = 8
ITEMS = 4
PAIRS = HEADS // 2
PAIR = 2 * HEAD_SIZE
SCALE = HEAD_SIZE ** (-0.5)
EPSILON = 1e-05
MASKED = -1e30
BLOCK = 128
TILE = 384
GROUPS = 16
SPAN = 4
VMEM = 60 * 1024 * 1024

bf16 = jnp.bfloat16
f32 = jnp.float32


def cost(micros):
    return pl.CostEstimate(flops=int(micros * 1.1e9), bytes_accessed=1, transcendentals=0)


def product(former, latter):
    return jnp.dot(former, latter, preferred_element_type=f32)


def transposed_product(former, latter):
    return lax.dot_general(former, latter, (((0,), (0,)), ((), ())), preferred_element_type=f32)


def product_transposed(former, latter):
    return lax.dot_general(former, latter, (((1,), (1,)), ((), ())), preferred_element_type=f32)


def normalise(values):
    average = jnp.mean(values, axis=-1, keepdims=True)
    centered = values - average
    inverse_root = lax.rsqrt(jnp.mean(centered * centered, axis=-1, keepdims=True) + EPSILON)
    return centered * inverse_root, inverse_root


def layer_norm(values, gain, bias):
    return normalise(values)[0] * gain + bias


def layer_norm_back(values, gain, grad):
    unit, inverse_root = normalise(values)
    scaled = grad * gain
    grad_values = inverse_root * (
        scaled
        - jnp.mean(scaled, axis=-1, keepdims=True)
        - unit * jnp.mean(scaled * unit, axis=-1, keepdims=True)
    )
    return (
        grad_values,
        jnp.sum(grad * unit, axis=0, keepdims=True),
        jnp.sum(grad, axis=0, keepdims=True),
    )


def slot_of(q, count):
    if count != GROUPS:
        return q
    return (q % SPAN) * (GROUPS // SPAN) + q // SPAN


def store_rows(buffer, value, count, start, columns=slice(None)):
    rows = value.shape[0] // GROUPS
    for q in range(GROUPS):
        buffer[slot_of(q, count), pl.ds(start, rows), columns] = value[
            q * rows : (q + 1) * rows
        ].astype(bf16)


def patch_bias(live_row):
    rows = lax.broadcasted_iota(jnp.int32, (BLOCK, BLOCK), 0)
    columns = lax.broadcasted_iota(jnp.int32, (BLOCK, BLOCK), 1)
    same = (rows // PATCH) == (columns // PATCH)
    allowed = same & (columns <= rows) & ((live_row > 0) | (columns == rows))
    bias = jnp.where(allowed, 0.0, MASKED)
    return jnp.concatenate([bias, bias], axis=0)


def softmax_rows(scores):
    peak = jnp.max(scores, axis=-1, keepdims=True)
    exponents = jnp.exp(scores - peak)
    return exponents * (1.0 / jnp.sum(exponents, axis=-1, keepdims=True))


def lane_masks():
    lanes = lax.broadcasted_iota(jnp.int32, (1, PAIR), 1)
    low = jnp.where(lanes < HEAD_SIZE, 1.0, 0.0)
    return lanes < HEAD_SIZE, low.astype(bf16), (1.0 - low).astype(bf16)


def stacked(values, low, high, scale=1.0):
    return jnp.concatenate([values * (low * scale), values * (high * scale)], axis=0)


def unstacked(values, is_low):
    half = values.shape[0] // 2
    return jnp.where(is_low, values[:half], values[half:])


def pair_probabilities(queries, keys, bias, masks):
    _, low, high = masks
    return softmax_rows(product_transposed(stacked(queries, low, high, SCALE), keys) + bias)


def pair_forward(queries, keys, values, bias, masks):
    probabilities = pair_probabilities(queries, keys, bias, masks)
    return unstacked(product(probabilities.astype(bf16), values), masks[0])


def pair_backward(queries, keys, values, grads, probabilities, masks):
    is_low, low, high = masks
    both = stacked(queries, low, high, SCALE)
    both_grads = stacked(grads, low, high)
    prob_grads = product_transposed(both_grads, values)
    delta = jnp.sum(probabilities * prob_grads, axis=-1, keepdims=True)
    score_grads = (probabilities * (prob_grads - delta)).astype(bf16)
    return (
        unstacked(product(score_grads, keys), is_low) * SCALE,
        transposed_product(score_grads, both),
        transposed_product(probabilities.astype(bf16), both_grads),
    )


def gelu_and_slope(x):
    root = 0.7978845608028654
    cubic = 0.044715
    square = x * x
    bent = jnp.tanh(x * (root + (root * cubic) * square))
    half = 0.5 * (1.0 + bent)
    slope = half + (0.5 * x) * (1.0 - bent * bent) * (root + (3.0 * root * cubic) * square)
    return x * half, slope


def fetch(section, own, arrived, target, sem):
    @pl.when(section == 0)
    def _():
        pltpu.make_async_copy(arrived, target, sem).start()

    @pl.when(section != 0)
    def _():
        pltpu.make_async_copy(own, target, sem).start()


def section_columns(hidden_width, width):
    tables = []
    for names in (
        ("hidden", "branch", "attended", "attend_branch", "normed", "queries", "stream"),
        ("upward", "normed_two", "normed", "keys", "values"),
    ):
        table, start = {}, 0
        for name in names:
            size = hidden_width if start == 0 else width
            table[name] = slice(start, start + size)
            start += size
        tables.append((table, start))
    return tables


SMALL_ROWS = 16


def item_spans(numbers_ref, first, batch):
    spans, start = [], 0
    for k in range(ITEMS):
        length = numbers_ref[first + batch * ITEMS + k]
        stop = start + (length + PATCH - 1) // PATCH * PATCH
        spans.append((start, start + length, stop))
        start = stop
    return spans


def is_live(positions, spans):
    live = jnp.zeros(positions.shape, jnp.bool_)
    for start, live_end, _ in spans:
        live = live | ((positions >= start) & (positions < live_end))
    return live


def owner_of(positions, spans):
    owner = jnp.full(positions.shape, ITEMS, jnp.int32)
    for k, (start, _, stop) in enumerate(spans):
        owner = jnp.where((positions >= start) & (positions < stop), k, owner)
    return owner


def local_kernel(
    patch_rows,
    numbers_ref,
    ids_ref,
    own_table_ref,
    new_table_ref,
    sent_ref,
    edge_ref,
    near_ref,
    own_norms_ref,
    new_norms_ref,
    out_grad_hbm,
    own_in,
    own_out,
    own_expand,
    own_contract,
    new_in,
    new_out,
    new_expand,
    new_contract,
    act_ref,
    grad_shifted_ref,
    grad_edge_ref,
    keep_ref,
    send_ref,
    w_in,
    w_out,
    w_expand,
    w_contract,
    first,
    second,
    out_grad_ref,
    source_ref,
    stream_ref,
    mixed_ref,
    middle_ref,
    slope_ref,
    grad_middle_ref,
    grad_attended_ref,
    grad_stream_ref,
    probability_ref,
    table_ref,
    sems,
    out_sems,
):
    section, offset, chunk = numbers_ref[0], numbers_ref[1], numbers_ref[2]
    rows, width = act_ref.shape
    batches = rows // BLOCK
    hidden_width = w_expand.shape[1]
    half = patch_rows // 2
    block_patches = BLOCK // PATCH
    lane = pl.multiple_of(section * (half * PATCH) + chunk * BLOCK, BLOCK)
    base = offset + lane
    grads_in = [
        pltpu.make_async_copy(
            out_grad_hbm.at[m, pl.ds(lane, BLOCK)],
            out_grad_ref.at[m * BLOCK : (m + 1) * BLOCK],
            sems.at[4 + m],
        )
        for m in range(batches)
    ]
    fetch(section, own_in, new_in, w_in, sems.at[0])
    for copy in grads_in:
        copy.start()
    fetch(section, own_out, new_out, w_out, sems.at[1])
    fetch(section, own_expand, new_expand, w_expand, sems.at[2])
    fetch(section, own_contract, new_contract, w_contract, sems.at[3])
    (to_first, first_width), (to_second, second_width) = section_columns(hidden_width, width)
    body = slice(0, rows)
    norms = jnp.where(section == 0, new_norms_ref[...], own_norms_ref[...])
    gains, biases = norms[0:2], norms[2:4]

    @pl.when(section == 0)
    def _():
        table_ref[...] = new_table_ref[...]

    @pl.when(section != 0)
    def _():
        table_ref[...] = own_table_ref[...]

    out_count = [0]

    def leave(from_first, columns, at_rows=body):
        source = first if from_first else second
        sem = out_sems.at[out_count[0]]
        out_count[0] += 1
        part = source.at[at_rows, columns]

        @pl.when(section == (0 if from_first else 1))
        def _():
            pltpu.make_async_copy(part, keep_ref.at[at_rows, columns], sem).start()

        @pl.when(section != (0 if from_first else 1))
        def _():
            pltpu.make_async_copy(part, send_ref.at[at_rows, columns], sem).start()

        return pltpu.make_async_copy(part, keep_ref.at[at_rows, columns], sem)

    blocks = [slice(m * BLOCK, (m + 1) * BLOCK) for m in range(batches)]
    spans = [item_spans(numbers_ref, 3, m) for m in range(batches)]
    column = lax.broadcasted_iota(jnp.int32, (BLOCK, 1), 0)
    row = lax.broadcasted_iota(jnp.int32, (1, BLOCK), 1)
    live_columns = [is_live(base + column, span) for span in spans]
    biases_of = [
        patch_bias(jnp.where(is_live(base + row, span), 1, 0)) for span in spans
    ]
    sent_rows, edge_rows = sent_ref.shape[0], edge_ref.shape[0]
    source_ref[0:sent_rows, :] = sent_ref[...]
    source_ref[sent_rows : sent_rows + edge_rows, :] = edge_ref[...]
    source_ref[sent_rows + edge_rows :, :] = near_ref[...]

    for copy in grads_in:
        copy.wait()
    for m, at in enumerate(blocks):
        vocabulary = lax.broadcasted_iota(jnp.int32, (VOCAB, BLOCK), 0)
        ids = ids_ref[m : m + 1, pl.ds(lane, BLOCK)]
        onehot = jnp.where(ids == vocabulary, 1.0, 0.0).astype(bf16)
        patch = column // PATCH
        place = chunk * block_patches + patch
        start = base + patch * PATCH
        same = owner_of(start, spans[m]) == owner_of(start - PATCH, spans[m])
        inside = jnp.where(place == 0, sent_rows + m, m * patch_rows + place - 1)
        chosen = jnp.where(section == 0, inside, sent_rows + edge_rows + m * half + place)
        chosen = jnp.where(same, chosen, -1)
        columns = lax.broadcasted_iota(jnp.int32, (BLOCK, source_ref.shape[0]), 1)
        spread = jnp.where(columns == chosen, 1.0, 0.0).astype(bf16)
        stream = transposed_product(onehot, table_ref[...]) + product(spread, source_ref[...])
        stream_ref[at, :] = stream
        normed = layer_norm(stream, gains[0:1], biases[0:1]).astype(bf16)
        first[at, to_first["normed"]] = normed
        second[at, to_second["normed"]] = normed
        first[at, to_first["branch"]] = jnp.where(
            live_columns[m], out_grad_ref[at, :].astype(f32), 0.0
        ).astype(bf16)

    pltpu.make_async_copy(own_in, w_in, sems.at[0]).wait()
    for i in range(3 * width // TILE):
        at = slice(i * TILE, (i + 1) * TILE)
        mixed_ref[:, at] = product(first[body, to_first["normed"]], w_in[:, at]).astype(bf16)

    masks = lane_masks()

    def pair_columns(pair, start=0):
        return slice(start + pair * PAIR, start + (pair + 1) * PAIR)

    for m, at in enumerate(blocks):
        for pair in range(PAIRS):
            probabilities = pair_probabilities(
                mixed_ref[at, pair_columns(pair)],
                mixed_ref[at, pair_columns(pair, width)],
                biases_of[m],
                masks,
            )
            probability_ref[m * PAIRS + pair] = probabilities
            attended = product(
                probabilities.astype(bf16), mixed_ref[at, pair_columns(pair, 2 * width)]
            )
            first[at, pair_columns(pair, to_first["attended"].start)] = unstacked(
                attended, masks[0]
            ).astype(bf16)

    pltpu.make_async_copy(own_out, w_out, sems.at[1]).wait()
    for at in blocks:
        middle = stream_ref[at, :] + product(first[at, to_first["attended"]], w_out[...])
        middle_ref[at, :] = middle
        normed_two = layer_norm(middle, gains[1:2], biases[1:2]).astype(bf16)
        second[at, to_second["normed_two"]] = normed_two

    pltpu.make_async_copy(own_expand, w_expand, sems.at[2]).wait()
    for i in range(hidden_width // TILE):
        at = slice(i * TILE, (i + 1) * TILE)
        hidden, slope = gelu_and_slope(
            product(second[body, to_second["normed_two"]], w_expand[:, at])
        )
        first[body, at] = hidden.astype(bf16)
        slope_ref[:, at] = slope.astype(bf16)

    copies = [leave(True, slice(0, to_first["attended"].stop))]
    pltpu.make_async_copy(own_contract, w_contract, sems.at[3]).wait()
    live_column = jnp.concatenate([jnp.where(x, 1, 0) for x in live_columns], axis=0)
    for i in range(width // 256):
        at = slice(i * 256, (i + 1) * 256)
        result = middle_ref[:, at] + product(first[body, to_first["hidden"]], w_contract[:, at])
        act_ref[:, at] = jnp.where(live_column > 0, result, 0.0).astype(bf16)

    for i in range(hidden_width // TILE):
        at = slice(i * TILE, (i + 1) * TILE)
        grad_hidden = product_transposed(first[body, to_first["branch"]], w_contract[at, :])
        second[body, at] = (grad_hidden * slope_ref[:, at].astype(f32)).astype(bf16)

    copies.append(leave(False, slice(0, to_second["normed"].stop)))
    for i in range(width // 256):
        at = slice(i * 256, (i + 1) * 256)
        grad_middle_ref[:, at] = product_transposed(
            second[body, to_second["upward"]], w_expand[at, :]
        )

    gain_two = bias_two = gain_one = bias_one = jnp.zeros((1, width), f32)
    for at in blocks:
        back, gain, bias = layer_norm_back(
            middle_ref[at, :], gains[1:2], grad_middle_ref[at, :]
        )
        grad_middle = back + first[at, to_first["branch"]].astype(f32)
        grad_middle_ref[at, :] = grad_middle
        branch = grad_middle.astype(bf16)
        first[at, to_first["attend_branch"]] = branch
        grad_attended_ref[at, :] = product_transposed(branch, w_out[...]).astype(bf16)
        gain_two, bias_two = gain_two + gain, bias_two + bias

    copies.append(leave(True, slice(to_first["attend_branch"].start, to_first["normed"].stop)))
    for m, at in enumerate(blocks):
        for pair in range(PAIRS):
            parts = pair_backward(
                mixed_ref[at, pair_columns(pair)],
                mixed_ref[at, pair_columns(pair, width)],
                mixed_ref[at, pair_columns(pair, 2 * width)],
                grad_attended_ref[at, pair_columns(pair)],
                probability_ref[m * PAIRS + pair],
                masks,
            )
            first[at, pair_columns(pair, to_first["queries"].start)] = parts[0].astype(bf16)
            second[at, pair_columns(pair, to_second["keys"].start)] = parts[1].astype(bf16)
            second[at, pair_columns(pair, to_second["values"].start)] = parts[2].astype(bf16)

    keys_values = slice(to_second["keys"].start, to_second["values"].stop)
    copies.append(leave(False, keys_values))
    for i in range(width // 256):
        at = slice(i * 256, (i + 1) * 256)
        grad_stream_ref[:, at] = product_transposed(
            first[body, to_first["queries"]], w_in[at, 0:width]
        ) + product_transposed(second[body, keys_values], w_in[at, width:])

    for m, at in enumerate(blocks):
        back, gain, bias = layer_norm_back(
            stream_ref[at, :], gains[0:1], grad_stream_ref[at, :]
        )
        grad_stream = back + grad_middle_ref[at, :]
        first[at, to_first["stream"]] = grad_stream.astype(bf16)
        gain_one, bias_one = gain_one + gain, bias_one + bias
        summed = jnp.sum(grad_stream.reshape(block_patches, PATCH, width), axis=1)
        start = base + PATCH * lax.broadcasted_iota(jnp.int32, (block_patches, 1), 0)
        same = owner_of(start, spans[m]) == owner_of(start - PATCH, spans[m])
        summed = jnp.where(same, summed, 0.0).astype(bf16)
        grad_shifted_ref[m * block_patches : (m + 1) * block_patches, :] = summed
        grad_edge_ref[m : m + 1, :] = summed[0:1]

    grad_edge_ref[batches:, :] = jnp.zeros((SMALL_ROWS - batches, width), bf16)
    small = jnp.concatenate(
        [gain_one, gain_two, bias_one, bias_two, jnp.zeros((SMALL_ROWS - 4, width), f32)], axis=0
    )
    second[rows:, 0:width] = small.astype(bf16)
    copies.append(leave(False, slice(0, width), slice(rows, rows + SMALL_ROWS)))
    copies.append(leave(True, slice(to_first["queries"].start, first_width)))
    for copy in copies:
        copy.wait()


ANY = pl.BlockSpec(memory_space=pl.ANY)
WHOLE = pl.BlockSpec(memory_space=pltpu.VMEM)
SCALARS = pl.BlockSpec(memory_space=pltpu.SMEM)


def vmem(*shape, kind=bf16):
    return pltpu.VMEM(shape, kind)


def local_block(numbers, ids, tables, sent, edge, near, norms, out_grad, patch_rows, own, new):
    batches, width = out_grad.shape[0], out_grad.shape[2]
    rows = batches * BLOCK
    hidden_width = own[3].shape[0]
    (_, first_width), (_, second_width) = section_columns(hidden_width, width)
    part = jax.ShapeDtypeStruct((rows + SMALL_ROWS, first_width), bf16)
    return pl.pallas_call(
        partial(local_kernel, patch_rows),
        in_specs=[SCALARS] + [WHOLE] * 8 + [ANY] * 9,
        out_specs=[WHOLE] * 3 + [ANY] * 2,
        out_shape=[
            jax.ShapeDtypeStruct((rows, width), bf16),
            jax.ShapeDtypeStruct((rows // PATCH, width), bf16),
            jax.ShapeDtypeStruct((SMALL_ROWS, width), bf16),
            part,
            part,
        ],
        scratch_shapes=[
            vmem(*own[0].shape),
            vmem(*own[1].shape),
            vmem(*own[2].shape),
            vmem(*own[3].shape),
            vmem(*part.shape),
            vmem(part.shape[0], second_width),
            vmem(rows, width),
            vmem(sent.shape[0] + edge.shape[0] + near.shape[0], width),
            vmem(rows, width, kind=f32),
            vmem(rows, 3 * width),
            vmem(rows, width, kind=f32),
            vmem(rows, hidden_width),
            vmem(rows, width, kind=f32),
            vmem(rows, width),
            vmem(rows, width, kind=f32),
            vmem(batches * PAIRS, 2 * BLOCK, BLOCK, kind=f32),
            vmem(*tables[0].shape),
            pltpu.SemaphoreType.DMA((4 + batches,)),
            pltpu.SemaphoreType.DMA((6,)),
        ],
        compiler_params=pltpu.CompilerParams(vmem_limit_bytes=VMEM),
        cost_estimate=cost(35),
    )(numbers, ids, *tables, sent, edge, near, *norms, out_grad, *own, *new)


def local_gradients(count, numbers, ids, keep, arrived, hidden_width, width, half, deps=()):
    rows = keep.shape[0] - SMALL_ROWS
    (to_first, first_width), (to_second, _) = section_columns(hidden_width, width)
    deep, shard, room = hidden_width // GROUPS, width // GROUPS, VOCAB // GROUPS
    block = deep + 2 * shard + room
    cuts = (slice(0, hidden_width + width), slice(hidden_width + width, first_width))

    def kernel(numbers_ref, ids_ref, keep_ref, new_ref, *rest):
        out_ref, held, smalls, sums, sems, out_sems = rest[len(deps) :]
        copies = []
        for k, cut in enumerate(cuts):
            for j, ref in enumerate((keep_ref, new_ref)):
                copies.append(
                    pltpu.make_async_copy(
                        ref.at[0:rows, cut], held.at[j * rows : (j + 1) * rows, cut], sems.at[2 * k + j]
                    )
                )
        for j, ref in enumerate((keep_ref, new_ref)):
            copies.append(
                pltpu.make_async_copy(
                    ref.at[rows : rows + SMALL_ROWS, 0:width], smalls.at[j], sems.at[4 + j]
                )
            )
        for copy in copies:
            copy.start()
        section_now, chunk = numbers_ref[0], numbers_ref[2]
        tile_shards = TILE // deep

        copies[0].wait()
        copies[1].wait()

        @pl.when(section_now == 0)
        def _():
            for i in range(hidden_width // TILE):
                part = transposed_product(
                    held[:, i * TILE : (i + 1) * TILE], held[:, to_first["branch"]]
                )
                for k in range(tile_shards):
                    slot = slot_of(i * tile_shards + k, count)
                    sums[slot, 0:deep, :] = part[k * deep : (k + 1) * deep].astype(bf16)

        @pl.when(section_now != 0)
        def _():
            for i in range(hidden_width // TILE):
                part = transposed_product(
                    held[:, to_second["normed_two"]], held[:, i * TILE : (i + 1) * TILE]
                )
                chunk, at = i * TILE // width, i * TILE % width
                store_rows(sums, part, count, chunk * shard, slice(at, at + TILE))

        feed = pl.ds(0, deep)
        pltpu.make_async_copy(sums.at[:, feed], out_ref.at[:, feed], out_sems.at[0]).start()
        for copy in copies[2:]:
            copy.wait()

        @pl.when(section_now == 0)
        def _():
            part = transposed_product(
                held[:, to_first["attended"]], held[:, to_first["attend_branch"]]
            )
            store_rows(sums, part, count, deep)
            part = transposed_product(held[:, to_first["normed"]], held[:, to_first["queries"]])
            store_rows(sums, part, count, deep + shard)
            vocabulary = lax.broadcasted_iota(jnp.int32, (VOCAB, BLOCK), 0)
            onehots = []
            for where in (section_now, 1 - section_now):
                lane = pl.multiple_of(where * half + chunk * BLOCK, BLOCK)
                for m in range(rows // BLOCK):
                    ids_row = ids_ref[m : m + 1, pl.ds(lane, BLOCK)]
                    onehots.append(jnp.where(ids_row == vocabulary, 1.0, 0.0).astype(bf16))
            part = product(jnp.concatenate(onehots, axis=1), held[:, to_first["stream"]])
            store_rows(sums, part, count, deep + 2 * shard)

        @pl.when(section_now != 0)
        def _():
            for k, name in enumerate(("keys", "values")):
                part = transposed_product(held[:, to_second["normed"]], held[:, to_second[name]])
                store_rows(sums, part, count, deep + k * shard)
            small = (smalls[0].astype(f32) + smalls[1].astype(f32)).astype(bf16)
            for q in range(GROUPS):
                sums[q, deep + 2 * shard :, :] = small

        heads = pl.ds(deep, block - deep)
        pltpu.make_async_copy(sums.at[:, heads], out_ref.at[:, heads], out_sems.at[1]).start()
        pltpu.make_async_copy(sums.at[:, feed], out_ref.at[:, feed], out_sems.at[0]).wait()
        pltpu.make_async_copy(sums.at[:, heads], out_ref.at[:, heads], out_sems.at[1]).wait()

    return pl.pallas_call(
        kernel,
        in_specs=[SCALARS, WHOLE, ANY, ANY] + [ANY] * len(deps),
        out_specs=ANY,
        out_shape=jax.ShapeDtypeStruct((GROUPS, block, width), bf16),
        scratch_shapes=[
            vmem(2 * rows, first_width),
            vmem(2, SMALL_ROWS, width),
            vmem(GROUPS, block, width),
            pltpu.SemaphoreType.DMA((6,)),
            pltpu.SemaphoreType.DMA((2,)),
        ],
        compiler_params=pltpu.CompilerParams(vmem_limit_bytes=VMEM),
        cost_estimate=cost(12),
    )(numbers, ids, keep, arrived, *deps)


def global_sums_kernel(
    count, hidden_ref, branch_ref, normed_two_ref, upward_ref, normed_ref, grad_mixed_ref,
    attended_ref, attend_branch_ref, small_ref, first, second,
):
    hidden_width, width = hidden_ref.shape[1], branch_ref.shape[1]
    deep, shard, room = hidden_width // GROUPS, width // GROUPS, VOCAB // GROUPS
    tile_shards = TILE // deep
    for i in range(hidden_width // TILE):
        columns = slice(i * TILE, (i + 1) * TILE)
        part = transposed_product(hidden_ref[:, columns], branch_ref[...])
        for k in range(tile_shards):
            slot = slot_of(i * tile_shards + k, count)
            first[slot, 0:deep, :] = part[k * deep : (k + 1) * deep].astype(bf16)
        part = transposed_product(normed_two_ref[...], upward_ref[:, columns])
        chunk, at = i * TILE // width, i * TILE % width
        store_rows(second, part, count, chunk * shard, slice(at, at + TILE))
    part = transposed_product(attended_ref[...], attend_branch_ref[...])
    store_rows(first, part, count, deep)
    targets = ((first, deep + shard), (second, deep), (second, deep + shard))
    for chunk, (target, start) in enumerate(targets):
        columns = slice(chunk * width, (chunk + 1) * width)
        part = transposed_product(normed_ref[...], grad_mixed_ref[:, columns])
        store_rows(target, part, count, start)
    small = jnp.concatenate([small_ref[...], jnp.zeros((room - 4, width), f32)], axis=0)
    for q in range(GROUPS):
        first[q, deep + 2 * shard :, :] = jnp.zeros((room, width), bf16)
        second[q, deep + 2 * shard :, :] = small.astype(bf16)


def global_sums_of(count, *arrays):
    hidden, branch = arrays[:2]
    hidden_width, width = hidden.shape[1], branch.shape[1]
    block = hidden_width // GROUPS + (2 * width + VOCAB) // GROUPS
    sums = jax.ShapeDtypeStruct((GROUPS, block, width), bf16)
    return pl.pallas_call(
        partial(global_sums_kernel, count),
        out_shape=[sums, sums],
        compiler_params=pltpu.CompilerParams(vmem_limit_bytes=VMEM),
        cost_estimate=cost(14),
    )(*arrays)


def causal_bias(start, count, numbers_ref):
    spans = item_spans(numbers_ref, 1, numbers_ref[0])
    rows = lax.broadcasted_iota(jnp.int32, (BLOCK, 1), 0) + start
    columns = lax.broadcasted_iota(jnp.int32, (1, count), 1)
    same = owner_of(rows * PATCH, spans) == owner_of(columns * PATCH, spans)
    bias = jnp.where((columns <= rows) & same, 0.0, MASKED)
    return jnp.concatenate([bias, bias], axis=0)


def global_forward_kernel(numbers_ref, qkv_ref, out_ref):
    start = pl.multiple_of(pl.program_id(0) * BLOCK, BLOCK)
    bias = causal_bias(start, qkv_ref.shape[0], numbers_ref)
    out_ref[...] = pair_forward(
        qkv_ref[pl.ds(start, BLOCK), 0:PAIR],
        qkv_ref[:, PAIR : 2 * PAIR],
        qkv_ref[:, 2 * PAIR : 3 * PAIR],
        bias,
        lane_masks(),
    ).astype(bf16)


def global_backward_kernel(numbers_ref, qkv_ref, grad_ref, out_ref, key_sum, value_sum):
    step = pl.program_id(0)
    start = pl.multiple_of(step * BLOCK, BLOCK)
    bias = causal_bias(start, qkv_ref.shape[0], numbers_ref)

    @pl.when(step == 0)
    def _():
        key_sum[...] = jnp.zeros_like(key_sum)
        value_sum[...] = jnp.zeros_like(value_sum)

    queries, keys = qkv_ref[pl.ds(start, BLOCK), 0:PAIR], qkv_ref[:, PAIR : 2 * PAIR]
    masks = lane_masks()
    grad_queries, grad_keys, grad_values = pair_backward(
        queries,
        keys,
        qkv_ref[:, 2 * PAIR : 3 * PAIR],
        grad_ref[...],
        pair_probabilities(queries, keys, bias, masks),
        masks,
    )
    out_ref[pl.ds(start, BLOCK), 0:PAIR] = grad_queries.astype(bf16)
    key_sum[...] += grad_keys
    value_sum[...] += grad_values

    @pl.when(step == pl.num_programs(0) - 1)
    def _():
        out_ref[:, PAIR : 2 * PAIR] = key_sum[...].astype(bf16)
        out_ref[:, 2 * PAIR : 3 * PAIR] = value_sum[...].astype(bf16)


def global_attention(qkv, numbers, grads=None, deps=()):
    count = qkv.shape[0]
    specs = [
        SCALARS,
        pl.BlockSpec((count, 3 * PAIR), lambda i: (0, 0)),
    ]
    blocks = pl.BlockSpec((BLOCK, PAIR), lambda i: (i, 0))
    if grads is None:
        return pl.pallas_call(
            global_forward_kernel,
            grid=(count // BLOCK,),
            in_specs=specs,
            out_specs=blocks,
            out_shape=jax.ShapeDtypeStruct((count, PAIR), bf16),
            compiler_params=pltpu.CompilerParams(vmem_limit_bytes=VMEM),
            cost_estimate=cost(15),
        )(numbers, qkv)

    def body(*refs):
        global_backward_kernel(*refs[:3], *refs[3 + len(deps) :])

    return pl.pallas_call(
        body,
        grid=(count // BLOCK,),
        in_specs=specs + [blocks] + [ANY] * len(deps),
        out_specs=pl.BlockSpec((count, 3 * PAIR), lambda i: (0, 0)),
        out_shape=jax.ShapeDtypeStruct((count, 3 * PAIR), bf16),
        scratch_shapes=[pltpu.VMEM((count, PAIR), f32), pltpu.VMEM((count, PAIR), f32)],
        compiler_params=pltpu.CompilerParams(vmem_limit_bytes=VMEM),
        cost_estimate=cost(30),
    )(numbers, qkv, grads, *deps)


def call(kernel, args, specs, out_shape, out_specs, scratch=(), deps=(), micros=1):
    count = len(args)

    def body(*refs):
        kernel(*refs[:count], *refs[count + len(deps) :])

    return pl.pallas_call(
        body,
        in_specs=list(specs) + [ANY] * len(deps),
        out_specs=out_specs,
        out_shape=out_shape,
        scratch_shapes=list(scratch),
        compiler_params=pltpu.CompilerParams(vmem_limit_bytes=VMEM),
        cost_estimate=cost(micros),
    )(*args, *deps)


def shaped(*shape, kind=bf16):
    return jax.ShapeDtypeStruct(shape, kind)


def patch_forward(numbers, patch_rows, byte_rows, own_table, new_table, pieces, deps=()):
    batches, width = byte_rows[0].shape[0], own_table.shape[1]
    segments = len(byte_rows) * batches
    rows = segments * patch_rows
    shard = pieces[0].shape[0]
    span, count = len(pieces), len(byte_rows)
    room = (segments + 15) // 16 * 16

    def kernel(numbers_ref, own_ref, new_ref, *rest):
        byte_refs, piece_refs, rest = rest[:count], rest[count : count + span], rest[count + span :]
        embedded_ref, weight_ref, share_ref, low_ref, onehot_ref, table_ref = rest
        member_now = numbers_ref[1]
        for k in range(span):
            start = pl.multiple_of((member_now ^ k) * shard, shard)
            weight_ref[pl.ds(start, shard), :] = piece_refs[k][...]

        @pl.when(numbers_ref[0] == 0)
        def _():
            table_ref[...] = own_ref[...]

        @pl.when(numbers_ref[0] != 0)
        def _():
            table_ref[...] = new_ref[...]

        some = [ref[...].astype(f32) for ref in byte_refs]
        some.append(jnp.zeros((room - segments, some[0].shape[1]), f32))
        some = jnp.concatenate(some, axis=0).astype(bf16)
        shape = (some.shape[1], rows)
        place = lax.broadcasted_iota(jnp.int32, shape, 1) % patch_rows * PATCH + numbers_ref[2]
        picked = lax.broadcasted_iota(jnp.int32, shape, 0) == place
        wide = product(some, jnp.where(picked, 1.0, 0.0).astype(bf16))
        segment = lax.broadcasted_iota(jnp.int32, (room, rows), 1) // patch_rows
        here = lax.broadcasted_iota(jnp.int32, (room, rows), 0) == segment
        ids = jnp.sum(jnp.where(here, wide, 0.0), axis=0, keepdims=True).astype(jnp.int32)
        vocabulary = lax.broadcasted_iota(jnp.int32, (VOCAB, rows), 0)
        onehot = jnp.where(ids == vocabulary, 1.0, 0.0).astype(bf16)
        onehot_ref[...] = onehot
        embedded_ref[...] = transposed_product(onehot, table_ref[...]).astype(bf16)
        share = product(embedded_ref[...], weight_ref[...])
        share_ref[...] = share
        low_ref[...] = share.astype(bf16)

    return call(
        kernel,
        (numbers, own_table, new_table, *byte_rows, *pieces),
        [SCALARS] + [WHOLE] * (2 + count + span),
        [
            shaped(rows, width),
            shaped(span * shard, width),
            shaped(rows, width, kind=f32),
            shaped(rows, width),
            shaped(VOCAB, rows),
        ],
        [WHOLE] * 5,
        [pltpu.VMEM(own_table.shape, bf16)],
        deps=deps,
        micros=4,
    )


def split_heads(values, targets, batches, part):
    patch_rows = values.shape[0] // batches
    first = targets[0].shape[0]
    for t in range(batches * PAIRS):
        m, pair = t // PAIRS, t % PAIRS
        target = targets[0].at[t] if t < first else targets[1].at[t - first]
        target[:, part * PAIR : (part + 1) * PAIR] = values[
            m * patch_rows : (m + 1) * patch_rows, pair * PAIR : (pair + 1) * PAIR
        ]


def task_shapes(batches, first, patch_rows, columns):
    rest = batches * PAIRS - first
    return [shaped(first, patch_rows, columns)] + ([shaped(rest, patch_rows, columns)] if rest else [])


def merge_heads(blocks, target, batches, parts):
    patch_rows = target.shape[0] // batches
    width = PAIRS * PAIR
    for t in range(batches * PAIRS):
        m, pair = t // PAIRS, t % PAIRS
        first = blocks[0].shape[0]
        block = blocks[0].at[t] if t < first else blocks[1].at[t - first]
        for part in range(parts):
            at = part * width + pair * PAIR
            target[m * patch_rows : (m + 1) * patch_rows, at : at + PAIR] = block[
                :, part * PAIR : (part + 1) * PAIR
            ]


def strided(values, target, span, offset):
    size = values.shape[1] // (4 * span)
    for k in range(span):
        parts = [
            values[:, (group * span + k) * size : (group * span + k + 1) * size]
            for group in range(4)
        ]
        target[k, :, offset : offset + 4 * size] = jnp.concatenate(parts, axis=1)


def global_start(batches, first_tasks, own, others, gains, biases, heads_in):
    rows, width = own.shape
    patch_rows = rows // batches
    tasks = task_shapes(batches, first_tasks, patch_rows, 3 * PAIR)

    def kernel(own_ref, gains_ref, biases_ref, weight_hbm, *rest):
        other_refs, rest = rest[: len(others)], rest[len(others) :]
        (stream_ref, normed_ref, share_ref), task_refs = rest[:3], rest[3 : 3 + len(tasks)]
        weight, sem = rest[3 + len(tasks) :]
        load = pltpu.make_async_copy(weight_hbm, weight, sem)
        load.start()
        stream = own_ref[...]
        for ref in other_refs:
            stream = stream + ref[...].astype(f32)
        stream_ref[...] = stream
        normed = layer_norm(stream, gains_ref[0:1], biases_ref[0:1]).astype(bf16)
        normed_ref[...] = normed
        strided(normed, share_ref, SPAN, 0)
        load.wait()
        for part in range(3):
            mixed = product(normed, weight[:, part * width : (part + 1) * width]).astype(bf16)
            split_heads(mixed, task_refs, batches, part)

    return call(
        kernel,
        (own, gains, biases, heads_in, *others),
        [WHOLE] * 3 + [ANY] + [WHOLE] * len(others),
        [
            shaped(rows, width, kind=f32),
            shaped(rows, width),
            shaped(SPAN, rows, width // SPAN),
            *tasks,
        ],
        [WHOLE] * (3 + len(tasks)),
        [pltpu.VMEM(heads_in.shape, bf16), pltpu.SemaphoreType.DMA],
        micros=5,
    )


def global_feed_forward(batches, blocks, stream, gains, biases, heads_out, expand, contract):
    rows, width = stream.shape
    hidden_width = expand.shape[1]
    n = len(blocks)
    patch_rows = rows // batches
    half = patch_rows // 2

    def kernel(stream_ref, gains_ref, biases_ref, out_hbm, expand_hbm, contract_hbm, *rest):
        block_refs, rest = rest[:n], rest[n:]
        (attended_ref, middle_ref, normed_two_ref, slope_ref, hidden_ref, sent_ref) = rest[:6]
        share_ref, other_share_ref, edge_ref, near_ref, w_out, w_expand, w_contract, sems = rest[6:]
        loads = [
            pltpu.make_async_copy(out_hbm, w_out, sems.at[0]),
            pltpu.make_async_copy(expand_hbm, w_expand, sems.at[1]),
            pltpu.make_async_copy(contract_hbm, w_contract, sems.at[2]),
        ]
        for load in loads:
            load.start()
        merge_heads(block_refs, attended_ref, batches, 1)
        loads[0].wait()
        middle = stream_ref[...] + product(attended_ref[...], w_out[...])
        middle_ref[...] = middle
        normed_two_ref[...] = layer_norm(middle, gains_ref[1:2], biases_ref[1:2]).astype(bf16)
        loads[1].wait()

        @pl.loop(0, hidden_width // width)
        def _(i):
            at = pl.ds(pl.multiple_of(i * width, 128), width)
            hidden, slope = gelu_and_slope(product(normed_two_ref[...], w_expand[:, at]))
            hidden_ref[:, at] = hidden.astype(bf16)
            slope_ref[:, at] = slope.astype(bf16)

        loads[2].wait()
        result = middle_ref[...] + product(hidden_ref[...], w_contract[...])
        sent = result.astype(bf16)
        sent_ref[...] = sent
        edge_ref[...] = jnp.zeros(edge_ref.shape, bf16)
        for m in range(batches):
            stop = (m + 1) * patch_rows
            edge_ref[m : m + 1, :] = sent[stop - 1 : stop]
            near_ref[m * half : (m + 1) * half, :] = sent[stop - half - 1 : stop - 1]
        strided(hidden_ref[...], share_ref, SPAN, 0)
        strided(normed_two_ref[...], other_share_ref, SPAN, 0)
        strided(attended_ref[...], other_share_ref, SPAN, width // SPAN)

    return call(
        kernel,
        (stream, gains, biases, heads_out, expand, contract, *blocks),
        [WHOLE] * 3 + [ANY] * 3 + [WHOLE] * n,
        [
            shaped(rows, width),
            shaped(rows, width, kind=f32),
            shaped(rows, width),
            shaped(rows, hidden_width),
            shaped(rows, hidden_width),
            shaped(rows, width),
            shaped(SPAN, rows, hidden_width // SPAN),
            shaped(SPAN, rows, 2 * width // SPAN),
            shaped(SMALL_ROWS, width),
            shaped(batches * half, width),
        ],
        [WHOLE] * 10,
        [
            pltpu.VMEM(heads_out.shape, bf16),
            pltpu.VMEM(expand.shape, bf16),
            pltpu.VMEM(contract.shape, bf16),
            pltpu.SemaphoreType.DMA((3,)),
        ],
        micros=8,
    )


def global_feed_backward(
    batches, first_tasks, own, near, edge, middle, slope, gains, heads_out, expand, contract, deps=()
):
    rows, width = middle.shape
    hidden_width = expand.shape[1]
    patch_rows = rows // batches
    half = patch_rows // 2
    tasks = task_shapes(batches, first_tasks, patch_rows, PAIR)

    def kernel(
        own_ref, near_ref, edge_ref, middle_ref, slope_ref, gains_ref, out_hbm, expand_hbm,
        contract_hbm, upward_ref, grad_middle_ref, branch_ref, small_ref, grad_ref, *rest,
    ):
        task_refs, (w_out, w_expand, w_contract, sems) = rest[: len(tasks)], rest[len(tasks) :]
        loads = [
            pltpu.make_async_copy(contract_hbm, w_contract, sems.at[2]),
            pltpu.make_async_copy(expand_hbm, w_expand, sems.at[1]),
            pltpu.make_async_copy(out_hbm, w_out, sems.at[0]),
        ]
        for load in loads:
            load.start()
        source = jnp.concatenate([own_ref[...], near_ref[...], edge_ref[...]], axis=0)
        index = lax.broadcasted_iota(jnp.int32, (rows, 1), 0)
        batch, place = index // patch_rows, index % patch_rows
        chosen = jnp.where(
            place < half - 1,
            batch * half + place + 1,
            jnp.where(
                place < patch_rows - 1,
                batches * half + batch * half + place - (half - 1),
                2 * batches * half + batch,
            ),
        )
        columns = lax.broadcasted_iota(jnp.int32, (rows, source.shape[0]), 1)
        picked = jnp.where(columns == chosen, 1.0, 0.0).astype(bf16)
        grad_ref[...] = product(picked, source).astype(bf16)
        loads[0].wait()

        @pl.loop(0, hidden_width // width)
        def _(i):
            at = pl.ds(pl.multiple_of(i * width, 128), width)
            grad_hidden = product_transposed(grad_ref[...], w_contract[at, :])
            upward_ref[:, at] = (grad_hidden * slope_ref[:, at].astype(f32)).astype(bf16)

        loads[1].wait()
        grad_normed = product_transposed(upward_ref[...], w_expand[...])
        back, gain, bias = layer_norm_back(middle_ref[...], gains_ref[1:2], grad_normed)
        grad_middle = back + grad_ref[...].astype(f32)
        grad_middle_ref[...] = grad_middle
        branch = grad_middle.astype(bf16)
        branch_ref[...] = branch
        small_ref[...] = jnp.concatenate([gain, bias], axis=0)
        loads[2].wait()
        attended = product_transposed(branch, w_out[...]).astype(bf16)
        split_heads(attended, task_refs, batches, 0)

    return call(
        kernel,
        (own, near, edge, middle, slope, gains, heads_out, expand, contract),
        [WHOLE] * 6 + [ANY] * 3,
        [
            shaped(rows, hidden_width),
            shaped(rows, width, kind=f32),
            shaped(rows, width),
            shaped(2, width, kind=f32),
            shaped(rows, width),
            *tasks,
        ],
        [WHOLE] * (5 + len(tasks)),
        [
            pltpu.VMEM(heads_out.shape, bf16),
            pltpu.VMEM(expand.shape, bf16),
            pltpu.VMEM(contract.shape, bf16),
            pltpu.SemaphoreType.DMA((3,)),
        ],
        deps=deps,
        micros=10,
    )


def global_end(batches, blocks, stream, grad_middle, small, gains, heads_in, deps=()):
    rows, width = stream.shape
    n = len(blocks)

    def kernel(stream_ref, grad_middle_ref, small_ref, gains_ref, weight_hbm, *rest):
        block_refs, (mixed_ref, low_ref, all_small_ref, weight, sem) = rest[:n], rest[n:]
        load = pltpu.make_async_copy(weight_hbm, weight, sem)
        load.start()
        merge_heads(block_refs, mixed_ref, batches, 3)
        load.wait()
        grad_normed = product_transposed(mixed_ref[...], weight[...])
        back, gain, bias = layer_norm_back(stream_ref[...], gains_ref[0:1], grad_normed)
        low_ref[0:rows, :] = (back + grad_middle_ref[...]).astype(bf16)
        smalls = jnp.concatenate([gain, small_ref[0:1], bias, small_ref[1:2]], axis=0)
        all_small_ref[...] = smalls
        rest = jnp.zeros((SMALL_ROWS - 4, width), f32)
        low_ref[rows:, :] = jnp.concatenate([smalls, rest], axis=0).astype(bf16)

    return call(
        kernel,
        (stream, grad_middle, small, gains, heads_in, *blocks),
        [WHOLE] * 4 + [ANY] + [WHOLE] * n,
        [
            shaped(rows, 3 * width),
            shaped(rows + SMALL_ROWS, width),
            shaped(4, width, kind=f32),
        ],
        [WHOLE] * 3,
        [pltpu.VMEM(heads_in.shape, bf16), pltpu.SemaphoreType.DMA],
        deps=deps,
        micros=6,
    )


def patch_backward(section, onehot, embedded, weight, own, crossed, span, deps=()):
    rows, width = embedded.shape
    block = own[0].shape[0]
    n = len(own)
    used = rows // n
    shard = weight.shape[0] // span

    def kernel(section_ref, onehot_ref, embedded_ref, weight_ref, crossed_ref, *rest):
        own_refs, (patch_ref, table_ref, gathered, small) = rest[:n], rest[n:]

        @pl.when(section_ref[0] == 0)
        def _():
            for k in range(n):
                gathered[k * used : (k + 1) * used, :] = own_refs[k][0:used, :]
            total = sum(ref[used:, :].astype(f32) for ref in own_refs)
            small[...] = total.astype(bf16)

        @pl.when(section_ref[0] != 0)
        def _():
            for k in range(n):
                gathered[k * used : (k + 1) * used, :] = crossed_ref[k * block : k * block + used, :]
            small[...] = jnp.zeros_like(small)

        part = transposed_product(embedded_ref[...], gathered[...]).astype(bf16)
        for k in range(span):
            patch_ref[k, 0:shard, :] = part[k * shard : (k + 1) * shard]
            patch_ref[k, shard:, :] = small[...]
        grad_embedded = product_transposed(gathered[...], weight_ref[...]).astype(bf16)
        table_ref[...] = product(onehot_ref[...], grad_embedded).astype(bf16)

    return call(
        kernel,
        (section, onehot, embedded, weight, crossed, *own),
        [SCALARS] + [WHOLE] * (4 + n),
        [shaped(span, shard + SMALL_ROWS, width), shaped(VOCAB, width)],
        [WHOLE] * 2,
        [pltpu.VMEM((rows, width), bf16), pltpu.VMEM((SMALL_ROWS, width), bf16)],
        deps=deps,
        micros=6,
    )


def leave_by_group(group, buffer, targets, sems):
    for j in range(len(targets)):
        for k in range(len(targets)):

            @pl.when((group ^ j) == k)
            def _(j=j, k=k):
                pltpu.make_async_copy(buffer.at[j], targets[k], sems.at[k]).start()

    for k in range(len(targets)):
        pltpu.make_async_copy(buffer.at[0], targets[k], sems.at[k]).wait()


def pack_columns(hidden_width, width):
    deep, thin = hidden_width // SPAN, width // SPAN
    first = [
        (slice(0, deep), slice(deep, deep + width)),
        (slice(deep + width, deep + width + thin), slice(deep + width + thin, deep + 4 * width + thin)),
    ]
    right = 2 * thin
    second = [
        (slice(0, thin), slice(right, right + hidden_width)),
        (slice(thin, right), slice(right + hidden_width, right + hidden_width + width)),
    ]
    return first, second, max(first[-1][1].stop, second[-1][1].stop)


def pack_second(member, share, attend_branch, upward, whole, deps=()):
    rows, width = attend_branch.shape
    own, hidden_width = share.shape[2], upward.shape[1]

    def kernel(member_ref, share_ref, attend_ref, upward_ref, out_ref):
        for k in range(SPAN):
            out_ref[k, :, 0:own] = share_ref[member_ref[0] ^ k]
            out_ref[k, :, own : own + hidden_width] = upward_ref[...]
            out_ref[k, :, own + hidden_width : own + hidden_width + width] = attend_ref[...]

    return call(
        kernel,
        (member, share, attend_branch, upward),
        [SCALARS] + [WHOLE] * 3,
        shaped(SPAN, rows, whole),
        WHOLE,
        deps=deps,
        micros=3,
    )


def pack(section, member, share, normed_share, branch, mixed, second, passed, deps=()):
    rows, width = branch.shape
    deep, thin, whole = share.shape[2], normed_share.shape[2], second.shape[2]

    def kernel(
        section_ref, member_ref, share_ref, normed_ref, branch_ref, mixed_ref, passed_ref,
        second_ref, *rest,
    ):
        sent_refs, same_ref, sems = rest[:SPAN], rest[SPAN], rest[SPAN + 1]
        same_ref[...] = passed_ref[...]

        @pl.when(section_ref[0] == 0)
        def _():
            for k in range(SPAN):
                sent_refs[k][:, 0:deep] = share_ref[member_ref[0] ^ k]
                sent_refs[k][:, deep : deep + width] = branch_ref[...]
                sent_refs[k][:, deep + width : deep + width + thin] = normed_ref[member_ref[0] ^ k]
                sent_refs[k][:, deep + width + thin : deep + 4 * width + thin] = mixed_ref[...]

        @pl.when(section_ref[0] != 0)
        def _():
            copies = [
                pltpu.make_async_copy(second_ref.at[k], sent_refs[k], sems.at[k])
                for k in range(SPAN)
            ]
            for copy in copies:
                copy.start()
            for copy in copies:
                copy.wait()

    return call(
        kernel,
        (section, member, share, normed_share, branch, mixed, passed, second),
        [SCALARS] * 2 + [WHOLE] * 5 + [ANY],
        [shaped(rows, whole)] * SPAN + [shaped(*passed.shape)],
        [WHOLE] * (SPAN + 1),
        [pltpu.SemaphoreType.DMA((SPAN,))],
        deps=deps,
        micros=4,
    )


def plane_gradients(section, group, sent, hidden_width, width, deps=()):
    halves = pack_columns(hidden_width, width)[:2]
    rows_of = [
        sum(
            (left.stop - left.start) // 4 * ((right.stop - right.start) // width)
            for left, right in pairs
        )
        for pairs in halves
    ]
    block = max(rows_of)

    def kernel(section_ref, group_ref, *refs):
        sent_refs, (keep_ref, leave_ref, buffer, sems) = refs[: len(sent)], refs[len(sent) :]

        def columns(at):
            return jnp.concatenate([ref[:, at] for ref in sent_refs], axis=0)

        def fill(pairs):
            start = 0
            for left, right in pairs:
                former, size = columns(left), (left.stop - left.start) // 4
                for first in range(right.start, right.stop, width):
                    part = transposed_product(former, columns(slice(first, first + width)))
                    for j in range(4):
                        buffer[j, start : start + size, :] = part[
                            j * size : (j + 1) * size
                        ].astype(bf16)
                    start += size
            if start < block:
                for j in range(4):
                    buffer[j, start:block, :] = jnp.zeros((block - start, width), bf16)

        @pl.when(section_ref[0] == 0)
        def _():
            fill(halves[0])

        @pl.when(section_ref[0] != 0)
        def _():
            fill(halves[1])

        for j in range(4):
            mine = ((group_ref[0] ^ j) & 1) == 0

            @pl.when(mine)
            def _(j=j):
                pltpu.make_async_copy(buffer.at[j], keep_ref.at[j >> 1], sems.at[j]).start()

            @pl.when(jnp.logical_not(mine))
            def _(j=j):
                pltpu.make_async_copy(buffer.at[j], leave_ref.at[j >> 1], sems.at[j]).start()

        for j in range(4):
            pltpu.make_async_copy(buffer.at[j], keep_ref.at[j >> 1], sems.at[j]).wait()

    return call(
        kernel,
        (section, group, *sent),
        [SCALARS] * 2 + [WHOLE] * len(sent),
        [shaped(2, block, width)] * 2,
        [ANY] * 2,
        [pltpu.VMEM((4, block, width), bf16), pltpu.SemaphoreType.DMA((4,))],
        deps=deps,
        micros=6,
    )


def by_parity(parity, sums, deps=()):
    count, rows, width = sums.shape

    def kernel(parity_ref, sums_ref, kept_ref, leaving_ref):
        for k in range(count // 2):
            kept_ref[k] = sums_ref[2 * k + parity_ref[0]]
            leaving_ref[k] = sums_ref[2 * k + 1 - parity_ref[0]]

    return call(
        kernel,
        (parity, sums),
        [SCALARS, WHOLE],
        [shaped(count // 2, rows, width)] * 2,
        [WHOLE] * 2,
        deps=deps,
        micros=3,
    )


def half_sums(upper, kept, near, deps=()):
    shape = kept.shape[1:]

    def kernel(upper_ref, kept_ref, near_ref, far_ref, mine_ref):
        for k in range(2):
            total = (kept_ref[k].astype(f32) + near_ref[k].astype(f32)).astype(bf16)

            @pl.when(upper_ref[0] == k)
            def _():
                mine_ref[...] = total

            @pl.when(upper_ref[0] != k)
            def _():
                far_ref[...] = total

    return call(
        kernel,
        (upper, kept, near),
        [SCALARS, WHOLE, WHOLE],
        [shaped(*shape)] * 2,
        [WHOLE] * 2,
        deps=deps,
        micros=2,
    )


def finish(section, deep, shard, room, own_global, own_local, crossed, fars, table_parts, patch_parts):
    width = own_local.shape[1]
    chunks = deep // shard
    p = len(patch_parts)

    def kernel(section_ref, global_ref, local_ref, crossed_ref, table_ref, *refs):
        (global_one, global_two, local_one, local_two), refs = refs[:4], refs[4:]
        patch_refs = refs[:p]
        contract, expand, ins, out, table, small, patch = refs[p:]

        def total(some, start, size):
            return sum(ref[start : start + size, :].astype(f32) for ref in some)

        total_patch = sum(ref[...].astype(f32) for ref in patch_refs)
        patch[...] = total_patch[: patch.shape[0]]

        @pl.when(section_ref[0] == 0)
        def _():
            one, two = (global_ref, global_one), (crossed_ref, global_two)
            contract[...] = total(one, 0, deep)
            for c in range(3):
                ins[:, c * width : (c + 1) * width] = total(one, deep + c * shard, shard)
            for c in range(chunks):
                expand[:, c * width : (c + 1) * width] = total(two, c * shard, shard)
            out[...] = total(two, chunks * shard, shard)
            small[...] = total_patch[patch.shape[0] :]
            sums = jnp.zeros((room, width), f32)
            for k in range(table_ref.shape[0]):
                sums = sums + table_ref[k].astype(f32)
            table[...] = sums

        @pl.when(section_ref[0] != 0)
        def _():
            one, two = (crossed_ref, local_one), (local_ref, local_two)
            contract[...] = total(one, 0, deep)
            out[...] = total(one, deep, shard)
            ins[:, 0:width] = total(one, deep + shard, shard)
            table[...] = total(one, deep + 2 * shard, room)
            for c in range(chunks):
                expand[:, c * width : (c + 1) * width] = total(two, c * shard, shard)
            for c in range(2):
                ins[:, (c + 1) * width : (c + 2) * width] = total(two, deep + c * shard, shard)
            small[...] = total(two, deep + 2 * shard, small.shape[0])

    return call(
        kernel,
        (section, own_global, own_local, crossed, table_parts, *fars, *patch_parts),
        [SCALARS] + [WHOLE] * (8 + p),
        [
            shaped(deep, width, kind=f32),
            shaped(shard, chunks * width, kind=f32),
            shaped(shard, 3 * width, kind=f32),
            shaped(shard, width, kind=f32),
            shaped(room, width, kind=f32),
            shaped(SMALL_ROWS, width, kind=f32),
            shaped(patch_parts[0].shape[0] - SMALL_ROWS, width, kind=f32),
        ],
        [WHOLE] * 7,
        micros=4,
    )


def activation_rows(numbers, sent, other, own, deps=()):
    batches, half, width = own.shape
    patch_rows = sent.shape[0] // batches
    byte_rows = patch_rows * PATCH

    def kernel(numbers_ref, sent_ref, other_ref, own_ref, out_ref):
        @pl.when(numbers_ref[0] == 0)
        def _():
            rows = lax.broadcasted_iota(jnp.int32, (byte_rows, 1), 0)
            columns = lax.broadcasted_iota(jnp.int32, (byte_rows, patch_rows), 1)
            for m in range(batches):
                live = is_live(numbers_ref[1] + rows, item_spans(numbers_ref, 3, m))
                chosen = jnp.where(live, rows // PATCH, -1)
                spread = jnp.where(columns == chosen, 1.0, 0.0).astype(bf16)
                part = sent_ref[m * patch_rows : (m + 1) * patch_rows, :]
                out_ref[m] = product(spread, part).astype(bf16)

        @pl.when(numbers_ref[0] != 0)
        def _():
            for m in range(batches):
                out_ref[m, 0:half, :] = other_ref[m]
                out_ref[m, half:, :] = own_ref[m]

    return call(
        kernel,
        (numbers, sent, other, own),
        [SCALARS] + [WHOLE] * 3,
        shaped(batches, byte_rows, width),
        WHOLE,
        deps=deps,
        micros=2,
    )


SEQ = ("group", "member")


def section_send(x, origin, target, pairs):
    count = lax.axis_size(SEQ)
    joint = [(origin * count + i, target * count + j) for i, j in pairs]
    return lax.ppermute(x, ("section",) + SEQ, joint)


def section_swap(x):
    return lax.ppermute(x, "section", [(0, 1), (1, 0)])


def by_slot(buffer, count, pieces):
    split = count // GROUPS
    parts, start = [], 0
    for size, shared in pieces:
        part = buffer[:, start : start + size]
        start += size
        kept = shared or size // split
        if shared:
            part = jnp.broadcast_to(part[:, None, :shared], (GROUPS, split, shared, part.shape[2]))
        parts.append(part.reshape(count, kept, part.shape[-1]))
    whole = jnp.concatenate(parts, axis=1)
    turned = whole.reshape((4, count // 4) + whole.shape[1:])
    return jnp.swapaxes(turned, 0, 1).reshape(whole.shape)


def place_sum(shares):
    shares = lax.psum_scatter(shares, "member", scatter_dimension=0, tiled=True)
    return lax.psum_scatter(shares, "group", scatter_dimension=0, tiled=True)[0]


def on_device(
    byte_values,
    item_lengths,
    embed_tables,
    patch_weight,
    norm_gains,
    norm_biases,
    heads_in,
    heads_out,
    expand_weight,
    contract_weight,
    out_grad,
):
    place = lax.axis_index(SEQ)
    count = lax.axis_size(SEQ)
    section = lax.axis_index("section")
    is_global = section == 0
    batches, byte_rows = byte_values.shape
    patch_rows = byte_rows // PATCH
    width = heads_out.shape[2]
    rows = batches * patch_rows
    total_patches = patch_rows * count
    gains, biases = norm_gains[0], norm_biases[0]
    heads_in, heads_out = heads_in[0], heads_out[0]
    expand, contract = expand_weight[0], contract_weight[0]
    own_table = embed_tables[0]
    straight = [(i, i) for i in range(count)]

    quarters = PATCH // 2
    span = count // quarters
    group, member = place // span, place % span
    shard_rows = patch_weight.shape[0]
    pieces = [patch_weight]
    for k in range(1, span):
        pieces.append(lax.ppermute(patch_weight, SEQ, [(i, i ^ k) for i in range(count)]))
    other_table = section_swap(own_table)
    theirs = [byte_values]
    for k in range(1, quarters):
        theirs.append(
            lax.ppermute(byte_values, SEQ, [(i, i ^ (k * span)) for i in range(count)])
        )
    place_numbers = jnp.stack([section, member, section * quarters + group]).astype(jnp.int32)
    embedded, byte_weight, shares, low_shares, byte_onehot = patch_forward(
        place_numbers, patch_rows, theirs, own_table, other_table, pieces
    )
    shares = shares + section_send(low_shares, 1, 0, straight).astype(f32)
    shares = shares.reshape(quarters, rows, width)
    parts = []
    for k in range(1, quarters):
        pairs = [(i, i ^ (k * span)) for i in range(count)]
        parts.append(section_send(shares[k].astype(bf16), 0, 0, pairs))

    arrived = [section_send(w, 1, 0, straight) for w in (heads_in, heads_out, expand, contract)]
    own_norms = jnp.concatenate([gains, biases])
    other_norms = section_swap(own_norms)

    tasks = batches * PAIRS
    first_tasks = min(tasks, count)
    spare_tasks = tasks - first_tasks

    def to_tasks(first, spare=None):
        columns = first.shape[2]
        slots = jnp.pad(first, ((0, count - first_tasks), (0, 0), (0, 0)))
        if spare_tasks:
            spare = section_send(spare, 0, 1, straight)
            spare = jnp.pad(spare, ((0, count - spare_tasks), (0, 0), (0, 0)))
            slots = jnp.where(is_global, slots, spare)
        landed = lax.all_to_all(slots, SEQ, 0, 0)
        return landed.reshape(total_patches, columns)

    def from_tasks(results):
        columns = results.shape[1]
        slots = lax.all_to_all(results.reshape(count, patch_rows, columns), SEQ, 0, 0)
        if spare_tasks:
            return [slots, section_send(slots[:spare_tasks], 1, 0, straight)]
        return [slots]

    task = jnp.minimum(jnp.where(is_global, place, first_tasks + place), tasks - 1)
    lengths = item_lengths.reshape(-1)
    task_numbers = jnp.concatenate([(task // PAIRS).reshape(1).astype(jnp.int32), lengths])

    stream, normed, normed_share, *tasks_out = global_start(
        batches, first_tasks, shares[0], parts, gains, biases, heads_in
    )
    qkv = to_tasks(*tasks_out)
    attended, middle, normed_two, slope, hidden, sent, feed_share, other_share, edge, near = global_feed_forward(
        batches,
        from_tasks(global_attention(qkv, task_numbers)),
        stream,
        gains,
        biases,
        heads_out,
        expand,
        contract,
    )
    half = patch_rows // 2
    half_bytes = half * PATCH
    chunks = half_bytes // BLOCK
    onward = [(i, i + 1) for i in range(count - 1)]
    backward = [(i + 1, i) for i in range(count - 1)]
    near = section_send(near, 0, 1, straight)
    edge = section_send(edge, 0, 0, onward)
    weights = (heads_in, heads_out, expand, contract)
    flag = section.reshape(1).astype(jnp.int32)
    block_patches = BLOCK // PATCH
    local_outs, activations_of, grads_shifted, grads_edge = [], [], [], []
    for c in range(chunks):
        numbers = jnp.concatenate(
            [
                jnp.stack([section, place * byte_rows, jnp.int32(c)]).astype(jnp.int32),
                lengths,
            ]
        )
        act, grad_shifted, grad_edge, keep, send = local_block(
            numbers,
            byte_values,
            (own_table, other_table),
            sent,
            edge,
            near,
            (own_norms, other_norms),
            out_grad,
            patch_rows,
            weights,
            arrived,
        )
        local_outs.append(act.reshape(batches, BLOCK, width))
        grads_shifted.append(grad_shifted.reshape(batches, block_patches, width))
        grads_edge.append(grad_edge)
        activations_of.append((numbers, keep, section_swap(send)))
    local_out = jnp.concatenate(local_outs, axis=1)
    grad_shifted = jnp.concatenate(grads_shifted, axis=1).reshape(batches * half, width)

    other_out = section_send(local_out, 0, 1, straight)
    activations = activation_rows(numbers, sent, other_out, local_out)

    shard = width // count
    room = VOCAB // count
    group_shard, group_room = width // GROUPS, VOCAB // GROUPS
    small_rows = max(4, room)
    pieces = {
        False: [(contract.shape[0] // GROUPS, 0), (group_shard, 0), (group_shard, 0), (group_room, 0)],
        True: [(group_shard, 0)] * (expand.shape[1] // width + 2) + [(group_room, small_rows)],
    }

    def ordered(buffer):
        if count == GROUPS:
            return buffer
        upper, lower = by_slot(buffer, count, pieces[False]), by_slot(buffer, count, pieces[True])
        rows_of = max(upper.shape[1], lower.shape[1])
        upper, lower = (
            jnp.pad(x, ((0, 0), (0, rows_of - x.shape[1]), (0, 0))) for x in (upper, lower)
        )
        return jnp.where(is_global, upper, lower)

    near_back = section_send(grad_shifted, 1, 0, straight)
    edge_back = section_send(grads_edge[0], 0, 0, backward)
    in_plane = span == SPAN and count == GROUPS
    member_flag = (member % SPAN).reshape(1).astype(jnp.int32)
    group_flag = group.reshape(1).astype(jnp.int32)

    def plane_send(blocks):
        return [blocks[0]] + [
            both_send(blocks[k], [(i, i ^ k) for i in range(count)]) for k in range(1, SPAN)
        ]

    upper = (group >> 1) & 1
    upper_flag = upper.reshape(1).astype(jnp.int32)

    def group_pairs(step):
        return [(i, i ^ (step * span)) for i in range(count)]

    def both_send(x, pairs):
        joint = [(s * count + i, s * count + j) for s in range(2) for i, j in pairs]
        return lax.ppermute(x, ("section",) + SEQ, joint)

    half_locals = [
        ordered(
            local_gradients(
                count,
                numbers,
                byte_values,
                keep,
                crossed,
                contract.shape[0],
                width,
                half_bytes,
                [near_back, edge_back],
            )
        )
        for numbers, keep, crossed in activations_of
    ]
    if chunks > 1:
        half_locals = [sum(x.astype(f32) for x in half_locals).astype(bf16)]
    half_locals = half_locals[0]
    grad_upward, grad_middle, attend_branch, small, grad_sent, *task_grads = global_feed_backward(
        batches,
        first_tasks,
        grad_shifted,
        near_back,
        edge_back,
        middle,
        slope,
        gains,
        heads_out,
        expand,
        contract,
        [half_locals],
    )
    if in_plane:
        whole = pack_columns(contract.shape[0], width)[2]
        second_parts = section_send(
            pack_second(member_flag, other_share, attend_branch, grad_upward, whole), 0, 1, straight
        )
    task_grads = to_tasks(*task_grads)
    task_mixed = global_attention(qkv, task_numbers, task_grads)
    grad_mixed, own_rows, small = global_end(
        batches,
        from_tasks(task_mixed),
        stream,
        grad_middle,
        small,
        gains,
        heads_in,
    )

    if in_plane:
        *sent_parts, own_rows = pack(
            flag, member_flag, feed_share, normed_share, grad_sent, grad_mixed, second_parts, own_rows
        )
        arrived_parts = plane_send(sent_parts)

    gathered = [own_rows]
    for k in range(1, quarters):
        pairs = [(i, i ^ (k * span)) for i in range(count)]
        gathered.append(section_send(own_rows, 0, 0, pairs))
    crossed = section_send(jnp.concatenate(gathered), 0, 1, straight)
    patch_share, table_share = patch_backward(
        flag,
        byte_onehot,
        embedded,
        byte_weight,
        gathered,
        crossed,
        span,
        arrived_parts[1:] if in_plane else (),
    )
    if in_plane:
        in_planes = lax.psum_scatter(half_locals, "member", scatter_dimension=0, tiled=True)
        parity_flag = (group & 1).reshape(1).astype(jnp.int32)
        local_kept, local_leaving = by_parity(parity_flag, in_planes, [crossed])
        local_near = both_send(local_leaving, group_pairs(1))
    else:
        own_local = place_sum(half_locals)
    patch_parts = [lax.dynamic_index_in_dim(patch_share, member, 0, keepdims=False)]
    for k in range(1, span):
        leaving = lax.dynamic_index_in_dim(patch_share, member ^ k, 0, keepdims=False)
        patch_parts.append(lax.ppermute(leaving, SEQ, [(i, i ^ k) for i in range(count)]))
    table_share = table_share + section_send(table_share, 1, 0, straight)
    table_parts = lax.all_to_all(table_share.reshape(count, VOCAB // count, width), SEQ, 0, 0)

    def ordered_rows(first, second):
        feed_rows = contract.shape[0] // count
        expand_sum = [second[k * shard : (k + 1) * shard] for k in range(feed_rows // shard)]
        rest, others = first[feed_rows:], second[feed_rows:]
        ins = [rest[shard : 2 * shard], others[:shard], others[shard : 2 * shard]]
        return (
            first[:feed_rows],
            jnp.concatenate(expand_sum, axis=1),
            jnp.concatenate(ins, axis=1),
            rest[:shard],
            rest[2 * shard : 2 * shard + room],
            others[2 * shard : 2 * shard + 4],
        )

    if in_plane:
        local_far, local_mine = half_sums(upper_flag, local_kept, local_near)
        across = group_pairs(2)
        local_fars = [
            section_send(local_far, 0, 1, across),
            section_send(local_far, 1, 1, across),
        ]
        kept, leaving = plane_gradients(
            flag,
            group_flag,
            arrived_parts,
            contract.shape[0],
            width,
            [patch_share, *local_fars],
        )
        near = both_send(leaving, group_pairs(1))
        far, mine = half_sums(upper_flag, kept, near, patch_parts[1:])
        extra = mine.shape[0] - local_mine.shape[0]
        crossed = section_swap(
            jnp.where(is_global, jnp.pad(local_mine, ((0, extra), (0, 0))), mine)
        )
        fars = [
            section_send(far, 0, 0, across),
            section_send(far, 1, 0, across),
            *local_fars,
        ]
        contract_grad, expand_grad, in_grad, out_grads, table_grad, small, patch_grads = finish(
            flag,
            contract.shape[0] // count,
            shard,
            room,
            mine,
            local_mine,
            crossed,
            fars,
            table_parts,
            patch_parts,
        )
        small = small[:4]
    else:
        upper, lower = global_sums_of(
            count, hidden, grad_sent, normed_two, grad_upward, normed, grad_mixed, attended,
            attend_branch, small,
        )
        own_global = ordered(jnp.where(is_global, upper, section_send(lower, 0, 1, straight)))
        own_global = place_sum(own_global)
        crossed = section_swap(jnp.where(is_global, own_local, own_global)).astype(f32)
        global_sums = ordered_rows(own_global.astype(f32), crossed)
        global_table = jnp.sum(table_parts.astype(f32), axis=0)
        global_sums = global_sums[:4] + (global_table, global_sums[5])
        local_sums = ordered_rows(crossed, own_local.astype(f32))
        contract_grad, expand_grad, in_grad, out_grads, table_grad, small = (
            jnp.where(is_global, upper, lower) for upper, lower in zip(global_sums, local_sums)
        )
        patch_grads = sum(x.astype(f32) for x in patch_parts)[:shard_rows]
    small = lax.dynamic_slice_in_dim(small, place * shard, shard, 1)
    return (
        activations[None],
        table_grad[None],
        patch_grads,
        small[None, 0:2],
        small[None, 2:4],
        in_grad[None],
        out_grads[None],
        expand_grad[None],
        contract_grad[None],
    )


def solution(mesh):
    devices = mesh.devices
    groups = PATCH // 2
    split = jax.sharding.Mesh(
        devices.reshape(devices.shape[0], groups, devices.shape[1] // groups), ("section",) + SEQ
    )
    both = ("section",) + SEQ
    placed = (
        P(None, SEQ),
        P(),
        P("section", None, None),
        P(both, None),
        P("section", None, None),
        P("section", None, None),
        P("section", None, None),
        P("section", None, None),
        P("section", None, None),
        P("section", None, None),
        P(None, SEQ, None),
    )
    return jax.shard_map(
        on_device,
        mesh=split,
        in_specs=placed,
        out_specs=(
            P("section", None, SEQ, None),
            P("section", SEQ, None),
            P(both, None),
            P("section", None, SEQ),
            P("section", None, SEQ),
            P("section", SEQ, None),
            P("section", SEQ, None),
            P("section", SEQ, None),
            P("section", SEQ, None),
        ),
        check_vma=False,
    )
```

```python
from functools import partial

import jax
import jax.numpy as jnp
from jax import lax
from jax.experimental import pallas as pl
from jax.experimental.pallas import tpu as pltpu
from jax.sharding import PartitionSpec as P

HEADS = 12
HEAD_SIZE = 64
VOCAB = 256
PATCH = 8
ITEMS = 4
PAIRS = HEADS // 2
PAIR = 2 * HEAD_SIZE
SCALE = HEAD_SIZE ** (-0.5)
EPSILON = 1e-05
MASKED = -1e30
BLOCK = 128
TILE = 384
GROUPS = 16
SPAN = 4
VMEM = 60 * 1024 * 1024

bf16 = jnp.bfloat16
f32 = jnp.float32


def cost(micros):
    return pl.CostEstimate(flops=int(micros * 1.1e9), bytes_accessed=1, transcendentals=0)


def product(former, latter):
    return jnp.dot(former, latter, preferred_element_type=f32)


def transposed_product(former, latter):
    return lax.dot_general(former, latter, (((0,), (0,)), ((), ())), preferred_element_type=f32)


def product_transposed(former, latter):
    return lax.dot_general(former, latter, (((1,), (1,)), ((), ())), preferred_element_type=f32)


def normalise(values):
    average = jnp.mean(values, axis=-1, keepdims=True)
    centered = values - average
    inverse_root = lax.rsqrt(jnp.mean(centered * centered, axis=-1, keepdims=True) + EPSILON)
    return centered * inverse_root, inverse_root


def layer_norm(values, gain, bias):
    return normalise(values)[0] * gain + bias


def layer_norm_back(values, gain, grad):
    unit, inverse_root = normalise(values)
    scaled = grad * gain
    grad_values = inverse_root * (
        scaled
        - jnp.mean(scaled, axis=-1, keepdims=True)
        - unit * jnp.mean(scaled * unit, axis=-1, keepdims=True)
    )
    return (
        grad_values,
        jnp.sum(grad * unit, axis=0, keepdims=True),
        jnp.sum(grad, axis=0, keepdims=True),
    )


def slot_of(q, count):
    if count != GROUPS:
        return q
    return (q % SPAN) * (GROUPS // SPAN) + q // SPAN


def store_rows(buffer, value, count, start, columns=slice(None)):
    rows = value.shape[0] // GROUPS
    for q in range(GROUPS):
        buffer[slot_of(q, count), pl.ds(start, rows), columns] = value[
            q * rows : (q + 1) * rows
        ].astype(bf16)


def patch_bias(live_row):
    rows = lax.broadcasted_iota(jnp.int32, (BLOCK, BLOCK), 0)
    columns = lax.broadcasted_iota(jnp.int32, (BLOCK, BLOCK), 1)
    same = (rows // PATCH) == (columns // PATCH)
    allowed = same & (columns <= rows) & ((live_row > 0) | (columns == rows))
    bias = jnp.where(allowed, 0.0, MASKED)
    return jnp.concatenate([bias, bias], axis=0)


def softmax_rows(scores):
    peak = jnp.max(scores, axis=-1, keepdims=True)
    exponents = jnp.exp(scores - peak)
    return exponents * (1.0 / jnp.sum(exponents, axis=-1, keepdims=True))


def lane_masks():
    lanes = lax.broadcasted_iota(jnp.int32, (1, PAIR), 1)
    low = jnp.where(lanes < HEAD_SIZE, 1.0, 0.0)
    return lanes < HEAD_SIZE, low.astype(bf16), (1.0 - low).astype(bf16)


def stacked(values, low, high, scale=1.0):
    return jnp.concatenate([values * (low * scale), values * (high * scale)], axis=0)


def unstacked(values, is_low):
    half = values.shape[0] // 2
    return jnp.where(is_low, values[:half], values[half:])


def pair_probabilities(queries, keys, bias, masks):
    _, low, high = masks
    return softmax_rows(product_transposed(stacked(queries, low, high, SCALE), keys) + bias)


def pair_forward(queries, keys, values, bias, masks):
    probabilities = pair_probabilities(queries, keys, bias, masks)
    return unstacked(product(probabilities.astype(bf16), values), masks[0])


def pair_backward(queries, keys, values, grads, probabilities, masks):
    is_low, low, high = masks
    both = stacked(queries, low, high, SCALE)
    both_grads = stacked(grads, low, high)
    prob_grads = product_transposed(both_grads, values)
    delta = jnp.sum(probabilities * prob_grads, axis=-1, keepdims=True)
    score_grads = (probabilities * (prob_grads - delta)).astype(bf16)
    return (
        unstacked(product(score_grads, keys), is_low) * SCALE,
        transposed_product(score_grads, both),
        transposed_product(probabilities.astype(bf16), both_grads),
    )


def gelu_and_slope(x):
    root = 0.7978845608028654
    cubic = 0.044715
    square = x * x
    bent = jnp.tanh(x * (root + (root * cubic) * square))
    half = 0.5 * (1.0 + bent)
    slope = half + (0.5 * x) * (1.0 - bent * bent) * (root + (3.0 * root * cubic) * square)
    return x * half, slope


def fetch(section, own, arrived, target, sem):
    @pl.when(section == 0)
    def _():
        pltpu.make_async_copy(arrived, target, sem).start()

    @pl.when(section != 0)
    def _():
        pltpu.make_async_copy(own, target, sem).start()


def section_columns(hidden_width, width):
    tables = []
    for names in (
        ("hidden", "branch", "attended", "attend_branch", "normed", "queries", "stream"),
        ("upward", "normed_two", "normed", "keys", "values"),
    ):
        table, start = {}, 0
        for name in names:
            size = hidden_width if start == 0 else width
            table[name] = slice(start, start + size)
            start += size
        tables.append((table, start))
    return tables


SMALL_ROWS = 16


def item_spans(numbers_ref, first, batch):
    spans, start = [], 0
    for k in range(ITEMS):
        length = numbers_ref[first + batch * ITEMS + k]
        stop = start + (length + PATCH - 1) // PATCH * PATCH
        spans.append((start, start + length, stop))
        start = stop
    return spans


def is_live(positions, spans):
    live = jnp.zeros(positions.shape, jnp.bool_)
    for start, live_end, _ in spans:
        live = live | ((positions >= start) & (positions < live_end))
    return live


def owner_of(positions, spans):
    owner = jnp.full(positions.shape, ITEMS, jnp.int32)
    for k, (start, _, stop) in enumerate(spans):
        owner = jnp.where((positions >= start) & (positions < stop), k, owner)
    return owner


def local_kernel(
    patch_rows,
    numbers_ref,
    ids_ref,
    own_table_ref,
    new_table_ref,
    sent_ref,
    edge_ref,
    near_ref,
    own_norms_ref,
    new_norms_ref,
    out_grad_hbm,
    own_in,
    own_out,
    own_expand,
    own_contract,
    new_in,
    new_out,
    new_expand,
    new_contract,
    act_ref,
    grad_shifted_ref,
    grad_edge_ref,
    keep_ref,
    send_ref,
    w_in,
    w_out,
    w_expand,
    w_contract,
    first,
    second,
    out_grad_ref,
    source_ref,
    stream_ref,
    mixed_ref,
    middle_ref,
    slope_ref,
    grad_middle_ref,
    grad_attended_ref,
    grad_stream_ref,
    probability_ref,
    table_ref,
    sems,
    out_sems,
):
    section, offset, chunk = numbers_ref[0], numbers_ref[1], numbers_ref[2]
    rows, width = act_ref.shape
    batches = rows // BLOCK
    hidden_width = w_expand.shape[1]
    half = patch_rows // 2
    block_patches = BLOCK // PATCH
    lane = pl.multiple_of(section * (half * PATCH) + chunk * BLOCK, BLOCK)
    base = offset + lane
    grads_in = [
        pltpu.make_async_copy(
            out_grad_hbm.at[m, pl.ds(lane, BLOCK)],
            out_grad_ref.at[m * BLOCK : (m + 1) * BLOCK],
            sems.at[4 + m],
        )
        for m in range(batches)
    ]
    fetch(section, own_in, new_in, w_in, sems.at[0])
    for copy in grads_in:
        copy.start()
    fetch(section, own_out, new_out, w_out, sems.at[1])
    fetch(section, own_expand, new_expand, w_expand, sems.at[2])
    fetch(section, own_contract, new_contract, w_contract, sems.at[3])
    (to_first, first_width), (to_second, second_width) = section_columns(hidden_width, width)
    body = slice(0, rows)
    norms = jnp.where(section == 0, new_norms_ref[...], own_norms_ref[...])
    gains, biases = norms[0:2], norms[2:4]

    @pl.when(section == 0)
    def _():
        table_ref[...] = new_table_ref[...]

    @pl.when(section != 0)
    def _():
        table_ref[...] = own_table_ref[...]

    out_count = [0]

    def leave(from_first, columns, at_rows=body):
        source = first if from_first else second
        sem = out_sems.at[out_count[0]]
        out_count[0] += 1
        part = source.at[at_rows, columns]

        @pl.when(section == (0 if from_first else 1))
        def _():
            pltpu.make_async_copy(part, keep_ref.at[at_rows, columns], sem).start()

        @pl.when(section != (0 if from_first else 1))
        def _():
            pltpu.make_async_copy(part, send_ref.at[at_rows, columns], sem).start()

        return pltpu.make_async_copy(part, keep_ref.at[at_rows, columns], sem)

    blocks = [slice(m * BLOCK, (m + 1) * BLOCK) for m in range(batches)]
    spans = [item_spans(numbers_ref, 3, m) for m in range(batches)]
    column = lax.broadcasted_iota(jnp.int32, (BLOCK, 1), 0)
    row = lax.broadcasted_iota(jnp.int32, (1, BLOCK), 1)
    live_columns = [is_live(base + column, span) for span in spans]
    biases_of = [
        patch_bias(jnp.where(is_live(base + row, span), 1, 0)) for span in spans
    ]
    sent_rows, edge_rows = sent_ref.shape[0], edge_ref.shape[0]
    source_ref[0:sent_rows, :] = sent_ref[...]
    source_ref[sent_rows : sent_rows + edge_rows, :] = edge_ref[...]
    source_ref[sent_rows + edge_rows :, :] = near_ref[...]

    for copy in grads_in:
        copy.wait()
    for m, at in enumerate(blocks):
        vocabulary = lax.broadcasted_iota(jnp.int32, (VOCAB, BLOCK), 0)
        ids = ids_ref[m : m + 1, pl.ds(lane, BLOCK)]
        onehot = jnp.where(ids == vocabulary, 1.0, 0.0).astype(bf16)
        patch = column // PATCH
        place = chunk * block_patches + patch
        start = base + patch * PATCH
        same = owner_of(start, spans[m]) == owner_of(start - PATCH, spans[m])
        inside = jnp.where(place == 0, sent_rows + m, m * patch_rows + place - 1)
        chosen = jnp.where(section == 0, inside, sent_rows + edge_rows + m * half + place)
        chosen = jnp.where(same, chosen, -1)
        columns = lax.broadcasted_iota(jnp.int32, (BLOCK, source_ref.shape[0]), 1)
        spread = jnp.where(columns == chosen, 1.0, 0.0).astype(bf16)
        stream = transposed_product(onehot, table_ref[...]) + product(spread, source_ref[...])
        stream_ref[at, :] = stream
        normed = layer_norm(stream, gains[0:1], biases[0:1]).astype(bf16)
        first[at, to_first["normed"]] = normed
        second[at, to_second["normed"]] = normed
        first[at, to_first["branch"]] = jnp.where(
            live_columns[m], out_grad_ref[at, :].astype(f32), 0.0
        ).astype(bf16)

    pltpu.make_async_copy(own_in, w_in, sems.at[0]).wait()
    for i in range(3 * width // TILE):
        at = slice(i * TILE, (i + 1) * TILE)
        mixed_ref[:, at] = product(first[body, to_first["normed"]], w_in[:, at]).astype(bf16)

    masks = lane_masks()

    def pair_columns(pair, start=0):
        return slice(start + pair * PAIR, start + (pair + 1) * PAIR)

    for m, at in enumerate(blocks):
        for pair in range(PAIRS):
            probabilities = pair_probabilities(
                mixed_ref[at, pair_columns(pair)],
                mixed_ref[at, pair_columns(pair, width)],
                biases_of[m],
                masks,
            )
            probability_ref[m * PAIRS + pair] = probabilities
            attended = product(
                probabilities.astype(bf16), mixed_ref[at, pair_columns(pair, 2 * width)]
            )
            first[at, pair_columns(pair, to_first["attended"].start)] = unstacked(
                attended, masks[0]
            ).astype(bf16)

    pltpu.make_async_copy(own_out, w_out, sems.at[1]).wait()
    for at in blocks:
        middle = stream_ref[at, :] + product(first[at, to_first["attended"]], w_out[...])
        middle_ref[at, :] = middle
        normed_two = layer_norm(middle, gains[1:2], biases[1:2]).astype(bf16)
        second[at, to_second["normed_two"]] = normed_two

    pltpu.make_async_copy(own_expand, w_expand, sems.at[2]).wait()
    for i in range(hidden_width // TILE):
        at = slice(i * TILE, (i + 1) * TILE)
        hidden, slope = gelu_and_slope(
            product(second[body, to_second["normed_two"]], w_expand[:, at])
        )
        first[body, at] = hidden.astype(bf16)
        slope_ref[:, at] = slope.astype(bf16)

    copies = [leave(True, slice(0, to_first["attended"].stop))]
    pltpu.make_async_copy(own_contract, w_contract, sems.at[3]).wait()
    live_column = jnp.concatenate([jnp.where(x, 1, 0) for x in live_columns], axis=0)
    for i in range(width // 256):
        at = slice(i * 256, (i + 1) * 256)
        result = middle_ref[:, at] + product(first[body, to_first["hidden"]], w_contract[:, at])
        act_ref[:, at] = jnp.where(live_column > 0, result, 0.0).astype(bf16)

    for i in range(hidden_width // TILE):
        at = slice(i * TILE, (i + 1) * TILE)
        grad_hidden = product_transposed(first[body, to_first["branch"]], w_contract[at, :])
        second[body, at] = (grad_hidden * slope_ref[:, at].astype(f32)).astype(bf16)

    copies.append(leave(False, slice(0, to_second["normed"].stop)))
    for i in range(width // 256):
        at = slice(i * 256, (i + 1) * 256)
        grad_middle_ref[:, at] = product_transposed(
            second[body, to_second["upward"]], w_expand[at, :]
        )

    gain_two = bias_two = gain_one = bias_one = jnp.zeros((1, width), f32)
    for at in blocks:
        back, gain, bias = layer_norm_back(
            middle_ref[at, :], gains[1:2], grad_middle_ref[at, :]
        )
        grad_middle = back + first[at, to_first["branch"]].astype(f32)
        grad_middle_ref[at, :] = grad_middle
        branch = grad_middle.astype(bf16)
        first[at, to_first["attend_branch"]] = branch
        grad_attended_ref[at, :] = product_transposed(branch, w_out[...]).astype(bf16)
        gain_two, bias_two = gain_two + gain, bias_two + bias

    copies.append(leave(True, slice(to_first["attend_branch"].start, to_first["normed"].stop)))
    for m, at in enumerate(blocks):
        for pair in range(PAIRS):
            parts = pair_backward(
                mixed_ref[at, pair_columns(pair)],
                mixed_ref[at, pair_columns(pair, width)],
                mixed_ref[at, pair_columns(pair, 2 * width)],
                grad_attended_ref[at, pair_columns(pair)],
                probability_ref[m * PAIRS + pair],
                masks,
            )
            first[at, pair_columns(pair, to_first["queries"].start)] = parts[0].astype(bf16)
            second[at, pair_columns(pair, to_second["keys"].start)] = parts[1].astype(bf16)
            second[at, pair_columns(pair, to_second["values"].start)] = parts[2].astype(bf16)

    keys_values = slice(to_second["keys"].start, to_second["values"].stop)
    copies.append(leave(False, keys_values))
    for i in range(width // 256):
        at = slice(i * 256, (i + 1) * 256)
        grad_stream_ref[:, at] = product_transposed(
            first[body, to_first["queries"]], w_in[at, 0:width]
        ) + product_transposed(second[body, keys_values], w_in[at, width:])

    for m, at in enumerate(blocks):
        back, gain, bias = layer_norm_back(
            stream_ref[at, :], gains[0:1], grad_stream_ref[at, :]
        )
        grad_stream = back + grad_middle_ref[at, :]
        first[at, to_first["stream"]] = grad_stream.astype(bf16)
        gain_one, bias_one = gain_one + gain, bias_one + bias
        summed = jnp.sum(grad_stream.reshape(block_patches, PATCH, width), axis=1)
        start = base + PATCH * lax.broadcasted_iota(jnp.int32, (block_patches, 1), 0)
        same = owner_of(start, spans[m]) == owner_of(start - PATCH, spans[m])
        summed = jnp.where(same, summed, 0.0).astype(bf16)
        grad_shifted_ref[m * block_patches : (m + 1) * block_patches, :] = summed
        grad_edge_ref[m : m + 1, :] = summed[0:1]

    grad_edge_ref[batches:, :] = jnp.zeros((SMALL_ROWS - batches, width), bf16)
    small = jnp.concatenate(
        [gain_one, gain_two, bias_one, bias_two, jnp.zeros((SMALL_ROWS - 4, width), f32)], axis=0
    )
    second[rows:, 0:width] = small.astype(bf16)
    copies.append(leave(False, slice(0, width), slice(rows, rows + SMALL_ROWS)))
    copies.append(leave(True, slice(to_first["queries"].start, first_width)))
    for copy in copies:
        copy.wait()


ANY = pl.BlockSpec(memory_space=pl.ANY)
WHOLE = pl.BlockSpec(memory_space=pltpu.VMEM)
SCALARS = pl.BlockSpec(memory_space=pltpu.SMEM)


def vmem(*shape, kind=bf16):
    return pltpu.VMEM(shape, kind)


def local_block(numbers, ids, tables, sent, edge, near, norms, out_grad, patch_rows, own, new):
    batches, width = out_grad.shape[0], out_grad.shape[2]
    rows = batches * BLOCK
    hidden_width = own[3].shape[0]
    (_, first_width), (_, second_width) = section_columns(hidden_width, width)
    part = jax.ShapeDtypeStruct((rows + SMALL_ROWS, first_width), bf16)
    return pl.pallas_call(
        partial(local_kernel, patch_rows),
        in_specs=[SCALARS] + [WHOLE] * 8 + [ANY] * 9,
        out_specs=[WHOLE] * 3 + [ANY] * 2,
        out_shape=[
            jax.ShapeDtypeStruct((rows, width), bf16),
            jax.ShapeDtypeStruct((rows // PATCH, width), bf16),
            jax.ShapeDtypeStruct((SMALL_ROWS, width), bf16),
            part,
            part,
        ],
        scratch_shapes=[
            vmem(*own[0].shape),
            vmem(*own[1].shape),
            vmem(*own[2].shape),
            vmem(*own[3].shape),
            vmem(*part.shape),
            vmem(part.shape[0], second_width),
            vmem(rows, width),
            vmem(sent.shape[0] + edge.shape[0] + near.shape[0], width),
            vmem(rows, width, kind=f32),
            vmem(rows, 3 * width),
            vmem(rows, width, kind=f32),
            vmem(rows, hidden_width),
            vmem(rows, width, kind=f32),
            vmem(rows, width),
            vmem(rows, width, kind=f32),
            vmem(batches * PAIRS, 2 * BLOCK, BLOCK, kind=f32),
            vmem(*tables[0].shape),
            pltpu.SemaphoreType.DMA((4 + batches,)),
            pltpu.SemaphoreType.DMA((6,)),
        ],
        compiler_params=pltpu.CompilerParams(vmem_limit_bytes=VMEM),
        cost_estimate=cost(35),
    )(numbers, ids, *tables, sent, edge, near, *norms, out_grad, *own, *new)


def local_gradients(count, numbers, ids, keep, arrived, hidden_width, width, half, deps=()):
    rows = keep.shape[0] - SMALL_ROWS
    (to_first, first_width), (to_second, _) = section_columns(hidden_width, width)
    deep, shard, room = hidden_width // GROUPS, width // GROUPS, VOCAB // GROUPS
    block = deep + 2 * shard + room
    cuts = (slice(0, hidden_width + width), slice(hidden_width + width, first_width))

    def kernel(numbers_ref, ids_ref, keep_ref, new_ref, *rest):
        out_ref, held, smalls, sums, sems, out_sems = rest[len(deps) :]
        copies = []
        for k, cut in enumerate(cuts):
            for j, ref in enumerate((keep_ref, new_ref)):
                copies.append(
                    pltpu.make_async_copy(
                        ref.at[0:rows, cut], held.at[j * rows : (j + 1) * rows, cut], sems.at[2 * k + j]
                    )
                )
        for j, ref in enumerate((keep_ref, new_ref)):
            copies.append(
                pltpu.make_async_copy(
                    ref.at[rows : rows + SMALL_ROWS, 0:width], smalls.at[j], sems.at[4 + j]
                )
            )
        for copy in copies:
            copy.start()
        section_now, chunk = numbers_ref[0], numbers_ref[2]
        tile_shards = TILE // deep

        copies[0].wait()
        copies[1].wait()

        @pl.when(section_now == 0)
        def _():
            for i in range(hidden_width // TILE):
                part = transposed_product(
                    held[:, i * TILE : (i + 1) * TILE], held[:, to_first["branch"]]
                )
                for k in range(tile_shards):
                    slot = slot_of(i * tile_shards + k, count)
                    sums[slot, 0:deep, :] = part[k * deep : (k + 1) * deep].astype(bf16)

        @pl.when(section_now != 0)
        def _():
            for i in range(hidden_width // TILE):
                part = transposed_product(
                    held[:, to_second["normed_two"]], held[:, i * TILE : (i + 1) * TILE]
                )
                chunk, at = i * TILE // width, i * TILE % width
                store_rows(sums, part, count, chunk * shard, slice(at, at + TILE))

        feed = pl.ds(0, deep)
        pltpu.make_async_copy(sums.at[:, feed], out_ref.at[:, feed], out_sems.at[0]).start()
        for copy in copies[2:]:
            copy.wait()

        @pl.when(section_now == 0)
        def _():
            part = transposed_product(
                held[:, to_first["attended"]], held[:, to_first["attend_branch"]]
            )
            store_rows(sums, part, count, deep)
            part = transposed_product(held[:, to_first["normed"]], held[:, to_first["queries"]])
            store_rows(sums, part, count, deep + shard)
            vocabulary = lax.broadcasted_iota(jnp.int32, (VOCAB, BLOCK), 0)
            onehots = []
            for where in (section_now, 1 - section_now):
                lane = pl.multiple_of(where * half + chunk * BLOCK, BLOCK)
                for m in range(rows // BLOCK):
                    ids_row = ids_ref[m : m + 1, pl.ds(lane, BLOCK)]
                    onehots.append(jnp.where(ids_row == vocabulary, 1.0, 0.0).astype(bf16))
            part = product(jnp.concatenate(onehots, axis=1), held[:, to_first["stream"]])
            store_rows(sums, part, count, deep + 2 * shard)

        @pl.when(section_now != 0)
        def _():
            for k, name in enumerate(("keys", "values")):
                part = transposed_product(held[:, to_second["normed"]], held[:, to_second[name]])
                store_rows(sums, part, count, deep + k * shard)
            small = (smalls[0].astype(f32) + smalls[1].astype(f32)).astype(bf16)
            for q in range(GROUPS):
                sums[q, deep + 2 * shard :, :] = small

        heads = pl.ds(deep, block - deep)
        pltpu.make_async_copy(sums.at[:, heads], out_ref.at[:, heads], out_sems.at[1]).start()
        pltpu.make_async_copy(sums.at[:, feed], out_ref.at[:, feed], out_sems.at[0]).wait()
        pltpu.make_async_copy(sums.at[:, heads], out_ref.at[:, heads], out_sems.at[1]).wait()

    return pl.pallas_call(
        kernel,
        in_specs=[SCALARS, WHOLE, ANY, ANY] + [ANY] * len(deps),
        out_specs=ANY,
        out_shape=jax.ShapeDtypeStruct((GROUPS, block, width), bf16),
        scratch_shapes=[
            vmem(2 * rows, first_width),
            vmem(2, SMALL_ROWS, width),
            vmem(GROUPS, block, width),
            pltpu.SemaphoreType.DMA((6,)),
            pltpu.SemaphoreType.DMA((2,)),
        ],
        compiler_params=pltpu.CompilerParams(vmem_limit_bytes=VMEM),
        cost_estimate=cost(12),
    )(numbers, ids, keep, arrived, *deps)


def global_sums_kernel(
    count, hidden_ref, branch_ref, normed_two_ref, upward_ref, normed_ref, grad_mixed_ref,
    attended_ref, attend_branch_ref, small_ref, first, second,
):
    hidden_width, width = hidden_ref.shape[1], branch_ref.shape[1]
    deep, shard, room = hidden_width // GROUPS, width // GROUPS, VOCAB // GROUPS
    tile_shards = TILE // deep
    for i in range(hidden_width // TILE):
        columns = slice(i * TILE, (i + 1) * TILE)
        part = transposed_product(hidden_ref[:, columns], branch_ref[...])
        for k in range(tile_shards):
            slot = slot_of(i * tile_shards + k, count)
            first[slot, 0:deep, :] = part[k * deep : (k + 1) * deep].astype(bf16)
        part = transposed_product(normed_two_ref[...], upward_ref[:, columns])
        chunk, at = i * TILE // width, i * TILE % width
        store_rows(second, part, count, chunk * shard, slice(at, at + TILE))
    part = transposed_product(attended_ref[...], attend_branch_ref[...])
    store_rows(first, part, count, deep)
    targets = ((first, deep + shard), (second, deep), (second, deep + shard))
    for chunk, (target, start) in enumerate(targets):
        columns = slice(chunk * width, (chunk + 1) * width)
        part = transposed_product(normed_ref[...], grad_mixed_ref[:, columns])
        store_rows(target, part, count, start)
    small = jnp.concatenate([small_ref[...], jnp.zeros((room - 4, width), f32)], axis=0)
    for q in range(GROUPS):
        first[q, deep + 2 * shard :, :] = jnp.zeros((room, width), bf16)
        second[q, deep + 2 * shard :, :] = small.astype(bf16)


def global_sums_of(count, *arrays):
    hidden, branch = arrays[:2]
    hidden_width, width = hidden.shape[1], branch.shape[1]
    block = hidden_width // GROUPS + (2 * width + VOCAB) // GROUPS
    sums = jax.ShapeDtypeStruct((GROUPS, block, width), bf16)
    return pl.pallas_call(
        partial(global_sums_kernel, count),
        out_shape=[sums, sums],
        compiler_params=pltpu.CompilerParams(vmem_limit_bytes=VMEM),
        cost_estimate=cost(14),
    )(*arrays)


def causal_bias(start, count, numbers_ref):
    spans = item_spans(numbers_ref, 1, numbers_ref[0])
    rows = lax.broadcasted_iota(jnp.int32, (BLOCK, 1), 0) + start
    columns = lax.broadcasted_iota(jnp.int32, (1, count), 1)
    same = owner_of(rows * PATCH, spans) == owner_of(columns * PATCH, spans)
    bias = jnp.where((columns <= rows) & same, 0.0, MASKED)
    return jnp.concatenate([bias, bias], axis=0)


def global_forward_kernel(numbers_ref, qkv_ref, out_ref):
    start = pl.multiple_of(pl.program_id(0) * BLOCK, BLOCK)
    bias = causal_bias(start, qkv_ref.shape[0], numbers_ref)
    out_ref[...] = pair_forward(
        qkv_ref[pl.ds(start, BLOCK), 0:PAIR],
        qkv_ref[:, PAIR : 2 * PAIR],
        qkv_ref[:, 2 * PAIR : 3 * PAIR],
        bias,
        lane_masks(),
    ).astype(bf16)


def global_backward_kernel(numbers_ref, qkv_ref, grad_ref, out_ref, key_sum, value_sum):
    step = pl.program_id(0)
    start = pl.multiple_of(step * BLOCK, BLOCK)
    bias = causal_bias(start, qkv_ref.shape[0], numbers_ref)

    @pl.when(step == 0)
    def _():
        key_sum[...] = jnp.zeros_like(key_sum)
        value_sum[...] = jnp.zeros_like(value_sum)

    queries, keys = qkv_ref[pl.ds(start, BLOCK), 0:PAIR], qkv_ref[:, PAIR : 2 * PAIR]
    masks = lane_masks()
    grad_queries, grad_keys, grad_values = pair_backward(
        queries,
        keys,
        qkv_ref[:, 2 * PAIR : 3 * PAIR],
        grad_ref[...],
        pair_probabilities(queries, keys, bias, masks),
        masks,
    )
    out_ref[pl.ds(start, BLOCK), 0:PAIR] = grad_queries.astype(bf16)
    key_sum[...] += grad_keys
    value_sum[...] += grad_values

    @pl.when(step == pl.num_programs(0) - 1)
    def _():
        out_ref[:, PAIR : 2 * PAIR] = key_sum[...].astype(bf16)
        out_ref[:, 2 * PAIR : 3 * PAIR] = value_sum[...].astype(bf16)


def global_attention(qkv, numbers, grads=None, deps=()):
    count = qkv.shape[0]
    specs = [
        SCALARS,
        pl.BlockSpec((count, 3 * PAIR), lambda i: (0, 0)),
    ]
    blocks = pl.BlockSpec((BLOCK, PAIR), lambda i: (i, 0))
    if grads is None:
        return pl.pallas_call(
            global_forward_kernel,
            grid=(count // BLOCK,),
            in_specs=specs,
            out_specs=blocks,
            out_shape=jax.ShapeDtypeStruct((count, PAIR), bf16),
            compiler_params=pltpu.CompilerParams(vmem_limit_bytes=VMEM),
            cost_estimate=cost(15),
        )(numbers, qkv)

    def body(*refs):
        global_backward_kernel(*refs[:3], *refs[3 + len(deps) :])

    return pl.pallas_call(
        body,
        grid=(count // BLOCK,),
        in_specs=specs + [blocks] + [ANY] * len(deps),
        out_specs=pl.BlockSpec((count, 3 * PAIR), lambda i: (0, 0)),
        out_shape=jax.ShapeDtypeStruct((count, 3 * PAIR), bf16),
        scratch_shapes=[pltpu.VMEM((count, PAIR), f32), pltpu.VMEM((count, PAIR), f32)],
        compiler_params=pltpu.CompilerParams(vmem_limit_bytes=VMEM),
        cost_estimate=cost(30),
    )(numbers, qkv, grads, *deps)


def call(kernel, args, specs, out_shape, out_specs, scratch=(), deps=(), micros=1):
    count = len(args)

    def body(*refs):
        kernel(*refs[:count], *refs[count + len(deps) :])

    return pl.pallas_call(
        body,
        in_specs=list(specs) + [ANY] * len(deps),
        out_specs=out_specs,
        out_shape=out_shape,
        scratch_shapes=list(scratch),
        compiler_params=pltpu.CompilerParams(vmem_limit_bytes=VMEM),
        cost_estimate=cost(micros),
    )(*args, *deps)


def shaped(*shape, kind=bf16):
    return jax.ShapeDtypeStruct(shape, kind)


def patch_forward(numbers, patch_rows, byte_rows, own_table, new_table, pieces, deps=()):
    batches, width = byte_rows[0].shape[0], own_table.shape[1]
    segments = len(byte_rows) * batches
    rows = segments * patch_rows
    shard = pieces[0].shape[0]
    span, count = len(pieces), len(byte_rows)
    room = (segments + 15) // 16 * 16

    def kernel(numbers_ref, own_ref, new_ref, *rest):
        byte_refs, piece_refs, rest = rest[:count], rest[count : count + span], rest[count + span :]
        embedded_ref, weight_ref, share_ref, low_ref, onehot_ref, table_ref = rest
        member_now = numbers_ref[1]
        for k in range(span):
            start = pl.multiple_of((member_now ^ k) * shard, shard)
            weight_ref[pl.ds(start, shard), :] = piece_refs[k][...]

        @pl.when(numbers_ref[0] == 0)
        def _():
            table_ref[...] = own_ref[...]

        @pl.when(numbers_ref[0] != 0)
        def _():
            table_ref[...] = new_ref[...]

        some = [ref[...].astype(f32) for ref in byte_refs]
        some.append(jnp.zeros((room - segments, some[0].shape[1]), f32))
        some = jnp.concatenate(some, axis=0).astype(bf16)
        shape = (some.shape[1], rows)
        place = lax.broadcasted_iota(jnp.int32, shape, 1) % patch_rows * PATCH + numbers_ref[2]
        picked = lax.broadcasted_iota(jnp.int32, shape, 0) == place
        wide = product(some, jnp.where(picked, 1.0, 0.0).astype(bf16))
        segment = lax.broadcasted_iota(jnp.int32, (room, rows), 1) // patch_rows
        here = lax.broadcasted_iota(jnp.int32, (room, rows), 0) == segment
        ids = jnp.sum(jnp.where(here, wide, 0.0), axis=0, keepdims=True).astype(jnp.int32)
        vocabulary = lax.broadcasted_iota(jnp.int32, (VOCAB, rows), 0)
        onehot = jnp.where(ids == vocabulary, 1.0, 0.0).astype(bf16)
        onehot_ref[...] = onehot
        embedded_ref[...] = transposed_product(onehot, table_ref[...]).astype(bf16)
        share = product(embedded_ref[...], weight_ref[...])
        share_ref[...] = share
        low_ref[...] = share.astype(bf16)

    return call(
        kernel,
        (numbers, own_table, new_table, *byte_rows, *pieces),
        [SCALARS] + [WHOLE] * (2 + count + span),
        [
            shaped(rows, width),
            shaped(span * shard, width),
            shaped(rows, width, kind=f32),
            shaped(rows, width),
            shaped(VOCAB, rows),
        ],
        [WHOLE] * 5,
        [pltpu.VMEM(own_table.shape, bf16)],
        deps=deps,
        micros=4,
    )


def split_heads(values, targets, batches, part):
    patch_rows = values.shape[0] // batches
    first = targets[0].shape[0]
    for t in range(batches * PAIRS):
        m, pair = t // PAIRS, t % PAIRS
        target = targets[0].at[t] if t < first else targets[1].at[t - first]
        target[:, part * PAIR : (part + 1) * PAIR] = values[
            m * patch_rows : (m + 1) * patch_rows, pair * PAIR : (pair + 1) * PAIR
        ]


def task_shapes(batches, first, patch_rows, columns):
    rest = batches * PAIRS - first
    return [shaped(first, patch_rows, columns)] + ([shaped(rest, patch_rows, columns)] if rest else [])


def merge_heads(blocks, target, batches, parts):
    patch_rows = target.shape[0] // batches
    width = PAIRS * PAIR
    for t in range(batches * PAIRS):
        m, pair = t // PAIRS, t % PAIRS
        first = blocks[0].shape[0]
        block = blocks[0].at[t] if t < first else blocks[1].at[t - first]
        for part in range(parts):
            at = part * width + pair * PAIR
            target[m * patch_rows : (m + 1) * patch_rows, at : at + PAIR] = block[
                :, part * PAIR : (part + 1) * PAIR
            ]


def strided(values, target, span, offset):
    size = values.shape[1] // (4 * span)
    for k in range(span):
        parts = [
            values[:, (group * span + k) * size : (group * span + k + 1) * size]
            for group in range(4)
        ]
        target[k, :, offset : offset + 4 * size] = jnp.concatenate(parts, axis=1)


def global_start(batches, first_tasks, own, others, gains, biases, heads_in):
    rows, width = own.shape
    patch_rows = rows // batches
    tasks = task_shapes(batches, first_tasks, patch_rows, 3 * PAIR)

    def kernel(own_ref, gains_ref, biases_ref, weight_hbm, *rest):
        other_refs, rest = rest[: len(others)], rest[len(others) :]
        (stream_ref, normed_ref, share_ref), task_refs = rest[:3], rest[3 : 3 + len(tasks)]
        weight, sem = rest[3 + len(tasks) :]
        load = pltpu.make_async_copy(weight_hbm, weight, sem)
        load.start()
        stream = own_ref[...]
        for ref in other_refs:
            stream = stream + ref[...].astype(f32)
        stream_ref[...] = stream
        normed = layer_norm(stream, gains_ref[0:1], biases_ref[0:1]).astype(bf16)
        normed_ref[...] = normed
        strided(normed, share_ref, SPAN, 0)
        load.wait()
        for part in range(3):
            mixed = product(normed, weight[:, part * width : (part + 1) * width]).astype(bf16)
            split_heads(mixed, task_refs, batches, part)

    return call(
        kernel,
        (own, gains, biases, heads_in, *others),
        [WHOLE] * 3 + [ANY] + [WHOLE] * len(others),
        [
            shaped(rows, width, kind=f32),
            shaped(rows, width),
            shaped(SPAN, rows, width // SPAN),
            *tasks,
        ],
        [WHOLE] * (3 + len(tasks)),
        [pltpu.VMEM(heads_in.shape, bf16), pltpu.SemaphoreType.DMA],
        micros=5,
    )


def global_feed_forward(batches, blocks, stream, gains, biases, heads_out, expand, contract):
    rows, width = stream.shape
    hidden_width = expand.shape[1]
    n = len(blocks)
    patch_rows = rows // batches
    half = patch_rows // 2

    def kernel(stream_ref, gains_ref, biases_ref, out_hbm, expand_hbm, contract_hbm, *rest):
        block_refs, rest = rest[:n], rest[n:]
        (attended_ref, middle_ref, normed_two_ref, slope_ref, hidden_ref, sent_ref) = rest[:6]
        share_ref, other_share_ref, edge_ref, near_ref, w_out, w_expand, w_contract, sems = rest[6:]
        loads = [
            pltpu.make_async_copy(out_hbm, w_out, sems.at[0]),
            pltpu.make_async_copy(expand_hbm, w_expand, sems.at[1]),
            pltpu.make_async_copy(contract_hbm, w_contract, sems.at[2]),
        ]
        for load in loads:
            load.start()
        merge_heads(block_refs, attended_ref, batches, 1)
        loads[0].wait()
        middle = stream_ref[...] + product(attended_ref[...], w_out[...])
        middle_ref[...] = middle
        normed_two_ref[...] = layer_norm(middle, gains_ref[1:2], biases_ref[1:2]).astype(bf16)
        loads[1].wait()

        @pl.loop(0, hidden_width // width, unroll=True)
        def _(i):
            at = pl.ds(pl.multiple_of(i * width, 128), width)
            hidden, slope = gelu_and_slope(product(normed_two_ref[...], w_expand[:, at]))
            hidden_ref[:, at] = hidden.astype(bf16)
            slope_ref[:, at] = slope.astype(bf16)

        loads[2].wait()
        result = middle_ref[...] + product(hidden_ref[...], w_contract[...])
        sent = result.astype(bf16)
        sent_ref[...] = sent
        edge_ref[...] = jnp.zeros(edge_ref.shape, bf16)
        for m in range(batches):
            stop = (m + 1) * patch_rows
            edge_ref[m : m + 1, :] = sent[stop - 1 : stop]
            near_ref[m * half : (m + 1) * half, :] = sent[stop - half - 1 : stop - 1]
        strided(hidden_ref[...], share_ref, SPAN, 0)
        strided(normed_two_ref[...], other_share_ref, SPAN, 0)
        strided(attended_ref[...], other_share_ref, SPAN, width // SPAN)

    return call(
        kernel,
        (stream, gains, biases, heads_out, expand, contract, *blocks),
        [WHOLE] * 3 + [ANY] * 3 + [WHOLE] * n,
        [
            shaped(rows, width),
            shaped(rows, width, kind=f32),
            shaped(rows, width),
            shaped(rows, hidden_width),
            shaped(rows, hidden_width),
            shaped(rows, width),
            shaped(SPAN, rows, hidden_width // SPAN),
            shaped(SPAN, rows, 2 * width // SPAN),
            shaped(SMALL_ROWS, width),
            shaped(batches * half, width),
        ],
        [WHOLE] * 10,
        [
            pltpu.VMEM(heads_out.shape, bf16),
            pltpu.VMEM(expand.shape, bf16),
            pltpu.VMEM(contract.shape, bf16),
            pltpu.SemaphoreType.DMA((3,)),
        ],
        micros=8,
    )


def global_feed_backward(
    batches, first_tasks, own, near, edge, middle, slope, gains, heads_out, expand, contract, deps=()
):
    rows, width = middle.shape
    hidden_width = expand.shape[1]
    patch_rows = rows // batches
    half = patch_rows // 2
    tasks = task_shapes(batches, first_tasks, patch_rows, PAIR)

    def kernel(
        own_ref, near_ref, edge_ref, middle_ref, slope_ref, gains_ref, out_hbm, expand_hbm,
        contract_hbm, upward_ref, grad_middle_ref, branch_ref, small_ref, grad_ref, *rest,
    ):
        task_refs, (w_out, w_expand, w_contract, sems) = rest[: len(tasks)], rest[len(tasks) :]
        loads = [
            pltpu.make_async_copy(contract_hbm, w_contract, sems.at[2]),
            pltpu.make_async_copy(expand_hbm, w_expand, sems.at[1]),
            pltpu.make_async_copy(out_hbm, w_out, sems.at[0]),
        ]
        for load in loads:
            load.start()
        source = jnp.concatenate([own_ref[...], near_ref[...], edge_ref[...]], axis=0)
        index = lax.broadcasted_iota(jnp.int32, (rows, 1), 0)
        batch, place = index // patch_rows, index % patch_rows
        chosen = jnp.where(
            place < half - 1,
            batch * half + place + 1,
            jnp.where(
                place < patch_rows - 1,
                batches * half + batch * half + place - (half - 1),
                2 * batches * half + batch,
            ),
        )
        columns = lax.broadcasted_iota(jnp.int32, (rows, source.shape[0]), 1)
        picked = jnp.where(columns == chosen, 1.0, 0.0).astype(bf16)
        grad_ref[...] = product(picked, source).astype(bf16)
        loads[0].wait()

        @pl.loop(0, hidden_width // width, unroll=True)
        def _(i):
            at = pl.ds(pl.multiple_of(i * width, 128), width)
            grad_hidden = product_transposed(grad_ref[...], w_contract[at, :])
            upward_ref[:, at] = (grad_hidden * slope_ref[:, at].astype(f32)).astype(bf16)

        loads[1].wait()
        grad_normed = product_transposed(upward_ref[...], w_expand[...])
        back, gain, bias = layer_norm_back(middle_ref[...], gains_ref[1:2], grad_normed)
        grad_middle = back + grad_ref[...].astype(f32)
        grad_middle_ref[...] = grad_middle
        branch = grad_middle.astype(bf16)
        branch_ref[...] = branch
        small_ref[...] = jnp.concatenate([gain, bias], axis=0)
        loads[2].wait()
        attended = product_transposed(branch, w_out[...]).astype(bf16)
        split_heads(attended, task_refs, batches, 0)

    return call(
        kernel,
        (own, near, edge, middle, slope, gains, heads_out, expand, contract),
        [WHOLE] * 6 + [ANY] * 3,
        [
            shaped(rows, hidden_width),
            shaped(rows, width, kind=f32),
            shaped(rows, width),
            shaped(2, width, kind=f32),
            shaped(rows, width),
            *tasks,
        ],
        [WHOLE] * (5 + len(tasks)),
        [
            pltpu.VMEM(heads_out.shape, bf16),
            pltpu.VMEM(expand.shape, bf16),
            pltpu.VMEM(contract.shape, bf16),
            pltpu.SemaphoreType.DMA((3,)),
        ],
        deps=deps,
        micros=10,
    )


def global_end(batches, blocks, stream, grad_middle, small, gains, heads_in, deps=()):
    rows, width = stream.shape
    n = len(blocks)

    def kernel(stream_ref, grad_middle_ref, small_ref, gains_ref, weight_hbm, *rest):
        block_refs, (mixed_ref, low_ref, all_small_ref, weight, sem) = rest[:n], rest[n:]
        load = pltpu.make_async_copy(weight_hbm, weight, sem)
        load.start()
        merge_heads(block_refs, mixed_ref, batches, 3)
        load.wait()
        grad_normed = product_transposed(mixed_ref[...], weight[...])
        back, gain, bias = layer_norm_back(stream_ref[...], gains_ref[0:1], grad_normed)
        low_ref[0:rows, :] = (back + grad_middle_ref[...]).astype(bf16)
        smalls = jnp.concatenate([gain, small_ref[0:1], bias, small_ref[1:2]], axis=0)
        all_small_ref[...] = smalls
        rest = jnp.zeros((SMALL_ROWS - 4, width), f32)
        low_ref[rows:, :] = jnp.concatenate([smalls, rest], axis=0).astype(bf16)

    return call(
        kernel,
        (stream, grad_middle, small, gains, heads_in, *blocks),
        [WHOLE] * 4 + [ANY] + [WHOLE] * n,
        [
            shaped(rows, 3 * width),
            shaped(rows + SMALL_ROWS, width),
            shaped(4, width, kind=f32),
        ],
        [WHOLE] * 3,
        [pltpu.VMEM(heads_in.shape, bf16), pltpu.SemaphoreType.DMA],
        deps=deps,
        micros=6,
    )


def patch_backward(section, onehot, embedded, weight, own, crossed, span, deps=()):
    rows, width = embedded.shape
    block = own[0].shape[0]
    n = len(own)
    used = rows // n
    shard = weight.shape[0] // span

    def kernel(section_ref, onehot_ref, embedded_ref, weight_ref, crossed_ref, *rest):
        own_refs, (patch_ref, table_ref, gathered, small) = rest[:n], rest[n:]

        @pl.when(section_ref[0] == 0)
        def _():
            for k in range(n):
                gathered[k * used : (k + 1) * used, :] = own_refs[k][0:used, :]
            total = sum(ref[used:, :].astype(f32) for ref in own_refs)
            small[...] = total.astype(bf16)

        @pl.when(section_ref[0] != 0)
        def _():
            for k in range(n):
                gathered[k * used : (k + 1) * used, :] = crossed_ref[k * block : k * block + used, :]
            small[...] = jnp.zeros_like(small)

        part = transposed_product(embedded_ref[...], gathered[...]).astype(bf16)
        for k in range(span):
            patch_ref[k, 0:shard, :] = part[k * shard : (k + 1) * shard]
            patch_ref[k, shard:, :] = small[...]
        grad_embedded = product_transposed(gathered[...], weight_ref[...]).astype(bf16)
        table_ref[...] = product(onehot_ref[...], grad_embedded).astype(bf16)

    return call(
        kernel,
        (section, onehot, embedded, weight, crossed, *own),
        [SCALARS] + [WHOLE] * (4 + n),
        [shaped(span, shard + SMALL_ROWS, width), shaped(VOCAB, width)],
        [WHOLE] * 2,
        [pltpu.VMEM((rows, width), bf16), pltpu.VMEM((SMALL_ROWS, width), bf16)],
        deps=deps,
        micros=6,
    )


def leave_by_group(group, buffer, targets, sems):
    for j in range(len(targets)):
        for k in range(len(targets)):

            @pl.when((group ^ j) == k)
            def _(j=j, k=k):
                pltpu.make_async_copy(buffer.at[j], targets[k], sems.at[k]).start()

    for k in range(len(targets)):
        pltpu.make_async_copy(buffer.at[0], targets[k], sems.at[k]).wait()


def pack_columns(hidden_width, width):
    deep, thin = hidden_width // SPAN, width // SPAN
    first = [
        (slice(0, deep), slice(deep, deep + width)),
        (slice(deep + width, deep + width + thin), slice(deep + width + thin, deep + 4 * width + thin)),
    ]
    right = 2 * thin
    second = [
        (slice(0, thin), slice(right, right + hidden_width)),
        (slice(thin, right), slice(right + hidden_width, right + hidden_width + width)),
    ]
    return first, second, max(first[-1][1].stop, second[-1][1].stop)


def pack_second(member, share, attend_branch, upward, whole, deps=()):
    rows, width = attend_branch.shape
    own, hidden_width = share.shape[2], upward.shape[1]

    def kernel(member_ref, share_ref, attend_ref, upward_ref, out_ref):
        for k in range(SPAN):
            out_ref[k, :, 0:own] = share_ref[member_ref[0] ^ k]
            out_ref[k, :, own : own + hidden_width] = upward_ref[...]
            out_ref[k, :, own + hidden_width : own + hidden_width + width] = attend_ref[...]

    return call(
        kernel,
        (member, share, attend_branch, upward),
        [SCALARS] + [WHOLE] * 3,
        shaped(SPAN, rows, whole),
        WHOLE,
        deps=deps,
        micros=3,
    )


def pack(section, member, share, normed_share, branch, mixed, second, passed, deps=()):
    rows, width = branch.shape
    deep, thin, whole = share.shape[2], normed_share.shape[2], second.shape[2]

    def kernel(
        section_ref, member_ref, share_ref, normed_ref, branch_ref, mixed_ref, passed_ref,
        second_ref, *rest,
    ):
        sent_refs, same_ref, sems = rest[:SPAN], rest[SPAN], rest[SPAN + 1]
        same_ref[...] = passed_ref[...]

        @pl.when(section_ref[0] == 0)
        def _():
            for k in range(SPAN):
                sent_refs[k][:, 0:deep] = share_ref[member_ref[0] ^ k]
                sent_refs[k][:, deep : deep + width] = branch_ref[...]
                sent_refs[k][:, deep + width : deep + width + thin] = normed_ref[member_ref[0] ^ k]
                sent_refs[k][:, deep + width + thin : deep + 4 * width + thin] = mixed_ref[...]

        @pl.when(section_ref[0] != 0)
        def _():
            copies = [
                pltpu.make_async_copy(second_ref.at[k], sent_refs[k], sems.at[k])
                for k in range(SPAN)
            ]
            for copy in copies:
                copy.start()
            for copy in copies:
                copy.wait()

    return call(
        kernel,
        (section, member, share, normed_share, branch, mixed, passed, second),
        [SCALARS] * 2 + [WHOLE] * 5 + [ANY],
        [shaped(rows, whole)] * SPAN + [shaped(*passed.shape)],
        [WHOLE] * (SPAN + 1),
        [pltpu.SemaphoreType.DMA((SPAN,))],
        deps=deps,
        micros=4,
    )


def plane_gradients(section, group, sent, hidden_width, width, deps=()):
    halves = pack_columns(hidden_width, width)[:2]
    rows_of = [
        sum(
            (left.stop - left.start) // 4 * ((right.stop - right.start) // width)
            for left, right in pairs
        )
        for pairs in halves
    ]
    block = max(rows_of)

    def kernel(section_ref, group_ref, *refs):
        sent_refs, (keep_ref, leave_ref, buffer, sems) = refs[: len(sent)], refs[len(sent) :]

        def columns(at):
            return jnp.concatenate([ref[:, at] for ref in sent_refs], axis=0)

        def fill(pairs):
            start = 0
            for left, right in pairs:
                former, size = columns(left), (left.stop - left.start) // 4
                for first in range(right.start, right.stop, width):
                    part = transposed_product(former, columns(slice(first, first + width)))
                    for j in range(4):
                        buffer[j, start : start + size, :] = part[
                            j * size : (j + 1) * size
                        ].astype(bf16)
                    start += size
            if start < block:
                for j in range(4):
                    buffer[j, start:block, :] = jnp.zeros((block - start, width), bf16)

        @pl.when(section_ref[0] == 0)
        def _():
            fill(halves[0])

        @pl.when(section_ref[0] != 0)
        def _():
            fill(halves[1])

        for j in range(4):
            mine = ((group_ref[0] ^ j) & 1) == 0

            @pl.when(mine)
            def _(j=j):
                pltpu.make_async_copy(buffer.at[j], keep_ref.at[j >> 1], sems.at[j]).start()

            @pl.when(jnp.logical_not(mine))
            def _(j=j):
                pltpu.make_async_copy(buffer.at[j], leave_ref.at[j >> 1], sems.at[j]).start()

        for j in range(4):
            pltpu.make_async_copy(buffer.at[j], keep_ref.at[j >> 1], sems.at[j]).wait()

    return call(
        kernel,
        (section, group, *sent),
        [SCALARS] * 2 + [WHOLE] * len(sent),
        [shaped(2, block, width)] * 2,
        [ANY] * 2,
        [pltpu.VMEM((4, block, width), bf16), pltpu.SemaphoreType.DMA((4,))],
        deps=deps,
        micros=6,
    )


def by_parity(parity, sums, deps=()):
    count, rows, width = sums.shape

    def kernel(parity_ref, sums_ref, *rest):
        rest[-1][...] = sums_ref[...]

    block = (1, rows, width)
    return pl.pallas_call(
        kernel,
        grid_spec=pltpu.PrefetchScalarGridSpec(
            num_scalar_prefetch=1,
            grid=(count // 2,),
            in_specs=[pl.BlockSpec(block, lambda i, ref: (2 * i + 1 - ref[0], 0, 0))]
            + [ANY] * len(deps),
            out_specs=pl.BlockSpec(block, lambda i, ref: (i, 0, 0)),
        ),
        out_shape=shaped(count // 2, rows, width),
        compiler_params=pltpu.CompilerParams(vmem_limit_bytes=VMEM),
        cost_estimate=cost(3),
    )(parity, sums, *deps)


def half_sums(flags, kept, near, deps=()):
    shape = kept.shape[1:]
    every = kept.shape[0] == 4

    def kernel(flags_ref, kept_ref, near_ref, far_ref, mine_ref):
        for k in range(2):
            own = kept_ref[2 * k + flags_ref[2]] if every else kept_ref[k]
            total = (own.astype(f32) + near_ref[k].astype(f32)).astype(bf16)

            @pl.when(flags_ref[1] == k)
            def _():
                mine_ref[...] = total

            @pl.when(flags_ref[1] != k)
            def _():
                far_ref[...] = total

    return call(
        kernel,
        (flags, kept, near),
        [SCALARS, WHOLE, WHOLE],
        [shaped(*shape)] * 2,
        [WHOLE] * 2,
        deps=deps,
        micros=2,
    )


def half_sums_and_cross(flags, kept, near, other, other_far, deps=()):
    shape = kept.shape[1:]
    held = other.shape[0]

    def kernel(flags_ref, kept_ref, near_ref, other_ref, more_ref, far_ref, mine_ref, cross_ref):
        for k in range(2):
            total = (kept_ref[k].astype(f32) + near_ref[k].astype(f32)).astype(bf16)

            @pl.when(flags_ref[1] == k)
            def _():
                mine_ref[...] = total
                cross_ref[...] = total

            @pl.when(flags_ref[1] != k)
            def _():
                far_ref[...] = total

        @pl.when(flags_ref[0] == 0)
        def _():
            total = other_ref[...].astype(f32) + more_ref[...].astype(f32)
            cross_ref[0:held, :] = total.astype(bf16)

    return call(
        kernel,
        (flags, kept, near, other, other_far),
        [SCALARS] + [WHOLE] * 4,
        [shaped(*shape)] * 3,
        [WHOLE] * 3,
        deps=deps,
        micros=2,
    )


def finish(section, deep, shard, room, own_global, own_local, crossed, fars, table_parts, patch_parts):
    width = own_local.shape[1]
    chunks = deep // shard
    p = len(patch_parts)

    def kernel(section_ref, global_ref, local_ref, crossed_ref, table_ref, *refs):
        (global_one, global_two, local_two), refs = refs[:3], refs[3:]
        patch_refs = refs[:p]
        contract, expand, ins, out, table, small, patch = refs[p:]

        def total(some, start, size):
            return sum(ref[start : start + size, :].astype(f32) for ref in some)

        total_patch = sum(ref[...].astype(f32) for ref in patch_refs)
        patch[...] = total_patch[: patch.shape[0]]

        @pl.when(section_ref[0] == 0)
        def _():
            one, two = (global_ref, global_one), (crossed_ref, global_two)
            contract[...] = total(one, 0, deep)
            for c in range(3):
                ins[:, c * width : (c + 1) * width] = total(one, deep + c * shard, shard)
            for c in range(chunks):
                expand[:, c * width : (c + 1) * width] = total(two, c * shard, shard)
            out[...] = total(two, chunks * shard, shard)
            small[...] = total_patch[patch.shape[0] :]
            sums = jnp.zeros((room, width), f32)
            for k in range(table_ref.shape[0]):
                sums = sums + table_ref[k].astype(f32)
            table[...] = sums

        @pl.when(section_ref[0] != 0)
        def _():
            one, two = (crossed_ref,), (local_ref, local_two)
            contract[...] = total(one, 0, deep)
            out[...] = total(one, deep, shard)
            ins[:, 0:width] = total(one, deep + shard, shard)
            table[...] = total(one, deep + 2 * shard, room)
            for c in range(chunks):
                expand[:, c * width : (c + 1) * width] = total(two, c * shard, shard)
            for c in range(2):
                ins[:, (c + 1) * width : (c + 2) * width] = total(two, deep + c * shard, shard)
            small[...] = total(two, deep + 2 * shard, small.shape[0])

    return call(
        kernel,
        (section, own_global, own_local, crossed, table_parts, *fars, *patch_parts),
        [SCALARS] + [WHOLE] * (7 + p),
        [
            shaped(deep, width, kind=f32),
            shaped(shard, chunks * width, kind=f32),
            shaped(shard, 3 * width, kind=f32),
            shaped(shard, width, kind=f32),
            shaped(room, width, kind=f32),
            shaped(SMALL_ROWS, width, kind=f32),
            shaped(patch_parts[0].shape[0] - SMALL_ROWS, width, kind=f32),
        ],
        [WHOLE] * 7,
        micros=4,
    )


def activation_rows(numbers, sent, other, own, deps=()):
    batches, half, width = own.shape
    patch_rows = sent.shape[0] // batches
    byte_rows = patch_rows * PATCH

    def kernel(numbers_ref, sent_ref, other_ref, own_ref, out_ref):
        @pl.when(numbers_ref[0] == 0)
        def _():
            rows = lax.broadcasted_iota(jnp.int32, (byte_rows, 1), 0)
            columns = lax.broadcasted_iota(jnp.int32, (byte_rows, patch_rows), 1)
            for m in range(batches):
                live = is_live(numbers_ref[1] + rows, item_spans(numbers_ref, 3, m))
                chosen = jnp.where(live, rows // PATCH, -1)
                spread = jnp.where(columns == chosen, 1.0, 0.0).astype(bf16)
                part = sent_ref[m * patch_rows : (m + 1) * patch_rows, :]
                out_ref[m] = product(spread, part).astype(bf16)

        @pl.when(numbers_ref[0] != 0)
        def _():
            for m in range(batches):
                out_ref[m, 0:half, :] = other_ref[m]
                out_ref[m, half:, :] = own_ref[m]

    return call(
        kernel,
        (numbers, sent, other, own),
        [SCALARS] + [WHOLE] * 3,
        shaped(batches, byte_rows, width),
        WHOLE,
        deps=deps,
        micros=2,
    )


SEQ = ("group", "member")


def section_send(x, origin, target, pairs):
    count = lax.axis_size(SEQ)
    joint = [(origin * count + i, target * count + j) for i, j in pairs]
    return lax.ppermute(x, ("section",) + SEQ, joint)


def section_swap(x):
    return lax.ppermute(x, "section", [(0, 1), (1, 0)])


def by_slot(buffer, count, pieces):
    split = count // GROUPS
    parts, start = [], 0
    for size, shared in pieces:
        part = buffer[:, start : start + size]
        start += size
        kept = shared or size // split
        if shared:
            part = jnp.broadcast_to(part[:, None, :shared], (GROUPS, split, shared, part.shape[2]))
        parts.append(part.reshape(count, kept, part.shape[-1]))
    whole = jnp.concatenate(parts, axis=1)
    turned = whole.reshape((4, count // 4) + whole.shape[1:])
    return jnp.swapaxes(turned, 0, 1).reshape(whole.shape)


def place_sum(shares):
    shares = lax.psum_scatter(shares, "member", scatter_dimension=0, tiled=True)
    return lax.psum_scatter(shares, "group", scatter_dimension=0, tiled=True)[0]


def on_device(
    byte_values,
    item_lengths,
    embed_tables,
    patch_weight,
    norm_gains,
    norm_biases,
    heads_in,
    heads_out,
    expand_weight,
    contract_weight,
    out_grad,
):
    place = lax.axis_index(SEQ)
    count = lax.axis_size(SEQ)
    section = lax.axis_index("section")
    is_global = section == 0
    batches, byte_rows = byte_values.shape
    patch_rows = byte_rows // PATCH
    width = heads_out.shape[2]
    rows = batches * patch_rows
    total_patches = patch_rows * count
    gains, biases = norm_gains[0], norm_biases[0]
    heads_in, heads_out = heads_in[0], heads_out[0]
    expand, contract = expand_weight[0], contract_weight[0]
    own_table = embed_tables[0]
    straight = [(i, i) for i in range(count)]

    quarters = PATCH // 2
    span = count // quarters
    group, member = place // span, place % span
    shard_rows = patch_weight.shape[0]
    pieces = [patch_weight]
    for k in range(1, span):
        pieces.append(lax.ppermute(patch_weight, SEQ, [(i, i ^ k) for i in range(count)]))
    other_table = section_swap(own_table)
    theirs = [byte_values]
    for k in range(1, quarters):
        theirs.append(
            lax.ppermute(byte_values, SEQ, [(i, i ^ (k * span)) for i in range(count)])
        )
    place_numbers = jnp.stack([section, member, section * quarters + group]).astype(jnp.int32)
    embedded, byte_weight, shares, low_shares, byte_onehot = patch_forward(
        place_numbers, patch_rows, theirs, own_table, other_table, pieces
    )
    shares = shares + section_send(low_shares, 1, 0, straight).astype(f32)
    shares = shares.reshape(quarters, rows, width)
    parts = []
    for k in range(1, quarters):
        pairs = [(i, i ^ (k * span)) for i in range(count)]
        parts.append(section_send(shares[k].astype(bf16), 0, 0, pairs))

    arrived = [section_send(w, 1, 0, straight) for w in (heads_in, heads_out, expand, contract)]
    own_norms = jnp.concatenate([gains, biases])
    other_norms = section_swap(own_norms)

    tasks = batches * PAIRS
    first_tasks = min(tasks, count)
    spare_tasks = tasks - first_tasks

    def to_tasks(first, spare=None):
        columns = first.shape[2]
        slots = jnp.pad(first, ((0, count - first_tasks), (0, 0), (0, 0)))
        if spare_tasks:
            spare = section_send(spare, 0, 1, straight)
            spare = jnp.pad(spare, ((0, count - spare_tasks), (0, 0), (0, 0)))
            slots = jnp.where(is_global, slots, spare)
        landed = lax.all_to_all(slots, SEQ, 0, 0)
        return landed.reshape(total_patches, columns)

    def from_tasks(results):
        columns = results.shape[1]
        slots = lax.all_to_all(results.reshape(count, patch_rows, columns), SEQ, 0, 0)
        if spare_tasks:
            return [slots, section_send(slots[:spare_tasks], 1, 0, straight)]
        return [slots]

    task = jnp.minimum(jnp.where(is_global, place, first_tasks + place), tasks - 1)
    lengths = item_lengths.reshape(-1)
    task_numbers = jnp.concatenate([(task // PAIRS).reshape(1).astype(jnp.int32), lengths])

    stream, normed, normed_share, *tasks_out = global_start(
        batches, first_tasks, shares[0], parts, gains, biases, heads_in
    )
    qkv = to_tasks(*tasks_out)
    attended, middle, normed_two, slope, hidden, sent, feed_share, other_share, edge, near = global_feed_forward(
        batches,
        from_tasks(global_attention(qkv, task_numbers)),
        stream,
        gains,
        biases,
        heads_out,
        expand,
        contract,
    )
    half = patch_rows // 2
    half_bytes = half * PATCH
    chunks = half_bytes // BLOCK
    onward = [(i, i + 1) for i in range(count - 1)]
    backward = [(i + 1, i) for i in range(count - 1)]
    near = section_send(near, 0, 1, straight)
    edge = section_send(edge, 0, 0, onward)
    weights = (heads_in, heads_out, expand, contract)
    flag = section.reshape(1).astype(jnp.int32)
    block_patches = BLOCK // PATCH
    local_outs, activations_of, grads_shifted, grads_edge = [], [], [], []
    for c in range(chunks):
        numbers = jnp.concatenate(
            [
                jnp.stack([section, place * byte_rows, jnp.int32(c)]).astype(jnp.int32),
                lengths,
            ]
        )
        act, grad_shifted, grad_edge, keep, send = local_block(
            numbers,
            byte_values,
            (own_table, other_table),
            sent,
            edge,
            near,
            (own_norms, other_norms),
            out_grad,
            patch_rows,
            weights,
            arrived,
        )
        local_outs.append(act.reshape(batches, BLOCK, width))
        grads_shifted.append(grad_shifted.reshape(batches, block_patches, width))
        grads_edge.append(grad_edge)
        activations_of.append((numbers, keep, section_swap(send)))
    local_out = jnp.concatenate(local_outs, axis=1)
    grad_shifted = jnp.concatenate(grads_shifted, axis=1).reshape(batches * half, width)

    other_out = section_send(local_out, 0, 1, straight)
    activations = activation_rows(numbers, sent, other_out, local_out)

    shard = width // count
    room = VOCAB // count
    group_shard, group_room = width // GROUPS, VOCAB // GROUPS
    small_rows = max(4, room)
    pieces = {
        False: [(contract.shape[0] // GROUPS, 0), (group_shard, 0), (group_shard, 0), (group_room, 0)],
        True: [(group_shard, 0)] * (expand.shape[1] // width + 2) + [(group_room, small_rows)],
    }

    def ordered(buffer):
        if count == GROUPS:
            return buffer
        upper, lower = by_slot(buffer, count, pieces[False]), by_slot(buffer, count, pieces[True])
        rows_of = max(upper.shape[1], lower.shape[1])
        upper, lower = (
            jnp.pad(x, ((0, 0), (0, rows_of - x.shape[1]), (0, 0))) for x in (upper, lower)
        )
        return jnp.where(is_global, upper, lower)

    near_back = section_send(grad_shifted, 1, 0, straight)
    edge_back = section_send(grads_edge[0], 0, 0, backward)
    in_plane = span == SPAN and count == GROUPS
    member_flag = (member % SPAN).reshape(1).astype(jnp.int32)
    group_flag = group.reshape(1).astype(jnp.int32)

    def plane_send(blocks):
        return [blocks[0]] + [
            both_send(blocks[k], [(i, i ^ k) for i in range(count)]) for k in range(1, SPAN)
        ]

    upper = (group >> 1) & 1
    half_flags = jnp.stack([section, upper, group & 1]).astype(jnp.int32)

    def group_pairs(step):
        return [(i, i ^ (step * span)) for i in range(count)]

    def both_send(x, pairs):
        joint = [(s * count + i, s * count + j) for s in range(2) for i, j in pairs]
        return lax.ppermute(x, ("section",) + SEQ, joint)

    half_locals = [
        ordered(
            local_gradients(
                count,
                numbers,
                byte_values,
                keep,
                crossed,
                contract.shape[0],
                width,
                half_bytes,
                [near_back, edge_back],
            )
        )
        for numbers, keep, crossed in activations_of
    ]
    if chunks > 1:
        half_locals = [sum(x.astype(f32) for x in half_locals).astype(bf16)]
    half_locals = half_locals[0]
    grad_upward, grad_middle, attend_branch, small, grad_sent, *task_grads = global_feed_backward(
        batches,
        first_tasks,
        grad_shifted,
        near_back,
        edge_back,
        middle,
        slope,
        gains,
        heads_out,
        expand,
        contract,
        [half_locals],
    )
    if in_plane:
        whole = pack_columns(contract.shape[0], width)[2]
        second_parts = section_send(
            pack_second(member_flag, other_share, attend_branch, grad_upward, whole), 0, 1, straight
        )
    task_grads = to_tasks(*task_grads)
    task_mixed = global_attention(qkv, task_numbers, task_grads)
    grad_mixed, own_rows, small = global_end(
        batches,
        from_tasks(task_mixed),
        stream,
        grad_middle,
        small,
        gains,
        heads_in,
    )

    if in_plane:
        *sent_parts, own_rows = pack(
            flag, member_flag, feed_share, normed_share, grad_sent, grad_mixed, second_parts, own_rows
        )
        arrived_parts = plane_send(sent_parts)

    gathered = [own_rows]
    for k in range(1, quarters):
        pairs = [(i, i ^ (k * span)) for i in range(count)]
        gathered.append(section_send(own_rows, 0, 0, pairs))
    crossed = section_send(jnp.concatenate(gathered), 0, 1, straight)
    patch_share, table_share = patch_backward(
        flag,
        byte_onehot,
        embedded,
        byte_weight,
        gathered,
        crossed,
        span,
        arrived_parts[1:] if in_plane else (),
    )
    if in_plane:
        in_planes = lax.psum_scatter(half_locals, "member", scatter_dimension=0, tiled=True)
        parity_flag = (group & 1).reshape(1).astype(jnp.int32)
        local_leaving = by_parity(parity_flag, in_planes, [crossed])
        local_near = both_send(local_leaving, group_pairs(1))
    else:
        own_local = place_sum(half_locals)
    patch_parts = [lax.dynamic_index_in_dim(patch_share, member, 0, keepdims=False)]
    for k in range(1, span):
        leaving = lax.dynamic_index_in_dim(patch_share, member ^ k, 0, keepdims=False)
        patch_parts.append(lax.ppermute(leaving, SEQ, [(i, i ^ k) for i in range(count)]))
    table_share = table_share + section_send(table_share, 1, 0, straight)
    table_parts = lax.all_to_all(table_share.reshape(count, VOCAB // count, width), SEQ, 0, 0)

    def ordered_rows(first, second):
        feed_rows = contract.shape[0] // count
        expand_sum = [second[k * shard : (k + 1) * shard] for k in range(feed_rows // shard)]
        rest, others = first[feed_rows:], second[feed_rows:]
        ins = [rest[shard : 2 * shard], others[:shard], others[shard : 2 * shard]]
        return (
            first[:feed_rows],
            jnp.concatenate(expand_sum, axis=1),
            jnp.concatenate(ins, axis=1),
            rest[:shard],
            rest[2 * shard : 2 * shard + room],
            others[2 * shard : 2 * shard + 4],
        )

    if in_plane:
        local_far, local_mine = half_sums(half_flags, in_planes, local_near)
        across = group_pairs(2)
        local_far = both_send(local_far, across)
        kept, leaving = plane_gradients(
            flag,
            group_flag,
            arrived_parts,
            contract.shape[0],
            width,
            [patch_share, local_far],
        )
        near = both_send(leaving, group_pairs(1))
        far, mine, crossed = half_sums_and_cross(
            half_flags, kept, near, local_mine, local_far, patch_parts[1:]
        )
        crossed = section_swap(crossed)
        fars = [
            section_send(far, 0, 0, across),
            section_send(far, 1, 0, across),
            local_far,
        ]
        contract_grad, expand_grad, in_grad, out_grads, table_grad, small, patch_grads = finish(
            flag,
            contract.shape[0] // count,
            shard,
            room,
            mine,
            local_mine,
            crossed,
            fars,
            table_parts,
            patch_parts,
        )
        small = small[:4]
    else:
        upper, lower = global_sums_of(
            count, hidden, grad_sent, normed_two, grad_upward, normed, grad_mixed, attended,
            attend_branch, small,
        )
        own_global = ordered(jnp.where(is_global, upper, section_send(lower, 0, 1, straight)))
        own_global = place_sum(own_global)
        crossed = section_swap(jnp.where(is_global, own_local, own_global)).astype(f32)
        global_sums = ordered_rows(own_global.astype(f32), crossed)
        global_table = jnp.sum(table_parts.astype(f32), axis=0)
        global_sums = global_sums[:4] + (global_table, global_sums[5])
        local_sums = ordered_rows(crossed, own_local.astype(f32))
        contract_grad, expand_grad, in_grad, out_grads, table_grad, small = (
            jnp.where(is_global, upper, lower) for upper, lower in zip(global_sums, local_sums)
        )
        patch_grads = sum(x.astype(f32) for x in patch_parts)[:shard_rows]
    small = lax.dynamic_slice_in_dim(small, place * shard, shard, 1)
    return (
        activations[None],
        table_grad[None],
        patch_grads,
        small[None, 0:2],
        small[None, 2:4],
        in_grad[None],
        out_grads[None],
        expand_grad[None],
        contract_grad[None],
    )


def solution(mesh):
    devices = mesh.devices
    groups = PATCH // 2
    split = jax.sharding.Mesh(
        devices.reshape(devices.shape[0], groups, devices.shape[1] // groups), ("section",) + SEQ
    )
    both = ("section",) + SEQ
    placed = (
        P(None, SEQ),
        P(),
        P("section", None, None),
        P(both, None),
        P("section", None, None),
        P("section", None, None),
        P("section", None, None),
        P("section", None, None),
        P("section", None, None),
        P("section", None, None),
        P(None, SEQ, None),
    )
    return jax.shard_map(
        on_device,
        mesh=split,
        in_specs=placed,
        out_specs=(
            P("section", None, SEQ, None),
            P("section", SEQ, None),
            P(both, None),
            P("section", None, SEQ),
            P("section", None, SEQ),
            P("section", SEQ, None),
            P("section", SEQ, None),
            P("section", SEQ, None),
            P("section", SEQ, None),
        ),
        check_vma=False,
    )
```

```python
from functools import partial

import jax
import jax.numpy as jnp
from jax import lax
from jax.experimental import pallas as pl
from jax.experimental.pallas import tpu as pltpu
from jax.sharding import PartitionSpec as P

HEADS = 12
HEAD_SIZE = 64
VOCAB = 256
PATCH = 8
ITEMS = 4
PAIRS = HEADS // 2
PAIR = 2 * HEAD_SIZE
SCALE = HEAD_SIZE ** (-0.5)
EPSILON = 1e-05
MASKED = -1e30
BLOCK = 128
TILE = 384
GROUPS = 16
SPAN = 4
VMEM = 60 * 1024 * 1024

bf16 = jnp.bfloat16
f32 = jnp.float32


def cost(micros):
    return pl.CostEstimate(flops=int(micros * 1.1e9), bytes_accessed=1, transcendentals=0)


def product(former, latter):
    return jnp.dot(former, latter, preferred_element_type=f32)


def transposed_product(former, latter):
    return lax.dot_general(former, latter, (((0,), (0,)), ((), ())), preferred_element_type=f32)


def product_transposed(former, latter):
    return lax.dot_general(former, latter, (((1,), (1,)), ((), ())), preferred_element_type=f32)


def normalise(values):
    average = jnp.mean(values, axis=-1, keepdims=True)
    centered = values - average
    inverse_root = lax.rsqrt(jnp.mean(centered * centered, axis=-1, keepdims=True) + EPSILON)
    return centered * inverse_root, inverse_root


def layer_norm(values, gain, bias):
    return normalise(values)[0] * gain + bias


def layer_norm_back(values, gain, grad):
    unit, inverse_root = normalise(values)
    scaled = grad * gain
    grad_values = inverse_root * (
        scaled
        - jnp.mean(scaled, axis=-1, keepdims=True)
        - unit * jnp.mean(scaled * unit, axis=-1, keepdims=True)
    )
    return (
        grad_values,
        jnp.sum(grad * unit, axis=0, keepdims=True),
        jnp.sum(grad, axis=0, keepdims=True),
    )


def slot_of(q, count):
    if count != GROUPS:
        return q
    return (q % SPAN) * (GROUPS // SPAN) + q // SPAN


def store_rows(buffer, value, count, start, columns=slice(None)):
    rows = value.shape[0] // GROUPS
    for q in range(GROUPS):
        buffer[slot_of(q, count), pl.ds(start, rows), columns] = value[
            q * rows : (q + 1) * rows
        ].astype(bf16)


def patch_bias(live_row):
    rows = lax.broadcasted_iota(jnp.int32, (BLOCK, BLOCK), 0)
    columns = lax.broadcasted_iota(jnp.int32, (BLOCK, BLOCK), 1)
    same = (rows // PATCH) == (columns // PATCH)
    allowed = same & (columns <= rows) & ((live_row > 0) | (columns == rows))
    bias = jnp.where(allowed, 0.0, MASKED)
    return jnp.concatenate([bias, bias], axis=0)


def softmax_rows(scores):
    peak = jnp.max(scores, axis=-1, keepdims=True)
    exponents = jnp.exp(scores - peak)
    return exponents * (1.0 / jnp.sum(exponents, axis=-1, keepdims=True))


def lane_masks():
    lanes = lax.broadcasted_iota(jnp.int32, (1, PAIR), 1)
    low = jnp.where(lanes < HEAD_SIZE, 1.0, 0.0)
    return lanes < HEAD_SIZE, low.astype(bf16), (1.0 - low).astype(bf16)


def stacked(values, low, high, scale=1.0):
    return jnp.concatenate([values * (low * scale), values * (high * scale)], axis=0)


def unstacked(values, is_low):
    half = values.shape[0] // 2
    return jnp.where(is_low, values[:half], values[half:])


def pair_probabilities(queries, keys, bias, masks):
    _, low, high = masks
    return softmax_rows(product_transposed(stacked(queries, low, high, SCALE), keys) + bias)


def pair_forward(queries, keys, values, bias, masks):
    probabilities = pair_probabilities(queries, keys, bias, masks)
    return unstacked(product(probabilities.astype(bf16), values), masks[0])


def pair_backward(queries, keys, values, grads, probabilities, masks):
    is_low, low, high = masks
    both = stacked(queries, low, high, SCALE)
    both_grads = stacked(grads, low, high)
    prob_grads = product_transposed(both_grads, values)
    delta = jnp.sum(probabilities * prob_grads, axis=-1, keepdims=True)
    score_grads = (probabilities * (prob_grads - delta)).astype(bf16)
    return (
        unstacked(product(score_grads, keys), is_low) * SCALE,
        transposed_product(score_grads, both),
        transposed_product(probabilities.astype(bf16), both_grads),
    )


def gelu_and_slope(x):
    root = 0.7978845608028654
    cubic = 0.044715
    square = x * x
    bent = jnp.tanh(x * (root + (root * cubic) * square))
    half = 0.5 * (1.0 + bent)
    slope = half + (0.5 * x) * (1.0 - bent * bent) * (root + (3.0 * root * cubic) * square)
    return x * half, slope


def fetch(section, own, arrived, target, sem):
    @pl.when(section == 0)
    def _():
        pltpu.make_async_copy(arrived, target, sem).start()

    @pl.when(section != 0)
    def _():
        pltpu.make_async_copy(own, target, sem).start()


def section_columns(hidden_width, width):
    tables = []
    for names in (
        ("hidden", "branch", "attended", "attend_branch", "normed", "queries", "stream"),
        ("upward", "normed_two", "normed", "keys", "values"),
    ):
        table, start = {}, 0
        for name in names:
            size = hidden_width if start == 0 else width
            table[name] = slice(start, start + size)
            start += size
        tables.append((table, start))
    return tables


SMALL_ROWS = 16


def item_spans(numbers_ref, first, batch):
    spans, start = [], 0
    for k in range(ITEMS):
        length = numbers_ref[first + batch * ITEMS + k]
        stop = start + (length + PATCH - 1) // PATCH * PATCH
        spans.append((start, start + length, stop))
        start = stop
    return spans


def is_live(positions, spans):
    live = jnp.zeros(positions.shape, jnp.bool_)
    for start, live_end, _ in spans:
        live = live | ((positions >= start) & (positions < live_end))
    return live


def owner_of(positions, spans):
    owner = jnp.full(positions.shape, ITEMS, jnp.int32)
    for k, (start, _, stop) in enumerate(spans):
        owner = jnp.where((positions >= start) & (positions < stop), k, owner)
    return owner


def local_kernel(
    patch_rows,
    numbers_ref,
    ids_ref,
    own_table_ref,
    new_table_ref,
    sent_ref,
    edge_ref,
    near_ref,
    own_norms_ref,
    new_norms_ref,
    out_grad_hbm,
    own_in,
    own_out,
    own_expand,
    own_contract,
    new_in,
    new_out,
    new_expand,
    new_contract,
    act_ref,
    grad_shifted_ref,
    grad_edge_ref,
    keep_ref,
    send_ref,
    w_in,
    w_out,
    w_expand,
    w_contract,
    first,
    second,
    out_grad_ref,
    source_ref,
    stream_ref,
    mixed_ref,
    middle_ref,
    slope_ref,
    grad_middle_ref,
    grad_attended_ref,
    grad_stream_ref,
    probability_ref,
    table_ref,
    sems,
    out_sems,
):
    section, offset, chunk = numbers_ref[0], numbers_ref[1], numbers_ref[2]
    rows, width = act_ref.shape
    batches = rows // BLOCK
    hidden_width = w_expand.shape[1]
    half = patch_rows // 2
    block_patches = BLOCK // PATCH
    lane = pl.multiple_of(section * (half * PATCH) + chunk * BLOCK, BLOCK)
    base = offset + lane
    grads_in = [
        pltpu.make_async_copy(
            out_grad_hbm.at[m, pl.ds(lane, BLOCK)],
            out_grad_ref.at[m * BLOCK : (m + 1) * BLOCK],
            sems.at[4 + m],
        )
        for m in range(batches)
    ]
    fetch(section, own_in, new_in, w_in, sems.at[0])
    for copy in grads_in:
        copy.start()
    fetch(section, own_out, new_out, w_out, sems.at[1])
    fetch(section, own_expand, new_expand, w_expand, sems.at[2])
    fetch(section, own_contract, new_contract, w_contract, sems.at[3])
    (to_first, first_width), (to_second, second_width) = section_columns(hidden_width, width)
    body = slice(0, rows)
    norms = jnp.where(section == 0, new_norms_ref[...], own_norms_ref[...])
    gains, biases = norms[0:2], norms[2:4]

    @pl.when(section == 0)
    def _():
        table_ref[...] = new_table_ref[...]

    @pl.when(section != 0)
    def _():
        table_ref[...] = own_table_ref[...]

    out_count = [0]

    def leave(from_first, columns, at_rows=body):
        source = first if from_first else second
        sem = out_sems.at[out_count[0]]
        out_count[0] += 1
        part = source.at[at_rows, columns]

        @pl.when(section == (0 if from_first else 1))
        def _():
            pltpu.make_async_copy(part, keep_ref.at[at_rows, columns], sem).start()

        @pl.when(section != (0 if from_first else 1))
        def _():
            pltpu.make_async_copy(part, send_ref.at[at_rows, columns], sem).start()

        return pltpu.make_async_copy(part, keep_ref.at[at_rows, columns], sem)

    blocks = [slice(m * BLOCK, (m + 1) * BLOCK) for m in range(batches)]
    spans = [item_spans(numbers_ref, 3, m) for m in range(batches)]
    column = lax.broadcasted_iota(jnp.int32, (BLOCK, 1), 0)
    row = lax.broadcasted_iota(jnp.int32, (1, BLOCK), 1)
    live_columns = [is_live(base + column, span) for span in spans]
    biases_of = [
        patch_bias(jnp.where(is_live(base + row, span), 1, 0)) for span in spans
    ]
    sent_rows, edge_rows = sent_ref.shape[0], edge_ref.shape[0]
    source_ref[0:sent_rows, :] = sent_ref[...]
    source_ref[sent_rows : sent_rows + edge_rows, :] = edge_ref[...]
    source_ref[sent_rows + edge_rows :, :] = near_ref[...]

    for copy in grads_in:
        copy.wait()
    for m, at in enumerate(blocks):
        vocabulary = lax.broadcasted_iota(jnp.int32, (VOCAB, BLOCK), 0)
        ids = ids_ref[m : m + 1, pl.ds(lane, BLOCK)]
        onehot = jnp.where(ids == vocabulary, 1.0, 0.0).astype(bf16)
        patch = column // PATCH
        place = chunk * block_patches + patch
        start = base + patch * PATCH
        same = owner_of(start, spans[m]) == owner_of(start - PATCH, spans[m])
        inside = jnp.where(place == 0, sent_rows + m, m * patch_rows + place - 1)
        chosen = jnp.where(section == 0, inside, sent_rows + edge_rows + m * half + place)
        chosen = jnp.where(same, chosen, -1)
        columns = lax.broadcasted_iota(jnp.int32, (BLOCK, source_ref.shape[0]), 1)
        spread = jnp.where(columns == chosen, 1.0, 0.0).astype(bf16)
        stream = transposed_product(onehot, table_ref[...]) + product(spread, source_ref[...])
        stream_ref[at, :] = stream
        normed = layer_norm(stream, gains[0:1], biases[0:1]).astype(bf16)
        first[at, to_first["normed"]] = normed
        second[at, to_second["normed"]] = normed
        first[at, to_first["branch"]] = jnp.where(
            live_columns[m], out_grad_ref[at, :].astype(f32), 0.0
        ).astype(bf16)

    pltpu.make_async_copy(own_in, w_in, sems.at[0]).wait()
    for i in range(3 * width // TILE):
        at = slice(i * TILE, (i + 1) * TILE)
        mixed_ref[:, at] = product(first[body, to_first["normed"]], w_in[:, at]).astype(bf16)

    masks = lane_masks()

    def pair_columns(pair, start=0):
        return slice(start + pair * PAIR, start + (pair + 1) * PAIR)

    for m, at in enumerate(blocks):
        for pair in range(PAIRS):
            probabilities = pair_probabilities(
                mixed_ref[at, pair_columns(pair)],
                mixed_ref[at, pair_columns(pair, width)],
                biases_of[m],
                masks,
            )
            probability_ref[m * PAIRS + pair] = probabilities
            attended = product(
                probabilities.astype(bf16), mixed_ref[at, pair_columns(pair, 2 * width)]
            )
            first[at, pair_columns(pair, to_first["attended"].start)] = unstacked(
                attended, masks[0]
            ).astype(bf16)

    pltpu.make_async_copy(own_out, w_out, sems.at[1]).wait()
    for at in blocks:
        middle = stream_ref[at, :] + product(first[at, to_first["attended"]], w_out[...])
        middle_ref[at, :] = middle
        normed_two = layer_norm(middle, gains[1:2], biases[1:2]).astype(bf16)
        second[at, to_second["normed_two"]] = normed_two

    pltpu.make_async_copy(own_expand, w_expand, sems.at[2]).wait()
    for i in range(hidden_width // TILE):
        at = slice(i * TILE, (i + 1) * TILE)
        hidden, slope = gelu_and_slope(
            product(second[body, to_second["normed_two"]], w_expand[:, at])
        )
        first[body, at] = hidden.astype(bf16)
        slope_ref[:, at] = slope.astype(bf16)

    copies = [leave(True, slice(0, to_first["attended"].stop))]
    pltpu.make_async_copy(own_contract, w_contract, sems.at[3]).wait()
    live_column = jnp.concatenate([jnp.where(x, 1, 0) for x in live_columns], axis=0)
    for i in range(width // 256):
        at = slice(i * 256, (i + 1) * 256)
        result = middle_ref[:, at] + product(first[body, to_first["hidden"]], w_contract[:, at])
        act_ref[:, at] = jnp.where(live_column > 0, result, 0.0).astype(bf16)

    for i in range(hidden_width // TILE):
        at = slice(i * TILE, (i + 1) * TILE)
        grad_hidden = product_transposed(first[body, to_first["branch"]], w_contract[at, :])
        second[body, at] = (grad_hidden * slope_ref[:, at].astype(f32)).astype(bf16)

    copies.append(leave(False, slice(0, to_second["normed"].stop)))
    for i in range(width // 256):
        at = slice(i * 256, (i + 1) * 256)
        grad_middle_ref[:, at] = product_transposed(
            second[body, to_second["upward"]], w_expand[at, :]
        )

    gain_two = bias_two = gain_one = bias_one = jnp.zeros((1, width), f32)
    for at in blocks:
        back, gain, bias = layer_norm_back(
            middle_ref[at, :], gains[1:2], grad_middle_ref[at, :]
        )
        grad_middle = back + first[at, to_first["branch"]].astype(f32)
        grad_middle_ref[at, :] = grad_middle
        branch = grad_middle.astype(bf16)
        first[at, to_first["attend_branch"]] = branch
        grad_attended_ref[at, :] = product_transposed(branch, w_out[...]).astype(bf16)
        gain_two, bias_two = gain_two + gain, bias_two + bias

    copies.append(leave(True, slice(to_first["attend_branch"].start, to_first["normed"].stop)))
    for m, at in enumerate(blocks):
        for pair in range(PAIRS):
            parts = pair_backward(
                mixed_ref[at, pair_columns(pair)],
                mixed_ref[at, pair_columns(pair, width)],
                mixed_ref[at, pair_columns(pair, 2 * width)],
                grad_attended_ref[at, pair_columns(pair)],
                probability_ref[m * PAIRS + pair],
                masks,
            )
            first[at, pair_columns(pair, to_first["queries"].start)] = parts[0].astype(bf16)
            second[at, pair_columns(pair, to_second["keys"].start)] = parts[1].astype(bf16)
            second[at, pair_columns(pair, to_second["values"].start)] = parts[2].astype(bf16)

    keys_values = slice(to_second["keys"].start, to_second["values"].stop)
    copies.append(leave(False, keys_values))
    for i in range(width // 256):
        at = slice(i * 256, (i + 1) * 256)
        grad_stream_ref[:, at] = product_transposed(
            first[body, to_first["queries"]], w_in[at, 0:width]
        ) + product_transposed(second[body, keys_values], w_in[at, width:])

    for m, at in enumerate(blocks):
        back, gain, bias = layer_norm_back(
            stream_ref[at, :], gains[0:1], grad_stream_ref[at, :]
        )
        grad_stream = back + grad_middle_ref[at, :]
        first[at, to_first["stream"]] = grad_stream.astype(bf16)
        gain_one, bias_one = gain_one + gain, bias_one + bias
        summed = jnp.sum(grad_stream.reshape(block_patches, PATCH, width), axis=1)
        start = base + PATCH * lax.broadcasted_iota(jnp.int32, (block_patches, 1), 0)
        same = owner_of(start, spans[m]) == owner_of(start - PATCH, spans[m])
        summed = jnp.where(same, summed, 0.0).astype(bf16)
        grad_shifted_ref[m * block_patches : (m + 1) * block_patches, :] = summed
        grad_edge_ref[m : m + 1, :] = summed[0:1]

    grad_edge_ref[batches:, :] = jnp.zeros((SMALL_ROWS - batches, width), bf16)
    small = jnp.concatenate(
        [gain_one, gain_two, bias_one, bias_two, jnp.zeros((SMALL_ROWS - 4, width), f32)], axis=0
    )
    second[rows:, 0:width] = small.astype(bf16)
    copies.append(leave(False, slice(0, width), slice(rows, rows + SMALL_ROWS)))
    copies.append(leave(True, slice(to_first["queries"].start, first_width)))
    for copy in copies:
        copy.wait()


ANY = pl.BlockSpec(memory_space=pl.ANY)
WHOLE = pl.BlockSpec(memory_space=pltpu.VMEM)
SCALARS = pl.BlockSpec(memory_space=pltpu.SMEM)


def vmem(*shape, kind=bf16):
    return pltpu.VMEM(shape, kind)


def local_block(numbers, ids, tables, sent, edge, near, norms, out_grad, patch_rows, own, new):
    batches, width = out_grad.shape[0], out_grad.shape[2]
    rows = batches * BLOCK
    hidden_width = own[3].shape[0]
    (_, first_width), (_, second_width) = section_columns(hidden_width, width)
    part = jax.ShapeDtypeStruct((rows + SMALL_ROWS, first_width), bf16)
    return pl.pallas_call(
        partial(local_kernel, patch_rows),
        in_specs=[SCALARS] + [WHOLE] * 8 + [ANY] * 9,
        out_specs=[WHOLE] * 3 + [ANY] * 2,
        out_shape=[
            jax.ShapeDtypeStruct((rows, width), bf16),
            jax.ShapeDtypeStruct((rows // PATCH, width), bf16),
            jax.ShapeDtypeStruct((SMALL_ROWS, width), bf16),
            part,
            part,
        ],
        scratch_shapes=[
            vmem(*own[0].shape),
            vmem(*own[1].shape),
            vmem(*own[2].shape),
            vmem(*own[3].shape),
            vmem(*part.shape),
            vmem(part.shape[0], second_width),
            vmem(rows, width),
            vmem(sent.shape[0] + edge.shape[0] + near.shape[0], width),
            vmem(rows, width, kind=f32),
            vmem(rows, 3 * width),
            vmem(rows, width, kind=f32),
            vmem(rows, hidden_width),
            vmem(rows, width, kind=f32),
            vmem(rows, width),
            vmem(rows, width, kind=f32),
            vmem(batches * PAIRS, 2 * BLOCK, BLOCK, kind=f32),
            vmem(*tables[0].shape),
            pltpu.SemaphoreType.DMA((4 + batches,)),
            pltpu.SemaphoreType.DMA((6,)),
        ],
        compiler_params=pltpu.CompilerParams(vmem_limit_bytes=VMEM),
        cost_estimate=cost(35),
    )(numbers, ids, *tables, sent, edge, near, *norms, out_grad, *own, *new)


def local_gradients(count, numbers, ids, keep, arrived, hidden_width, width, half, deps=()):
    rows = keep.shape[0] - SMALL_ROWS
    (to_first, first_width), (to_second, _) = section_columns(hidden_width, width)
    deep, shard, room = hidden_width // GROUPS, width // GROUPS, VOCAB // GROUPS
    block = deep + 2 * shard + room
    cuts = (slice(0, hidden_width + width), slice(hidden_width + width, first_width))

    def kernel(numbers_ref, ids_ref, keep_ref, new_ref, *rest):
        out_ref, held, smalls, sums, sems, out_sems = rest[len(deps) :]
        copies = []
        for k, cut in enumerate(cuts):
            for j, ref in enumerate((keep_ref, new_ref)):
                copies.append(
                    pltpu.make_async_copy(
                        ref.at[0:rows, cut], held.at[j * rows : (j + 1) * rows, cut], sems.at[2 * k + j]
                    )
                )
        for j, ref in enumerate((keep_ref, new_ref)):
            copies.append(
                pltpu.make_async_copy(
                    ref.at[rows : rows + SMALL_ROWS, 0:width], smalls.at[j], sems.at[4 + j]
                )
            )
        for copy in copies:
            copy.start()
        section_now, chunk = numbers_ref[0], numbers_ref[2]
        tile_shards = TILE // deep

        copies[0].wait()
        copies[1].wait()

        @pl.when(section_now == 0)
        def _():
            for i in range(hidden_width // TILE):
                part = transposed_product(
                    held[:, i * TILE : (i + 1) * TILE], held[:, to_first["branch"]]
                )
                for k in range(tile_shards):
                    slot = slot_of(i * tile_shards + k, count)
                    sums[slot, 0:deep, :] = part[k * deep : (k + 1) * deep].astype(bf16)

        @pl.when(section_now != 0)
        def _():
            for i in range(hidden_width // TILE):
                part = transposed_product(
                    held[:, to_second["normed_two"]], held[:, i * TILE : (i + 1) * TILE]
                )
                chunk, at = i * TILE // width, i * TILE % width
                store_rows(sums, part, count, chunk * shard, slice(at, at + TILE))

        feed = pl.ds(0, deep)
        pltpu.make_async_copy(sums.at[:, feed], out_ref.at[:, feed], out_sems.at[0]).start()
        for copy in copies[2:]:
            copy.wait()

        @pl.when(section_now == 0)
        def _():
            part = transposed_product(
                held[:, to_first["attended"]], held[:, to_first["attend_branch"]]
            )
            store_rows(sums, part, count, deep)
            part = transposed_product(held[:, to_first["normed"]], held[:, to_first["queries"]])
            store_rows(sums, part, count, deep + shard)
            vocabulary = lax.broadcasted_iota(jnp.int32, (VOCAB, BLOCK), 0)
            onehots = []
            for where in (section_now, 1 - section_now):
                lane = pl.multiple_of(where * half + chunk * BLOCK, BLOCK)
                for m in range(rows // BLOCK):
                    ids_row = ids_ref[m : m + 1, pl.ds(lane, BLOCK)]
                    onehots.append(jnp.where(ids_row == vocabulary, 1.0, 0.0).astype(bf16))
            part = product(jnp.concatenate(onehots, axis=1), held[:, to_first["stream"]])
            store_rows(sums, part, count, deep + 2 * shard)

        @pl.when(section_now != 0)
        def _():
            for k, name in enumerate(("keys", "values")):
                part = transposed_product(held[:, to_second["normed"]], held[:, to_second[name]])
                store_rows(sums, part, count, deep + k * shard)
            small = (smalls[0].astype(f32) + smalls[1].astype(f32)).astype(bf16)
            for q in range(GROUPS):
                sums[q, deep + 2 * shard :, :] = small

        heads = pl.ds(deep, block - deep)
        pltpu.make_async_copy(sums.at[:, heads], out_ref.at[:, heads], out_sems.at[1]).start()
        pltpu.make_async_copy(sums.at[:, feed], out_ref.at[:, feed], out_sems.at[0]).wait()
        pltpu.make_async_copy(sums.at[:, heads], out_ref.at[:, heads], out_sems.at[1]).wait()

    return pl.pallas_call(
        kernel,
        in_specs=[SCALARS, WHOLE, ANY, ANY] + [ANY] * len(deps),
        out_specs=ANY,
        out_shape=jax.ShapeDtypeStruct((GROUPS, block, width), bf16),
        scratch_shapes=[
            vmem(2 * rows, first_width),
            vmem(2, SMALL_ROWS, width),
            vmem(GROUPS, block, width),
            pltpu.SemaphoreType.DMA((6,)),
            pltpu.SemaphoreType.DMA((2,)),
        ],
        compiler_params=pltpu.CompilerParams(vmem_limit_bytes=VMEM),
        cost_estimate=cost(12),
    )(numbers, ids, keep, arrived, *deps)


def global_sums_kernel(
    count, hidden_ref, branch_ref, normed_two_ref, upward_ref, normed_ref, grad_mixed_ref,
    attended_ref, attend_branch_ref, small_ref, first, second,
):
    hidden_width, width = hidden_ref.shape[1], branch_ref.shape[1]
    deep, shard, room = hidden_width // GROUPS, width // GROUPS, VOCAB // GROUPS
    tile_shards = TILE // deep
    for i in range(hidden_width // TILE):
        columns = slice(i * TILE, (i + 1) * TILE)
        part = transposed_product(hidden_ref[:, columns], branch_ref[...])
        for k in range(tile_shards):
            slot = slot_of(i * tile_shards + k, count)
            first[slot, 0:deep, :] = part[k * deep : (k + 1) * deep].astype(bf16)
        part = transposed_product(normed_two_ref[...], upward_ref[:, columns])
        chunk, at = i * TILE // width, i * TILE % width
        store_rows(second, part, count, chunk * shard, slice(at, at + TILE))
    part = transposed_product(attended_ref[...], attend_branch_ref[...])
    store_rows(first, part, count, deep)
    targets = ((first, deep + shard), (second, deep), (second, deep + shard))
    for chunk, (target, start) in enumerate(targets):
        columns = slice(chunk * width, (chunk + 1) * width)
        part = transposed_product(normed_ref[...], grad_mixed_ref[:, columns])
        store_rows(target, part, count, start)
    small = jnp.concatenate([small_ref[...], jnp.zeros((room - 4, width), f32)], axis=0)
    for q in range(GROUPS):
        first[q, deep + 2 * shard :, :] = jnp.zeros((room, width), bf16)
        second[q, deep + 2 * shard :, :] = small.astype(bf16)


def global_sums_of(count, *arrays):
    hidden, branch = arrays[:2]
    hidden_width, width = hidden.shape[1], branch.shape[1]
    block = hidden_width // GROUPS + (2 * width + VOCAB) // GROUPS
    sums = jax.ShapeDtypeStruct((GROUPS, block, width), bf16)
    return pl.pallas_call(
        partial(global_sums_kernel, count),
        out_shape=[sums, sums],
        compiler_params=pltpu.CompilerParams(vmem_limit_bytes=VMEM),
        cost_estimate=cost(14),
    )(*arrays)


def causal_bias(start, count, numbers_ref):
    spans = item_spans(numbers_ref, 1, numbers_ref[0])
    rows = lax.broadcasted_iota(jnp.int32, (BLOCK, 1), 0) + start
    columns = lax.broadcasted_iota(jnp.int32, (1, count), 1)
    same = owner_of(rows * PATCH, spans) == owner_of(columns * PATCH, spans)
    bias = jnp.where((columns <= rows) & same, 0.0, MASKED)
    return jnp.concatenate([bias, bias], axis=0)


def global_forward_kernel(numbers_ref, qkv_ref, out_ref):
    start = pl.multiple_of(pl.program_id(0) * BLOCK, BLOCK)
    bias = causal_bias(start, qkv_ref.shape[0], numbers_ref)
    out_ref[...] = pair_forward(
        qkv_ref[pl.ds(start, BLOCK), 0:PAIR],
        qkv_ref[:, PAIR : 2 * PAIR],
        qkv_ref[:, 2 * PAIR : 3 * PAIR],
        bias,
        lane_masks(),
    ).astype(bf16)


def global_backward_kernel(numbers_ref, qkv_ref, grad_ref, out_ref, key_sum, value_sum):
    step = pl.program_id(0)
    start = pl.multiple_of(step * BLOCK, BLOCK)
    bias = causal_bias(start, qkv_ref.shape[0], numbers_ref)

    @pl.when(step == 0)
    def _():
        key_sum[...] = jnp.zeros_like(key_sum)
        value_sum[...] = jnp.zeros_like(value_sum)

    queries, keys = qkv_ref[pl.ds(start, BLOCK), 0:PAIR], qkv_ref[:, PAIR : 2 * PAIR]
    masks = lane_masks()
    grad_queries, grad_keys, grad_values = pair_backward(
        queries,
        keys,
        qkv_ref[:, 2 * PAIR : 3 * PAIR],
        grad_ref[...],
        pair_probabilities(queries, keys, bias, masks),
        masks,
    )
    out_ref[pl.ds(start, BLOCK), 0:PAIR] = grad_queries.astype(bf16)
    key_sum[...] += grad_keys
    value_sum[...] += grad_values

    @pl.when(step == pl.num_programs(0) - 1)
    def _():
        out_ref[:, PAIR : 2 * PAIR] = key_sum[...].astype(bf16)
        out_ref[:, 2 * PAIR : 3 * PAIR] = value_sum[...].astype(bf16)


def global_attention(qkv, numbers, grads=None, deps=()):
    count = qkv.shape[0]
    specs = [
        SCALARS,
        pl.BlockSpec((count, 3 * PAIR), lambda i: (0, 0)),
    ]
    blocks = pl.BlockSpec((BLOCK, PAIR), lambda i: (i, 0))
    if grads is None:
        return pl.pallas_call(
            global_forward_kernel,
            grid=(count // BLOCK,),
            in_specs=specs,
            out_specs=blocks,
            out_shape=jax.ShapeDtypeStruct((count, PAIR), bf16),
            compiler_params=pltpu.CompilerParams(vmem_limit_bytes=VMEM),
            cost_estimate=cost(15),
        )(numbers, qkv)

    def body(*refs):
        global_backward_kernel(*refs[:3], *refs[3 + len(deps) :])

    return pl.pallas_call(
        body,
        grid=(count // BLOCK,),
        in_specs=specs + [blocks] + [ANY] * len(deps),
        out_specs=pl.BlockSpec((count, 3 * PAIR), lambda i: (0, 0)),
        out_shape=jax.ShapeDtypeStruct((count, 3 * PAIR), bf16),
        scratch_shapes=[pltpu.VMEM((count, PAIR), f32), pltpu.VMEM((count, PAIR), f32)],
        compiler_params=pltpu.CompilerParams(vmem_limit_bytes=VMEM),
        cost_estimate=cost(30),
    )(numbers, qkv, grads, *deps)


def call(kernel, args, specs, out_shape, out_specs, scratch=(), deps=(), micros=1):
    count = len(args)

    def body(*refs):
        kernel(*refs[:count], *refs[count + len(deps) :])

    return pl.pallas_call(
        body,
        in_specs=list(specs) + [ANY] * len(deps),
        out_specs=out_specs,
        out_shape=out_shape,
        scratch_shapes=list(scratch),
        compiler_params=pltpu.CompilerParams(vmem_limit_bytes=VMEM),
        cost_estimate=cost(micros),
    )(*args, *deps)


def shaped(*shape, kind=bf16):
    return jax.ShapeDtypeStruct(shape, kind)


def patch_forward(numbers, patch_rows, byte_rows, own_table, new_table, pieces, deps=()):
    batches, width = byte_rows[0].shape[0], own_table.shape[1]
    segments = len(byte_rows) * batches
    rows = segments * patch_rows
    shard = pieces[0].shape[0]
    span, count = len(pieces), len(byte_rows)
    room = (segments + 15) // 16 * 16

    def kernel(numbers_ref, own_ref, new_ref, *rest):
        byte_refs, piece_refs, rest = rest[:count], rest[count : count + span], rest[count + span :]
        embedded_ref, weight_ref, share_ref, low_ref, onehot_ref, table_ref = rest
        member_now = numbers_ref[1]
        for k in range(span):
            start = pl.multiple_of((member_now ^ k) * shard, shard)
            weight_ref[pl.ds(start, shard), :] = piece_refs[k][...]

        @pl.when(numbers_ref[0] == 0)
        def _():
            table_ref[...] = own_ref[...]

        @pl.when(numbers_ref[0] != 0)
        def _():
            table_ref[...] = new_ref[...]

        some = [ref[...].astype(f32) for ref in byte_refs]
        some.append(jnp.zeros((room - segments, some[0].shape[1]), f32))
        some = jnp.concatenate(some, axis=0).astype(bf16)
        shape = (some.shape[1], rows)
        place = lax.broadcasted_iota(jnp.int32, shape, 1) % patch_rows * PATCH + numbers_ref[2]
        picked = lax.broadcasted_iota(jnp.int32, shape, 0) == place
        wide = product(some, jnp.where(picked, 1.0, 0.0).astype(bf16))
        segment = lax.broadcasted_iota(jnp.int32, (room, rows), 1) // patch_rows
        here = lax.broadcasted_iota(jnp.int32, (room, rows), 0) == segment
        ids = jnp.sum(jnp.where(here, wide, 0.0), axis=0, keepdims=True).astype(jnp.int32)
        vocabulary = lax.broadcasted_iota(jnp.int32, (VOCAB, rows), 0)
        onehot = jnp.where(ids == vocabulary, 1.0, 0.0).astype(bf16)
        onehot_ref[...] = onehot
        embedded_ref[...] = transposed_product(onehot, table_ref[...]).astype(bf16)
        share = product(embedded_ref[...], weight_ref[...])
        share_ref[...] = share
        low_ref[...] = share.astype(bf16)

    return call(
        kernel,
        (numbers, own_table, new_table, *byte_rows, *pieces),
        [SCALARS] + [WHOLE] * (2 + count + span),
        [
            shaped(rows, width),
            shaped(span * shard, width),
            shaped(rows, width, kind=f32),
            shaped(rows, width),
            shaped(VOCAB, rows),
        ],
        [WHOLE] * 5,
        [pltpu.VMEM(own_table.shape, bf16)],
        deps=deps,
        micros=4,
    )


def split_heads(values, targets, batches, part):
    patch_rows = values.shape[0] // batches
    first = targets[0].shape[0]
    for t in range(batches * PAIRS):
        m, pair = t // PAIRS, t % PAIRS
        target = targets[0].at[t] if t < first else targets[1].at[t - first]
        target[:, part * PAIR : (part + 1) * PAIR] = values[
            m * patch_rows : (m + 1) * patch_rows, pair * PAIR : (pair + 1) * PAIR
        ]


def task_shapes(batches, first, patch_rows, columns):
    rest = batches * PAIRS - first
    return [shaped(first, patch_rows, columns)] + ([shaped(rest, patch_rows, columns)] if rest else [])


def merge_heads(blocks, target, batches, parts):
    patch_rows = target.shape[0] // batches
    width = PAIRS * PAIR
    for t in range(batches * PAIRS):
        m, pair = t // PAIRS, t % PAIRS
        first = blocks[0].shape[0]
        block = blocks[0].at[t] if t < first else blocks[1].at[t - first]
        for part in range(parts):
            at = part * width + pair * PAIR
            target[m * patch_rows : (m + 1) * patch_rows, at : at + PAIR] = block[
                :, part * PAIR : (part + 1) * PAIR
            ]


def strided(values, target, span, offset):
    size = values.shape[1] // (4 * span)
    for k in range(span):
        parts = [
            values[:, (group * span + k) * size : (group * span + k + 1) * size]
            for group in range(4)
        ]
        target[k, :, offset : offset + 4 * size] = jnp.concatenate(parts, axis=1)


def global_start(batches, first_tasks, own, others, gains, biases, heads_in):
    rows, width = own.shape
    patch_rows = rows // batches
    tasks = task_shapes(batches, first_tasks, patch_rows, 3 * PAIR)

    def kernel(own_ref, gains_ref, biases_ref, weight_hbm, *rest):
        other_refs, rest = rest[: len(others)], rest[len(others) :]
        (stream_ref, normed_ref, share_ref), task_refs = rest[:3], rest[3 : 3 + len(tasks)]
        weight, sem = rest[3 + len(tasks) :]
        load = pltpu.make_async_copy(weight_hbm, weight, sem)
        load.start()
        stream = own_ref[...]
        for ref in other_refs:
            stream = stream + ref[...].astype(f32)
        stream_ref[...] = stream
        normed = layer_norm(stream, gains_ref[0:1], biases_ref[0:1]).astype(bf16)
        normed_ref[...] = normed
        strided(normed, share_ref, SPAN, 0)
        load.wait()
        for part in range(3):
            mixed = product(normed, weight[:, part * width : (part + 1) * width]).astype(bf16)
            split_heads(mixed, task_refs, batches, part)

    return call(
        kernel,
        (own, gains, biases, heads_in, *others),
        [WHOLE] * 3 + [ANY] + [WHOLE] * len(others),
        [
            shaped(rows, width, kind=f32),
            shaped(rows, width),
            shaped(SPAN, rows, width // SPAN),
            *tasks,
        ],
        [WHOLE] * (3 + len(tasks)),
        [pltpu.VMEM(heads_in.shape, bf16), pltpu.SemaphoreType.DMA],
        micros=5,
    )


def global_feed_forward(batches, blocks, stream, gains, biases, heads_out, expand, contract):
    rows, width = stream.shape
    hidden_width = expand.shape[1]
    n = len(blocks)
    patch_rows = rows // batches
    half = patch_rows // 2

    def kernel(stream_ref, gains_ref, biases_ref, out_hbm, expand_hbm, contract_hbm, *rest):
        block_refs, rest = rest[:n], rest[n:]
        (attended_ref, middle_ref, normed_two_ref, slope_ref, hidden_ref, sent_ref) = rest[:6]
        share_ref, other_share_ref, edge_ref, near_ref, w_out, w_expand, w_contract, sems = rest[6:]
        loads = [
            pltpu.make_async_copy(out_hbm, w_out, sems.at[0]),
            pltpu.make_async_copy(expand_hbm, w_expand, sems.at[1]),
            pltpu.make_async_copy(contract_hbm, w_contract, sems.at[2]),
        ]
        for load in loads:
            load.start()
        merge_heads(block_refs, attended_ref, batches, 1)
        loads[0].wait()
        middle = stream_ref[...] + product(attended_ref[...], w_out[...])
        middle_ref[...] = middle
        normed_two_ref[...] = layer_norm(middle, gains_ref[1:2], biases_ref[1:2]).astype(bf16)
        loads[1].wait()

        @pl.loop(0, hidden_width // width, unroll=True)
        def _(i):
            at = pl.ds(pl.multiple_of(i * width, 128), width)
            hidden, slope = gelu_and_slope(product(normed_two_ref[...], w_expand[:, at]))
            hidden_ref[:, at] = hidden.astype(bf16)
            slope_ref[:, at] = slope.astype(bf16)

        loads[2].wait()
        result = middle_ref[...] + product(hidden_ref[...], w_contract[...])
        sent = result.astype(bf16)
        sent_ref[...] = sent
        edge_ref[...] = jnp.zeros(edge_ref.shape, bf16)
        for m in range(batches):
            stop = (m + 1) * patch_rows
            edge_ref[m : m + 1, :] = sent[stop - 1 : stop]
            near_ref[m * half : (m + 1) * half, :] = sent[stop - half - 1 : stop - 1]
        strided(hidden_ref[...], share_ref, SPAN, 0)
        strided(normed_two_ref[...], other_share_ref, SPAN, 0)
        strided(attended_ref[...], other_share_ref, SPAN, width // SPAN)

    return call(
        kernel,
        (stream, gains, biases, heads_out, expand, contract, *blocks),
        [WHOLE] * 3 + [ANY] * 3 + [WHOLE] * n,
        [
            shaped(rows, width),
            shaped(rows, width, kind=f32),
            shaped(rows, width),
            shaped(rows, hidden_width),
            shaped(rows, hidden_width),
            shaped(rows, width),
            shaped(SPAN, rows, hidden_width // SPAN),
            shaped(SPAN, rows, 2 * width // SPAN),
            shaped(SMALL_ROWS, width),
            shaped(batches * half, width),
        ],
        [WHOLE] * 10,
        [
            pltpu.VMEM(heads_out.shape, bf16),
            pltpu.VMEM(expand.shape, bf16),
            pltpu.VMEM(contract.shape, bf16),
            pltpu.SemaphoreType.DMA((3,)),
        ],
        micros=8,
    )


def global_feed_backward(
    batches, first_tasks, own, near, edge, middle, slope, gains, heads_out, expand, contract, deps=()
):
    rows, width = middle.shape
    hidden_width = expand.shape[1]
    patch_rows = rows // batches
    half = patch_rows // 2
    tasks = task_shapes(batches, first_tasks, patch_rows, PAIR)

    def kernel(
        own_ref, near_ref, edge_ref, middle_ref, slope_ref, gains_ref, out_hbm, expand_hbm,
        contract_hbm, upward_ref, grad_middle_ref, branch_ref, small_ref, grad_ref, *rest,
    ):
        task_refs, (w_out, w_expand, w_contract, sems) = rest[: len(tasks)], rest[len(tasks) :]
        loads = [
            pltpu.make_async_copy(contract_hbm, w_contract, sems.at[2]),
            pltpu.make_async_copy(expand_hbm, w_expand, sems.at[1]),
            pltpu.make_async_copy(out_hbm, w_out, sems.at[0]),
        ]
        for load in loads:
            load.start()
        source = jnp.concatenate([own_ref[...], near_ref[...], edge_ref[...]], axis=0)
        index = lax.broadcasted_iota(jnp.int32, (rows, 1), 0)
        batch, place = index // patch_rows, index % patch_rows
        chosen = jnp.where(
            place < half - 1,
            batch * half + place + 1,
            jnp.where(
                place < patch_rows - 1,
                batches * half + batch * half + place - (half - 1),
                2 * batches * half + batch,
            ),
        )
        columns = lax.broadcasted_iota(jnp.int32, (rows, source.shape[0]), 1)
        picked = jnp.where(columns == chosen, 1.0, 0.0).astype(bf16)
        grad_ref[...] = product(picked, source).astype(bf16)
        loads[0].wait()

        @pl.loop(0, hidden_width // width, unroll=True)
        def _(i):
            at = pl.ds(pl.multiple_of(i * width, 128), width)
            grad_hidden = product_transposed(grad_ref[...], w_contract[at, :])
            upward_ref[:, at] = (grad_hidden * slope_ref[:, at].astype(f32)).astype(bf16)

        loads[1].wait()
        grad_normed = product_transposed(upward_ref[...], w_expand[...])
        back, gain, bias = layer_norm_back(middle_ref[...], gains_ref[1:2], grad_normed)
        grad_middle = back + grad_ref[...].astype(f32)
        grad_middle_ref[...] = grad_middle
        branch = grad_middle.astype(bf16)
        branch_ref[...] = branch
        small_ref[...] = jnp.concatenate([gain, bias], axis=0)
        loads[2].wait()
        attended = product_transposed(branch, w_out[...]).astype(bf16)
        split_heads(attended, task_refs, batches, 0)

    return call(
        kernel,
        (own, near, edge, middle, slope, gains, heads_out, expand, contract),
        [WHOLE] * 6 + [ANY] * 3,
        [
            shaped(rows, hidden_width),
            shaped(rows, width, kind=f32),
            shaped(rows, width),
            shaped(2, width, kind=f32),
            shaped(rows, width),
            *tasks,
        ],
        [WHOLE] * (5 + len(tasks)),
        [
            pltpu.VMEM(heads_out.shape, bf16),
            pltpu.VMEM(expand.shape, bf16),
            pltpu.VMEM(contract.shape, bf16),
            pltpu.SemaphoreType.DMA((3,)),
        ],
        deps=deps,
        micros=10,
    )


def global_end(batches, blocks, stream, grad_middle, small, gains, heads_in, deps=()):
    rows, width = stream.shape
    n = len(blocks)

    def kernel(stream_ref, grad_middle_ref, small_ref, gains_ref, weight_hbm, *rest):
        block_refs, (mixed_ref, low_ref, all_small_ref, weight, sem) = rest[:n], rest[n:]
        load = pltpu.make_async_copy(weight_hbm, weight, sem)
        load.start()
        merge_heads(block_refs, mixed_ref, batches, 3)
        load.wait()
        grad_normed = product_transposed(mixed_ref[...], weight[...])
        back, gain, bias = layer_norm_back(stream_ref[...], gains_ref[0:1], grad_normed)
        low_ref[0:rows, :] = (back + grad_middle_ref[...]).astype(bf16)
        smalls = jnp.concatenate([gain, small_ref[0:1], bias, small_ref[1:2]], axis=0)
        all_small_ref[...] = smalls
        rest = jnp.zeros((SMALL_ROWS - 4, width), f32)
        low_ref[rows:, :] = jnp.concatenate([smalls, rest], axis=0).astype(bf16)

    return call(
        kernel,
        (stream, grad_middle, small, gains, heads_in, *blocks),
        [WHOLE] * 4 + [ANY] + [WHOLE] * n,
        [
            shaped(rows, 3 * width),
            shaped(rows + SMALL_ROWS, width),
            shaped(4, width, kind=f32),
        ],
        [WHOLE] * 3,
        [pltpu.VMEM(heads_in.shape, bf16), pltpu.SemaphoreType.DMA],
        deps=deps,
        micros=6,
    )


def patch_backward(section, onehot, embedded, weight, own, crossed, span, deps=()):
    rows, width = embedded.shape
    block = own[0].shape[0]
    n = len(own)
    used = rows // n
    shard = weight.shape[0] // span

    def kernel(section_ref, onehot_ref, embedded_ref, weight_ref, crossed_ref, *rest):
        own_refs, (patch_ref, table_ref, gathered, small) = rest[:n], rest[n:]

        @pl.when(section_ref[0] == 0)
        def _():
            for k in range(n):
                gathered[k * used : (k + 1) * used, :] = own_refs[k][0:used, :]
            total = sum(ref[used:, :].astype(f32) for ref in own_refs)
            small[...] = total.astype(bf16)

        @pl.when(section_ref[0] != 0)
        def _():
            for k in range(n):
                gathered[k * used : (k + 1) * used, :] = crossed_ref[k * block : k * block + used, :]
            small[...] = jnp.zeros_like(small)

        part = transposed_product(embedded_ref[...], gathered[...]).astype(bf16)
        for k in range(span):
            patch_ref[k, 0:shard, :] = part[k * shard : (k + 1) * shard]
            patch_ref[k, shard:, :] = small[...]
        grad_embedded = product_transposed(gathered[...], weight_ref[...]).astype(bf16)
        table_ref[...] = product(onehot_ref[...], grad_embedded).astype(bf16)

    return call(
        kernel,
        (section, onehot, embedded, weight, crossed, *own),
        [SCALARS] + [WHOLE] * (4 + n),
        [shaped(span, shard + SMALL_ROWS, width), shaped(VOCAB, width)],
        [WHOLE] * 2,
        [pltpu.VMEM((rows, width), bf16), pltpu.VMEM((SMALL_ROWS, width), bf16)],
        deps=deps,
        micros=6,
    )


def leave_by_group(group, buffer, targets, sems):
    for j in range(len(targets)):
        for k in range(len(targets)):

            @pl.when((group ^ j) == k)
            def _(j=j, k=k):
                pltpu.make_async_copy(buffer.at[j], targets[k], sems.at[k]).start()

    for k in range(len(targets)):
        pltpu.make_async_copy(buffer.at[0], targets[k], sems.at[k]).wait()


def pack_columns(hidden_width, width):
    deep, thin = hidden_width // SPAN, width // SPAN
    first = [
        (slice(0, deep), slice(deep, deep + width)),
        (slice(deep + width, deep + width + thin), slice(deep + width + thin, deep + 4 * width + thin)),
    ]
    right = 2 * thin
    second = [
        (slice(0, thin), slice(right, right + hidden_width)),
        (slice(thin, right), slice(right + hidden_width, right + hidden_width + width)),
    ]
    return first, second, max(first[-1][1].stop, second[-1][1].stop)


def pack_second(member, share, attend_branch, upward, whole, deps=()):
    rows, width = attend_branch.shape
    own, hidden_width = share.shape[2], upward.shape[1]

    def kernel(member_ref, share_ref, attend_ref, upward_ref, out_ref):
        for k in range(SPAN):
            out_ref[k, :, 0:own] = share_ref[member_ref[0] ^ k]
            out_ref[k, :, own : own + hidden_width] = upward_ref[...]
            out_ref[k, :, own + hidden_width : own + hidden_width + width] = attend_ref[...]

    return call(
        kernel,
        (member, share, attend_branch, upward),
        [SCALARS] + [WHOLE] * 3,
        shaped(SPAN, rows, whole),
        WHOLE,
        deps=deps,
        micros=3,
    )


def pack(section, member, share, normed_share, branch, mixed, second, passed, deps=()):
    rows, width = branch.shape
    deep, thin, whole = share.shape[2], normed_share.shape[2], second.shape[2]

    def kernel(
        section_ref, member_ref, share_ref, normed_ref, branch_ref, mixed_ref, passed_ref,
        second_ref, *rest,
    ):
        sent_refs, same_ref, sems = rest[:SPAN], rest[SPAN], rest[SPAN + 1]
        same_ref[...] = passed_ref[...]

        @pl.when(section_ref[0] == 0)
        def _():
            for k in range(SPAN):
                sent_refs[k][:, 0:deep] = share_ref[member_ref[0] ^ k]
                sent_refs[k][:, deep : deep + width] = branch_ref[...]
                sent_refs[k][:, deep + width : deep + width + thin] = normed_ref[member_ref[0] ^ k]
                sent_refs[k][:, deep + width + thin : deep + 4 * width + thin] = mixed_ref[...]

        @pl.when(section_ref[0] != 0)
        def _():
            copies = [
                pltpu.make_async_copy(second_ref.at[k], sent_refs[k], sems.at[k])
                for k in range(SPAN)
            ]
            for copy in copies:
                copy.start()
            for copy in copies:
                copy.wait()

    return call(
        kernel,
        (section, member, share, normed_share, branch, mixed, passed, second),
        [SCALARS] * 2 + [WHOLE] * 5 + [ANY],
        [shaped(rows, whole)] * SPAN + [shaped(*passed.shape)],
        [WHOLE] * (SPAN + 1),
        [pltpu.SemaphoreType.DMA((SPAN,))],
        deps=deps,
        micros=4,
    )


def plane_gradients(section, group, sent, hidden_width, width, deps=()):
    halves = pack_columns(hidden_width, width)[:2]
    rows_of = [
        sum(
            (left.stop - left.start) // 4 * ((right.stop - right.start) // width)
            for left, right in pairs
        )
        for pairs in halves
    ]
    block = max(rows_of)

    def kernel(section_ref, group_ref, *refs):
        sent_refs, (keep_ref, leave_ref, buffer, sems) = refs[: len(sent)], refs[len(sent) :]

        def columns(at):
            return jnp.concatenate([ref[:, at] for ref in sent_refs], axis=0)

        def fill(pairs):
            start = 0
            for left, right in pairs:
                former, size = columns(left), (left.stop - left.start) // 4
                for first in range(right.start, right.stop, width):
                    part = transposed_product(former, columns(slice(first, first + width)))
                    for j in range(4):
                        buffer[j, start : start + size, :] = part[
                            j * size : (j + 1) * size
                        ].astype(bf16)
                    start += size
            if start < block:
                for j in range(4):
                    buffer[j, start:block, :] = jnp.zeros((block - start, width), bf16)

        @pl.when(section_ref[0] == 0)
        def _():
            fill(halves[0])

        @pl.when(section_ref[0] != 0)
        def _():
            fill(halves[1])

        for j in range(4):
            mine = ((group_ref[0] ^ j) & 1) == 0

            @pl.when(mine)
            def _(j=j):
                pltpu.make_async_copy(buffer.at[j], keep_ref.at[j >> 1], sems.at[j]).start()

            @pl.when(jnp.logical_not(mine))
            def _(j=j):
                pltpu.make_async_copy(buffer.at[j], leave_ref.at[j >> 1], sems.at[j]).start()

        for j in range(4):
            pltpu.make_async_copy(buffer.at[j], keep_ref.at[j >> 1], sems.at[j]).wait()

    return call(
        kernel,
        (section, group, *sent),
        [SCALARS] * 2 + [WHOLE] * len(sent),
        [shaped(2, block, width)] * 2,
        [ANY] * 2,
        [pltpu.VMEM((4, block, width), bf16), pltpu.SemaphoreType.DMA((4,))],
        deps=deps,
        micros=6,
    )


def by_parity(parity, sums, deps=()):
    count, rows, width = sums.shape

    def kernel(parity_ref, sums_ref, *rest):
        rest[-1][...] = sums_ref[...]

    block = (1, rows, width)
    return pl.pallas_call(
        kernel,
        grid_spec=pltpu.PrefetchScalarGridSpec(
            num_scalar_prefetch=1,
            grid=(count // 2,),
            in_specs=[pl.BlockSpec(block, lambda i, ref: (2 * i + 1 - ref[0], 0, 0))]
            + [ANY] * len(deps),
            out_specs=pl.BlockSpec(block, lambda i, ref: (i, 0, 0)),
        ),
        out_shape=shaped(count // 2, rows, width),
        compiler_params=pltpu.CompilerParams(vmem_limit_bytes=VMEM),
        cost_estimate=cost(3),
    )(parity, sums, *deps)


def half_sums(flags, kept, near, deps=()):
    shape = kept.shape[1:]
    every = kept.shape[0] == 4

    def kernel(flags_ref, kept_ref, near_ref, far_ref, mine_ref):
        for k in range(2):
            own = kept_ref[2 * k + flags_ref[2]] if every else kept_ref[k]
            total = (own.astype(f32) + near_ref[k].astype(f32)).astype(bf16)

            @pl.when(flags_ref[1] == k)
            def _():
                mine_ref[...] = total

            @pl.when(flags_ref[1] != k)
            def _():
                far_ref[...] = total

    return call(
        kernel,
        (flags, kept, near),
        [SCALARS, WHOLE, WHOLE],
        [shaped(*shape)] * 2,
        [WHOLE] * 2,
        deps=deps,
        micros=2,
    )


def half_sums_and_cross(flags, kept, near, other, other_far, short, deps=()):
    shape = kept.shape[1:]
    held = other.shape[0]

    def kernel(
        flags_ref, kept_ref, near_ref, other_ref, more_ref, far_ref, short_ref, mine_ref, cross_ref
    ):
        for k in range(2):
            total = (kept_ref[k].astype(f32) + near_ref[k].astype(f32)).astype(bf16)

            @pl.when(flags_ref[1] == k)
            def _():
                mine_ref[...] = total
                cross_ref[...] = total

            @pl.when(flags_ref[1] != k)
            def _():
                far_ref[...] = total
                short_ref[...] = total[0:short]

        @pl.when(flags_ref[0] == 0)
        def _():
            total = other_ref[...].astype(f32) + more_ref[...].astype(f32)
            cross_ref[0:held, :] = total.astype(bf16)

    return call(
        kernel,
        (flags, kept, near, other, other_far),
        [SCALARS] + [WHOLE] * 4,
        [shaped(*shape), shaped(short, shape[1]), shaped(*shape), shaped(*shape)],
        [WHOLE] * 4,
        deps=deps,
        micros=2,
    )


def finish(section, deep, shard, room, own_global, own_local, crossed, fars, table_parts, patch_parts):
    width = own_local.shape[1]
    chunks = deep // shard
    p = len(patch_parts)

    def kernel(section_ref, global_ref, local_ref, crossed_ref, table_ref, *refs):
        (global_one, global_two, local_two), refs = refs[:3], refs[3:]
        patch_refs = refs[:p]
        contract, expand, ins, out, table, small, patch = refs[p:]

        def total(some, start, size):
            return sum(ref[start : start + size, :].astype(f32) for ref in some)

        total_patch = sum(ref[...].astype(f32) for ref in patch_refs)
        patch[...] = total_patch[: patch.shape[0]]

        @pl.when(section_ref[0] == 0)
        def _():
            one, two = (global_ref, global_one), (crossed_ref, global_two)
            contract[...] = total(one, 0, deep)
            for c in range(3):
                ins[:, c * width : (c + 1) * width] = total(one, deep + c * shard, shard)
            for c in range(chunks):
                expand[:, c * width : (c + 1) * width] = total(two, c * shard, shard)
            out[...] = total(two, chunks * shard, shard)
            small[...] = total_patch[patch.shape[0] :]
            sums = jnp.zeros((room, width), f32)
            for k in range(table_ref.shape[0]):
                sums = sums + table_ref[k].astype(f32)
            table[...] = sums

        @pl.when(section_ref[0] != 0)
        def _():
            one, two = (crossed_ref,), (local_ref, local_two)
            contract[...] = total(one, 0, deep)
            out[...] = total(one, deep, shard)
            ins[:, 0:width] = total(one, deep + shard, shard)
            table[...] = total(one, deep + 2 * shard, room)
            for c in range(chunks):
                expand[:, c * width : (c + 1) * width] = total(two, c * shard, shard)
            for c in range(2):
                ins[:, (c + 1) * width : (c + 2) * width] = total(two, deep + c * shard, shard)
            small[...] = total(two, deep + 2 * shard, small.shape[0])

    return call(
        kernel,
        (section, own_global, own_local, crossed, table_parts, *fars, *patch_parts),
        [SCALARS] + [WHOLE] * (7 + p),
        [
            shaped(deep, width, kind=f32),
            shaped(shard, chunks * width, kind=f32),
            shaped(shard, 3 * width, kind=f32),
            shaped(shard, width, kind=f32),
            shaped(room, width, kind=f32),
            shaped(SMALL_ROWS, width, kind=f32),
            shaped(patch_parts[0].shape[0] - SMALL_ROWS, width, kind=f32),
        ],
        [WHOLE] * 7,
        micros=4,
    )


def activation_rows(numbers, sent, other, own, deps=()):
    batches, half, width = own.shape
    patch_rows = sent.shape[0] // batches
    byte_rows = patch_rows * PATCH

    def kernel(numbers_ref, sent_ref, other_ref, own_ref, out_ref):
        @pl.when(numbers_ref[0] == 0)
        def _():
            rows = lax.broadcasted_iota(jnp.int32, (byte_rows, 1), 0)
            columns = lax.broadcasted_iota(jnp.int32, (byte_rows, patch_rows), 1)
            for m in range(batches):
                live = is_live(numbers_ref[1] + rows, item_spans(numbers_ref, 3, m))
                chosen = jnp.where(live, rows // PATCH, -1)
                spread = jnp.where(columns == chosen, 1.0, 0.0).astype(bf16)
                part = sent_ref[m * patch_rows : (m + 1) * patch_rows, :]
                out_ref[m] = product(spread, part).astype(bf16)

        @pl.when(numbers_ref[0] != 0)
        def _():
            for m in range(batches):
                out_ref[m, 0:half, :] = other_ref[m]
                out_ref[m, half:, :] = own_ref[m]

    return call(
        kernel,
        (numbers, sent, other, own),
        [SCALARS] + [WHOLE] * 3,
        shaped(batches, byte_rows, width),
        WHOLE,
        deps=deps,
        micros=2,
    )


SEQ = ("group", "member")


def section_send(x, origin, target, pairs):
    count = lax.axis_size(SEQ)
    joint = [(origin * count + i, target * count + j) for i, j in pairs]
    return lax.ppermute(x, ("section",) + SEQ, joint)


def section_swap(x):
    return lax.ppermute(x, "section", [(0, 1), (1, 0)])


def by_slot(buffer, count, pieces):
    split = count // GROUPS
    parts, start = [], 0
    for size, shared in pieces:
        part = buffer[:, start : start + size]
        start += size
        kept = shared or size // split
        if shared:
            part = jnp.broadcast_to(part[:, None, :shared], (GROUPS, split, shared, part.shape[2]))
        parts.append(part.reshape(count, kept, part.shape[-1]))
    whole = jnp.concatenate(parts, axis=1)
    turned = whole.reshape((4, count // 4) + whole.shape[1:])
    return jnp.swapaxes(turned, 0, 1).reshape(whole.shape)


def place_sum(shares):
    shares = lax.psum_scatter(shares, "member", scatter_dimension=0, tiled=True)
    return lax.psum_scatter(shares, "group", scatter_dimension=0, tiled=True)[0]


def on_device(
    byte_values,
    item_lengths,
    embed_tables,
    patch_weight,
    norm_gains,
    norm_biases,
    heads_in,
    heads_out,
    expand_weight,
    contract_weight,
    out_grad,
):
    place = lax.axis_index(SEQ)
    count = lax.axis_size(SEQ)
    section = lax.axis_index("section")
    is_global = section == 0
    batches, byte_rows = byte_values.shape
    patch_rows = byte_rows // PATCH
    width = heads_out.shape[2]
    rows = batches * patch_rows
    total_patches = patch_rows * count
    gains, biases = norm_gains[0], norm_biases[0]
    heads_in, heads_out = heads_in[0], heads_out[0]
    expand, contract = expand_weight[0], contract_weight[0]
    own_table = embed_tables[0]
    straight = [(i, i) for i in range(count)]

    quarters = PATCH // 2
    span = count // quarters
    group, member = place // span, place % span
    shard_rows = patch_weight.shape[0]
    pieces = [patch_weight]
    for k in range(1, span):
        pieces.append(lax.ppermute(patch_weight, SEQ, [(i, i ^ k) for i in range(count)]))
    other_table = section_swap(own_table)
    theirs = [byte_values]
    for k in range(1, quarters):
        theirs.append(
            lax.ppermute(byte_values, SEQ, [(i, i ^ (k * span)) for i in range(count)])
        )
    place_numbers = jnp.stack([section, member, section * quarters + group]).astype(jnp.int32)
    embedded, byte_weight, shares, low_shares, byte_onehot = patch_forward(
        place_numbers, patch_rows, theirs, own_table, other_table, pieces
    )
    shares = shares + section_send(low_shares, 1, 0, straight).astype(f32)
    shares = shares.reshape(quarters, rows, width)
    parts = []
    for k in range(1, quarters):
        pairs = [(i, i ^ (k * span)) for i in range(count)]
        parts.append(section_send(shares[k].astype(bf16), 0, 0, pairs))

    arrived = [section_send(w, 1, 0, straight) for w in (heads_in, heads_out, expand, contract)]
    own_norms = jnp.concatenate([gains, biases])
    other_norms = section_swap(own_norms)

    tasks = batches * PAIRS
    first_tasks = min(tasks, count)
    spare_tasks = tasks - first_tasks

    def to_tasks(first, spare=None):
        columns = first.shape[2]
        slots = jnp.pad(first, ((0, count - first_tasks), (0, 0), (0, 0)))
        if spare_tasks:
            spare = section_send(spare, 0, 1, straight)
            spare = jnp.pad(spare, ((0, count - spare_tasks), (0, 0), (0, 0)))
            slots = jnp.where(is_global, slots, spare)
        landed = lax.all_to_all(slots, SEQ, 0, 0)
        return landed.reshape(total_patches, columns)

    def from_tasks(results):
        columns = results.shape[1]
        slots = lax.all_to_all(results.reshape(count, patch_rows, columns), SEQ, 0, 0)
        if spare_tasks:
            return [slots, section_send(slots[:spare_tasks], 1, 0, straight)]
        return [slots]

    task = jnp.minimum(jnp.where(is_global, place, first_tasks + place), tasks - 1)
    lengths = item_lengths.reshape(-1)
    task_numbers = jnp.concatenate([(task // PAIRS).reshape(1).astype(jnp.int32), lengths])

    stream, normed, normed_share, *tasks_out = global_start(
        batches, first_tasks, shares[0], parts, gains, biases, heads_in
    )
    qkv = to_tasks(*tasks_out)
    attended, middle, normed_two, slope, hidden, sent, feed_share, other_share, edge, near = global_feed_forward(
        batches,
        from_tasks(global_attention(qkv, task_numbers)),
        stream,
        gains,
        biases,
        heads_out,
        expand,
        contract,
    )
    half = patch_rows // 2
    half_bytes = half * PATCH
    chunks = half_bytes // BLOCK
    onward = [(i, i + 1) for i in range(count - 1)]
    backward = [(i + 1, i) for i in range(count - 1)]
    near = section_send(near, 0, 1, straight)
    edge = section_send(edge, 0, 0, onward)
    weights = (heads_in, heads_out, expand, contract)
    flag = section.reshape(1).astype(jnp.int32)
    block_patches = BLOCK // PATCH
    local_outs, activations_of, grads_shifted, grads_edge = [], [], [], []
    for c in range(chunks):
        numbers = jnp.concatenate(
            [
                jnp.stack([section, place * byte_rows, jnp.int32(c)]).astype(jnp.int32),
                lengths,
            ]
        )
        act, grad_shifted, grad_edge, keep, send = local_block(
            numbers,
            byte_values,
            (own_table, other_table),
            sent,
            edge,
            near,
            (own_norms, other_norms),
            out_grad,
            patch_rows,
            weights,
            arrived,
        )
        local_outs.append(act.reshape(batches, BLOCK, width))
        grads_shifted.append(grad_shifted.reshape(batches, block_patches, width))
        grads_edge.append(grad_edge)
        activations_of.append((numbers, keep, section_swap(send)))
    local_out = jnp.concatenate(local_outs, axis=1)
    grad_shifted = jnp.concatenate(grads_shifted, axis=1).reshape(batches * half, width)

    other_out = section_send(local_out, 0, 1, straight)
    activations = activation_rows(numbers, sent, other_out, local_out)

    shard = width // count
    room = VOCAB // count
    group_shard, group_room = width // GROUPS, VOCAB // GROUPS
    small_rows = max(4, room)
    pieces = {
        False: [(contract.shape[0] // GROUPS, 0), (group_shard, 0), (group_shard, 0), (group_room, 0)],
        True: [(group_shard, 0)] * (expand.shape[1] // width + 2) + [(group_room, small_rows)],
    }

    def ordered(buffer):
        if count == GROUPS:
            return buffer
        upper, lower = by_slot(buffer, count, pieces[False]), by_slot(buffer, count, pieces[True])
        rows_of = max(upper.shape[1], lower.shape[1])
        upper, lower = (
            jnp.pad(x, ((0, 0), (0, rows_of - x.shape[1]), (0, 0))) for x in (upper, lower)
        )
        return jnp.where(is_global, upper, lower)

    near_back = section_send(grad_shifted, 1, 0, straight)
    edge_back = section_send(grads_edge[0], 0, 0, backward)
    in_plane = span == SPAN and count == GROUPS
    member_flag = (member % SPAN).reshape(1).astype(jnp.int32)
    group_flag = group.reshape(1).astype(jnp.int32)

    def plane_send(blocks):
        return [blocks[0]] + [
            both_send(blocks[k], [(i, i ^ k) for i in range(count)]) for k in range(1, SPAN)
        ]

    upper = (group >> 1) & 1
    half_flags = jnp.stack([section, upper, group & 1]).astype(jnp.int32)

    def group_pairs(step):
        return [(i, i ^ (step * span)) for i in range(count)]

    def both_send(x, pairs):
        joint = [(s * count + i, s * count + j) for s in range(2) for i, j in pairs]
        return lax.ppermute(x, ("section",) + SEQ, joint)

    half_locals = [
        ordered(
            local_gradients(
                count,
                numbers,
                byte_values,
                keep,
                crossed,
                contract.shape[0],
                width,
                half_bytes,
                [near_back, edge_back],
            )
        )
        for numbers, keep, crossed in activations_of
    ]
    if chunks > 1:
        half_locals = [sum(x.astype(f32) for x in half_locals).astype(bf16)]
    half_locals = half_locals[0]
    grad_upward, grad_middle, attend_branch, small, grad_sent, *task_grads = global_feed_backward(
        batches,
        first_tasks,
        grad_shifted,
        near_back,
        edge_back,
        middle,
        slope,
        gains,
        heads_out,
        expand,
        contract,
        [half_locals],
    )
    if in_plane:
        whole = pack_columns(contract.shape[0], width)[2]
        second_parts = section_send(
            pack_second(member_flag, other_share, attend_branch, grad_upward, whole), 0, 1, straight
        )
    task_grads = to_tasks(*task_grads)
    task_mixed = global_attention(qkv, task_numbers, task_grads)
    grad_mixed, own_rows, small = global_end(
        batches,
        from_tasks(task_mixed),
        stream,
        grad_middle,
        small,
        gains,
        heads_in,
    )

    if in_plane:
        *sent_parts, own_rows = pack(
            flag, member_flag, feed_share, normed_share, grad_sent, grad_mixed, second_parts, own_rows
        )
        arrived_parts = plane_send(sent_parts)

    gathered = [own_rows]
    for k in range(1, quarters):
        pairs = [(i, i ^ (k * span)) for i in range(count)]
        gathered.append(section_send(own_rows, 0, 0, pairs))
    crossed = section_send(jnp.concatenate(gathered), 0, 1, straight)
    if in_plane:
        in_planes = lax.psum_scatter(half_locals, "member", scatter_dimension=0, tiled=True)
        parity_flag = (group & 1).reshape(1).astype(jnp.int32)
        local_leaving = by_parity(parity_flag, in_planes, [crossed])
        local_near = both_send(local_leaving, group_pairs(1))
    else:
        own_local = place_sum(half_locals)
    patch_share, table_share = patch_backward(
        flag,
        byte_onehot,
        embedded,
        byte_weight,
        gathered,
        crossed,
        span,
        [local_leaving] if in_plane else (),
    )
    patch_parts = [lax.dynamic_index_in_dim(patch_share, member, 0, keepdims=False)]
    for k in range(1, span):
        leaving = lax.dynamic_index_in_dim(patch_share, member ^ k, 0, keepdims=False)
        patch_parts.append(lax.ppermute(leaving, SEQ, [(i, i ^ k) for i in range(count)]))
    table_share = table_share + section_send(table_share, 1, 0, straight)
    table_parts = lax.all_to_all(table_share.reshape(count, VOCAB // count, width), SEQ, 0, 0)

    def ordered_rows(first, second):
        feed_rows = contract.shape[0] // count
        expand_sum = [second[k * shard : (k + 1) * shard] for k in range(feed_rows // shard)]
        rest, others = first[feed_rows:], second[feed_rows:]
        ins = [rest[shard : 2 * shard], others[:shard], others[shard : 2 * shard]]
        return (
            first[:feed_rows],
            jnp.concatenate(expand_sum, axis=1),
            jnp.concatenate(ins, axis=1),
            rest[:shard],
            rest[2 * shard : 2 * shard + room],
            others[2 * shard : 2 * shard + 4],
        )

    if in_plane:
        local_far, local_mine = half_sums(half_flags, in_planes, local_near)
        across = group_pairs(2)
        local_far = both_send(local_far, across)
        kept, leaving = plane_gradients(
            flag,
            group_flag,
            arrived_parts,
            contract.shape[0],
            width,
            [table_parts, local_far],
        )
        near = both_send(leaving, group_pairs(1))
        short = expand.shape[1] // GROUPS + shard
        far, far_short, mine, crossed = half_sums_and_cross(
            half_flags, kept, near, local_mine, local_far, short, patch_parts[1:]
        )
        crossed = section_swap(crossed)
        fars = [
            section_send(far, 0, 0, across),
            section_send(far_short, 1, 0, across),
            local_far,
        ]
        contract_grad, expand_grad, in_grad, out_grads, table_grad, small, patch_grads = finish(
            flag,
            contract.shape[0] // count,
            shard,
            room,
            mine,
            local_mine,
            crossed,
            fars,
            table_parts,
            patch_parts,
        )
        small = small[:4]
    else:
        upper, lower = global_sums_of(
            count, hidden, grad_sent, normed_two, grad_upward, normed, grad_mixed, attended,
            attend_branch, small,
        )
        own_global = ordered(jnp.where(is_global, upper, section_send(lower, 0, 1, straight)))
        own_global = place_sum(own_global)
        crossed = section_swap(jnp.where(is_global, own_local, own_global)).astype(f32)
        global_sums = ordered_rows(own_global.astype(f32), crossed)
        global_table = jnp.sum(table_parts.astype(f32), axis=0)
        global_sums = global_sums[:4] + (global_table, global_sums[5])
        local_sums = ordered_rows(crossed, own_local.astype(f32))
        contract_grad, expand_grad, in_grad, out_grads, table_grad, small = (
            jnp.where(is_global, upper, lower) for upper, lower in zip(global_sums, local_sums)
        )
        patch_grads = sum(x.astype(f32) for x in patch_parts)[:shard_rows]
    small = lax.dynamic_slice_in_dim(small, place * shard, shard, 1)
    return (
        activations[None],
        table_grad[None],
        patch_grads,
        small[None, 0:2],
        small[None, 2:4],
        in_grad[None],
        out_grads[None],
        expand_grad[None],
        contract_grad[None],
    )


def solution(mesh):
    devices = mesh.devices
    groups = PATCH // 2
    split = jax.sharding.Mesh(
        devices.reshape(devices.shape[0], groups, devices.shape[1] // groups), ("section",) + SEQ
    )
    both = ("section",) + SEQ
    placed = (
        P(None, SEQ),
        P(),
        P("section", None, None),
        P(both, None),
        P("section", None, None),
        P("section", None, None),
        P("section", None, None),
        P("section", None, None),
        P("section", None, None),
        P("section", None, None),
        P(None, SEQ, None),
    )
    return jax.shard_map(
        on_device,
        mesh=split,
        in_specs=placed,
        out_specs=(
            P("section", None, SEQ, None),
            P("section", SEQ, None),
            P(both, None),
            P("section", None, SEQ),
            P("section", None, SEQ),
            P("section", SEQ, None),
            P("section", SEQ, None),
            P("section", SEQ, None),
            P("section", SEQ, None),
        ),
        check_vma=False,
    )
```

```python
from functools import partial

import jax
import jax.numpy as jnp
from jax import lax
from jax.experimental import pallas as pl
from jax.experimental.pallas import tpu as pltpu
from jax.sharding import PartitionSpec as P

HEADS = 12
HEAD_SIZE = 64
VOCAB = 256
PATCH = 8
ITEMS = 4
PAIRS = HEADS // 2
PAIR = 2 * HEAD_SIZE
SCALE = HEAD_SIZE ** (-0.5)
EPSILON = 1e-05
MASKED = -1e30
BLOCK = 128
TILE = 384
GROUPS = 16
SPAN = 4
VMEM = 60 * 1024 * 1024

bf16 = jnp.bfloat16
f32 = jnp.float32


def cost(micros):
    return pl.CostEstimate(flops=int(micros * 1.1e9), bytes_accessed=1, transcendentals=0)


def product(former, latter):
    return jnp.dot(former, latter, preferred_element_type=f32)


def transposed_product(former, latter):
    return lax.dot_general(former, latter, (((0,), (0,)), ((), ())), preferred_element_type=f32)


def product_transposed(former, latter):
    return lax.dot_general(former, latter, (((1,), (1,)), ((), ())), preferred_element_type=f32)


def normalise(values):
    average = jnp.mean(values, axis=-1, keepdims=True)
    centered = values - average
    inverse_root = lax.rsqrt(jnp.mean(centered * centered, axis=-1, keepdims=True) + EPSILON)
    return centered * inverse_root, inverse_root


def layer_norm(values, gain, bias):
    return normalise(values)[0] * gain + bias


def layer_norm_back(values, gain, grad):
    unit, inverse_root = normalise(values)
    scaled = grad * gain
    grad_values = inverse_root * (
        scaled
        - jnp.mean(scaled, axis=-1, keepdims=True)
        - unit * jnp.mean(scaled * unit, axis=-1, keepdims=True)
    )
    return (
        grad_values,
        jnp.sum(grad * unit, axis=0, keepdims=True),
        jnp.sum(grad, axis=0, keepdims=True),
    )


def slot_of(q, count):
    if count != GROUPS:
        return q
    return (q % SPAN) * (GROUPS // SPAN) + q // SPAN


def store_rows(buffer, value, count, start, columns=slice(None)):
    rows = value.shape[0] // GROUPS
    for q in range(GROUPS):
        buffer[slot_of(q, count), pl.ds(start, rows), columns] = value[
            q * rows : (q + 1) * rows
        ].astype(bf16)


def patch_bias(live_row):
    rows = lax.broadcasted_iota(jnp.int32, (BLOCK, BLOCK), 0)
    columns = lax.broadcasted_iota(jnp.int32, (BLOCK, BLOCK), 1)
    same = (rows // PATCH) == (columns // PATCH)
    allowed = same & (columns <= rows) & ((live_row > 0) | (columns == rows))
    bias = jnp.where(allowed, 0.0, MASKED)
    return jnp.concatenate([bias, bias], axis=0)


def softmax_rows(scores):
    peak = jnp.max(scores, axis=-1, keepdims=True)
    exponents = jnp.exp(scores - peak)
    return exponents * (1.0 / jnp.sum(exponents, axis=-1, keepdims=True))


def lane_masks():
    lanes = lax.broadcasted_iota(jnp.int32, (1, PAIR), 1)
    low = jnp.where(lanes < HEAD_SIZE, 1.0, 0.0)
    return lanes < HEAD_SIZE, low.astype(bf16), (1.0 - low).astype(bf16)


def stacked(values, low, high, scale=1.0):
    return jnp.concatenate([values * (low * scale), values * (high * scale)], axis=0)


def unstacked(values, is_low):
    half = values.shape[0] // 2
    return jnp.where(is_low, values[:half], values[half:])


def pair_probabilities(queries, keys, bias, masks):
    _, low, high = masks
    return softmax_rows(product_transposed(stacked(queries, low, high, SCALE), keys) + bias)


def pair_forward(queries, keys, values, bias, masks):
    probabilities = pair_probabilities(queries, keys, bias, masks)
    return unstacked(product(probabilities.astype(bf16), values), masks[0])


def pair_backward(queries, keys, values, grads, probabilities, masks):
    is_low, low, high = masks
    both = stacked(queries, low, high, SCALE)
    both_grads = stacked(grads, low, high)
    prob_grads = product_transposed(both_grads, values)
    delta = jnp.sum(probabilities * prob_grads, axis=-1, keepdims=True)
    score_grads = (probabilities * (prob_grads - delta)).astype(bf16)
    return (
        unstacked(product(score_grads, keys), is_low) * SCALE,
        transposed_product(score_grads, both),
        transposed_product(probabilities.astype(bf16), both_grads),
    )


def gelu_and_slope(x):
    root = 0.7978845608028654
    cubic = 0.044715
    square = x * x
    bent = jnp.tanh(x * (root + (root * cubic) * square))
    half = 0.5 * (1.0 + bent)
    slope = half + (0.5 * x) * (1.0 - bent * bent) * (root + (3.0 * root * cubic) * square)
    return x * half, slope


def fetch(section, own, arrived, target, sem):
    @pl.when(section == 0)
    def _():
        pltpu.make_async_copy(arrived, target, sem).start()

    @pl.when(section != 0)
    def _():
        pltpu.make_async_copy(own, target, sem).start()


def section_columns(hidden_width, width):
    tables = []
    for names in (
        ("hidden", "branch", "attended", "attend_branch", "normed", "queries", "stream"),
        ("upward", "normed_two", "normed", "keys", "values"),
    ):
        table, start = {}, 0
        for name in names:
            size = hidden_width if start == 0 else width
            table[name] = slice(start, start + size)
            start += size
        tables.append((table, start))
    return tables


SMALL_ROWS = 16


def item_spans(numbers_ref, first, batch):
    spans, start = [], 0
    for k in range(ITEMS):
        length = numbers_ref[first + batch * ITEMS + k]
        stop = start + (length + PATCH - 1) // PATCH * PATCH
        spans.append((start, start + length, stop))
        start = stop
    return spans


def is_live(positions, spans):
    live = jnp.zeros(positions.shape, jnp.bool_)
    for start, live_end, _ in spans:
        live = live | ((positions >= start) & (positions < live_end))
    return live


def owner_of(positions, spans):
    owner = jnp.full(positions.shape, ITEMS, jnp.int32)
    for k, (start, _, stop) in enumerate(spans):
        owner = jnp.where((positions >= start) & (positions < stop), k, owner)
    return owner


def local_kernel(
    patch_rows,
    numbers_ref,
    ids_ref,
    own_table_ref,
    new_table_ref,
    sent_ref,
    edge_ref,
    near_ref,
    own_norms_ref,
    new_norms_ref,
    out_grad_hbm,
    own_in,
    own_out,
    own_expand,
    own_contract,
    new_in,
    new_out,
    new_expand,
    new_contract,
    act_ref,
    grad_shifted_ref,
    grad_edge_ref,
    keep_ref,
    send_ref,
    w_in,
    w_out,
    w_expand,
    w_contract,
    first,
    second,
    out_grad_ref,
    source_ref,
    stream_ref,
    mixed_ref,
    middle_ref,
    slope_ref,
    grad_middle_ref,
    grad_attended_ref,
    grad_stream_ref,
    probability_ref,
    table_ref,
    sems,
    out_sems,
):
    section, offset, chunk = numbers_ref[0], numbers_ref[1], numbers_ref[2]
    rows, width = act_ref.shape
    batches = rows // BLOCK
    hidden_width = w_expand.shape[1]
    half = patch_rows // 2
    block_patches = BLOCK // PATCH
    lane = pl.multiple_of(section * (half * PATCH) + chunk * BLOCK, BLOCK)
    base = offset + lane
    grads_in = [
        pltpu.make_async_copy(
            out_grad_hbm.at[m, pl.ds(lane, BLOCK)],
            out_grad_ref.at[m * BLOCK : (m + 1) * BLOCK],
            sems.at[4 + m],
        )
        for m in range(batches)
    ]
    fetch(section, own_in, new_in, w_in, sems.at[0])
    for copy in grads_in:
        copy.start()
    fetch(section, own_out, new_out, w_out, sems.at[1])
    fetch(section, own_expand, new_expand, w_expand, sems.at[2])
    fetch(section, own_contract, new_contract, w_contract, sems.at[3])
    (to_first, first_width), (to_second, second_width) = section_columns(hidden_width, width)
    body = slice(0, rows)
    norms = jnp.where(section == 0, new_norms_ref[...], own_norms_ref[...])
    gains, biases = norms[0:2], norms[2:4]

    @pl.when(section == 0)
    def _():
        table_ref[...] = new_table_ref[...]

    @pl.when(section != 0)
    def _():
        table_ref[...] = own_table_ref[...]

    out_count = [0]

    def leave(from_first, columns, at_rows=body):
        source = first if from_first else second
        sem = out_sems.at[out_count[0]]
        out_count[0] += 1
        part = source.at[at_rows, columns]

        @pl.when(section == (0 if from_first else 1))
        def _():
            pltpu.make_async_copy(part, keep_ref.at[at_rows, columns], sem).start()

        @pl.when(section != (0 if from_first else 1))
        def _():
            pltpu.make_async_copy(part, send_ref.at[at_rows, columns], sem).start()

        return pltpu.make_async_copy(part, keep_ref.at[at_rows, columns], sem)

    blocks = [slice(m * BLOCK, (m + 1) * BLOCK) for m in range(batches)]
    spans = [item_spans(numbers_ref, 3, m) for m in range(batches)]
    column = lax.broadcasted_iota(jnp.int32, (BLOCK, 1), 0)
    row = lax.broadcasted_iota(jnp.int32, (1, BLOCK), 1)
    live_columns = [is_live(base + column, span) for span in spans]
    biases_of = [
        patch_bias(jnp.where(is_live(base + row, span), 1, 0)) for span in spans
    ]
    sent_rows, edge_rows = sent_ref.shape[0], edge_ref.shape[0]
    source_ref[0:sent_rows, :] = sent_ref[...]
    source_ref[sent_rows : sent_rows + edge_rows, :] = edge_ref[...]
    source_ref[sent_rows + edge_rows :, :] = near_ref[...]

    for copy in grads_in:
        copy.wait()
    for m, at in enumerate(blocks):
        vocabulary = lax.broadcasted_iota(jnp.int32, (VOCAB, BLOCK), 0)
        ids = ids_ref[m : m + 1, pl.ds(lane, BLOCK)]
        onehot = jnp.where(ids == vocabulary, 1.0, 0.0).astype(bf16)
        patch = column // PATCH
        place = chunk * block_patches + patch
        start = base + patch * PATCH
        same = owner_of(start, spans[m]) == owner_of(start - PATCH, spans[m])
        inside = jnp.where(place == 0, sent_rows + m, m * patch_rows + place - 1)
        chosen = jnp.where(section == 0, inside, sent_rows + edge_rows + m * half + place)
        chosen = jnp.where(same, chosen, -1)
        columns = lax.broadcasted_iota(jnp.int32, (BLOCK, source_ref.shape[0]), 1)
        spread = jnp.where(columns == chosen, 1.0, 0.0).astype(bf16)
        stream = transposed_product(onehot, table_ref[...]) + product(spread, source_ref[...])
        stream_ref[at, :] = stream
        normed = layer_norm(stream, gains[0:1], biases[0:1]).astype(bf16)
        first[at, to_first["normed"]] = normed
        second[at, to_second["normed"]] = normed
        first[at, to_first["branch"]] = jnp.where(
            live_columns[m], out_grad_ref[at, :].astype(f32), 0.0
        ).astype(bf16)

    pltpu.make_async_copy(own_in, w_in, sems.at[0]).wait()
    for i in range(3 * width // TILE):
        at = slice(i * TILE, (i + 1) * TILE)
        mixed_ref[:, at] = product(first[body, to_first["normed"]], w_in[:, at]).astype(bf16)

    masks = lane_masks()

    def pair_columns(pair, start=0):
        return slice(start + pair * PAIR, start + (pair + 1) * PAIR)

    for m, at in enumerate(blocks):
        for pair in range(PAIRS):
            probabilities = pair_probabilities(
                mixed_ref[at, pair_columns(pair)],
                mixed_ref[at, pair_columns(pair, width)],
                biases_of[m],
                masks,
            )
            probability_ref[m * PAIRS + pair] = probabilities
            attended = product(
                probabilities.astype(bf16), mixed_ref[at, pair_columns(pair, 2 * width)]
            )
            first[at, pair_columns(pair, to_first["attended"].start)] = unstacked(
                attended, masks[0]
            ).astype(bf16)

    pltpu.make_async_copy(own_out, w_out, sems.at[1]).wait()
    for at in blocks:
        middle = stream_ref[at, :] + product(first[at, to_first["attended"]], w_out[...])
        middle_ref[at, :] = middle
        normed_two = layer_norm(middle, gains[1:2], biases[1:2]).astype(bf16)
        second[at, to_second["normed_two"]] = normed_two

    pltpu.make_async_copy(own_expand, w_expand, sems.at[2]).wait()
    for i in range(hidden_width // TILE):
        at = slice(i * TILE, (i + 1) * TILE)
        hidden, slope = gelu_and_slope(
            product(second[body, to_second["normed_two"]], w_expand[:, at])
        )
        first[body, at] = hidden.astype(bf16)
        slope_ref[:, at] = slope.astype(bf16)

    copies = [leave(True, slice(0, to_first["attended"].stop))]
    pltpu.make_async_copy(own_contract, w_contract, sems.at[3]).wait()
    live_column = jnp.concatenate([jnp.where(x, 1, 0) for x in live_columns], axis=0)
    for i in range(width // 256):
        at = slice(i * 256, (i + 1) * 256)
        result = middle_ref[:, at] + product(first[body, to_first["hidden"]], w_contract[:, at])
        act_ref[:, at] = jnp.where(live_column > 0, result, 0.0).astype(bf16)

    for i in range(hidden_width // TILE):
        at = slice(i * TILE, (i + 1) * TILE)
        grad_hidden = product_transposed(first[body, to_first["branch"]], w_contract[at, :])
        second[body, at] = (grad_hidden * slope_ref[:, at].astype(f32)).astype(bf16)

    copies.append(leave(False, slice(0, to_second["normed"].stop)))
    for i in range(width // 256):
        at = slice(i * 256, (i + 1) * 256)
        grad_middle_ref[:, at] = product_transposed(
            second[body, to_second["upward"]], w_expand[at, :]
        )

    gain_two = bias_two = gain_one = bias_one = jnp.zeros((1, width), f32)
    for at in blocks:
        back, gain, bias = layer_norm_back(
            middle_ref[at, :], gains[1:2], grad_middle_ref[at, :]
        )
        grad_middle = back + first[at, to_first["branch"]].astype(f32)
        grad_middle_ref[at, :] = grad_middle
        branch = grad_middle.astype(bf16)
        first[at, to_first["attend_branch"]] = branch
        grad_attended_ref[at, :] = product_transposed(branch, w_out[...]).astype(bf16)
        gain_two, bias_two = gain_two + gain, bias_two + bias

    copies.append(leave(True, slice(to_first["attend_branch"].start, to_first["normed"].stop)))
    for m, at in enumerate(blocks):
        for pair in range(PAIRS):
            parts = pair_backward(
                mixed_ref[at, pair_columns(pair)],
                mixed_ref[at, pair_columns(pair, width)],
                mixed_ref[at, pair_columns(pair, 2 * width)],
                grad_attended_ref[at, pair_columns(pair)],
                probability_ref[m * PAIRS + pair],
                masks,
            )
            first[at, pair_columns(pair, to_first["queries"].start)] = parts[0].astype(bf16)
            second[at, pair_columns(pair, to_second["keys"].start)] = parts[1].astype(bf16)
            second[at, pair_columns(pair, to_second["values"].start)] = parts[2].astype(bf16)

    keys_values = slice(to_second["keys"].start, to_second["values"].stop)
    copies.append(leave(False, keys_values))
    for i in range(width // 256):
        at = slice(i * 256, (i + 1) * 256)
        grad_stream_ref[:, at] = product_transposed(
            first[body, to_first["queries"]], w_in[at, 0:width]
        ) + product_transposed(second[body, keys_values], w_in[at, width:])

    for m, at in enumerate(blocks):
        back, gain, bias = layer_norm_back(
            stream_ref[at, :], gains[0:1], grad_stream_ref[at, :]
        )
        grad_stream = back + grad_middle_ref[at, :]
        first[at, to_first["stream"]] = grad_stream.astype(bf16)
        gain_one, bias_one = gain_one + gain, bias_one + bias
        summed = jnp.sum(grad_stream.reshape(block_patches, PATCH, width), axis=1)
        start = base + PATCH * lax.broadcasted_iota(jnp.int32, (block_patches, 1), 0)
        same = owner_of(start, spans[m]) == owner_of(start - PATCH, spans[m])
        summed = jnp.where(same, summed, 0.0).astype(bf16)
        grad_shifted_ref[m * block_patches : (m + 1) * block_patches, :] = summed
        grad_edge_ref[m : m + 1, :] = summed[0:1]

    grad_edge_ref[batches:, :] = jnp.zeros((SMALL_ROWS - batches, width), bf16)
    small = jnp.concatenate(
        [gain_one, gain_two, bias_one, bias_two, jnp.zeros((SMALL_ROWS - 4, width), f32)], axis=0
    )
    second[rows:, 0:width] = small.astype(bf16)
    copies.append(leave(False, slice(0, width), slice(rows, rows + SMALL_ROWS)))
    copies.append(leave(True, slice(to_first["queries"].start, first_width)))
    for copy in copies:
        copy.wait()


ANY = pl.BlockSpec(memory_space=pl.ANY)
WHOLE = pl.BlockSpec(memory_space=pltpu.VMEM)
SCALARS = pl.BlockSpec(memory_space=pltpu.SMEM)


def vmem(*shape, kind=bf16):
    return pltpu.VMEM(shape, kind)


def local_block(numbers, ids, tables, sent, edge, near, norms, out_grad, patch_rows, own, new):
    batches, width = out_grad.shape[0], out_grad.shape[2]
    rows = batches * BLOCK
    hidden_width = own[3].shape[0]
    (_, first_width), (_, second_width) = section_columns(hidden_width, width)
    part = jax.ShapeDtypeStruct((rows + SMALL_ROWS, first_width), bf16)
    return pl.pallas_call(
        partial(local_kernel, patch_rows),
        in_specs=[SCALARS] + [WHOLE] * 8 + [ANY] * 9,
        out_specs=[WHOLE] * 3 + [ANY] * 2,
        out_shape=[
            jax.ShapeDtypeStruct((rows, width), bf16),
            jax.ShapeDtypeStruct((rows // PATCH, width), bf16),
            jax.ShapeDtypeStruct((SMALL_ROWS, width), bf16),
            part,
            part,
        ],
        scratch_shapes=[
            vmem(*own[0].shape),
            vmem(*own[1].shape),
            vmem(*own[2].shape),
            vmem(*own[3].shape),
            vmem(*part.shape),
            vmem(part.shape[0], second_width),
            vmem(rows, width),
            vmem(sent.shape[0] + edge.shape[0] + near.shape[0], width),
            vmem(rows, width, kind=f32),
            vmem(rows, 3 * width),
            vmem(rows, width, kind=f32),
            vmem(rows, hidden_width),
            vmem(rows, width, kind=f32),
            vmem(rows, width),
            vmem(rows, width, kind=f32),
            vmem(batches * PAIRS, 2 * BLOCK, BLOCK, kind=f32),
            vmem(*tables[0].shape),
            pltpu.SemaphoreType.DMA((4 + batches,)),
            pltpu.SemaphoreType.DMA((6,)),
        ],
        compiler_params=pltpu.CompilerParams(vmem_limit_bytes=VMEM),
        cost_estimate=cost(35),
    )(numbers, ids, *tables, sent, edge, near, *norms, out_grad, *own, *new)


def local_gradients(count, numbers, ids, keep, arrived, hidden_width, width, half, deps=()):
    rows = keep.shape[0] - SMALL_ROWS
    (to_first, first_width), (to_second, _) = section_columns(hidden_width, width)
    deep, shard, room = hidden_width // GROUPS, width // GROUPS, VOCAB // GROUPS
    block = deep + 2 * shard + room
    cuts = (slice(0, hidden_width + width), slice(hidden_width + width, first_width))

    def kernel(numbers_ref, ids_ref, keep_ref, new_ref, *rest):
        out_ref, held, smalls, sums, sems, out_sems = rest[len(deps) :]
        copies = []
        for k, cut in enumerate(cuts):
            for j, ref in enumerate((keep_ref, new_ref)):
                copies.append(
                    pltpu.make_async_copy(
                        ref.at[0:rows, cut], held.at[j * rows : (j + 1) * rows, cut], sems.at[2 * k + j]
                    )
                )
        for j, ref in enumerate((keep_ref, new_ref)):
            copies.append(
                pltpu.make_async_copy(
                    ref.at[rows : rows + SMALL_ROWS, 0:width], smalls.at[j], sems.at[4 + j]
                )
            )
        for copy in copies:
            copy.start()
        section_now, chunk = numbers_ref[0], numbers_ref[2]
        tile_shards = TILE // deep

        copies[0].wait()
        copies[1].wait()

        @pl.when(section_now == 0)
        def _():
            for i in range(hidden_width // TILE):
                part = transposed_product(
                    held[:, i * TILE : (i + 1) * TILE], held[:, to_first["branch"]]
                )
                for k in range(tile_shards):
                    slot = slot_of(i * tile_shards + k, count)
                    sums[slot, 0:deep, :] = part[k * deep : (k + 1) * deep].astype(bf16)

        @pl.when(section_now != 0)
        def _():
            for i in range(hidden_width // TILE):
                part = transposed_product(
                    held[:, to_second["normed_two"]], held[:, i * TILE : (i + 1) * TILE]
                )
                chunk, at = i * TILE // width, i * TILE % width
                store_rows(sums, part, count, chunk * shard, slice(at, at + TILE))

        feed = pl.ds(0, deep)
        pltpu.make_async_copy(sums.at[:, feed], out_ref.at[:, feed], out_sems.at[0]).start()
        for copy in copies[2:]:
            copy.wait()

        @pl.when(section_now == 0)
        def _():
            part = transposed_product(
                held[:, to_first["attended"]], held[:, to_first["attend_branch"]]
            )
            store_rows(sums, part, count, deep)
            part = transposed_product(held[:, to_first["normed"]], held[:, to_first["queries"]])
            store_rows(sums, part, count, deep + shard)
            vocabulary = lax.broadcasted_iota(jnp.int32, (VOCAB, BLOCK), 0)
            onehots = []
            for where in (section_now, 1 - section_now):
                lane = pl.multiple_of(where * half + chunk * BLOCK, BLOCK)
                for m in range(rows // BLOCK):
                    ids_row = ids_ref[m : m + 1, pl.ds(lane, BLOCK)]
                    onehots.append(jnp.where(ids_row == vocabulary, 1.0, 0.0).astype(bf16))
            part = product(jnp.concatenate(onehots, axis=1), held[:, to_first["stream"]])
            store_rows(sums, part, count, deep + 2 * shard)

        @pl.when(section_now != 0)
        def _():
            for k, name in enumerate(("keys", "values")):
                part = transposed_product(held[:, to_second["normed"]], held[:, to_second[name]])
                store_rows(sums, part, count, deep + k * shard)
            small = (smalls[0].astype(f32) + smalls[1].astype(f32)).astype(bf16)
            for q in range(GROUPS):
                sums[q, deep + 2 * shard :, :] = small

        heads = pl.ds(deep, block - deep)
        pltpu.make_async_copy(sums.at[:, heads], out_ref.at[:, heads], out_sems.at[1]).start()
        pltpu.make_async_copy(sums.at[:, feed], out_ref.at[:, feed], out_sems.at[0]).wait()
        pltpu.make_async_copy(sums.at[:, heads], out_ref.at[:, heads], out_sems.at[1]).wait()

    return pl.pallas_call(
        kernel,
        in_specs=[SCALARS, WHOLE, ANY, ANY] + [ANY] * len(deps),
        out_specs=ANY,
        out_shape=jax.ShapeDtypeStruct((GROUPS, block, width), bf16),
        scratch_shapes=[
            vmem(2 * rows, first_width),
            vmem(2, SMALL_ROWS, width),
            vmem(GROUPS, block, width),
            pltpu.SemaphoreType.DMA((6,)),
            pltpu.SemaphoreType.DMA((2,)),
        ],
        compiler_params=pltpu.CompilerParams(vmem_limit_bytes=VMEM),
        cost_estimate=cost(12),
    )(numbers, ids, keep, arrived, *deps)


def global_sums_kernel(
    count, hidden_ref, branch_ref, normed_two_ref, upward_ref, normed_ref, grad_mixed_ref,
    attended_ref, attend_branch_ref, small_ref, first, second,
):
    hidden_width, width = hidden_ref.shape[1], branch_ref.shape[1]
    deep, shard, room = hidden_width // GROUPS, width // GROUPS, VOCAB // GROUPS
    tile_shards = TILE // deep
    for i in range(hidden_width // TILE):
        columns = slice(i * TILE, (i + 1) * TILE)
        part = transposed_product(hidden_ref[:, columns], branch_ref[...])
        for k in range(tile_shards):
            slot = slot_of(i * tile_shards + k, count)
            first[slot, 0:deep, :] = part[k * deep : (k + 1) * deep].astype(bf16)
        part = transposed_product(normed_two_ref[...], upward_ref[:, columns])
        chunk, at = i * TILE // width, i * TILE % width
        store_rows(second, part, count, chunk * shard, slice(at, at + TILE))
    part = transposed_product(attended_ref[...], attend_branch_ref[...])
    store_rows(first, part, count, deep)
    targets = ((first, deep + shard), (second, deep), (second, deep + shard))
    for chunk, (target, start) in enumerate(targets):
        columns = slice(chunk * width, (chunk + 1) * width)
        part = transposed_product(normed_ref[...], grad_mixed_ref[:, columns])
        store_rows(target, part, count, start)
    small = jnp.concatenate([small_ref[...], jnp.zeros((room - 4, width), f32)], axis=0)
    for q in range(GROUPS):
        first[q, deep + 2 * shard :, :] = jnp.zeros((room, width), bf16)
        second[q, deep + 2 * shard :, :] = small.astype(bf16)


def global_sums_of(count, *arrays):
    hidden, branch = arrays[:2]
    hidden_width, width = hidden.shape[1], branch.shape[1]
    block = hidden_width // GROUPS + (2 * width + VOCAB) // GROUPS
    sums = jax.ShapeDtypeStruct((GROUPS, block, width), bf16)
    return pl.pallas_call(
        partial(global_sums_kernel, count),
        out_shape=[sums, sums],
        compiler_params=pltpu.CompilerParams(vmem_limit_bytes=VMEM),
        cost_estimate=cost(14),
    )(*arrays)


def causal_bias(start, count, numbers_ref):
    spans = item_spans(numbers_ref, 1, numbers_ref[0])
    rows = lax.broadcasted_iota(jnp.int32, (BLOCK, 1), 0) + start
    columns = lax.broadcasted_iota(jnp.int32, (1, count), 1)
    same = owner_of(rows * PATCH, spans) == owner_of(columns * PATCH, spans)
    bias = jnp.where((columns <= rows) & same, 0.0, MASKED)
    return jnp.concatenate([bias, bias], axis=0)


def global_forward_kernel(numbers_ref, qkv_ref, out_ref):
    start = pl.multiple_of(pl.program_id(0) * BLOCK, BLOCK)
    bias = causal_bias(start, qkv_ref.shape[0], numbers_ref)
    out_ref[...] = pair_forward(
        qkv_ref[pl.ds(start, BLOCK), 0:PAIR],
        qkv_ref[:, PAIR : 2 * PAIR],
        qkv_ref[:, 2 * PAIR : 3 * PAIR],
        bias,
        lane_masks(),
    ).astype(bf16)


def global_backward_kernel(numbers_ref, qkv_ref, grad_ref, out_ref, key_sum, value_sum):
    step = pl.program_id(0)
    start = pl.multiple_of(step * BLOCK, BLOCK)
    bias = causal_bias(start, qkv_ref.shape[0], numbers_ref)

    @pl.when(step == 0)
    def _():
        key_sum[...] = jnp.zeros_like(key_sum)
        value_sum[...] = jnp.zeros_like(value_sum)

    queries, keys = qkv_ref[pl.ds(start, BLOCK), 0:PAIR], qkv_ref[:, PAIR : 2 * PAIR]
    masks = lane_masks()
    grad_queries, grad_keys, grad_values = pair_backward(
        queries,
        keys,
        qkv_ref[:, 2 * PAIR : 3 * PAIR],
        grad_ref[...],
        pair_probabilities(queries, keys, bias, masks),
        masks,
    )
    out_ref[pl.ds(start, BLOCK), 0:PAIR] = grad_queries.astype(bf16)
    key_sum[...] += grad_keys
    value_sum[...] += grad_values

    @pl.when(step == pl.num_programs(0) - 1)
    def _():
        out_ref[:, PAIR : 2 * PAIR] = key_sum[...].astype(bf16)
        out_ref[:, 2 * PAIR : 3 * PAIR] = value_sum[...].astype(bf16)


def global_attention(qkv, numbers, grads=None, deps=()):
    count = qkv.shape[0]
    specs = [
        SCALARS,
        pl.BlockSpec((count, 3 * PAIR), lambda i: (0, 0)),
    ]
    blocks = pl.BlockSpec((BLOCK, PAIR), lambda i: (i, 0))
    if grads is None:
        return pl.pallas_call(
            global_forward_kernel,
            grid=(count // BLOCK,),
            in_specs=specs,
            out_specs=blocks,
            out_shape=jax.ShapeDtypeStruct((count, PAIR), bf16),
            compiler_params=pltpu.CompilerParams(vmem_limit_bytes=VMEM),
            cost_estimate=cost(15),
        )(numbers, qkv)

    def body(*refs):
        global_backward_kernel(*refs[:3], *refs[3 + len(deps) :])

    return pl.pallas_call(
        body,
        grid=(count // BLOCK,),
        in_specs=specs + [blocks] + [ANY] * len(deps),
        out_specs=pl.BlockSpec((count, 3 * PAIR), lambda i: (0, 0)),
        out_shape=jax.ShapeDtypeStruct((count, 3 * PAIR), bf16),
        scratch_shapes=[pltpu.VMEM((count, PAIR), f32), pltpu.VMEM((count, PAIR), f32)],
        compiler_params=pltpu.CompilerParams(vmem_limit_bytes=VMEM),
        cost_estimate=cost(30),
    )(numbers, qkv, grads, *deps)


def call(kernel, args, specs, out_shape, out_specs, scratch=(), deps=(), micros=1):
    count = len(args)

    def body(*refs):
        kernel(*refs[:count], *refs[count + len(deps) :])

    return pl.pallas_call(
        body,
        in_specs=list(specs) + [ANY] * len(deps),
        out_specs=out_specs,
        out_shape=out_shape,
        scratch_shapes=list(scratch),
        compiler_params=pltpu.CompilerParams(vmem_limit_bytes=VMEM),
        cost_estimate=cost(micros),
    )(*args, *deps)


def shaped(*shape, kind=bf16):
    return jax.ShapeDtypeStruct(shape, kind)


def patch_forward(numbers, patch_rows, byte_rows, own_table, new_table, pieces, deps=()):
    batches, width = byte_rows[0].shape[0], own_table.shape[1]
    segments = len(byte_rows) * batches
    rows = segments * patch_rows
    shard = pieces[0].shape[0]
    span, count = len(pieces), len(byte_rows)
    room = (segments + 15) // 16 * 16

    def kernel(numbers_ref, own_ref, new_ref, *rest):
        byte_refs, piece_refs, rest = rest[:count], rest[count : count + span], rest[count + span :]
        embedded_ref, weight_ref, share_ref, low_ref, onehot_ref, table_ref = rest
        member_now = numbers_ref[1]
        for k in range(span):
            start = pl.multiple_of((member_now ^ k) * shard, shard)
            weight_ref[pl.ds(start, shard), :] = piece_refs[k][...]

        @pl.when(numbers_ref[0] == 0)
        def _():
            table_ref[...] = own_ref[...]

        @pl.when(numbers_ref[0] != 0)
        def _():
            table_ref[...] = new_ref[...]

        some = [ref[...].astype(f32) for ref in byte_refs]
        some.append(jnp.zeros((room - segments, some[0].shape[1]), f32))
        some = jnp.concatenate(some, axis=0).astype(bf16)
        shape = (some.shape[1], rows)
        place = lax.broadcasted_iota(jnp.int32, shape, 1) % patch_rows * PATCH + numbers_ref[2]
        picked = lax.broadcasted_iota(jnp.int32, shape, 0) == place
        wide = product(some, jnp.where(picked, 1.0, 0.0).astype(bf16))
        segment = lax.broadcasted_iota(jnp.int32, (room, rows), 1) // patch_rows
        here = lax.broadcasted_iota(jnp.int32, (room, rows), 0) == segment
        ids = jnp.sum(jnp.where(here, wide, 0.0), axis=0, keepdims=True).astype(jnp.int32)
        vocabulary = lax.broadcasted_iota(jnp.int32, (VOCAB, rows), 0)
        onehot = jnp.where(ids == vocabulary, 1.0, 0.0).astype(bf16)
        onehot_ref[...] = onehot
        embedded_ref[...] = transposed_product(onehot, table_ref[...]).astype(bf16)
        share = product(embedded_ref[...], weight_ref[...])
        share_ref[...] = share
        low_ref[...] = share.astype(bf16)

    return call(
        kernel,
        (numbers, own_table, new_table, *byte_rows, *pieces),
        [SCALARS] + [WHOLE] * (2 + count + span),
        [
            shaped(rows, width),
            shaped(span * shard, width),
            shaped(rows, width, kind=f32),
            shaped(rows, width),
            shaped(VOCAB, rows),
        ],
        [WHOLE] * 5,
        [pltpu.VMEM(own_table.shape, bf16)],
        deps=deps,
        micros=4,
    )


def split_heads(values, targets, batches, part):
    patch_rows = values.shape[0] // batches
    first = targets[0].shape[0]
    for t in range(batches * PAIRS):
        m, pair = t // PAIRS, t % PAIRS
        target = targets[0].at[t] if t < first else targets[1].at[t - first]
        target[:, part * PAIR : (part + 1) * PAIR] = values[
            m * patch_rows : (m + 1) * patch_rows, pair * PAIR : (pair + 1) * PAIR
        ]


def task_shapes(batches, first, patch_rows, columns):
    rest = batches * PAIRS - first
    return [shaped(first, patch_rows, columns)] + ([shaped(rest, patch_rows, columns)] if rest else [])


def merge_heads(blocks, target, batches, parts):
    patch_rows = target.shape[0] // batches
    width = PAIRS * PAIR
    for t in range(batches * PAIRS):
        m, pair = t // PAIRS, t % PAIRS
        first = blocks[0].shape[0]
        block = blocks[0].at[t] if t < first else blocks[1].at[t - first]
        for part in range(parts):
            at = part * width + pair * PAIR
            target[m * patch_rows : (m + 1) * patch_rows, at : at + PAIR] = block[
                :, part * PAIR : (part + 1) * PAIR
            ]


def strided(values, target, span, offset):
    size = values.shape[1] // (4 * span)
    for k in range(span):
        parts = [
            values[:, (group * span + k) * size : (group * span + k + 1) * size]
            for group in range(4)
        ]
        target[k, :, offset : offset + 4 * size] = jnp.concatenate(parts, axis=1)


def global_start(batches, first_tasks, own, others, gains, biases, heads_in):
    rows, width = own.shape
    patch_rows = rows // batches
    tasks = task_shapes(batches, first_tasks, patch_rows, 3 * PAIR)

    def kernel(own_ref, gains_ref, biases_ref, weight_hbm, *rest):
        other_refs, rest = rest[: len(others)], rest[len(others) :]
        (stream_ref, normed_ref, share_ref), task_refs = rest[:3], rest[3 : 3 + len(tasks)]
        weight, sem = rest[3 + len(tasks) :]
        load = pltpu.make_async_copy(weight_hbm, weight, sem)
        load.start()
        stream = own_ref[...]
        for ref in other_refs:
            stream = stream + ref[...].astype(f32)
        stream_ref[...] = stream
        normed = layer_norm(stream, gains_ref[0:1], biases_ref[0:1]).astype(bf16)
        normed_ref[...] = normed
        strided(normed, share_ref, SPAN, 0)
        load.wait()
        for part in range(3):
            mixed = product(normed, weight[:, part * width : (part + 1) * width]).astype(bf16)
            split_heads(mixed, task_refs, batches, part)

    return call(
        kernel,
        (own, gains, biases, heads_in, *others),
        [WHOLE] * 3 + [ANY] + [WHOLE] * len(others),
        [
            shaped(rows, width, kind=f32),
            shaped(rows, width),
            shaped(SPAN, rows, width // SPAN),
            *tasks,
        ],
        [WHOLE] * (3 + len(tasks)),
        [pltpu.VMEM(heads_in.shape, bf16), pltpu.SemaphoreType.DMA],
        micros=5,
    )


def global_feed_forward(batches, blocks, stream, gains, biases, heads_out, expand, contract):
    rows, width = stream.shape
    hidden_width = expand.shape[1]
    n = len(blocks)
    patch_rows = rows // batches
    half = patch_rows // 2

    def kernel(stream_ref, gains_ref, biases_ref, out_hbm, expand_hbm, contract_hbm, *rest):
        block_refs, rest = rest[:n], rest[n:]
        (attended_ref, middle_ref, normed_two_ref, slope_ref, hidden_ref, sent_ref) = rest[:6]
        share_ref, other_share_ref, edge_ref, near_ref, w_out, w_expand, w_contract, sems = rest[6:]
        loads = [
            pltpu.make_async_copy(out_hbm, w_out, sems.at[0]),
            pltpu.make_async_copy(expand_hbm, w_expand, sems.at[1]),
            pltpu.make_async_copy(contract_hbm, w_contract, sems.at[2]),
        ]
        for load in loads:
            load.start()
        merge_heads(block_refs, attended_ref, batches, 1)
        loads[0].wait()
        middle = stream_ref[...] + product(attended_ref[...], w_out[...])
        middle_ref[...] = middle
        normed_two_ref[...] = layer_norm(middle, gains_ref[1:2], biases_ref[1:2]).astype(bf16)
        loads[1].wait()

        @pl.loop(0, hidden_width // width, unroll=True)
        def _(i):
            at = pl.ds(pl.multiple_of(i * width, 128), width)
            hidden, slope = gelu_and_slope(product(normed_two_ref[...], w_expand[:, at]))
            hidden_ref[:, at] = hidden.astype(bf16)
            slope_ref[:, at] = slope.astype(bf16)

        loads[2].wait()
        result = middle_ref[...] + product(hidden_ref[...], w_contract[...])
        sent = result.astype(bf16)
        sent_ref[...] = sent
        edge_ref[...] = jnp.zeros(edge_ref.shape, bf16)
        for m in range(batches):
            stop = (m + 1) * patch_rows
            edge_ref[m : m + 1, :] = sent[stop - 1 : stop]
            near_ref[m * half : (m + 1) * half, :] = sent[stop - half - 1 : stop - 1]
        strided(hidden_ref[...], share_ref, SPAN, 0)
        strided(normed_two_ref[...], other_share_ref, SPAN, 0)
        strided(attended_ref[...], other_share_ref, SPAN, width // SPAN)

    return call(
        kernel,
        (stream, gains, biases, heads_out, expand, contract, *blocks),
        [WHOLE] * 3 + [ANY] * 3 + [WHOLE] * n,
        [
            shaped(rows, width),
            shaped(rows, width, kind=f32),
            shaped(rows, width),
            shaped(rows, hidden_width),
            shaped(rows, hidden_width),
            shaped(rows, width),
            shaped(SPAN, rows, hidden_width // SPAN),
            shaped(SPAN, rows, 2 * width // SPAN),
            shaped(SMALL_ROWS, width),
            shaped(batches * half, width),
        ],
        [WHOLE] * 10,
        [
            pltpu.VMEM(heads_out.shape, bf16),
            pltpu.VMEM(expand.shape, bf16),
            pltpu.VMEM(contract.shape, bf16),
            pltpu.SemaphoreType.DMA((3,)),
        ],
        micros=8,
    )


def global_feed_backward(
    batches, first_tasks, own, near, edge, middle, slope, gains, heads_out, expand, contract, deps=()
):
    rows, width = middle.shape
    hidden_width = expand.shape[1]
    patch_rows = rows // batches
    half = patch_rows // 2
    tasks = task_shapes(batches, first_tasks, patch_rows, PAIR)

    def kernel(
        own_ref, near_ref, edge_ref, middle_ref, slope_ref, gains_ref, out_hbm, expand_hbm,
        contract_hbm, upward_ref, grad_middle_ref, branch_ref, small_ref, grad_ref, *rest,
    ):
        task_refs, (w_out, w_expand, w_contract, sems) = rest[: len(tasks)], rest[len(tasks) :]
        loads = [
            pltpu.make_async_copy(contract_hbm, w_contract, sems.at[2]),
            pltpu.make_async_copy(expand_hbm, w_expand, sems.at[1]),
            pltpu.make_async_copy(out_hbm, w_out, sems.at[0]),
        ]
        for load in loads:
            load.start()
        source = jnp.concatenate([own_ref[...], near_ref[...], edge_ref[...]], axis=0)
        index = lax.broadcasted_iota(jnp.int32, (rows, 1), 0)
        batch, place = index // patch_rows, index % patch_rows
        chosen = jnp.where(
            place < half - 1,
            batch * half + place + 1,
            jnp.where(
                place < patch_rows - 1,
                batches * half + batch * half + place - (half - 1),
                2 * batches * half + batch,
            ),
        )
        columns = lax.broadcasted_iota(jnp.int32, (rows, source.shape[0]), 1)
        picked = jnp.where(columns == chosen, 1.0, 0.0).astype(bf16)
        grad_ref[...] = product(picked, source).astype(bf16)
        loads[0].wait()

        @pl.loop(0, hidden_width // width, unroll=True)
        def _(i):
            at = pl.ds(pl.multiple_of(i * width, 128), width)
            grad_hidden = product_transposed(grad_ref[...], w_contract[at, :])
            upward_ref[:, at] = (grad_hidden * slope_ref[:, at].astype(f32)).astype(bf16)

        loads[1].wait()
        grad_normed = product_transposed(upward_ref[...], w_expand[...])
        back, gain, bias = layer_norm_back(middle_ref[...], gains_ref[1:2], grad_normed)
        grad_middle = back + grad_ref[...].astype(f32)
        grad_middle_ref[...] = grad_middle
        branch = grad_middle.astype(bf16)
        branch_ref[...] = branch
        small_ref[...] = jnp.concatenate([gain, bias], axis=0)
        loads[2].wait()
        attended = product_transposed(branch, w_out[...]).astype(bf16)
        split_heads(attended, task_refs, batches, 0)

    return call(
        kernel,
        (own, near, edge, middle, slope, gains, heads_out, expand, contract),
        [WHOLE] * 6 + [ANY] * 3,
        [
            shaped(rows, hidden_width),
            shaped(rows, width, kind=f32),
            shaped(rows, width),
            shaped(2, width, kind=f32),
            shaped(rows, width),
            *tasks,
        ],
        [WHOLE] * (5 + len(tasks)),
        [
            pltpu.VMEM(heads_out.shape, bf16),
            pltpu.VMEM(expand.shape, bf16),
            pltpu.VMEM(contract.shape, bf16),
            pltpu.SemaphoreType.DMA((3,)),
        ],
        deps=deps,
        micros=10,
    )


def global_end(batches, blocks, stream, grad_middle, small, gains, heads_in, deps=()):
    rows, width = stream.shape
    n = len(blocks)

    def kernel(stream_ref, grad_middle_ref, small_ref, gains_ref, weight_hbm, *rest):
        block_refs, (mixed_ref, low_ref, all_small_ref, weight, sem) = rest[:n], rest[n:]
        load = pltpu.make_async_copy(weight_hbm, weight, sem)
        load.start()
        merge_heads(block_refs, mixed_ref, batches, 3)
        load.wait()
        grad_normed = product_transposed(mixed_ref[...], weight[...])
        back, gain, bias = layer_norm_back(stream_ref[...], gains_ref[0:1], grad_normed)
        low_ref[0:rows, :] = (back + grad_middle_ref[...]).astype(bf16)
        smalls = jnp.concatenate([gain, small_ref[0:1], bias, small_ref[1:2]], axis=0)
        all_small_ref[...] = smalls
        rest = jnp.zeros((SMALL_ROWS - 4, width), f32)
        low_ref[rows:, :] = jnp.concatenate([smalls, rest], axis=0).astype(bf16)

    return call(
        kernel,
        (stream, grad_middle, small, gains, heads_in, *blocks),
        [WHOLE] * 4 + [ANY] + [WHOLE] * n,
        [
            shaped(rows, 3 * width),
            shaped(rows + SMALL_ROWS, width),
            shaped(4, width, kind=f32),
        ],
        [WHOLE] * 3,
        [pltpu.VMEM(heads_in.shape, bf16), pltpu.SemaphoreType.DMA],
        deps=deps,
        micros=6,
    )


def patch_backward(section, onehot, embedded, weight, own, crossed, span, deps=()):
    rows, width = embedded.shape
    block = own[0].shape[0]
    n = len(own)
    used = rows // n
    shard = weight.shape[0] // span

    def kernel(section_ref, onehot_ref, embedded_ref, weight_ref, crossed_ref, *rest):
        own_refs, (patch_ref, table_ref, gathered, small) = rest[:n], rest[n:]

        @pl.when(section_ref[0] == 0)
        def _():
            for k in range(n):
                gathered[k * used : (k + 1) * used, :] = own_refs[k][0:used, :]
            total = sum(ref[used:, :].astype(f32) for ref in own_refs)
            small[...] = total.astype(bf16)

        @pl.when(section_ref[0] != 0)
        def _():
            for k in range(n):
                gathered[k * used : (k + 1) * used, :] = crossed_ref[k * block : k * block + used, :]
            small[...] = jnp.zeros_like(small)

        part = transposed_product(embedded_ref[...], gathered[...]).astype(bf16)
        for k in range(span):
            patch_ref[k, 0:shard, :] = part[k * shard : (k + 1) * shard]
            patch_ref[k, shard:, :] = small[...]
        grad_embedded = product_transposed(gathered[...], weight_ref[...]).astype(bf16)
        table_ref[...] = product(onehot_ref[...], grad_embedded).astype(bf16)

    return call(
        kernel,
        (section, onehot, embedded, weight, crossed, *own),
        [SCALARS] + [WHOLE] * (4 + n),
        [shaped(span, shard + SMALL_ROWS, width), shaped(VOCAB, width)],
        [WHOLE] * 2,
        [pltpu.VMEM((rows, width), bf16), pltpu.VMEM((SMALL_ROWS, width), bf16)],
        deps=deps,
        micros=6,
    )


def leave_by_group(group, buffer, targets, sems):
    for j in range(len(targets)):
        for k in range(len(targets)):

            @pl.when((group ^ j) == k)
            def _(j=j, k=k):
                pltpu.make_async_copy(buffer.at[j], targets[k], sems.at[k]).start()

    for k in range(len(targets)):
        pltpu.make_async_copy(buffer.at[0], targets[k], sems.at[k]).wait()


def pack_columns(hidden_width, width):
    deep, thin = hidden_width // SPAN, width // SPAN
    first = [
        (slice(0, deep), slice(deep, deep + width)),
        (slice(deep + width, deep + width + thin), slice(deep + width + thin, deep + 4 * width + thin)),
    ]
    right = 2 * thin
    second = [
        (slice(0, thin), slice(right, right + hidden_width)),
        (slice(thin, right), slice(right + hidden_width, right + hidden_width + width)),
    ]
    return first, second, max(first[-1][1].stop, second[-1][1].stop)


def pack_second(member, share, attend_branch, upward, whole, deps=()):
    rows, width = attend_branch.shape
    own, hidden_width = share.shape[2], upward.shape[1]

    def kernel(member_ref, share_ref, attend_ref, upward_ref, out_ref):
        for k in range(SPAN):
            out_ref[k, :, 0:own] = share_ref[member_ref[0] ^ k]
            out_ref[k, :, own : own + hidden_width] = upward_ref[...]
            out_ref[k, :, own + hidden_width : own + hidden_width + width] = attend_ref[...]

    return call(
        kernel,
        (member, share, attend_branch, upward),
        [SCALARS] + [WHOLE] * 3,
        shaped(SPAN, rows, whole),
        WHOLE,
        deps=deps,
        micros=3,
    )


def pack(section, member, share, normed_share, branch, mixed, second, passed, deps=()):
    rows, width = branch.shape
    deep, thin, whole = share.shape[2], normed_share.shape[2], second.shape[2]

    def kernel(
        section_ref, member_ref, share_ref, normed_ref, branch_ref, mixed_ref, passed_ref,
        second_ref, *rest,
    ):
        sent_refs, same_ref, sems = rest[:SPAN], rest[SPAN], rest[SPAN + 1]
        same_ref[...] = passed_ref[...]

        @pl.when(section_ref[0] == 0)
        def _():
            for k in range(SPAN):
                sent_refs[k][:, 0:deep] = share_ref[member_ref[0] ^ k]
                sent_refs[k][:, deep : deep + width] = branch_ref[...]
                sent_refs[k][:, deep + width : deep + width + thin] = normed_ref[member_ref[0] ^ k]
                sent_refs[k][:, deep + width + thin : deep + 4 * width + thin] = mixed_ref[...]

        @pl.when(section_ref[0] != 0)
        def _():
            copies = [
                pltpu.make_async_copy(second_ref.at[k], sent_refs[k], sems.at[k])
                for k in range(SPAN)
            ]
            for copy in copies:
                copy.start()
            for copy in copies:
                copy.wait()

    return call(
        kernel,
        (section, member, share, normed_share, branch, mixed, passed, second),
        [SCALARS] * 2 + [WHOLE] * 5 + [ANY],
        [shaped(rows, whole)] * SPAN + [shaped(*passed.shape)],
        [WHOLE] * (SPAN + 1),
        [pltpu.SemaphoreType.DMA((SPAN,))],
        deps=deps,
        micros=4,
    )


def plane_gradients(section, group, sent, hidden_width, width, deps=()):
    halves = pack_columns(hidden_width, width)[:2]
    rows_of = [
        sum(
            (left.stop - left.start) // 4 * ((right.stop - right.start) // width)
            for left, right in pairs
        )
        for pairs in halves
    ]
    block, short = max(rows_of), rows_of[1]

    def kernel(section_ref, group_ref, *refs):
        sent_refs, (keep_ref, leave_ref, short_ref, buffer, sems) = refs[: len(sent)], refs[len(sent) :]

        def columns(at):
            return jnp.concatenate([ref[:, at] for ref in sent_refs], axis=0)

        def fill(pairs):
            start = 0
            for left, right in pairs:
                former, size = columns(left), (left.stop - left.start) // 4
                for first in range(right.start, right.stop, width):
                    part = transposed_product(former, columns(slice(first, first + width)))
                    for j in range(4):
                        buffer[j, start : start + size, :] = part[
                            j * size : (j + 1) * size
                        ].astype(bf16)
                    start += size
            if start < block:
                for j in range(4):
                    buffer[j, start:block, :] = jnp.zeros((block - start, width), bf16)

        @pl.when(section_ref[0] == 0)
        def _():
            fill(halves[0])

        @pl.when(section_ref[0] != 0)
        def _():
            fill(halves[1])

        def moves(j):
            mine = ((group_ref[0] ^ j) & 1) == 0
            other = jnp.logical_not(mine)
            sem = sems.at[j]
            return (
                (mine, pltpu.make_async_copy(buffer.at[j], keep_ref.at[j >> 1], sem)),
                (
                    other & (section_ref[0] == 0),
                    pltpu.make_async_copy(buffer.at[j], leave_ref.at[j >> 1], sem),
                ),
                (
                    other & (section_ref[0] != 0),
                    pltpu.make_async_copy(buffer.at[j, 0:short], short_ref.at[j >> 1], sem),
                ),
            )

        for j in range(4):
            for when, copy in moves(j):
                pl.when(when)(copy.start)
        for j in range(4):
            for when, copy in moves(j):
                pl.when(when)(copy.wait)

    return call(
        kernel,
        (section, group, *sent),
        [SCALARS] * 2 + [WHOLE] * len(sent),
        [shaped(2, block, width), shaped(2, block, width), shaped(2, short, width)],
        [ANY] * 3,
        [pltpu.VMEM((4, block, width), bf16), pltpu.SemaphoreType.DMA((4,))],
        deps=deps,
        micros=6,
    )


def by_parity(parity, sums, deps=()):
    count, rows, width = sums.shape

    def kernel(parity_ref, sums_ref, *rest):
        rest[-1][...] = sums_ref[...]

    block = (1, rows, width)
    return pl.pallas_call(
        kernel,
        grid_spec=pltpu.PrefetchScalarGridSpec(
            num_scalar_prefetch=1,
            grid=(count // 2,),
            in_specs=[pl.BlockSpec(block, lambda i, ref: (2 * i + 1 - ref[0], 0, 0))]
            + [ANY] * len(deps),
            out_specs=pl.BlockSpec(block, lambda i, ref: (i, 0, 0)),
        ),
        out_shape=shaped(count // 2, rows, width),
        compiler_params=pltpu.CompilerParams(vmem_limit_bytes=VMEM),
        cost_estimate=cost(3),
    )(parity, sums, *deps)


def half_sums(flags, kept, near, deps=()):
    shape = kept.shape[1:]
    every = kept.shape[0] == 4

    def kernel(flags_ref, kept_ref, near_ref, far_ref, mine_ref):
        for k in range(2):
            own = kept_ref[2 * k + flags_ref[2]] if every else kept_ref[k]
            total = (own.astype(f32) + near_ref[k].astype(f32)).astype(bf16)

            @pl.when(flags_ref[1] == k)
            def _():
                mine_ref[...] = total

            @pl.when(flags_ref[1] != k)
            def _():
                far_ref[...] = total

    return call(
        kernel,
        (flags, kept, near),
        [SCALARS, WHOLE, WHOLE],
        [shaped(*shape)] * 2,
        [WHOLE] * 2,
        deps=deps,
        micros=2,
    )


def half_sums_and_cross(flags, kept, near, near_short, other, other_far, deps=()):
    shape = kept.shape[1:]
    held, short = other.shape[0], near_short.shape[1]

    def kernel(
        flags_ref, kept_ref, near_ref, low_ref, other_ref, more_ref,
        far_ref, short_ref, mine_ref, cross_ref,
    ):
        for k in range(2):
            total = kept_ref[k].astype(f32) + near_ref[k].astype(f32)
            low = total[0:short] + low_ref[k].astype(f32)
            total = jnp.concatenate([low, total[short:]], axis=0).astype(bf16)

            @pl.when(flags_ref[1] == k)
            def _():
                mine_ref[...] = total
                cross_ref[...] = total

            @pl.when(flags_ref[1] != k)
            def _():
                far_ref[...] = total
                short_ref[...] = total[0:short]

        @pl.when(flags_ref[0] == 0)
        def _():
            total = other_ref[...].astype(f32) + more_ref[...].astype(f32)
            cross_ref[0:held, :] = total.astype(bf16)

    return call(
        kernel,
        (flags, kept, near, near_short, other, other_far),
        [SCALARS] + [WHOLE] * 5,
        [shaped(*shape), shaped(short, shape[1]), shaped(*shape), shaped(*shape)],
        [WHOLE] * 4,
        deps=deps,
        micros=2,
    )


def finish(section, deep, shard, room, own_global, own_local, crossed, fars, table_parts, patch_parts):
    width = own_local.shape[1]
    chunks = deep // shard
    p = len(patch_parts)

    def kernel(section_ref, global_ref, local_ref, crossed_ref, table_ref, *refs):
        (global_one, global_two, local_two), refs = refs[:3], refs[3:]
        patch_refs = refs[:p]
        contract, expand, ins, out, table, small, patch = refs[p:]

        def total(some, start, size):
            return sum(ref[start : start + size, :].astype(f32) for ref in some)

        total_patch = sum(ref[...].astype(f32) for ref in patch_refs)
        patch[...] = total_patch[: patch.shape[0]]

        @pl.when(section_ref[0] == 0)
        def _():
            one, two = (global_ref, global_one), (crossed_ref, global_two)
            contract[...] = total(one, 0, deep)
            for c in range(3):
                ins[:, c * width : (c + 1) * width] = total(one, deep + c * shard, shard)
            for c in range(chunks):
                expand[:, c * width : (c + 1) * width] = total(two, c * shard, shard)
            out[...] = total(two, chunks * shard, shard)
            small[...] = total_patch[patch.shape[0] :]
            sums = jnp.zeros((room, width), f32)
            for k in range(table_ref.shape[0]):
                sums = sums + table_ref[k].astype(f32)
            table[...] = sums

        @pl.when(section_ref[0] != 0)
        def _():
            one, two = (crossed_ref,), (local_ref, local_two)
            contract[...] = total(one, 0, deep)
            out[...] = total(one, deep, shard)
            ins[:, 0:width] = total(one, deep + shard, shard)
            table[...] = total(one, deep + 2 * shard, room)
            for c in range(chunks):
                expand[:, c * width : (c + 1) * width] = total(two, c * shard, shard)
            for c in range(2):
                ins[:, (c + 1) * width : (c + 2) * width] = total(two, deep + c * shard, shard)
            small[...] = total(two, deep + 2 * shard, small.shape[0])

    return call(
        kernel,
        (section, own_global, own_local, crossed, table_parts, *fars, *patch_parts),
        [SCALARS] + [WHOLE] * (7 + p),
        [
            shaped(deep, width, kind=f32),
            shaped(shard, chunks * width, kind=f32),
            shaped(shard, 3 * width, kind=f32),
            shaped(shard, width, kind=f32),
            shaped(room, width, kind=f32),
            shaped(SMALL_ROWS, width, kind=f32),
            shaped(patch_parts[0].shape[0] - SMALL_ROWS, width, kind=f32),
        ],
        [WHOLE] * 7,
        micros=4,
    )


def activation_rows(numbers, sent, other, own, deps=()):
    batches, half, width = own.shape
    patch_rows = sent.shape[0] // batches
    byte_rows = patch_rows * PATCH

    def kernel(numbers_ref, sent_ref, other_ref, own_ref, out_ref):
        @pl.when(numbers_ref[0] == 0)
        def _():
            rows = lax.broadcasted_iota(jnp.int32, (byte_rows, 1), 0)
            columns = lax.broadcasted_iota(jnp.int32, (byte_rows, patch_rows), 1)
            for m in range(batches):
                live = is_live(numbers_ref[1] + rows, item_spans(numbers_ref, 3, m))
                chosen = jnp.where(live, rows // PATCH, -1)
                spread = jnp.where(columns == chosen, 1.0, 0.0).astype(bf16)
                part = sent_ref[m * patch_rows : (m + 1) * patch_rows, :]
                out_ref[m] = product(spread, part).astype(bf16)

        @pl.when(numbers_ref[0] != 0)
        def _():
            for m in range(batches):
                out_ref[m, 0:half, :] = other_ref[m]
                out_ref[m, half:, :] = own_ref[m]

    return call(
        kernel,
        (numbers, sent, other, own),
        [SCALARS] + [WHOLE] * 3,
        shaped(batches, byte_rows, width),
        WHOLE,
        deps=deps,
        micros=2,
    )


SEQ = ("group", "member")


def section_send(x, origin, target, pairs):
    count = lax.axis_size(SEQ)
    joint = [(origin * count + i, target * count + j) for i, j in pairs]
    return lax.ppermute(x, ("section",) + SEQ, joint)


def section_swap(x):
    return lax.ppermute(x, "section", [(0, 1), (1, 0)])


def by_slot(buffer, count, pieces):
    split = count // GROUPS
    parts, start = [], 0
    for size, shared in pieces:
        part = buffer[:, start : start + size]
        start += size
        kept = shared or size // split
        if shared:
            part = jnp.broadcast_to(part[:, None, :shared], (GROUPS, split, shared, part.shape[2]))
        parts.append(part.reshape(count, kept, part.shape[-1]))
    whole = jnp.concatenate(parts, axis=1)
    turned = whole.reshape((4, count // 4) + whole.shape[1:])
    return jnp.swapaxes(turned, 0, 1).reshape(whole.shape)


def place_sum(shares):
    shares = lax.psum_scatter(shares, "member", scatter_dimension=0, tiled=True)
    return lax.psum_scatter(shares, "group", scatter_dimension=0, tiled=True)[0]


def on_device(
    byte_values,
    item_lengths,
    embed_tables,
    patch_weight,
    norm_gains,
    norm_biases,
    heads_in,
    heads_out,
    expand_weight,
    contract_weight,
    out_grad,
):
    place = lax.axis_index(SEQ)
    count = lax.axis_size(SEQ)
    section = lax.axis_index("section")
    is_global = section == 0
    batches, byte_rows = byte_values.shape
    patch_rows = byte_rows // PATCH
    width = heads_out.shape[2]
    rows = batches * patch_rows
    total_patches = patch_rows * count
    gains, biases = norm_gains[0], norm_biases[0]
    heads_in, heads_out = heads_in[0], heads_out[0]
    expand, contract = expand_weight[0], contract_weight[0]
    own_table = embed_tables[0]
    straight = [(i, i) for i in range(count)]

    quarters = PATCH // 2
    span = count // quarters
    group, member = place // span, place % span
    shard_rows = patch_weight.shape[0]
    pieces = [patch_weight]
    for k in range(1, span):
        pieces.append(lax.ppermute(patch_weight, SEQ, [(i, i ^ k) for i in range(count)]))
    other_table = section_swap(own_table)
    theirs = [byte_values]
    for k in range(1, quarters):
        theirs.append(
            lax.ppermute(byte_values, SEQ, [(i, i ^ (k * span)) for i in range(count)])
        )
    place_numbers = jnp.stack([section, member, section * quarters + group]).astype(jnp.int32)
    embedded, byte_weight, shares, low_shares, byte_onehot = patch_forward(
        place_numbers, patch_rows, theirs, own_table, other_table, pieces
    )
    shares = shares + section_send(low_shares, 1, 0, straight).astype(f32)
    shares = shares.reshape(quarters, rows, width)
    parts = []
    for k in range(1, quarters):
        pairs = [(i, i ^ (k * span)) for i in range(count)]
        parts.append(section_send(shares[k].astype(bf16), 0, 0, pairs))

    arrived = [section_send(w, 1, 0, straight) for w in (heads_in, heads_out, expand, contract)]
    own_norms = jnp.concatenate([gains, biases])
    other_norms = section_swap(own_norms)

    tasks = batches * PAIRS
    first_tasks = min(tasks, count)
    spare_tasks = tasks - first_tasks

    def to_tasks(first, spare=None):
        columns = first.shape[2]
        slots = jnp.pad(first, ((0, count - first_tasks), (0, 0), (0, 0)))
        if spare_tasks:
            spare = section_send(spare, 0, 1, straight)
            spare = jnp.pad(spare, ((0, count - spare_tasks), (0, 0), (0, 0)))
            slots = jnp.where(is_global, slots, spare)
        landed = lax.all_to_all(slots, SEQ, 0, 0)
        return landed.reshape(total_patches, columns)

    def from_tasks(results):
        columns = results.shape[1]
        slots = lax.all_to_all(results.reshape(count, patch_rows, columns), SEQ, 0, 0)
        if spare_tasks:
            return [slots, section_send(slots[:spare_tasks], 1, 0, straight)]
        return [slots]

    task = jnp.minimum(jnp.where(is_global, place, first_tasks + place), tasks - 1)
    lengths = item_lengths.reshape(-1)
    task_numbers = jnp.concatenate([(task // PAIRS).reshape(1).astype(jnp.int32), lengths])

    stream, normed, normed_share, *tasks_out = global_start(
        batches, first_tasks, shares[0], parts, gains, biases, heads_in
    )
    qkv = to_tasks(*tasks_out)
    attended, middle, normed_two, slope, hidden, sent, feed_share, other_share, edge, near = global_feed_forward(
        batches,
        from_tasks(global_attention(qkv, task_numbers)),
        stream,
        gains,
        biases,
        heads_out,
        expand,
        contract,
    )
    half = patch_rows // 2
    half_bytes = half * PATCH
    chunks = half_bytes // BLOCK
    onward = [(i, i + 1) for i in range(count - 1)]
    backward = [(i + 1, i) for i in range(count - 1)]
    near = section_send(near, 0, 1, straight)
    edge = section_send(edge, 0, 0, onward)
    weights = (heads_in, heads_out, expand, contract)
    flag = section.reshape(1).astype(jnp.int32)
    block_patches = BLOCK // PATCH
    local_outs, activations_of, grads_shifted, grads_edge = [], [], [], []
    for c in range(chunks):
        numbers = jnp.concatenate(
            [
                jnp.stack([section, place * byte_rows, jnp.int32(c)]).astype(jnp.int32),
                lengths,
            ]
        )
        act, grad_shifted, grad_edge, keep, send = local_block(
            numbers,
            byte_values,
            (own_table, other_table),
            sent,
            edge,
            near,
            (own_norms, other_norms),
            out_grad,
            patch_rows,
            weights,
            arrived,
        )
        local_outs.append(act.reshape(batches, BLOCK, width))
        grads_shifted.append(grad_shifted.reshape(batches, block_patches, width))
        grads_edge.append(grad_edge)
        activations_of.append((numbers, keep, section_swap(send)))
    local_out = jnp.concatenate(local_outs, axis=1)
    grad_shifted = jnp.concatenate(grads_shifted, axis=1).reshape(batches * half, width)

    other_out = section_send(local_out, 0, 1, straight)
    activations = activation_rows(numbers, sent, other_out, local_out)

    shard = width // count
    room = VOCAB // count
    group_shard, group_room = width // GROUPS, VOCAB // GROUPS
    small_rows = max(4, room)
    pieces = {
        False: [(contract.shape[0] // GROUPS, 0), (group_shard, 0), (group_shard, 0), (group_room, 0)],
        True: [(group_shard, 0)] * (expand.shape[1] // width + 2) + [(group_room, small_rows)],
    }

    def ordered(buffer):
        if count == GROUPS:
            return buffer
        upper, lower = by_slot(buffer, count, pieces[False]), by_slot(buffer, count, pieces[True])
        rows_of = max(upper.shape[1], lower.shape[1])
        upper, lower = (
            jnp.pad(x, ((0, 0), (0, rows_of - x.shape[1]), (0, 0))) for x in (upper, lower)
        )
        return jnp.where(is_global, upper, lower)

    near_back = section_send(grad_shifted, 1, 0, straight)
    edge_back = section_send(grads_edge[0], 0, 0, backward)
    in_plane = span == SPAN and count == GROUPS
    member_flag = (member % SPAN).reshape(1).astype(jnp.int32)
    group_flag = group.reshape(1).astype(jnp.int32)

    def plane_send(blocks):
        return [blocks[0]] + [
            both_send(blocks[k], [(i, i ^ k) for i in range(count)]) for k in range(1, SPAN)
        ]

    upper = (group >> 1) & 1
    half_flags = jnp.stack([section, upper, group & 1]).astype(jnp.int32)

    def group_pairs(step):
        return [(i, i ^ (step * span)) for i in range(count)]

    def both_send(x, pairs):
        joint = [(s * count + i, s * count + j) for s in range(2) for i, j in pairs]
        return lax.ppermute(x, ("section",) + SEQ, joint)

    half_locals = [
        ordered(
            local_gradients(
                count,
                numbers,
                byte_values,
                keep,
                crossed,
                contract.shape[0],
                width,
                half_bytes,
                [near_back, edge_back],
            )
        )
        for numbers, keep, crossed in activations_of
    ]
    if chunks > 1:
        half_locals = [sum(x.astype(f32) for x in half_locals).astype(bf16)]
    half_locals = half_locals[0]
    grad_upward, grad_middle, attend_branch, small, grad_sent, *task_grads = global_feed_backward(
        batches,
        first_tasks,
        grad_shifted,
        near_back,
        edge_back,
        middle,
        slope,
        gains,
        heads_out,
        expand,
        contract,
        [half_locals],
    )
    if in_plane:
        whole = pack_columns(contract.shape[0], width)[2]
        second_parts = section_send(
            pack_second(member_flag, other_share, attend_branch, grad_upward, whole), 0, 1, straight
        )
    task_grads = to_tasks(*task_grads)
    task_mixed = global_attention(qkv, task_numbers, task_grads)
    grad_mixed, own_rows, small = global_end(
        batches,
        from_tasks(task_mixed),
        stream,
        grad_middle,
        small,
        gains,
        heads_in,
    )

    if in_plane:
        *sent_parts, own_rows = pack(
            flag, member_flag, feed_share, normed_share, grad_sent, grad_mixed, second_parts, own_rows
        )
        arrived_parts = plane_send(sent_parts)

    gathered = [own_rows]
    for k in range(1, quarters):
        pairs = [(i, i ^ (k * span)) for i in range(count)]
        gathered.append(section_send(own_rows, 0, 0, pairs))
    crossed = section_send(jnp.concatenate(gathered), 0, 1, straight)
    if in_plane:
        in_planes = lax.psum_scatter(half_locals, "member", scatter_dimension=0, tiled=True)
        parity_flag = (group & 1).reshape(1).astype(jnp.int32)
        local_leaving = by_parity(parity_flag, in_planes, [crossed])
        local_near = both_send(local_leaving, group_pairs(1))
    else:
        own_local = place_sum(half_locals)
    patch_share, table_share = patch_backward(
        flag,
        byte_onehot,
        embedded,
        byte_weight,
        gathered,
        crossed,
        span,
        [local_leaving] if in_plane else (),
    )
    patch_parts = [lax.dynamic_index_in_dim(patch_share, member, 0, keepdims=False)]
    for k in range(1, span):
        leaving = lax.dynamic_index_in_dim(patch_share, member ^ k, 0, keepdims=False)
        patch_parts.append(lax.ppermute(leaving, SEQ, [(i, i ^ k) for i in range(count)]))
    table_share = table_share + section_send(table_share, 1, 0, straight)
    table_parts = lax.all_to_all(table_share.reshape(count, VOCAB // count, width), SEQ, 0, 0)

    def ordered_rows(first, second):
        feed_rows = contract.shape[0] // count
        expand_sum = [second[k * shard : (k + 1) * shard] for k in range(feed_rows // shard)]
        rest, others = first[feed_rows:], second[feed_rows:]
        ins = [rest[shard : 2 * shard], others[:shard], others[shard : 2 * shard]]
        return (
            first[:feed_rows],
            jnp.concatenate(expand_sum, axis=1),
            jnp.concatenate(ins, axis=1),
            rest[:shard],
            rest[2 * shard : 2 * shard + room],
            others[2 * shard : 2 * shard + 4],
        )

    if in_plane:
        local_far, local_mine = half_sums(half_flags, in_planes, local_near)
        across = group_pairs(2)
        local_far = both_send(local_far, across)
        kept, leaving, leaving_short = plane_gradients(
            flag,
            group_flag,
            arrived_parts,
            contract.shape[0],
            width,
            [table_parts, local_far],
        )
        near = section_send(leaving, 0, 0, group_pairs(1))
        near_short = section_send(leaving_short, 1, 1, group_pairs(1))
        far, far_short, mine, crossed = half_sums_and_cross(
            half_flags, kept, near, near_short, local_mine, local_far, patch_parts[1:]
        )
        crossed = section_swap(crossed)
        fars = [
            section_send(far, 0, 0, across),
            section_send(far_short, 1, 0, across),
            local_far,
        ]
        contract_grad, expand_grad, in_grad, out_grads, table_grad, small, patch_grads = finish(
            flag,
            contract.shape[0] // count,
            shard,
            room,
            mine,
            local_mine,
            crossed,
            fars,
            table_parts,
            patch_parts,
        )
        small = small[:4]
    else:
        upper, lower = global_sums_of(
            count, hidden, grad_sent, normed_two, grad_upward, normed, grad_mixed, attended,
            attend_branch, small,
        )
        own_global = ordered(jnp.where(is_global, upper, section_send(lower, 0, 1, straight)))
        own_global = place_sum(own_global)
        crossed = section_swap(jnp.where(is_global, own_local, own_global)).astype(f32)
        global_sums = ordered_rows(own_global.astype(f32), crossed)
        global_table = jnp.sum(table_parts.astype(f32), axis=0)
        global_sums = global_sums[:4] + (global_table, global_sums[5])
        local_sums = ordered_rows(crossed, own_local.astype(f32))
        contract_grad, expand_grad, in_grad, out_grads, table_grad, small = (
            jnp.where(is_global, upper, lower) for upper, lower in zip(global_sums, local_sums)
        )
        patch_grads = sum(x.astype(f32) for x in patch_parts)[:shard_rows]
    small = lax.dynamic_slice_in_dim(small, place * shard, shard, 1)
    return (
        activations[None],
        table_grad[None],
        patch_grads,
        small[None, 0:2],
        small[None, 2:4],
        in_grad[None],
        out_grads[None],
        expand_grad[None],
        contract_grad[None],
    )


def solution(mesh):
    devices = mesh.devices
    groups = PATCH // 2
    split = jax.sharding.Mesh(
        devices.reshape(devices.shape[0], groups, devices.shape[1] // groups), ("section",) + SEQ
    )
    both = ("section",) + SEQ
    placed = (
        P(None, SEQ),
        P(),
        P("section", None, None),
        P(both, None),
        P("section", None, None),
        P("section", None, None),
        P("section", None, None),
        P("section", None, None),
        P("section", None, None),
        P("section", None, None),
        P(None, SEQ, None),
    )
    return jax.shard_map(
        on_device,
        mesh=split,
        in_specs=placed,
        out_specs=(
            P("section", None, SEQ, None),
            P("section", SEQ, None),
            P(both, None),
            P("section", None, SEQ),
            P("section", None, SEQ),
            P("section", SEQ, None),
            P("section", SEQ, None),
            P("section", SEQ, None),
            P("section", SEQ, None),
        ),
        check_vma=False,
    )
```
